32 devices in a mesh: seq: 4 (over z), exp: 8 (over y, x, core).
Axes of the slice: x: 2, y: 2, z: 4, core: 2. Of those that a mesh axis runs over, the one named last changes fastest.
Arguments:
- attn_query: bfloat16 [1024, 6144], P('seq', 'exp'), may hold values from -6 to 6
- attn_key: bfloat16 [1024, 6144], P('seq', 'exp'), may hold values from -6 to 6
- attn_value: bfloat16 [1024, 6144], P('seq', 'exp'), may hold values from -40 to 40
- log_decay: float32 [48, 1024], P('exp', 'seq'), may hold values from -1.5 to 0
- residual: bfloat16 [1024, 6144], P('seq', 'exp'), may hold values from -6 to 6
- norm_gain: bfloat16 [6144], P('exp'), may hold values from 0.099609375 to 1.8984375
- expert_ids: int32 [1024, 2], P('seq'), may hold values from 0 to 7, as said below
- router_weight: bfloat16 [6144, 8], P(None, 'seq'), may hold values from -0.078125 to 0.078125
- gate_weight: bfloat16 [8, 6144, 4608], P('seq', None, 'exp'), may hold values from -0.078125 to 0.078125
- up_weight: bfloat16 [8, 6144, 4608], P('seq', None, 'exp'), may hold values from -0.078125 to 0.078125
- down_weight: bfloat16 [8, 4608, 6144], P('seq', 'exp'), may hold values from -0.125 to 0.125
Outputs:
- layer_out: bfloat16 [1024, 6144], P('seq', 'exp')
The draws below stay inside these ranges and needn't reach their ends.
Inputs may be any that keep to these rules, and one draw needn't show every extreme that they name: `expert_ids`: each row names two different experts. In every section of 256 consecutive rows no expert is named more than 128 times, and in every section some experts are named exactly 128 times.
All inputs are finite; a program needn't handle non-finite values.
Results may differ from the reference program's by a relative error of at most 0.017.
Values may be sent and summed in bfloat16 or wider, within the bound.
No kernel may reach another device: no remote copies, remote signals or barrier semaphores. Data moves between devices by JAX's collectives and lax.ppermute only.
A program may use at most 192 MiB of HBM per device.

```python
import jax
import jax.numpy as jnp
from jax import lax

H = 48
DH = 128
D = 6144
FF = 4608
EXP_DEV = 2
EXPERTS = 8
TOPK = 2
SEC_TOK = 256
TOKEN_TOTAL = 1024
CAP = 128


def draw_attn_value(key, part):
    split_random_keys = jax.random.split(key, 3)
    column_scale = jnp.exp(jax.random.uniform(split_random_keys[1], (1, D), minval=0.0, maxval=jnp.log(10.0)))
    row_scale = jnp.exp(jax.random.uniform(split_random_keys[2], (TOKEN_TOTAL, 1), minval=0.0, maxval=jnp.log(10.0)))
    base_draw = jnp.clip(jax.random.normal(split_random_keys[0], (TOKEN_TOTAL, D)), -4.0, 4.0)
    return (0.1 * base_draw * column_scale * row_scale).astype(jnp.bfloat16)


def draw_log_decay(key, part):
    split_random_keys = jax.random.split(key, 6)
    fast_share = 0.5
    fast_head = jax.random.uniform(split_random_keys[0], (H, 1)) < fast_share
    fast_rate = jnp.exp(jax.random.uniform(split_random_keys[1], (H, 1), minval=jnp.log(1.0 / 50.0), maxval=jnp.log(1.0 / 30.0)))
    slow_rate = jnp.exp(jax.random.uniform(split_random_keys[2], (H, 1), minval=jnp.log(0.02 / TOKEN_TOTAL), maxval=jnp.log(0.3 / TOKEN_TOTAL)))
    baseline_rate = jnp.where(fast_head, fast_rate, slow_rate)
    jitter_level = jax.random.uniform(split_random_keys[3], (H, TOKEN_TOTAL), minval=0.5, maxval=1.5)
    spike_position = jax.random.randint(split_random_keys[4], (2, 1), 0, TOKEN_TOTAL)
    retained_fraction = jax.random.uniform(split_random_keys[5], (2, H, 1), minval=0.5, maxval=0.8)
    spike_location_mask = jnp.arange(TOKEN_TOTAL)[None, None, :] == spike_position[:, :, None]
    spike_amount = jnp.sum(jnp.where(spike_location_mask, jnp.log(retained_fraction), 0.0), axis=0)
    return (-baseline_rate * jitter_level + spike_amount).astype(jnp.float32)


def draw_expert_ids(key, part):
    sections = TOKEN_TOTAL // SEC_TOK
    entries = SEC_TOK * TOPK
    group_count = EXPERTS // EXP_DEV
    full_groups = max(1, 3 * group_count // 8)
    full_count = full_groups * EXP_DEV
    remaining = entries - full_count * CAP

    def one_section(section_key):
        first_key, second_key, third_key = jax.random.split(section_key, 3)
        group_order = jax.random.permutation(first_key, group_count).astype(jnp.int32)
        expert_order = (group_order[:, None] * EXP_DEV + jnp.arange(EXP_DEV, dtype=jnp.int32)[None, :]).reshape(-1)
        full_labels = jnp.repeat(expert_order[:full_count], CAP)
        slots = jax.random.permutation(second_key, (EXPERTS - full_count) * CAP)[:remaining]
        others = expert_order[full_count + (slots // CAP).astype(jnp.int32)]
        labels = jnp.sort(jnp.concatenate([full_labels, others]).astype(jnp.int32))
        table = labels.reshape(TOPK, SEC_TOK).T
        row_order = jax.random.permutation(third_key, SEC_TOK)
        return table[row_order]
    section_keys = jax.random.split(jax.random.fold_in(key, 12), sections)
    return jax.vmap(one_section)(section_keys).reshape(TOKEN_TOTAL, TOPK).astype(jnp.int32)


def raised(values, stream_key, source, target, shards_of, factor):
    owner, partner = [(jnp.arange(values.shape[axis_at]) // (values.shape[axis_at] // shards_of)).reshape([-1 if axis == axis_at else 1 for axis in range(values.ndim)]) for axis_at in (source, target)]
    chosen = jax.random.permutation(stream_key, shards_of)[partner]
    strong = (owner == chosen) | (owner == (partner + shards_of // 2) % shards_of)
    return jnp.where(strong, factor * values, values)


def steps_of(rng, extent, pieces, low, top_value):
    loudness, own = 1.0, jax.random.fold_in(rng, 6)
    for dim, shards_of in pieces:
        draws = jnp.exp(jax.random.uniform(jax.random.fold_in(own, dim), (shards_of,), jnp.float32, low / len(pieces), top_value / len(pieces)))
        loudness = loudness * jnp.repeat(draws, extent[dim] // shards_of).reshape([-1 if axis == dim else 1 for axis in range(len(extent))])
    return loudness


def gaussian(own_key, extent, spread, limit, shards=(), held_as=jnp.bfloat16):
    factor_of = steps_of(own_key, extent, shards, -0.22, 0.18) if shards else 1.0
    array = jax.random.normal(own_key, extent, jnp.float32) * spread * factor_of
    return jnp.minimum(jnp.maximum(array, -limit), limit).astype(held_as)


def bell_draw_with(stream_key, extent, spread, limit, shards, heavy, kind=jnp.bfloat16):
    drawn = spread * jax.random.normal(stream_key, extent, jnp.float32)
    if shards:
        drawn = drawn * steps_of(stream_key, extent, shards, -0.22, 0.18)
    return jnp.clip(raised(drawn, jax.random.fold_in(stream_key, 3), *heavy), -limit, limit).astype(kind)


def setup_inputs(seed: int = 0) -> dict:
    key_list = jax.random.split(jax.random.key(seed), 12)
    return {
        "attn_query": gaussian(key_list[0], (TOKEN_TOTAL, D), 1.0, 6.0, ((0, 4), (1, 8))),
        "attn_key": gaussian(key_list[1], (TOKEN_TOTAL, D), 1.0, 6.0, ((0, 4), (1, 8))),
        "attn_value": draw_attn_value(jax.random.fold_in(key_list[11], 71), 0),
        "log_decay": draw_log_decay(jax.random.fold_in(key_list[11], 71), 0),
        "residual": gaussian(key_list[4], (TOKEN_TOTAL, D), 1.0, 6.0, ((0, 4), (1, 8))),
        "norm_gain": jnp.clip(1.0 + 0.18 * jax.random.normal(key_list[5], (D,), jnp.float32), 0.099609375, 1.8984375).astype(jnp.bfloat16),
        "expert_ids": draw_expert_ids(jax.random.fold_in(key_list[11], 71), 0),
        "router_weight": gaussian(key_list[7], (D, EXPERTS), D ** -0.5, 0.078125, ((1, 4),)),
        "gate_weight": gaussian(key_list[8], (EXPERTS, D, FF), D ** -0.5, 0.078125, ((0, 4), (2, 8))),
        "up_weight": gaussian(key_list[9], (EXPERTS, D, FF), D ** -0.5, 0.078125, ((0, 4), (2, 8))),
        "down_weight": bell_draw_with(key_list[10], (EXPERTS, FF, D), FF ** -0.5, 0.125, ((0, 4), (1, 8)), (1, 2, 8, 2.0)),
    }


def section_pass(query_rows, key_rows, value_rows, decay_rows, carry_state):
    cumulative = jnp.cumsum(decay_rows, axis=1)
    length = decay_rows.shape[1]
    causal = jnp.arange(length, dtype=jnp.int32)[:, None] >= jnp.arange(length, dtype=jnp.int32)[None, :]
    decay_gap = jnp.where(causal[None], cumulative[:, :, None] - cumulative[:, None, :], 0.0)
    decay_mask = jnp.where(causal[None], jnp.exp(decay_gap), 0.0)
    scores = jnp.einsum('htd,hsd->hts', query_rows.astype(jnp.float32), key_rows.astype(jnp.float32))
    weights = (scores * decay_mask).astype(jnp.bfloat16)
    intra_part = jnp.einsum('hts,hsd->htd', weights.astype(jnp.float32), value_rows.astype(jnp.float32))
    inter_part = jnp.einsum('htd,hde->hte', query_rows.astype(jnp.float32), carry_state, precision=lax.Precision.HIGHEST)
    attn_out = intra_part + jnp.exp(cumulative)[:, :, None] * inter_part
    key_fade = jnp.exp(cumulative[:, -1:] - cumulative)
    scaled = (key_fade[:, :, None] * key_rows.astype(jnp.float32)).astype(jnp.bfloat16)
    local_state = jnp.einsum('hsd,hse->hde', scaled.astype(jnp.float32), value_rows.astype(jnp.float32))
    next_state = jnp.exp(cumulative[:, -1])[:, None, None] * carry_state + local_state
    return (attn_out, next_state)

def run_expert(expert_parts):
    input_rows, gate_matrix, up_matrix, down_matrix, router_column = expert_parts
    gate_acc = jnp.dot(input_rows, gate_matrix, preferred_element_type=jnp.float32)
    upward = jnp.dot(input_rows, up_matrix, preferred_element_type=jnp.float32)
    hidden_act = (jax.nn.silu(gate_acc) * upward).astype(jnp.bfloat16)
    expert_out = jnp.dot(hidden_act, down_matrix, preferred_element_type=jnp.float32)
    score_rows = jnp.dot(input_rows, router_column, preferred_element_type=jnp.float32)
    return (jax.nn.sigmoid(score_rows)[:, None] * expert_out).astype(jnp.bfloat16)

def reference(attn_query, attn_key, attn_value, log_decay, residual, norm_gain, expert_ids, router_weight, gate_weight, up_weight, down_weight):
    sections = TOKEN_TOTAL // SEC_TOK

    def split_heads(array_rows):
        return array_rows.reshape(sections, SEC_TOK, H, DH).transpose(0, 2, 1, 3)
    query_blocks = split_heads(attn_query)
    key_blocks = split_heads(attn_key)
    value_blocks = split_heads(attn_value)
    decay_blocks = log_decay.reshape(H, sections, SEC_TOK).transpose(1, 0, 2)

    def one_section(carry_state, section_parts):
        section_out, carry_state = section_pass(section_parts[0], section_parts[1], section_parts[2], section_parts[3], carry_state)
        return (carry_state, section_out)
    initial = jnp.zeros((H, DH, DH), jnp.float32)
    _, attn_blocks = lax.scan(one_section, initial, (query_blocks, key_blocks, value_blocks, decay_blocks))
    mean_square = lax.optimization_barrier(jnp.mean(attn_blocks * attn_blocks, axis=-1, keepdims=True))
    normed = attn_blocks / jnp.sqrt(mean_square + 1e-06)
    normed = normed.transpose(0, 2, 1, 3).reshape(TOKEN_TOTAL, D)
    stream = (residual.astype(jnp.float32) + norm_gain.astype(jnp.float32) * normed).astype(jnp.bfloat16)
    entries = expert_ids.reshape(sections, SEC_TOK * TOPK)
    onehot = (entries[:, :, None] == jnp.arange(EXPERTS, dtype=jnp.int32)[None, None, :]).astype(jnp.int32)
    running = jnp.cumsum(onehot, axis=1)
    slot_index = lax.optimization_barrier(jnp.sum(running * onehot, axis=2)) - 1
    row_index = (jnp.arange(sections, dtype=jnp.int32)[:, None] * CAP + slot_index).astype(jnp.int32)
    token_index = jnp.repeat(jnp.arange(TOKEN_TOTAL, dtype=jnp.int32).reshape(sections, SEC_TOK), TOPK, axis=1)
    flat_expert = entries.reshape(-1).astype(jnp.int32)
    flat_row = row_index.reshape(-1).astype(jnp.int32)
    buffer = jnp.zeros((EXPERTS, sections * CAP, D), jnp.bfloat16)
    buffer = buffer.at[flat_expert, flat_row].set(stream[token_index.reshape(-1)])
    routed_all = lax.map(run_expert, (buffer, gate_weight, up_weight, down_weight, router_weight.T))
    picked = routed_all[flat_expert, flat_row].reshape(TOKEN_TOTAL, TOPK, D).astype(jnp.float32)
    return (stream.astype(jnp.float32) + lax.optimization_barrier(jnp.sum(picked, axis=1))).astype(jnp.bfloat16)
```

```python
import functools

import jax
import jax.numpy as jnp
from jax import lax
from jax.experimental import pallas as pl
from jax.experimental.pallas import tpu as pltpu
from jax.sharding import PartitionSpec as P

F32 = jnp.float32
BF16 = jnp.bfloat16
HIGHEST = lax.Precision.HIGHEST
VMEM_LIMIT = 48 * 1024 * 1024


def lower_ones(length):
    rows = lax.broadcasted_iota(jnp.int32, (length, length), 0)
    columns = lax.broadcasted_iota(jnp.int32, (length, length), 1)
    return rows >= columns


def shifted(array, axis, by, wrap=False):
    count = lax.axis_size(axis)
    if wrap:
        pairs = [(i, (i + by) % count) for i in range(count)]
    else:
        pairs = [(i, i + by) for i in range(count) if 0 <= i + by < count]
    return lax.ppermute(array, axis, pairs)


def state_kernel(key_ref, value_ref, decay_ref, message_ref, cumulative_ref):
    heads, length = decay_ref.shape
    size = key_ref.shape[1] // heads
    ones = lower_ones(length).astype(F32)
    cumulative = lax.dot_general(
        ones, decay_ref[...], (((1,), (1,)), ((), ())), precision=HIGHEST, preferred_element_type=F32
    )
    cumulative_ref[...] = cumulative
    last = cumulative[length - 1 : length, :]
    key_fade = jnp.exp(last - cumulative)
    message_ref[heads * size :, :] = jnp.zeros((message_ref.shape[0] - heads * size, size), BF16)
    half = (message_ref.shape[0] - heads * size) // 2
    rows = []
    for h in range(heads):
        columns = slice(h * size, (h + 1) * size)
        scaled = (key_fade[:, h : h + 1] * key_ref[:, columns].astype(F32)).astype(BF16)
        state = lax.dot_general(
            scaled, value_ref[:, columns], (((0,), (0,)), ((), ())), preferred_element_type=F32
        )
        message_ref[columns, :] = state.astype(BF16)
        rows.append(jnp.broadcast_to(jnp.exp(last[:, h : h + 1]), (1, size)))
    rows.append(jnp.zeros((half - heads, size), F32))
    fade = jnp.concatenate(rows, axis=0)
    leading = fade.astype(BF16)
    trailing = (fade - leading.astype(F32)).astype(BF16)
    message_ref[heads * size :, :] = jnp.concatenate([leading, trailing], axis=0)


def section_state(attn_key, attn_value, log_decay):
    heads, length = log_decay.shape
    width = attn_key.shape[1]
    half = -(-heads // 8) * 8
    return pl.pallas_call(
        state_kernel,
        out_shape=(
            jax.ShapeDtypeStruct((width + 2 * half, width // heads), BF16),
            jax.ShapeDtypeStruct((length, heads), F32),
        ),
        cost_estimate=pl.CostEstimate(
            flops=2 * length * width * (width // heads), bytes_accessed=4 * length * width, transcendentals=0
        ),
        compiler_params=pltpu.CompilerParams(vmem_limit_bytes=VMEM_LIMIT),
    )(attn_key, attn_value, log_decay)


def intra_kernel(query_ref, key_ref, value_ref, decay_ref, cumulative_ref, out_ref):
    heads, length = decay_ref.shape
    size = key_ref.shape[1] // heads
    causal = lower_ones(length)
    along = lax.dot_general(
        decay_ref[...],
        causal.astype(F32),
        (((1,), (1,)), ((), ())),
        precision=HIGHEST,
        preferred_element_type=F32,
    )
    for h in range(heads):
        columns = slice(h * size, (h + 1) * size)
        gap = jnp.where(causal, cumulative_ref[:, h : h + 1] - along[h : h + 1, :], 0.0)
        mask = jnp.where(causal, jnp.exp(gap), 0.0)
        scores = lax.dot_general(
            query_ref[:, columns], key_ref[:, columns], (((1,), (1,)), ((), ())), preferred_element_type=F32
        )
        weights = (scores * mask).astype(BF16)
        out_ref[:, columns] = jnp.dot(weights, value_ref[:, columns], preferred_element_type=F32)


def intra_section(attn_query, attn_key, attn_value, log_decay, cumulative):
    length, width = attn_query.shape
    return pl.pallas_call(
        intra_kernel,
        out_shape=jax.ShapeDtypeStruct((length, width), F32),
        cost_estimate=pl.CostEstimate(
            flops=4 * length * length * width, bytes_accessed=10 * length * width, transcendentals=0
        ),
        compiler_params=pltpu.CompilerParams(vmem_limit_bytes=VMEM_LIMIT),
    )(attn_query, attn_key, attn_value, log_decay, cumulative)


def stream_kernel(query_ref, intra_ref, cumulative_ref, incoming_ref, residual_ref, gain_ref, out_ref):
    heads, size = incoming_ref.shape[0], incoming_ref.shape[1]
    faded = jnp.exp(cumulative_ref[...])
    for h in range(heads):
        columns = slice(h * size, (h + 1) * size)
        state = incoming_ref[h]
        leading = state.astype(BF16)
        trailing = (state - leading.astype(F32)).astype(BF16)
        query = query_ref[:, columns]
        inter = jnp.dot(query, leading, preferred_element_type=F32) + jnp.dot(
            query, trailing, preferred_element_type=F32
        )
        attn_out = intra_ref[:, columns] + faded[:, h : h + 1] * inter
        mean_square = jnp.mean(attn_out * attn_out, axis=1, keepdims=True)
        normed = attn_out * lax.rsqrt(mean_square + 1e-06)
        out_ref[:, columns] = (
            residual_ref[:, columns].astype(F32) + gain_ref[:, columns].astype(F32) * normed
        ).astype(BF16)


def make_stream(attn_query, intra, cumulative, incoming, residual, norm_gain):
    length, width = attn_query.shape
    return pl.pallas_call(
        stream_kernel,
        out_shape=jax.ShapeDtypeStruct((length, width), BF16),
        compiler_params=pltpu.CompilerParams(vmem_limit_bytes=VMEM_LIMIT),
    )(attn_query, intra, cumulative, incoming, residual, norm_gain.reshape(1, width))


def read_message(message, heads):
    size = message.shape[1]
    half = (message.shape[0] - heads * size) // 2
    state = message[: heads * size].astype(F32).reshape(heads, size, size)
    tail = message[heads * size :].astype(F32)
    fade = tail[:heads] + tail[half : half + heads]
    return fade[:, None, :], state


def write_message(fade, state, rows):
    heads, size = state.shape[0], state.shape[1]
    half = (rows - heads * size) // 2
    leading = fade[:, 0, :].astype(BF16)
    trailing = (fade[:, 0, :] - leading.astype(F32)).astype(BF16)
    spare = jnp.zeros((half - heads, size), BF16)
    return jnp.concatenate(
        [state.astype(BF16).reshape(heads * size, size), leading, spare, trailing, spare], axis=0
    )


def incoming_state(message, heads):
    count = lax.axis_size("seq")
    window_fade, window = read_message(message, heads)
    incoming_fade, incoming = None, None
    distance = 1
    while distance < count:
        got_fade, got = read_message(shifted(message, "seq", distance), heads)
        if incoming is None:
            incoming_fade, incoming = got_fade, got
        else:
            incoming, incoming_fade = incoming + incoming_fade * got, incoming_fade * got_fade
        window, window_fade = window + window_fade * got, window_fade * got_fade
        distance *= 2
        if distance < count:
            message = write_message(window_fade, window, message.shape[0])
    return incoming


def expert_kernel(
    capacity, steps, first_ref, ids_ref, x_ref, router_ref, gate_ref, up_ref, down_ref, out_ref,
    gate_acc, up_acc, score_acc, place, hidden,
):
    step = pl.program_id(0)
    experts = gate_ref.shape[0]
    length = x_ref.shape[1]

    @pl.when(step == 0)
    def _():
        tokens_before = lower_ones(length)
        slot = lax.broadcasted_iota(jnp.int32, (capacity, length), 0)
        for j in range(experts):
            chosen = ids_ref[0:1, :] == first_ref[0] + j
            for choice in range(1, ids_ref.shape[0]):
                chosen = chosen | (ids_ref[choice : choice + 1, :] == first_ref[0] + j)
            flag = jnp.where(chosen, 1.0, 0.0)
            rank = lax.dot_general(
                jnp.broadcast_to(flag, (8, length)).astype(BF16),
                tokens_before.astype(BF16),
                (((1,), (1,)), ((), ())),
                preferred_element_type=F32,
            )[0:1, :]
            here = (rank.astype(jnp.int32) - 1 == slot) & (flag > 0.5)
            place[j * capacity : (j + 1) * capacity, :] = jnp.where(here, 1.0, 0.0).astype(BF16)
        gate_acc[...] = jnp.zeros_like(gate_acc)
        up_acc[...] = jnp.zeros_like(up_acc)
        score_acc[...] = jnp.zeros_like(score_acc)

    @pl.when(step < steps)
    def _():
        rows = jnp.dot(place[...], x_ref[0], preferred_element_type=F32).astype(BF16)
        score_acc[...] += lax.dot_general(
            rows, router_ref[0], (((1,), (1,)), ((), ())), preferred_element_type=F32
        )
        for j in range(experts):
            mine = slice(j * capacity, (j + 1) * capacity)
            gate_acc[mine, :] += jnp.dot(rows[mine], gate_ref[j], preferred_element_type=F32)
            up_acc[mine, :] += jnp.dot(rows[mine], up_ref[j], preferred_element_type=F32)

    @pl.when(step == steps - 1)
    def _():
        gate = gate_acc[...]
        hidden[...] = (gate / (1.0 + jnp.exp(-gate)) * up_acc[...]).astype(BF16)

    @pl.when(step >= steps)
    def _():
        parts = []
        for j in range(experts):
            mine = slice(j * capacity, (j + 1) * capacity)
            share = jnp.dot(hidden[mine, :], down_ref[j], preferred_element_type=F32)
            score = score_acc[mine, j : j + 1]
            parts.append((share / (1.0 + jnp.exp(-score))).astype(BF16))
        routed = jnp.concatenate(parts, axis=0)
        out_ref[0] = lax.dot_general(
            place[...], routed, (((0,), (0,)), ((), ())), preferred_element_type=F32
        ).astype(BF16)


def expert_section(first, ids, x, router_rows, gate_weight, up_weight, down_weight, capacity):
    steps, length, width = x.shape
    experts, _, units = gate_weight.shape
    slots = experts * capacity
    early = lambda i: jnp.minimum(i, steps - 1)
    late = lambda i: jnp.maximum(i - steps, 0)
    return pl.pallas_call(
        functools.partial(expert_kernel, capacity, steps),
        grid=(2 * steps,),
        in_specs=[
            pl.BlockSpec(memory_space=pltpu.SMEM),
            pl.BlockSpec(ids.shape, lambda i: (0, 0)),
            pl.BlockSpec((1, length, width), lambda i: (early(i), 0, 0)),
            pl.BlockSpec((1, experts, width), lambda i: (early(i), 0, 0)),
            pl.BlockSpec((experts, width, units), lambda i: (0, early(i), 0)),
            pl.BlockSpec((experts, width, units), lambda i: (0, early(i), 0)),
            pl.BlockSpec((experts, units, width), lambda i: (0, 0, late(i))),
        ],
        out_specs=pl.BlockSpec((1, length, width), lambda i: (late(i), 0, 0)),
        out_shape=jax.ShapeDtypeStruct((steps, length, width), BF16),
        scratch_shapes=[
            pltpu.VMEM((slots, units), F32),
            pltpu.VMEM((slots, units), F32),
            pltpu.VMEM((slots, experts), F32),
            pltpu.VMEM((slots, length), BF16),
            pltpu.VMEM((slots, units), BF16),
        ],
        cost_estimate=pl.CostEstimate(
            flops=6 * slots * steps * width * units,
            bytes_accessed=6 * experts * steps * width * units,
            transcendentals=0,
        ),
        compiler_params=pltpu.CompilerParams(vmem_limit_bytes=VMEM_LIMIT),
    )(first, ids, x, router_rows, gate_weight, up_weight, down_weight)


def on_device(
    attn_query,
    attn_key,
    attn_value,
    log_decay,
    residual,
    norm_gain,
    expert_ids,
    router_weight,
    gate_weight,
    up_weight,
    down_weight,
):
    heads_here, length = log_decay.shape
    groups = lax.axis_size("seq")
    shares = lax.axis_size("exp")
    width = attn_query.shape[1]
    experts_here = router_weight.shape[1]
    capacity = 4 * length // (experts_here * groups)
    section = lax.axis_index("seq")
    first = (section * experts_here).astype(jnp.int32).reshape(1)
    router_rows = router_weight.reshape(shares, width, experts_here).transpose(0, 2, 1)

    all_ids = lax.all_gather(expert_ids.T, "seq", axis=0)
    message, cumulative = section_state(attn_key, attn_value, log_decay)
    intra = intra_section(attn_query, attn_key, attn_value, log_decay, cumulative)
    incoming = incoming_state(message, heads_here)
    stream = make_stream(attn_query, intra, cumulative, incoming, residual, norm_gain)

    total = stream.astype(F32)
    for offset in range(groups):
        part = stream if offset == 0 else shifted(stream, "seq", offset, wrap=True)
        ids = lax.dynamic_index_in_dim(all_ids, (section - offset) % groups, 0, keepdims=False)
        gathered = lax.all_gather(part, "exp", axis=0)
        partial = expert_section(
            first, ids, gathered, router_rows, gate_weight, up_weight, down_weight, capacity
        )
        share = lax.psum_scatter(partial, "exp", scatter_dimension=0)
        if offset:
            share = shifted(share, "seq", -offset, wrap=True)
        total = total + share.astype(F32)
    return total.astype(BF16)


def solution(mesh):
    in_specs = (
        P("seq", "exp"),
        P("seq", "exp"),
        P("seq", "exp"),
        P("exp", "seq"),
        P("seq", "exp"),
        P("exp"),
        P("seq", None),
        P(None, "seq"),
        P("seq", None, "exp"),
        P("seq", None, "exp"),
        P("seq", "exp", None),
    )
    out_specs = P("seq", "exp")
    return jax.shard_map(
        on_device, mesh=mesh, in_specs=in_specs, out_specs=out_specs, check_vma=False
    )
```

```python
import functools

import jax
import jax.numpy as jnp
from jax import lax
from jax.experimental import pallas as pl
from jax.experimental.pallas import tpu as pltpu
from jax.sharding import PartitionSpec as P

F32 = jnp.float32
BF16 = jnp.bfloat16
HIGHEST = lax.Precision.HIGHEST
VMEM_LIMIT = 40 * 1024 * 1024


def lower_ones(length):
    rows = lax.broadcasted_iota(jnp.int32, (length, length), 0)
    columns = lax.broadcasted_iota(jnp.int32, (length, length), 1)
    return rows >= columns


def shifted(array, axis, by):
    count = lax.axis_size(axis)
    pairs = [(i, i + by) for i in range(count) if 0 <= i + by < count]
    return lax.ppermute(array, axis, pairs)


def state_kernel(key_ref, value_ref, decay_ref, message_ref, cumulative_ref):
    heads, length = decay_ref.shape
    size = key_ref.shape[1] // heads
    ones = lower_ones(length).astype(F32)
    cumulative = lax.dot_general(
        ones, decay_ref[...], (((1,), (1,)), ((), ())), precision=HIGHEST, preferred_element_type=F32
    )
    cumulative_ref[...] = cumulative
    last = cumulative[length - 1 : length, :]
    key_fade = jnp.exp(last - cumulative)
    message_ref[heads * size :, :] = jnp.zeros((message_ref.shape[0] - heads * size, size), BF16)
    half = (message_ref.shape[0] - heads * size) // 2
    rows = []
    for h in range(heads):
        columns = slice(h * size, (h + 1) * size)
        scaled = (key_fade[:, h : h + 1] * key_ref[:, columns].astype(F32)).astype(BF16)
        state = lax.dot_general(
            scaled, value_ref[:, columns], (((0,), (0,)), ((), ())), preferred_element_type=F32
        )
        message_ref[columns, :] = state.astype(BF16)
        rows.append(jnp.broadcast_to(jnp.exp(last[:, h : h + 1]), (1, size)))
    rows.append(jnp.zeros((half - heads, size), F32))
    fade = jnp.concatenate(rows, axis=0)
    leading = fade.astype(BF16)
    trailing = (fade - leading.astype(F32)).astype(BF16)
    message_ref[heads * size :, :] = jnp.concatenate([leading, trailing], axis=0)


def section_state(attn_key, attn_value, log_decay):
    heads, length = log_decay.shape
    width = attn_key.shape[1]
    half = -(-heads // 8) * 8
    return pl.pallas_call(
        state_kernel,
        out_shape=(
            jax.ShapeDtypeStruct((width + 2 * half, width // heads), BF16),
            jax.ShapeDtypeStruct((length, heads), F32),
        ),
        cost_estimate=pl.CostEstimate(
            flops=2 * length * width * (width // heads), bytes_accessed=4 * length * width, transcendentals=0
        ),
        compiler_params=pltpu.CompilerParams(vmem_limit_bytes=VMEM_LIMIT),
    )(attn_key, attn_value, log_decay)


def intra_kernel(query_ref, key_ref, value_ref, decay_ref, cumulative_ref, out_ref):
    heads, length = decay_ref.shape
    size = key_ref.shape[1] // heads
    causal = lower_ones(length)
    along = lax.dot_general(
        decay_ref[...],
        causal.astype(F32),
        (((1,), (1,)), ((), ())),
        precision=HIGHEST,
        preferred_element_type=F32,
    )
    for h in range(heads):
        columns = slice(h * size, (h + 1) * size)
        gap = jnp.where(causal, cumulative_ref[:, h : h + 1] - along[h : h + 1, :], 0.0)
        mask = jnp.where(causal, jnp.exp(gap), 0.0)
        scores = lax.dot_general(
            query_ref[:, columns], key_ref[:, columns], (((1,), (1,)), ((), ())), preferred_element_type=F32
        )
        weights = (scores * mask).astype(BF16)
        out_ref[:, columns] = jnp.dot(weights, value_ref[:, columns], preferred_element_type=F32)


def intra_section(attn_query, attn_key, attn_value, log_decay, cumulative):
    length, width = attn_query.shape
    return pl.pallas_call(
        intra_kernel,
        out_shape=jax.ShapeDtypeStruct((length, width), F32),
        cost_estimate=pl.CostEstimate(
            flops=4 * length * length * width, bytes_accessed=10 * length * width, transcendentals=0
        ),
        compiler_params=pltpu.CompilerParams(vmem_limit_bytes=VMEM_LIMIT),
    )(attn_query, attn_key, attn_value, log_decay, cumulative)


def stream_kernel(query_ref, intra_ref, cumulative_ref, incoming_ref, residual_ref, gain_ref, out_ref):
    heads, size = incoming_ref.shape[0], incoming_ref.shape[1]
    faded = jnp.exp(cumulative_ref[...])
    for h in range(heads):
        columns = slice(h * size, (h + 1) * size)
        state = incoming_ref[h]
        leading = state.astype(BF16)
        trailing = (state - leading.astype(F32)).astype(BF16)
        query = query_ref[:, columns]
        inter = jnp.dot(query, leading, preferred_element_type=F32) + jnp.dot(
            query, trailing, preferred_element_type=F32
        )
        attn_out = intra_ref[:, columns] + faded[:, h : h + 1] * inter
        mean_square = jnp.mean(attn_out * attn_out, axis=1, keepdims=True)
        normed = attn_out * lax.rsqrt(mean_square + 1e-06)
        out_ref[:, columns] = (
            residual_ref[:, columns].astype(F32) + gain_ref[:, columns].astype(F32) * normed
        ).astype(BF16)


def make_stream(attn_query, intra, cumulative, incoming, residual, norm_gain):
    length, width = attn_query.shape
    return pl.pallas_call(
        stream_kernel,
        out_shape=jax.ShapeDtypeStruct((length, width), BF16),
        compiler_params=pltpu.CompilerParams(vmem_limit_bytes=VMEM_LIMIT),
    )(attn_query, intra, cumulative, incoming, residual, norm_gain.reshape(1, width))


def read_message(message, heads):
    size = message.shape[1]
    half = (message.shape[0] - heads * size) // 2
    state = message[: heads * size].astype(F32).reshape(heads, size, size)
    tail = message[heads * size :].astype(F32)
    fade = tail[:heads] + tail[half : half + heads]
    return fade[:, None, :], state


def write_message(fade, state, rows):
    heads, size = state.shape[0], state.shape[1]
    half = (rows - heads * size) // 2
    leading = fade[:, 0, :].astype(BF16)
    trailing = (fade[:, 0, :] - leading.astype(F32)).astype(BF16)
    spare = jnp.zeros((half - heads, size), BF16)
    return jnp.concatenate(
        [state.astype(BF16).reshape(heads * size, size), leading, spare, trailing, spare], axis=0
    )


def incoming_state(message, heads):
    count = lax.axis_size("seq")
    window_fade, window = read_message(message, heads)
    incoming_fade, incoming = None, None
    distance = 1
    while distance < count:
        got_fade, got = read_message(shifted(message, "seq", distance), heads)
        if incoming is None:
            incoming_fade, incoming = got_fade, got
        else:
            incoming, incoming_fade = incoming + incoming_fade * got, incoming_fade * got_fade
        window, window_fade = window + window_fade * got, window_fade * got_fade
        distance *= 2
        if distance < count:
            message = write_message(window_fade, window, message.shape[0])
    return incoming


def gate_kernel(counts, last, plan_ref, ids_ref, *refs):
    step = pl.program_id(0)
    blocks = sum(counts)
    x_refs, refs = refs[: len(counts)], refs[len(counts) :]
    router_ref, gate_ref, up_ref = refs[:3]
    refs = refs[3:]
    if last:
        gate_in, up_in, score_in, hidden_ref, gate_acc, up_acc, score_acc = refs
    else:
        gate_acc, up_acc, score_acc = refs
    experts = gate_ref.shape[0]

    @pl.when(step == 0)
    def _():
        if last:
            gate_acc[...] = gate_in[...]
            up_acc[...] = up_in[...]
            score_acc[...] = score_in[...]
        else:
            gate_acc[...] = jnp.zeros_like(gate_acc)
            up_acc[...] = jnp.zeros_like(up_acc)
            score_acc[...] = jnp.zeros_like(score_acc)

    x = x_refs[-1][0]
    for i in range(len(counts) - 2, -1, -1):
        x = jnp.where(step < sum(counts[: i + 1]), x_refs[i][0], x)
    across = (((1,), (1,)), ((), ()))
    score_acc[...] += lax.dot_general(router_ref[0], x, across, preferred_element_type=F32)
    for j in range(experts):
        gate_acc[j] += lax.dot_general(gate_ref[j], x, across, preferred_element_type=F32)
        up_acc[j] += lax.dot_general(up_ref[j], x, across, preferred_element_type=F32)

    if last:

        @pl.when(step == blocks - 1)
        def _():
            parts = []
            for j in range(experts):
                chosen = ids_ref[0:1, :] == plan_ref[blocks] + j
                for choice in range(1, ids_ref.shape[0]):
                    chosen = chosen | (ids_ref[choice : choice + 1, :] == plan_ref[blocks] + j)
                gate = gate_acc[j]
                routed = gate / (1.0 + jnp.exp(-gate)) * up_acc[j]
                routed = routed / (1.0 + jnp.exp(-score_acc[j : j + 1, :]))
                parts.append(jnp.where(chosen, routed, 0.0))
            hidden_ref[...] = jnp.concatenate(parts, axis=0).T.astype(BF16)


def gate_part(plan, ids, xs, router_rows, gate_rows, up_rows, sums=None):
    counts = tuple(x.shape[0] for x in xs)
    blocks = sum(counts)
    _, length, width = xs[0].shape
    experts, units, _ = gate_rows.shape
    whole = pl.BlockSpec(memory_space=pltpu.VMEM)
    last = sums is not None

    def x_spec(i):
        before = sum(counts[:i])
        return pl.BlockSpec(
            (1, length, width), lambda p, plan: (jnp.clip(p - before, 0, counts[i] - 1), 0, 0)
        )

    weight_spec = pl.BlockSpec((experts, units, width), lambda p, plan: (0, 0, plan[p]))
    sum_shapes = [(experts, units, length), (experts, units, length), (experts, length)]
    if last:
        out_shape = jax.ShapeDtypeStruct((length, experts * units), BF16)
        out_specs = whole
        scratch = [pltpu.VMEM(shape, F32) for shape in sum_shapes]
    else:
        out_shape = tuple(jax.ShapeDtypeStruct(shape, F32) for shape in sum_shapes)
        out_specs = (whole, whole, whole)
        scratch = []
    return pl.pallas_call(
        functools.partial(gate_kernel, counts, last),
        grid_spec=pltpu.PrefetchScalarGridSpec(
            num_scalar_prefetch=1,
            grid=(blocks,),
            in_specs=[
                whole,
                *[x_spec(i) for i in range(len(counts))],
                pl.BlockSpec((1, experts, width), lambda p, plan: (plan[p], 0, 0)),
                weight_spec,
                weight_spec,
                *([whole] * 3 if last else []),
            ],
            out_specs=out_specs,
            scratch_shapes=scratch,
        ),
        out_shape=out_shape,
        cost_estimate=pl.CostEstimate(
            flops=4 * experts * length * blocks * width * units,
            bytes_accessed=4 * experts * blocks * width * units,
            transcendentals=0,
        ),
        compiler_params=pltpu.CompilerParams(vmem_limit_bytes=VMEM_LIMIT),
    )(plan, ids, *xs, router_rows, gate_rows, up_rows, *(sums if last else ()))


def down_kernel(plan_ref, hidden_ref, down_ref, out_ref):
    experts, units, width = down_ref.shape
    out_ref[0] = jnp.dot(
        hidden_ref[...], down_ref[...].reshape(experts * units, width), preferred_element_type=F32
    ).astype(BF16)


def down_part(plan, hidden, down_weight, width):
    blocks = plan.shape[0]
    length = hidden.shape[0]
    experts, units, _ = down_weight.shape
    return pl.pallas_call(
        down_kernel,
        grid_spec=pltpu.PrefetchScalarGridSpec(
            num_scalar_prefetch=1,
            grid=(blocks,),
            in_specs=[
                pl.BlockSpec(memory_space=pltpu.VMEM),
                pl.BlockSpec((experts, units, width), lambda p, plan: (0, 0, plan[p])),
            ],
            out_specs=pl.BlockSpec((1, length, width), lambda p, plan: (p, 0, 0)),
        ),
        out_shape=jax.ShapeDtypeStruct((blocks, length, width), BF16),
        cost_estimate=pl.CostEstimate(
            flops=2 * experts * length * blocks * width * units,
            bytes_accessed=2 * experts * blocks * width * units,
            transcendentals=0,
        ),
        compiler_params=pltpu.CompilerParams(vmem_limit_bytes=VMEM_LIMIT),
    )(plan, hidden, down_weight)


def added(left, right):
    return (left.astype(F32) + right.astype(F32)).astype(BF16)


def swapped(array, axis, even, odd):
    count = lax.axis_size(axis)
    pairs = [(i, i ^ (odd if i % 2 else even)) for i in range(count)]
    return lax.ppermute(array, axis, pairs)


class PairedPlane:
    def __init__(self):
        me = lax.axis_index("exp").astype(jnp.int32)
        other = me ^ 1
        near = jnp.where(me % 2 == 0, 2, 4)
        far = 6 - near
        self.early = jnp.stack([me, me ^ near, other, other ^ far])
        self.late = jnp.stack([me ^ far, me ^ 6, other ^ near, other ^ 6])
        self.mine = jnp.stack([me, me ^ near, me ^ far, me ^ 6])
        self.theirs = jnp.stack([other, other ^ far, other ^ near, other ^ 6])

    def first(self, part):
        return jnp.stack([part, swapped(part, "exp", 2, 4)])

    def second(self, two):
        return swapped(two, "exp", 4, 2)

    def across(self, two):
        return swapped(two, "exp", 1, 1)

    def scatter(self, mine, theirs):
        got = swapped(theirs, "exp", 1, 1)
        got_two = swapped(added(mine[2:], got[2:]), "exp", 4, 2)
        got_one = swapped(added(added(mine[1], got[1]), got_two[1]), "exp", 2, 4)
        return added(added(added(mine[0], got[0]), got_two[0]), got_one), got, got_two


def on_device(
    attn_query,
    attn_key,
    attn_value,
    log_decay,
    residual,
    norm_gain,
    expert_ids,
    router_weight,
    gate_weight,
    up_weight,
    down_weight,
):
    heads_here, length = log_decay.shape
    groups = lax.axis_size("seq")
    shares = lax.axis_size("exp")
    width = attn_query.shape[1]
    experts_here = router_weight.shape[1]
    base = (lax.axis_index("seq") * experts_here).astype(jnp.int32).reshape(1)
    router_rows = router_weight.reshape(shares, width, experts_here).transpose(0, 2, 1)
    gate_rows = gate_weight.swapaxes(1, 2)
    up_rows = up_weight.swapaxes(1, 2)

    ids = expert_ids.T[None]
    distance = 1
    while distance < groups:
        ids = jnp.concatenate([ids, swapped(ids, "seq", distance, distance)])
        distance *= 2

    message, cumulative = section_state(attn_key, attn_value, log_decay)
    intra = intra_section(attn_query, attn_key, attn_value, log_decay, cumulative)
    incoming = incoming_state(message, heads_here)
    incoming, ids = lax.optimization_barrier((incoming, ids))
    stream = make_stream(attn_query, intra, cumulative, incoming, residual, norm_gain)

    half = groups // 2
    chunks = [(i, i + half) for i in range(half)]
    parts = {0: stream}
    parts[half] = swapped(stream, "seq", half, half)
    later, _ = lax.optimization_barrier((stream, parts[half]))
    for i in range(1, half):
        for offset in chunks[i]:
            parts[offset] = swapped(later, "seq", offset, offset)

    total = stream.astype(F32)
    plane = PairedPlane() if shares == 8 else None
    links_free, core_free, sum_free = None, None, None
    for chunk in chunks:
        part = jnp.concatenate([parts[offset] for offset in chunk])
        chunk_ids = jnp.concatenate([ids[offset] for offset in chunk], axis=1)
        weights = (router_rows, gate_rows, up_rows)
        if plane:
            if links_free is not None:
                part, _ = lax.optimization_barrier((part, links_free))
            two = plane.first(part)
            far_two = plane.second(two)
            links_free = far_two
            near_two = plane.across(two)
            if core_free is not None:
                near_two, _ = lax.optimization_barrier((near_two, core_free))
            plan = jnp.concatenate([plane.early, base])
            sums = gate_part(plan, chunk_ids, [two, near_two], *weights)
            far_two, sums = lax.optimization_barrier((far_two, sums))
            plan = jnp.concatenate([plane.late, base])
            hidden = gate_part(plan, chunk_ids, [far_two, plane.across(far_two)], *weights, sums)
            if sum_free is not None:
                hidden, _ = lax.optimization_barrier((hidden, sum_free))
            theirs = down_part(plane.theirs, hidden, down_weight, width)
            hidden, theirs = lax.optimization_barrier((hidden, theirs))
            mine = down_part(plane.mine, hidden, down_weight, width)
            share, core_free, sum_free = plane.scatter(mine, theirs)
        else:
            gathered = lax.all_gather(part, "exp", axis=0)
            order = jnp.arange(shares, dtype=jnp.int32)
            middle = shares // 2
            plan = jnp.concatenate([order[:middle], base])
            sums = gate_part(plan, chunk_ids, [gathered[:middle]], *weights)
            plan = jnp.concatenate([order[middle:], base])
            hidden = gate_part(plan, chunk_ids, [gathered[middle:]], *weights, sums)
            partial = down_part(order, hidden, down_weight, width)
            share = lax.psum_scatter(partial, "exp", scatter_dimension=0)
        for i, offset in enumerate(chunk):
            piece = share[i * length : (i + 1) * length]
            if offset:
                piece = swapped(piece, "seq", offset, offset)
            total = total + piece.astype(F32)
    return total.astype(BF16)


def solution(mesh):
    in_specs = (
        P("seq", "exp"),
        P("seq", "exp"),
        P("seq", "exp"),
        P("exp", "seq"),
        P("seq", "exp"),
        P("exp"),
        P("seq", None),
        P(None, "seq"),
        P("seq", None, "exp"),
        P("seq", None, "exp"),
        P("seq", "exp", None),
    )
    out_specs = P("seq", "exp")
    return jax.shard_map(
        on_device, mesh=mesh, in_specs=in_specs, out_specs=out_specs, check_vma=False
    )
```

```python
import functools

import jax
import jax.numpy as jnp
from jax import lax
from jax.experimental import pallas as pl
from jax.experimental.pallas import tpu as pltpu
from jax.sharding import PartitionSpec as P

F32 = jnp.float32
BF16 = jnp.bfloat16
HIGHEST = lax.Precision.HIGHEST
VMEM_LIMIT = 40 * 1024 * 1024
ID_ROWS = 16


def lower_ones(length):
    rows = lax.broadcasted_iota(jnp.int32, (length, length), 0)
    columns = lax.broadcasted_iota(jnp.int32, (length, length), 1)
    return rows >= columns


def shifted(array, axis, by):
    count = lax.axis_size(axis)
    pairs = [(i, i + by) for i in range(count) if 0 <= i + by < count]
    return lax.ppermute(array, axis, pairs)


def state_kernel(key_ref, value_ref, decay_ref, message_ref, cumulative_ref):
    heads, length = decay_ref.shape
    size = key_ref.shape[1] // heads
    ones = lower_ones(length).astype(F32)
    cumulative = lax.dot_general(
        ones, decay_ref[...], (((1,), (1,)), ((), ())), precision=HIGHEST, preferred_element_type=F32
    )
    cumulative_ref[...] = cumulative
    last = cumulative[length - 1 : length, :]
    key_fade = jnp.exp(last - cumulative)
    message_ref[heads * size :, :] = jnp.zeros((message_ref.shape[0] - heads * size, size), BF16)
    half = (message_ref.shape[0] - heads * size) // 2
    rows = []
    for h in range(heads):
        columns = slice(h * size, (h + 1) * size)
        scaled = (key_fade[:, h : h + 1] * key_ref[:, columns].astype(F32)).astype(BF16)
        state = lax.dot_general(
            scaled, value_ref[:, columns], (((0,), (0,)), ((), ())), preferred_element_type=F32
        )
        message_ref[columns, :] = state.astype(BF16)
        rows.append(jnp.broadcast_to(jnp.exp(last[:, h : h + 1]), (1, size)))
    rows.append(jnp.zeros((half - heads, size), F32))
    fade = jnp.concatenate(rows, axis=0)
    leading = fade.astype(BF16)
    trailing = (fade - leading.astype(F32)).astype(BF16)
    message_ref[heads * size :, :] = jnp.concatenate([leading, trailing], axis=0)


def section_state(attn_key, attn_value, log_decay):
    heads, length = log_decay.shape
    width = attn_key.shape[1]
    half = -(-heads // 8) * 8
    return pl.pallas_call(
        state_kernel,
        out_shape=(
            jax.ShapeDtypeStruct((width + 2 * half, width // heads), BF16),
            jax.ShapeDtypeStruct((length, heads), F32),
        ),
        cost_estimate=pl.CostEstimate(
            flops=2 * length * width * (width // heads), bytes_accessed=4 * length * width, transcendentals=0
        ),
        compiler_params=pltpu.CompilerParams(vmem_limit_bytes=VMEM_LIMIT),
    )(attn_key, attn_value, log_decay)


def intra_kernel(query_ref, key_ref, value_ref, decay_ref, cumulative_ref, out_ref):
    heads, length = decay_ref.shape
    size = key_ref.shape[1] // heads
    causal = lower_ones(length)
    along = lax.dot_general(
        decay_ref[...],
        causal.astype(F32),
        (((1,), (1,)), ((), ())),
        precision=HIGHEST,
        preferred_element_type=F32,
    )
    for h in range(heads):
        columns = slice(h * size, (h + 1) * size)
        gap = jnp.where(causal, cumulative_ref[:, h : h + 1] - along[h : h + 1, :], 0.0)
        mask = jnp.where(causal, jnp.exp(gap), 0.0)
        scores = lax.dot_general(
            query_ref[:, columns], key_ref[:, columns], (((1,), (1,)), ((), ())), preferred_element_type=F32
        )
        weights = (scores * mask).astype(BF16)
        out_ref[:, columns] = jnp.dot(weights, value_ref[:, columns], preferred_element_type=F32)


def intra_section(attn_query, attn_key, attn_value, log_decay, cumulative):
    length, width = attn_query.shape
    return pl.pallas_call(
        intra_kernel,
        out_shape=jax.ShapeDtypeStruct((length, width), F32),
        cost_estimate=pl.CostEstimate(
            flops=4 * length * length * width, bytes_accessed=10 * length * width, transcendentals=0
        ),
        compiler_params=pltpu.CompilerParams(vmem_limit_bytes=VMEM_LIMIT),
    )(attn_query, attn_key, attn_value, log_decay, cumulative)


def stream_kernel(
    query_ref, intra_ref, cumulative_ref, incoming_ref, residual_ref, gain_ref, ids_ref, out_ref
):
    heads, size = incoming_ref.shape[0], incoming_ref.shape[1]
    length, width = residual_ref.shape
    choices = ids_ref.shape[0]
    below = jnp.concatenate(
        [
            ids_ref[...].astype(F32),
            jnp.zeros((ID_ROWS - choices, length), F32),
        ],
        axis=0,
    )
    out_ref[length:, :] = jnp.concatenate(
        [below, jnp.zeros((ID_ROWS, width - length), F32)], axis=1
    ).astype(BF16)
    faded = jnp.exp(cumulative_ref[...])
    for h in range(heads):
        columns = slice(h * size, (h + 1) * size)
        state = incoming_ref[h]
        leading = state.astype(BF16)
        trailing = (state - leading.astype(F32)).astype(BF16)
        query = query_ref[:, columns]
        inter = jnp.dot(query, leading, preferred_element_type=F32) + jnp.dot(
            query, trailing, preferred_element_type=F32
        )
        attn_out = intra_ref[:, columns] + faded[:, h : h + 1] * inter
        mean_square = jnp.mean(attn_out * attn_out, axis=1, keepdims=True)
        normed = attn_out * lax.rsqrt(mean_square + 1e-06)
        out_ref[:length, columns] = (
            residual_ref[:, columns].astype(F32) + gain_ref[:, columns].astype(F32) * normed
        ).astype(BF16)


def make_stream(attn_query, intra, cumulative, incoming, residual, norm_gain, ids):
    length, width = attn_query.shape
    return pl.pallas_call(
        stream_kernel,
        out_shape=jax.ShapeDtypeStruct((length + ID_ROWS, width), BF16),
        compiler_params=pltpu.CompilerParams(vmem_limit_bytes=VMEM_LIMIT),
    )(attn_query, intra, cumulative, incoming, residual, norm_gain.reshape(1, width), ids)


def read_message(message, heads):
    size = message.shape[1]
    half = (message.shape[0] - heads * size) // 2
    state = message[: heads * size].astype(F32).reshape(heads, size, size)
    tail = message[heads * size :].astype(F32)
    fade = tail[:heads] + tail[half : half + heads]
    return fade[:, None, :], state


def write_message(fade, state, rows):
    heads, size = state.shape[0], state.shape[1]
    half = (rows - heads * size) // 2
    leading = fade[:, 0, :].astype(BF16)
    trailing = (fade[:, 0, :] - leading.astype(F32)).astype(BF16)
    spare = jnp.zeros((half - heads, size), BF16)
    return jnp.concatenate(
        [state.astype(BF16).reshape(heads * size, size), leading, spare, trailing, spare], axis=0
    )


def incoming_state(message, heads):
    count = lax.axis_size("seq")
    window_fade, window = read_message(message, heads)
    incoming_fade, incoming = None, None
    distance = 1
    while distance < count:
        got_fade, got = read_message(shifted(message, "seq", distance), heads)
        if incoming is None:
            incoming_fade, incoming = got_fade, got
        else:
            incoming, incoming_fade = incoming + incoming_fade * got, incoming_fade * got_fade
        window, window_fade = window + window_fade * got, window_fade * got_fade
        distance *= 2
        if distance < count:
            message = write_message(window_fade, window, message.shape[0])
    return incoming


def select_kernel(capacity, choices, experts, base_ref, *refs):
    parts, (out_ref, place_ref) = refs[:-2], refs[-2:]
    length = parts[0].shape[0] - ID_ROWS
    before = lower_ones(length).astype(BF16)
    slot = lax.broadcasted_iota(jnp.int32, (capacity, length), 0).astype(F32)
    nothing = jnp.zeros((capacity, length), BF16)
    rows = []
    for j in range(experts):
        expert = (base_ref[0] + j).astype(F32)
        for i, part in enumerate(parts):
            ids = part[length:, :length].astype(F32)
            chosen = ids[0:1, :] == expert
            for choice in range(1, choices):
                chosen = chosen | (ids[choice : choice + 1, :] == expert)
            flag = jnp.where(chosen, 1.0, 0.0)
            rank = lax.dot_general(
                jnp.broadcast_to(flag, (16, length)).astype(BF16),
                before,
                (((1,), (1,)), ((), ())),
                preferred_element_type=F32,
            )[0:1, :]
            rank = jnp.where(chosen, rank - 1.0, -1.0)
            here = jnp.where(slot == rank, 1.0, 0.0).astype(BF16)
            rows.append(
                jnp.concatenate([here if k == i else nothing for k in range(len(parts))], axis=1)
            )
    place = jnp.concatenate(rows, axis=0)
    place_ref[...] = place
    tokens = jnp.concatenate([part[:length, :] for part in parts], axis=0)
    out_ref[...] = lax.dot_general(
        tokens, place, (((0,), (1,)), ((), ())), preferred_element_type=F32
    ).astype(BF16)


def select_slots(base, parts, capacity, choices, experts):
    rows, width = parts[0].shape
    length = rows - ID_ROWS
    slots = len(parts) * experts * capacity
    tokens = len(parts) * length
    whole = pl.BlockSpec(memory_space=pltpu.VMEM)
    return pl.pallas_call(
        functools.partial(select_kernel, capacity, choices, experts),
        in_specs=[pl.BlockSpec(memory_space=pltpu.SMEM), *([whole] * len(parts))],
        out_shape=(
            jax.ShapeDtypeStruct((width, slots), BF16),
            jax.ShapeDtypeStruct((slots, tokens), BF16),
        ),
        cost_estimate=pl.CostEstimate(
            flops=2 * slots * tokens * width, bytes_accessed=4 * slots * width, transcendentals=0
        ),
        compiler_params=pltpu.CompilerParams(vmem_limit_bytes=VMEM_LIMIT),
    )(base, *parts)


def combine_kernel(length, place_ref, *refs):
    sections = place_ref.shape[1] // length
    shares, outs = refs[:-sections], refs[-sections:]
    total = shares[0][...].astype(F32)
    for share in shares[1:]:
        total = total + share[...].astype(F32)
    tokens = lax.dot_general(
        place_ref[...], total.astype(BF16), (((0,), (0,)), ((), ())), preferred_element_type=F32
    ).astype(BF16)
    for i, out in enumerate(outs):
        out[...] = tokens[i * length : (i + 1) * length, :]


def combine_slots(place, shares, length):
    slots, tokens = place.shape
    width = shares[0].shape[1]
    return pl.pallas_call(
        functools.partial(combine_kernel, length),
        out_shape=tuple(
            jax.ShapeDtypeStruct((length, width), BF16) for _ in range(tokens // length)
        ),
        cost_estimate=pl.CostEstimate(
            flops=2 * slots * tokens * width, bytes_accessed=8 * slots * width, transcendentals=0
        ),
        compiler_params=pltpu.CompilerParams(vmem_limit_bytes=VMEM_LIMIT),
    )(place, *shares)


def gate_kernel(counts, last, plan_ref, *refs):
    step = pl.program_id(0)
    blocks = sum(counts)
    x_refs, refs = refs[: len(counts)], refs[len(counts) :]
    router_ref, gate_ref, up_ref = refs[:3]
    refs = refs[3:]
    if last:
        gate_in, up_in, score_in, hidden_ref, gate_acc, up_acc, score_acc = refs
    else:
        gate_acc, up_acc, score_acc = refs
    experts = gate_ref.shape[0]
    slots = gate_acc.shape[2]

    @pl.when(step == 0)
    def _():
        if last:
            gate_acc[...] = gate_in[...]
            up_acc[...] = up_in[...]
            score_acc[...] = score_in[...]
        else:
            gate_acc[...] = jnp.zeros_like(gate_acc)
            up_acc[...] = jnp.zeros_like(up_acc)
            score_acc[...] = jnp.zeros_like(score_acc)

    x = x_refs[-1][0]
    for i in range(len(counts) - 2, -1, -1):
        x = jnp.where(step < sum(counts[: i + 1]), x_refs[i][0], x)
    score_acc[...] += jnp.dot(router_ref[0], x, preferred_element_type=F32)
    for j in range(experts):
        mine = x[:, j * slots : (j + 1) * slots]
        gate_acc[j] += jnp.dot(gate_ref[j], mine, preferred_element_type=F32)
        up_acc[j] += jnp.dot(up_ref[j], mine, preferred_element_type=F32)

    if last:

        @pl.when(step == blocks - 1)
        def _():
            for j in range(experts):
                score = score_acc[j : j + 1, j * slots : (j + 1) * slots]
                gate = gate_acc[j]
                routed = gate / (1.0 + jnp.exp(-gate)) * up_acc[j]
                routed = routed / (1.0 + jnp.exp(-score))
                hidden_ref[j] = routed.T.astype(BF16)


def gate_part(plan, xs, router_rows, gate_rows, up_rows, sums=None):
    counts = tuple(x.shape[0] for x in xs)
    blocks = sum(counts)
    _, width, total = xs[0].shape
    experts, units, _ = gate_rows.shape
    slots = total // experts
    whole = pl.BlockSpec(memory_space=pltpu.VMEM)
    last = sums is not None

    def x_spec(i):
        before = sum(counts[:i])
        return pl.BlockSpec(
            (1, width, total), lambda p, plan: (jnp.clip(p - before, 0, counts[i] - 1), 0, 0)
        )

    weight_spec = pl.BlockSpec((experts, units, width), lambda p, plan: (0, 0, plan[p]))
    sum_shapes = [(experts, units, slots), (experts, units, slots), (experts, total)]
    if last:
        out_shape = jax.ShapeDtypeStruct((experts, slots, units), BF16)
        out_specs = whole
        scratch = [pltpu.VMEM(shape, F32) for shape in sum_shapes]
    else:
        out_shape = tuple(jax.ShapeDtypeStruct(shape, F32) for shape in sum_shapes)
        out_specs = (whole, whole, whole)
        scratch = []
    return pl.pallas_call(
        functools.partial(gate_kernel, counts, last),
        grid_spec=pltpu.PrefetchScalarGridSpec(
            num_scalar_prefetch=1,
            grid=(blocks,),
            in_specs=[
                *[x_spec(i) for i in range(len(counts))],
                pl.BlockSpec((1, experts, width), lambda p, plan: (plan[p], 0, 0)),
                weight_spec,
                weight_spec,
                *([whole] * 3 if last else []),
            ],
            out_specs=out_specs,
            scratch_shapes=scratch,
        ),
        out_shape=out_shape,
        cost_estimate=pl.CostEstimate(
            flops=4 * total * blocks * width * units,
            bytes_accessed=4 * experts * blocks * width * units,
            transcendentals=0,
        ),
        compiler_params=pltpu.CompilerParams(vmem_limit_bytes=VMEM_LIMIT),
    )(plan, *xs, router_rows, gate_rows, up_rows, *(sums if last else ()))


def down_kernel(plan_ref, hidden_ref, down_ref, out_ref):
    experts, slots, _ = hidden_ref.shape
    for j in range(experts):
        out_ref[0, j * slots : (j + 1) * slots, :] = jnp.dot(
            hidden_ref[j], down_ref[j], preferred_element_type=F32
        ).astype(BF16)


def down_part(plan, hidden, down_weight, width):
    blocks = plan.shape[0]
    experts, slots, units = hidden.shape
    return pl.pallas_call(
        down_kernel,
        grid_spec=pltpu.PrefetchScalarGridSpec(
            num_scalar_prefetch=1,
            grid=(blocks,),
            in_specs=[
                pl.BlockSpec(memory_space=pltpu.VMEM),
                pl.BlockSpec((experts, units, width), lambda p, plan: (0, 0, plan[p])),
            ],
            out_specs=pl.BlockSpec((1, experts * slots, width), lambda p, plan: (p, 0, 0)),
        ),
        out_shape=jax.ShapeDtypeStruct((blocks, experts * slots, width), BF16),
        cost_estimate=pl.CostEstimate(
            flops=2 * experts * slots * blocks * width * units,
            bytes_accessed=2 * experts * blocks * width * units,
            transcendentals=0,
        ),
        compiler_params=pltpu.CompilerParams(vmem_limit_bytes=VMEM_LIMIT),
    )(plan, hidden, down_weight)


def added(left, right):
    return (left.astype(F32) + right.astype(F32)).astype(BF16)


def swapped(array, axis, even, odd):
    count = lax.axis_size(axis)
    pairs = [(i, i ^ (odd if i % 2 else even)) for i in range(count)]
    return lax.ppermute(array, axis, pairs)


class PairedPlane:
    def __init__(self):
        me = lax.axis_index("exp").astype(jnp.int32)
        other = me ^ 1
        near = jnp.where(me % 2 == 0, 2, 4)
        far = 6 - near
        self.early = jnp.stack([me, me ^ near, other, other ^ far])
        self.late = jnp.stack([me ^ far, me ^ 6, other ^ near, other ^ 6])
        self.mine = jnp.stack([me, me ^ near, me ^ far, me ^ 6])
        self.theirs = jnp.stack([other, other ^ far, other ^ near, other ^ 6])

    def first(self, part):
        return jnp.stack([part, swapped(part, "exp", 2, 4)])

    def second(self, two):
        return swapped(two, "exp", 4, 2)

    def across(self, two):
        return swapped(two, "exp", 1, 1)

    def scatter(self, mine, theirs):
        got = swapped(theirs, "exp", 1, 1)
        sent_two = added(mine[2:], got[2:])
        got_two = swapped(sent_two, "exp", 4, 2)
        got_one = swapped(added(added(mine[1], got[1]), got_two[1]), "exp", 2, 4)
        return (mine[0], got[0], got_two[0], got_one), sent_two, got_two


def on_device(
    attn_query,
    attn_key,
    attn_value,
    log_decay,
    residual,
    norm_gain,
    expert_ids,
    router_weight,
    gate_weight,
    up_weight,
    down_weight,
):
    heads_here, length = log_decay.shape
    groups = lax.axis_size("seq")
    shares = lax.axis_size("exp")
    width = attn_query.shape[1]
    experts_here = router_weight.shape[1]
    base = (lax.axis_index("seq") * experts_here).astype(jnp.int32).reshape(1)
    router_rows = router_weight.reshape(shares, width, experts_here).transpose(0, 2, 1)
    gate_rows = gate_weight.swapaxes(1, 2)
    up_rows = up_weight.swapaxes(1, 2)

    message, cumulative = section_state(attn_key, attn_value, log_decay)
    intra = intra_section(attn_query, attn_key, attn_value, log_decay, cumulative)
    incoming = incoming_state(message, heads_here)
    stream = make_stream(
        attn_query, intra, cumulative, incoming, residual, norm_gain, expert_ids.T
    )

    half = groups // 2
    chunks = [(i, i + half) for i in range(half)]
    parts = {0: stream}
    parts[half] = swapped(stream, "seq", half, half)
    later, _ = lax.optimization_barrier((stream, parts[half]))
    for i in range(1, half):
        for offset in chunks[i]:
            parts[offset] = swapped(later, "seq", offset, offset)

    capacity = 4 * length // (experts_here * groups)
    weights = (router_rows, gate_rows, up_rows)
    total = stream[:length].astype(F32)
    if shares == 8:
        pieces = paired_chunks(
            PairedPlane(),
            [[parts[offset] for offset in chunk] for chunk in chunks],
            base,
            weights,
            down_weight,
            capacity,
            expert_ids.shape[1],
        )
    else:
        order = jnp.arange(shares, dtype=jnp.int32)
        middle = shares // 2
        pieces = []
        for chunk in chunks:
            chosen, place = select_slots(
                base, [parts[offset] for offset in chunk], capacity, expert_ids.shape[1], experts_here
            )
            gathered = lax.all_gather(chosen, "exp", axis=0)
            sums = gate_part(order[:middle], [gathered[:middle]], *weights)
            hidden = gate_part(order[middle:], [gathered[middle:]], *weights, sums)
            partial = down_part(order, hidden, down_weight, width)
            share = lax.psum_scatter(partial, "exp", scatter_dimension=0)
            pieces.append(combine_slots(place, [share], length))
    for chunk, chunk_pieces in zip(chunks, pieces):
        for offset, piece in zip(chunk, chunk_pieces):
            if offset:
                piece = swapped(piece, "seq", offset, offset)
            total = total + piece.astype(F32)
    return total.astype(BF16)


def paired_chunks(plane, chunk_parts, base, weights, down_weight, capacity, choices):
    experts = down_weight.shape[0]
    length = chunk_parts[0][0].shape[0] - ID_ROWS
    width = chunk_parts[0][0].shape[1]
    tie = lax.optimization_barrier
    chosen = [
        select_slots(base, parts, capacity, choices, experts) for parts in chunk_parts
    ]
    two = [plane.first(slots) for slots, _ in chosen]
    pieces = []
    sent_two, got_two = None, None
    for i, (_, place) in enumerate(chosen):
        follows = i + 1 < len(chosen)
        far_two = plane.second(two[i])
        near_two = plane.across(two[i])
        if follows:
            near_two, _ = tie((near_two, chosen[i + 1]))
        if sent_two is not None:
            near_two, _ = tie((near_two, sent_two))
        sums = gate_part(plane.early, [two[i], near_two], *weights)
        far_two, sums = tie((far_two, sums))
        near_far = plane.across(far_two)
        if follows:
            near_far, _ = tie((near_far, two[i + 1]))
        hidden = gate_part(plane.late, [far_two, near_far], *weights, sums)
        if got_two is not None:
            hidden, _ = tie((hidden, got_two))
        theirs = down_part(plane.theirs, hidden, down_weight, width)
        hidden, theirs = tie((hidden, theirs))
        mine = down_part(plane.mine, hidden, down_weight, width)
        share, sent_two, got_two = plane.scatter(mine, theirs)
        pieces.append(combine_slots(place, share, length))
    return pieces


def solution(mesh):
    in_specs = (
        P("seq", "exp"),
        P("seq", "exp"),
        P("seq", "exp"),
        P("exp", "seq"),
        P("seq", "exp"),
        P("exp"),
        P("seq", None),
        P(None, "seq"),
        P("seq", None, "exp"),
        P("seq", None, "exp"),
        P("seq", "exp", None),
    )
    out_specs = P("seq", "exp")
    return jax.shard_map(
        on_device, mesh=mesh, in_specs=in_specs, out_specs=out_specs, check_vma=False
    )
```

```python
import functools

import jax
import jax.numpy as jnp
from jax import lax
from jax.experimental import pallas as pl
from jax.experimental.pallas import tpu as pltpu
from jax.sharding import PartitionSpec as P

F32 = jnp.float32
BF16 = jnp.bfloat16
HIGHEST = lax.Precision.HIGHEST
VMEM_LIMIT = 50 * 1024 * 1024
ID_ROWS = 16


def lower_ones(length):
    rows = lax.broadcasted_iota(jnp.int32, (length, length), 0)
    columns = lax.broadcasted_iota(jnp.int32, (length, length), 1)
    return rows >= columns


def shifted(array, axis, by):
    count = lax.axis_size(axis)
    pairs = [(i, i + by) for i in range(count) if 0 <= i + by < count]
    return lax.ppermute(array, axis, pairs)


def state_kernel(key_ref, value_ref, decay_ref, message_ref, cumulative_ref):
    heads, length = decay_ref.shape
    size = key_ref.shape[1] // heads
    ones = lower_ones(length).astype(F32)
    cumulative = lax.dot_general(
        ones, decay_ref[...], (((1,), (1,)), ((), ())), precision=HIGHEST, preferred_element_type=F32
    )
    cumulative_ref[...] = cumulative
    last = cumulative[length - 1 : length, :]
    key_fade = jnp.exp(last - cumulative)
    message_ref[heads * size :, :] = jnp.zeros((message_ref.shape[0] - heads * size, size), BF16)
    half = (message_ref.shape[0] - heads * size) // 2
    rows = []
    for h in range(heads):
        columns = slice(h * size, (h + 1) * size)
        scaled = (key_fade[:, h : h + 1] * key_ref[:, columns].astype(F32)).astype(BF16)
        state = lax.dot_general(
            scaled, value_ref[:, columns], (((0,), (0,)), ((), ())), preferred_element_type=F32
        )
        message_ref[columns, :] = state.astype(BF16)
        rows.append(jnp.broadcast_to(jnp.exp(last[:, h : h + 1]), (1, size)))
    rows.append(jnp.zeros((half - heads, size), F32))
    fade = jnp.concatenate(rows, axis=0)
    leading = fade.astype(BF16)
    trailing = (fade - leading.astype(F32)).astype(BF16)
    message_ref[heads * size :, :] = jnp.concatenate([leading, trailing], axis=0)


def section_state(attn_key, attn_value, log_decay):
    heads, length = log_decay.shape
    width = attn_key.shape[1]
    half = -(-heads // 8) * 8
    return pl.pallas_call(
        state_kernel,
        out_shape=(
            jax.ShapeDtypeStruct((width + 2 * half, width // heads), BF16),
            jax.ShapeDtypeStruct((length, heads), F32),
        ),
        cost_estimate=pl.CostEstimate(
            flops=2 * length * width * (width // heads), bytes_accessed=4 * length * width, transcendentals=0
        ),
        compiler_params=pltpu.CompilerParams(vmem_limit_bytes=VMEM_LIMIT),
    )(attn_key, attn_value, log_decay)


def intra_kernel(query_ref, key_ref, value_ref, decay_ref, cumulative_ref, out_ref):
    heads, length = decay_ref.shape
    size = key_ref.shape[1] // heads
    causal = lower_ones(length)
    along = lax.dot_general(
        decay_ref[...],
        causal.astype(F32),
        (((1,), (1,)), ((), ())),
        precision=HIGHEST,
        preferred_element_type=F32,
    )
    for h in range(heads):
        columns = slice(h * size, (h + 1) * size)
        gap = jnp.where(causal, cumulative_ref[:, h : h + 1] - along[h : h + 1, :], 0.0)
        mask = jnp.where(causal, jnp.exp(gap), 0.0)
        scores = lax.dot_general(
            query_ref[:, columns], key_ref[:, columns], (((1,), (1,)), ((), ())), preferred_element_type=F32
        )
        weights = (scores * mask).astype(BF16)
        out_ref[:, columns] = jnp.dot(weights, value_ref[:, columns], preferred_element_type=F32)


def intra_section(attn_query, attn_key, attn_value, log_decay, cumulative):
    length, width = attn_query.shape
    return pl.pallas_call(
        intra_kernel,
        out_shape=jax.ShapeDtypeStruct((length, width), F32),
        cost_estimate=pl.CostEstimate(
            flops=4 * length * length * width, bytes_accessed=10 * length * width, transcendentals=0
        ),
        compiler_params=pltpu.CompilerParams(vmem_limit_bytes=VMEM_LIMIT),
    )(attn_query, attn_key, attn_value, log_decay, cumulative)


def stream_kernel(
    query_ref, intra_ref, cumulative_ref, incoming_ref, residual_ref, gain_ref, ids_ref, out_ref
):
    heads, size = incoming_ref.shape[0], incoming_ref.shape[1]
    length, width = residual_ref.shape
    choices = ids_ref.shape[0]
    below = jnp.concatenate(
        [
            ids_ref[...].astype(F32),
            jnp.zeros((ID_ROWS - choices, length), F32),
        ],
        axis=0,
    )
    out_ref[length:, :] = jnp.concatenate(
        [below, jnp.zeros((ID_ROWS, width - length), F32)], axis=1
    ).astype(BF16)
    faded = jnp.exp(cumulative_ref[...])
    for h in range(heads):
        columns = slice(h * size, (h + 1) * size)
        state = incoming_ref[h]
        leading = state.astype(BF16)
        trailing = (state - leading.astype(F32)).astype(BF16)
        query = query_ref[:, columns]
        inter = jnp.dot(query, leading, preferred_element_type=F32) + jnp.dot(
            query, trailing, preferred_element_type=F32
        )
        attn_out = intra_ref[:, columns] + faded[:, h : h + 1] * inter
        mean_square = jnp.mean(attn_out * attn_out, axis=1, keepdims=True)
        normed = attn_out * lax.rsqrt(mean_square + 1e-06)
        out_ref[:length, columns] = (
            residual_ref[:, columns].astype(F32) + gain_ref[:, columns].astype(F32) * normed
        ).astype(BF16)


def make_stream(attn_query, intra, cumulative, incoming, residual, norm_gain, ids):
    length, width = attn_query.shape
    return pl.pallas_call(
        stream_kernel,
        out_shape=jax.ShapeDtypeStruct((length + ID_ROWS, width), BF16),
        compiler_params=pltpu.CompilerParams(vmem_limit_bytes=VMEM_LIMIT),
    )(attn_query, intra, cumulative, incoming, residual, norm_gain.reshape(1, width), ids)


def read_message(message, heads):
    size = message.shape[1]
    half = (message.shape[0] - heads * size) // 2
    state = message[: heads * size].astype(F32).reshape(heads, size, size)
    tail = message[heads * size :].astype(F32)
    fade = tail[:heads] + tail[half : half + heads]
    return fade[:, None, :], state


def write_message(fade, state, rows):
    heads, size = state.shape[0], state.shape[1]
    half = (rows - heads * size) // 2
    leading = fade[:, 0, :].astype(BF16)
    trailing = (fade[:, 0, :] - leading.astype(F32)).astype(BF16)
    spare = jnp.zeros((half - heads, size), BF16)
    return jnp.concatenate(
        [state.astype(BF16).reshape(heads * size, size), leading, spare, trailing, spare], axis=0
    )


def incoming_state(message, heads):
    count = lax.axis_size("seq")
    window_fade, window = read_message(message, heads)
    incoming_fade, incoming = None, None
    distance = 1
    while distance < count:
        got_fade, got = read_message(shifted(message, "seq", distance), heads)
        if incoming is None:
            incoming_fade, incoming = got_fade, got
        else:
            incoming, incoming_fade = incoming + incoming_fade * got, incoming_fade * got_fade
        window, window_fade = window + window_fade * got, window_fade * got_fade
        distance *= 2
        if distance < count:
            message = write_message(window_fade, window, message.shape[0])
    return incoming


def select_kernel(capacity, choices, experts, base_ref, part_ref, out_ref, place_ref):
    length = part_ref.shape[0] - ID_ROWS
    before = lower_ones(length).astype(BF16)
    slot = lax.broadcasted_iota(jnp.int32, (capacity, length), 0).astype(F32)
    ids = part_ref[length:, :length].astype(F32)
    rows = []
    for j in range(experts):
        expert = (base_ref[0] + j).astype(F32)
        chosen = ids[0:1, :] == expert
        for choice in range(1, choices):
            chosen = chosen | (ids[choice : choice + 1, :] == expert)
        flag = jnp.where(chosen, 1.0, 0.0)
        rank = lax.dot_general(
            jnp.broadcast_to(flag, (16, length)).astype(BF16),
            before,
            (((1,), (1,)), ((), ())),
            preferred_element_type=F32,
        )[0:1, :]
        rank = jnp.where(chosen, rank - 1.0, -1.0)
        rows.append(jnp.where(slot == rank, 1.0, 0.0).astype(BF16))
    place = jnp.concatenate(rows, axis=0)
    place_ref[...] = place
    out_ref[...] = lax.dot_general(
        part_ref[:length, :], place, (((0,), (1,)), ((), ())), preferred_element_type=F32
    ).astype(BF16)


def select_slots(base, part, capacity, choices, experts):
    rows, width = part.shape
    length = rows - ID_ROWS
    slots = experts * capacity
    whole = pl.BlockSpec(memory_space=pltpu.VMEM)
    return pl.pallas_call(
        functools.partial(select_kernel, capacity, choices, experts),
        in_specs=[pl.BlockSpec(memory_space=pltpu.SMEM), whole],
        out_shape=(
            jax.ShapeDtypeStruct((width, slots), BF16),
            jax.ShapeDtypeStruct((slots, length), BF16),
        ),
        cost_estimate=pl.CostEstimate(
            flops=2 * slots * length * width, bytes_accessed=4 * slots * width, transcendentals=0
        ),
        compiler_params=pltpu.CompilerParams(vmem_limit_bytes=VMEM_LIMIT),
    )(base, part)


def combine_kernel(place_ref, *refs):
    shares, out_ref = refs[:-1], refs[-1]
    total = shares[0][...].astype(F32)
    for share in shares[1:]:
        total = total + share[...].astype(F32)
    out_ref[...] = lax.dot_general(
        place_ref[...], total.astype(BF16), (((0,), (0,)), ((), ())), preferred_element_type=F32
    ).astype(BF16)


def combine_slots(place, shares):
    slots, length = place.shape
    width = shares[0].shape[1]
    return pl.pallas_call(
        combine_kernel,
        out_shape=jax.ShapeDtypeStruct((length, width), BF16),
        cost_estimate=pl.CostEstimate(
            flops=2 * slots * length * width, bytes_accessed=8 * slots * width, transcendentals=0
        ),
        compiler_params=pltpu.CompilerParams(vmem_limit_bytes=VMEM_LIMIT),
    )(place, *shares)


def gate_kernel(counts, sections, last, plan_ref, *refs):
    step = pl.program_id(0)
    blocks = sum(counts)
    used = len(counts) * sections
    x_refs, refs = refs[:used], refs[used:]
    router_ref, gate_ref, up_ref = refs[:3]
    refs = refs[3:]
    if last:
        gate_in, up_in, score_in, hidden_ref, gate_acc, up_acc, score_acc = refs
    else:
        gate_acc, up_acc, score_acc = refs
    experts = gate_ref.shape[0]
    width = x_refs[0].shape[1]
    slots = gate_acc.shape[2]
    part = slots // sections

    @pl.when(step == 0)
    def _():
        if last:
            gate_acc[...] = gate_in[...]
            up_acc[...] = up_in[...]
            score_acc[...] = score_in[...]
        else:
            gate_acc[...] = jnp.zeros_like(gate_acc)
            up_acc[...] = jnp.zeros_like(up_acc)
            score_acc[...] = jnp.zeros_like(score_acc)

    xs = []
    for section in range(sections):
        mine = x_refs[section * len(counts) : (section + 1) * len(counts)]
        x = mine[-1][0]
        for i in range(len(counts) - 2, -1, -1):
            x = jnp.where(step < sum(counts[: i + 1]), mine[i][0], x)
        xs.append(x)
    for j in range(experts):
        x = jnp.concatenate([x[:, j * part : (j + 1) * part] for x in xs], axis=1)
        score_acc[j] += jnp.dot(router_ref[0], x, preferred_element_type=F32)
        gate_acc[j] += jnp.dot(gate_ref[j], x, preferred_element_type=F32)
        up_acc[j] += jnp.dot(up_ref[j], x, preferred_element_type=F32)

    if last:

        @pl.when(step == blocks - 1)
        def _():
            for j in range(experts):
                score = score_acc[j, j : j + 1, :]
                gate = gate_acc[j]
                routed = gate / (1.0 + jnp.exp(-gate)) * up_acc[j]
                routed = routed / (1.0 + jnp.exp(-score))
                hidden_ref[j] = routed.T.astype(BF16)


def gate_part(plan, xs, router_rows, gate_rows, up_rows, sums=None):
    counts = tuple(x.shape[0] for x in xs[0])
    blocks = sum(counts)
    _, width, total = xs[0][0].shape
    experts, units, _ = gate_rows.shape
    slots = total // experts * len(xs)
    whole = pl.BlockSpec(memory_space=pltpu.VMEM)
    last = sums is not None

    def x_spec(i):
        before = sum(counts[:i])
        return pl.BlockSpec(
            (1, width, total), lambda p, plan: (jnp.clip(p - before, 0, counts[i] - 1), 0, 0)
        )

    weight_spec = pl.BlockSpec((experts, units, width), lambda p, plan: (0, 0, plan[p]))
    sum_shapes = [(experts, units, slots), (experts, units, slots), (experts, experts, slots)]
    if last:
        out_shape = jax.ShapeDtypeStruct((experts, slots, units), BF16)
        out_specs = whole
        scratch = [pltpu.VMEM(shape, F32) for shape in sum_shapes]
    else:
        out_shape = tuple(jax.ShapeDtypeStruct(shape, F32) for shape in sum_shapes)
        out_specs = (whole, whole, whole)
        scratch = []
    return pl.pallas_call(
        functools.partial(gate_kernel, counts, len(xs), last),
        grid_spec=pltpu.PrefetchScalarGridSpec(
            num_scalar_prefetch=1,
            grid=(blocks,),
            in_specs=[
                *[x_spec(i) for _ in xs for i in range(len(counts))],
                pl.BlockSpec((1, experts, width), lambda p, plan: (plan[p], 0, 0)),
                weight_spec,
                weight_spec,
                *([whole] * 3 if last else []),
            ],
            out_specs=out_specs,
            scratch_shapes=scratch,
        ),
        out_shape=out_shape,
        cost_estimate=pl.CostEstimate(
            flops=4 * experts * slots * blocks * width * units,
            bytes_accessed=4 * experts * blocks * width * units,
            transcendentals=0,
        ),
        compiler_params=pltpu.CompilerParams(vmem_limit_bytes=VMEM_LIMIT),
    )(plan, *[x for section in xs for x in section], router_rows, gate_rows, up_rows, *(sums or ()))


def down_kernel(plan_ref, hidden_ref, down_ref, *out_refs):
    experts, slots, _ = hidden_ref.shape
    width = out_refs[0].shape[2]
    part = slots // len(out_refs)
    for j in range(experts):
        share = jnp.dot(hidden_ref[j], down_ref[j], preferred_element_type=F32).astype(BF16)
        for section, out_ref in enumerate(out_refs):
            out_ref[0, j * part : (j + 1) * part, :] = share[section * part : (section + 1) * part]


def down_part(plan, hidden, down_weight, width, sections):
    blocks = plan.shape[0]
    experts, slots, units = hidden.shape
    rows = experts * slots // sections
    return pl.pallas_call(
        down_kernel,
        grid_spec=pltpu.PrefetchScalarGridSpec(
            num_scalar_prefetch=1,
            grid=(blocks,),
            in_specs=[
                pl.BlockSpec(memory_space=pltpu.VMEM),
                pl.BlockSpec((experts, units, width), lambda p, plan: (0, 0, plan[p])),
            ],
            out_specs=[pl.BlockSpec((1, rows, width), lambda p, plan: (p, 0, 0))] * sections,
        ),
        out_shape=[jax.ShapeDtypeStruct((blocks, rows, width), BF16)] * sections,
        cost_estimate=pl.CostEstimate(
            flops=2 * experts * slots * blocks * width * units,
            bytes_accessed=2 * experts * blocks * width * units,
            transcendentals=0,
        ),
        compiler_params=pltpu.CompilerParams(vmem_limit_bytes=VMEM_LIMIT),
    )(plan, hidden, down_weight)


def added(left, right):
    return (left.astype(F32) + right.astype(F32)).astype(BF16)


def swapped(array, axis, even, odd):
    count = lax.axis_size(axis)
    pairs = [(i, i ^ (odd if i % 2 else even)) for i in range(count)]
    return lax.ppermute(array, axis, pairs)


class PairedPlane:
    def __init__(self):
        me = lax.axis_index("exp").astype(jnp.int32)
        other = me ^ 1
        near = jnp.where(me % 2 == 0, 2, 4)
        far = 6 - near
        self.early = jnp.stack([me, me ^ near, other, other ^ far])
        self.late = jnp.stack([me ^ far, me ^ 6, other ^ near, other ^ 6])
        self.mine = jnp.stack([me, me ^ near, me ^ far, me ^ 6])
        self.theirs = jnp.stack([other, other ^ far, other ^ near, other ^ 6])

    def once(self, part):
        return swapped(part, "exp", 2, 4)

    def first(self, part):
        return jnp.stack([part, self.once(part)])

    def second(self, two):
        return swapped(two, "exp", 4, 2)

    def across(self, two):
        return swapped(two, "exp", 1, 1)

def on_device(
    attn_query,
    attn_key,
    attn_value,
    log_decay,
    residual,
    norm_gain,
    expert_ids,
    router_weight,
    gate_weight,
    up_weight,
    down_weight,
):
    heads_here, length = log_decay.shape
    groups = lax.axis_size("seq")
    shares = lax.axis_size("exp")
    width = attn_query.shape[1]
    experts_here = router_weight.shape[1]
    base = (lax.axis_index("seq") * experts_here).astype(jnp.int32).reshape(1)
    router_rows = router_weight.reshape(shares, width, experts_here).transpose(0, 2, 1)
    gate_rows = gate_weight.swapaxes(1, 2)
    up_rows = up_weight.swapaxes(1, 2)

    message, cumulative = section_state(attn_key, attn_value, log_decay)
    intra = intra_section(attn_query, attn_key, attn_value, log_decay, cumulative)
    incoming = incoming_state(message, heads_here)
    stream = make_stream(
        attn_query, intra, cumulative, incoming, residual, norm_gain, expert_ids.T
    )

    half = groups // 2
    chunks = [(0, half)] + [(half + i, i) for i in range(1, half)]
    parts = {0: stream}
    parts[half] = swapped(stream, "seq", half, half)
    later, _ = lax.optimization_barrier((stream, parts[half]))
    for chunk in chunks[1:]:
        for offset in reversed(chunk):
            parts[offset] = swapped(later, "seq", offset, offset)

    capacity = 4 * length // (experts_here * groups)
    choices = expert_ids.shape[1]
    chosen = {
        offset: select_slots(base, parts[offset], capacity, choices, experts_here)
        for chunk in chunks
        for offset in chunk
    }
    weights = (router_rows, gate_rows, up_rows)
    if shares == 8:
        pieces = paired_chunks(PairedPlane(), chunks, chosen, weights, down_weight)
    else:
        order = jnp.arange(shares, dtype=jnp.int32)
        middle = shares // 2
        pieces = {}
        for chunk in chunks:
            gathered = [lax.all_gather(chosen[offset][0], "exp", axis=0) for offset in chunk]
            sums = gate_part(order[:middle], [[x[:middle]] for x in gathered], *weights)
            hidden = gate_part(order[middle:], [[x[middle:]] for x in gathered], *weights, sums)
            partial = down_part(order, hidden, down_weight, width, len(chunk))
            for offset, share in zip(chunk, partial):
                share = lax.psum_scatter(share, "exp", scatter_dimension=0)
                pieces[offset] = combine_slots(chosen[offset][1], [share])
    total = stream[:length].astype(F32)
    for offset, piece in pieces.items():
        if offset:
            piece = swapped(piece, "seq", offset, offset)
        total = total + piece.astype(F32)
    return total.astype(BF16)


def paired_chunks(plane, chunks, chosen, weights, down_weight):
    width = chosen[0][0].shape[0]
    tie = lax.optimization_barrier
    two, far_two, near, near_far = {}, {}, {}, {}
    for chunk in chunks:
        for offset in sorted(chunk):
            two[offset] = plane.first(chosen[offset][0])
            near[offset] = plane.across(two[offset])
            far_two[offset] = plane.second(two[offset])
            near_far[offset] = plane.across(far_two[offset])
    pieces = {}
    sent, got = [], []
    for i, chunk in enumerate(chunks):
        after = sorted(chunks[i + 1]) if i + 1 < len(chunks) else []
        early = [[two[offset], near[offset]] for offset in chunk]
        late = [[far_two[offset], near_far[offset]] for offset in chunk]
        if after:
            early, _ = tie((early, chosen[after[0]]))
        if sent:
            early, _ = tie((early, sent))
        sums = gate_part(plane.early, early, *weights)
        late, sums = tie((late, sums))
        if after:
            late, _ = tie((late, [two[after[0]], chosen[after[1]]]))
        hidden = gate_part(plane.late, late, *weights, sums)
        if after:
            hidden, _ = tie((hidden, two[after[1]]))
        if got:
            hidden, _ = tie((hidden, got))
        theirs = down_part(plane.theirs, hidden, down_weight, width, len(chunk))
        hidden, theirs = tie((hidden, theirs))
        mine = down_part(plane.mine, hidden, down_weight, width, len(chunk))
        sent, got = [], []
        for k, offset in enumerate(chunk):
            near_share = plane.across(theirs[k])
            two_share = added(mine[k][2:], near_share[2:])
            sent.append(two_share)
            if got:
                two_share, _ = tie((two_share, got))
            got_two = plane.second(two_share)
            got.append(got_two)
            one_share = added(added(mine[k][1], near_share[1]), got_two[1])
            got_one = plane.once(one_share)
            pieces[offset] = combine_slots(
                chosen[offset][1], [mine[k][0], near_share[0], got_two[0], got_one]
            )
    return pieces


def solution(mesh):
    in_specs = (
        P("seq", "exp"),
        P("seq", "exp"),
        P("seq", "exp"),
        P("exp", "seq"),
        P("seq", "exp"),
        P("exp"),
        P("seq", None),
        P(None, "seq"),
        P("seq", None, "exp"),
        P("seq", None, "exp"),
        P("seq", "exp", None),
    )
    out_specs = P("seq", "exp")
    return jax.shard_map(
        on_device, mesh=mesh, in_specs=in_specs, out_specs=out_specs, check_vma=False
    )
```

```python
import functools

import jax
import jax.numpy as jnp
from jax import lax
from jax.experimental import pallas as pl
from jax.experimental.pallas import tpu as pltpu
from jax.sharding import PartitionSpec as P

F32 = jnp.float32
BF16 = jnp.bfloat16
HIGHEST = lax.Precision.HIGHEST
VMEM_LIMIT = 40 * 1024 * 1024
ID_ROWS = 16


def lower_ones(length):
    rows = lax.broadcasted_iota(jnp.int32, (length, length), 0)
    columns = lax.broadcasted_iota(jnp.int32, (length, length), 1)
    return rows >= columns


def shifted(array, axis, by):
    count = lax.axis_size(axis)
    pairs = [(i, i + by) for i in range(count) if 0 <= i + by < count]
    return lax.ppermute(array, axis, pairs)


def state_kernel(key_ref, value_ref, decay_ref, message_ref, cumulative_ref):
    heads, length = decay_ref.shape
    size = key_ref.shape[1] // heads
    ones = lower_ones(length).astype(F32)
    cumulative = lax.dot_general(
        ones, decay_ref[...], (((1,), (1,)), ((), ())), precision=HIGHEST, preferred_element_type=F32
    )
    cumulative_ref[...] = cumulative
    last = cumulative[length - 1 : length, :]
    key_fade = jnp.exp(last - cumulative)
    message_ref[heads * size :, :] = jnp.zeros((message_ref.shape[0] - heads * size, size), BF16)
    half = (message_ref.shape[0] - heads * size) // 2
    rows = []
    for h in range(heads):
        columns = slice(h * size, (h + 1) * size)
        scaled = (key_fade[:, h : h + 1] * key_ref[:, columns].astype(F32)).astype(BF16)
        state = lax.dot_general(
            scaled, value_ref[:, columns], (((0,), (0,)), ((), ())), preferred_element_type=F32
        )
        message_ref[columns, :] = state.astype(BF16)
        rows.append(jnp.broadcast_to(jnp.exp(last[:, h : h + 1]), (1, size)))
    rows.append(jnp.zeros((half - heads, size), F32))
    fade = jnp.concatenate(rows, axis=0)
    leading = fade.astype(BF16)
    trailing = (fade - leading.astype(F32)).astype(BF16)
    message_ref[heads * size :, :] = jnp.concatenate([leading, trailing], axis=0)


def section_state(attn_key, attn_value, log_decay):
    heads, length = log_decay.shape
    width = attn_key.shape[1]
    half = -(-heads // 8) * 8
    return pl.pallas_call(
        state_kernel,
        out_shape=(
            jax.ShapeDtypeStruct((width + 2 * half, width // heads), BF16),
            jax.ShapeDtypeStruct((length, heads), F32),
        ),
        cost_estimate=pl.CostEstimate(
            flops=2 * length * width * (width // heads), bytes_accessed=4 * length * width, transcendentals=0
        ),
        compiler_params=pltpu.CompilerParams(vmem_limit_bytes=VMEM_LIMIT),
    )(attn_key, attn_value, log_decay)


def intra_kernel(query_ref, key_ref, value_ref, decay_ref, cumulative_ref, out_ref):
    heads, length = decay_ref.shape
    size = key_ref.shape[1] // heads
    causal = lower_ones(length)
    along = lax.dot_general(
        decay_ref[...],
        causal.astype(F32),
        (((1,), (1,)), ((), ())),
        precision=HIGHEST,
        preferred_element_type=F32,
    )
    for h in range(heads):
        columns = slice(h * size, (h + 1) * size)
        gap = jnp.where(causal, cumulative_ref[:, h : h + 1] - along[h : h + 1, :], 0.0)
        mask = jnp.where(causal, jnp.exp(gap), 0.0)
        scores = lax.dot_general(
            query_ref[:, columns], key_ref[:, columns], (((1,), (1,)), ((), ())), preferred_element_type=F32
        )
        weights = (scores * mask).astype(BF16)
        out_ref[:, columns] = jnp.dot(weights, value_ref[:, columns], preferred_element_type=F32)


def intra_section(attn_query, attn_key, attn_value, log_decay, cumulative):
    length, width = attn_query.shape
    return pl.pallas_call(
        intra_kernel,
        out_shape=jax.ShapeDtypeStruct((length, width), F32),
        cost_estimate=pl.CostEstimate(
            flops=4 * length * length * width, bytes_accessed=10 * length * width, transcendentals=0
        ),
        compiler_params=pltpu.CompilerParams(vmem_limit_bytes=VMEM_LIMIT),
    )(attn_query, attn_key, attn_value, log_decay, cumulative)


def stream_kernel(
    query_ref, intra_ref, cumulative_ref, incoming_ref, residual_ref, gain_ref, ids_ref, out_ref
):
    heads, size = incoming_ref.shape[0], incoming_ref.shape[1]
    length, width = residual_ref.shape
    choices = ids_ref.shape[0]
    below = jnp.concatenate(
        [
            ids_ref[...].astype(F32),
            jnp.zeros((ID_ROWS - choices, length), F32),
        ],
        axis=0,
    )
    out_ref[length:, :] = jnp.concatenate(
        [below, jnp.zeros((ID_ROWS, width - length), F32)], axis=1
    ).astype(BF16)
    faded = jnp.exp(cumulative_ref[...])
    for h in range(heads):
        columns = slice(h * size, (h + 1) * size)
        state = incoming_ref[h]
        leading = state.astype(BF16)
        trailing = (state - leading.astype(F32)).astype(BF16)
        query = query_ref[:, columns]
        inter = jnp.dot(query, leading, preferred_element_type=F32) + jnp.dot(
            query, trailing, preferred_element_type=F32
        )
        attn_out = intra_ref[:, columns] + faded[:, h : h + 1] * inter
        mean_square = jnp.mean(attn_out * attn_out, axis=1, keepdims=True)
        normed = attn_out * lax.rsqrt(mean_square + 1e-06)
        out_ref[:length, columns] = (
            residual_ref[:, columns].astype(F32) + gain_ref[:, columns].astype(F32) * normed
        ).astype(BF16)


def make_stream(attn_query, intra, cumulative, incoming, residual, norm_gain, ids):
    length, width = attn_query.shape
    return pl.pallas_call(
        stream_kernel,
        out_shape=jax.ShapeDtypeStruct((length + ID_ROWS, width), BF16),
        compiler_params=pltpu.CompilerParams(vmem_limit_bytes=VMEM_LIMIT),
    )(attn_query, intra, cumulative, incoming, residual, norm_gain.reshape(1, width), ids)


def read_message(message, heads):
    size = message.shape[1]
    half = (message.shape[0] - heads * size) // 2
    state = message[: heads * size].astype(F32).reshape(heads, size, size)
    tail = message[heads * size :].astype(F32)
    fade = tail[:heads] + tail[half : half + heads]
    return fade[:, None, :], state


def write_message(fade, state, rows):
    heads, size = state.shape[0], state.shape[1]
    half = (rows - heads * size) // 2
    leading = fade[:, 0, :].astype(BF16)
    trailing = (fade[:, 0, :] - leading.astype(F32)).astype(BF16)
    spare = jnp.zeros((half - heads, size), BF16)
    return jnp.concatenate(
        [state.astype(BF16).reshape(heads * size, size), leading, spare, trailing, spare], axis=0
    )


def incoming_state(message, heads):
    count = lax.axis_size("seq")
    window_fade, window = read_message(message, heads)
    incoming_fade, incoming = None, None
    distance = 1
    while distance < count:
        got_fade, got = read_message(shifted(message, "seq", distance), heads)
        if incoming is None:
            incoming_fade, incoming = got_fade, got
        else:
            incoming, incoming_fade = incoming + incoming_fade * got, incoming_fade * got_fade
        window, window_fade = window + window_fade * got, window_fade * got_fade
        distance *= 2
        if distance < count:
            message = write_message(window_fade, window, message.shape[0])
    return incoming


def select_kernel(capacity, choices, experts, base_ref, part_ref, out_ref, place_ref):
    length = part_ref.shape[0] - ID_ROWS
    before = lower_ones(length).astype(BF16)
    slot = lax.broadcasted_iota(jnp.int32, (capacity, length), 0).astype(F32)
    ids = part_ref[length:, :length].astype(F32)
    rows = []
    for j in range(experts):
        expert = (base_ref[0] + j).astype(F32)
        chosen = ids[0:1, :] == expert
        for choice in range(1, choices):
            chosen = chosen | (ids[choice : choice + 1, :] == expert)
        flag = jnp.where(chosen, 1.0, 0.0)
        rank = lax.dot_general(
            jnp.broadcast_to(flag, (16, length)).astype(BF16),
            before,
            (((1,), (1,)), ((), ())),
            preferred_element_type=F32,
        )[0:1, :]
        rank = jnp.where(chosen, rank - 1.0, -1.0)
        rows.append(jnp.where(slot == rank, 1.0, 0.0).astype(BF16))
    place = jnp.concatenate(rows, axis=0)
    place_ref[...] = place
    out_ref[...] = lax.dot_general(
        part_ref[:length, :], place, (((0,), (1,)), ((), ())), preferred_element_type=F32
    ).astype(BF16)


def select_slots(base, part, capacity, choices, experts):
    rows, width = part.shape
    length = rows - ID_ROWS
    slots = experts * capacity
    whole = pl.BlockSpec(memory_space=pltpu.VMEM)
    return pl.pallas_call(
        functools.partial(select_kernel, capacity, choices, experts),
        in_specs=[pl.BlockSpec(memory_space=pltpu.SMEM), whole],
        out_shape=(
            jax.ShapeDtypeStruct((width, slots), BF16),
            jax.ShapeDtypeStruct((slots, length), BF16),
        ),
        cost_estimate=pl.CostEstimate(
            flops=2 * slots * length * width, bytes_accessed=4 * slots * width, transcendentals=0
        ),
        compiler_params=pltpu.CompilerParams(vmem_limit_bytes=VMEM_LIMIT),
    )(base, part)


def combine_kernel(place_ref, *refs):
    shares, out_ref = refs[:-1], refs[-1]
    total = shares[0][...].astype(F32)
    for share in shares[1:]:
        total = total + share[...].astype(F32)
    out_ref[...] = lax.dot_general(
        place_ref[...], total.astype(BF16), (((0,), (0,)), ((), ())), preferred_element_type=F32
    ).astype(BF16)


def combine_slots(place, shares):
    slots, length = place.shape
    width = shares[0].shape[1]
    return pl.pallas_call(
        combine_kernel,
        out_shape=jax.ShapeDtypeStruct((length, width), BF16),
        cost_estimate=pl.CostEstimate(
            flops=2 * slots * length * width, bytes_accessed=8 * slots * width, transcendentals=0
        ),
        compiler_params=pltpu.CompilerParams(vmem_limit_bytes=VMEM_LIMIT),
    )(place, *shares)


def gate_kernel(counts, sections, last, plan_ref, *refs):
    step = pl.program_id(0)
    blocks = sum(counts)
    used = len(counts) * sections
    x_refs, refs = refs[:used], refs[used:]
    router_ref, gate_ref, up_ref = refs[:3]
    refs = refs[3:]
    if last:
        gate_in, up_in, score_in, hidden_ref, gate_acc, up_acc, score_acc = refs
    else:
        gate_acc, up_acc, score_acc = refs
    experts = gate_ref.shape[0]
    width = x_refs[0].shape[1]
    slots = gate_acc.shape[2]
    part = slots // sections

    @pl.when(step == 0)
    def _():
        if last:
            gate_acc[...] = gate_in[...]
            up_acc[...] = up_in[...]
            score_acc[...] = score_in[...]
        else:
            gate_acc[...] = jnp.zeros_like(gate_acc)
            up_acc[...] = jnp.zeros_like(up_acc)
            score_acc[...] = jnp.zeros_like(score_acc)

    xs = []
    for section in range(sections):
        mine = x_refs[section * len(counts) : (section + 1) * len(counts)]
        x = mine[-1][0]
        for i in range(len(counts) - 2, -1, -1):
            x = jnp.where(step < sum(counts[: i + 1]), mine[i][0], x)
        xs.append(x)
    for j in range(experts):
        x = jnp.concatenate([x[:, j * part : (j + 1) * part] for x in xs], axis=1)
        score_acc[j] += jnp.dot(router_ref[0], x, preferred_element_type=F32)
        gate_acc[j] += jnp.dot(gate_ref[j], x, preferred_element_type=F32)
        up_acc[j] += jnp.dot(up_ref[j], x, preferred_element_type=F32)

    if last:

        @pl.when(step == blocks - 1)
        def _():
            for j in range(experts):
                score = score_acc[j, j : j + 1, :]
                gate = gate_acc[j]
                routed = gate / (1.0 + jnp.exp(-gate)) * up_acc[j]
                routed = routed / (1.0 + jnp.exp(-score))
                hidden_ref[j] = routed.T.astype(BF16)


def gate_part(plan, xs, router_rows, gate_rows, up_rows, sums=None):
    counts = tuple(x.shape[0] for x in xs[0])
    blocks = sum(counts)
    _, width, total = xs[0][0].shape
    experts, units, _ = gate_rows.shape
    slots = total // experts * len(xs)
    whole = pl.BlockSpec(memory_space=pltpu.VMEM)
    last = sums is not None

    def x_spec(i):
        before = sum(counts[:i])
        return pl.BlockSpec(
            (1, width, total), lambda p, plan: (jnp.clip(p - before, 0, counts[i] - 1), 0, 0)
        )

    weight_spec = pl.BlockSpec((experts, units, width), lambda p, plan: (0, 0, plan[p]))
    sum_shapes = [(experts, units, slots), (experts, units, slots), (experts, experts, slots)]
    if last:
        out_shape = jax.ShapeDtypeStruct((experts, slots, units), BF16)
        out_specs = whole
        scratch = [pltpu.VMEM(shape, F32) for shape in sum_shapes]
    else:
        out_shape = tuple(jax.ShapeDtypeStruct(shape, F32) for shape in sum_shapes)
        out_specs = (whole, whole, whole)
        scratch = []
    return pl.pallas_call(
        functools.partial(gate_kernel, counts, len(xs), last),
        grid_spec=pltpu.PrefetchScalarGridSpec(
            num_scalar_prefetch=1,
            grid=(blocks,),
            in_specs=[
                *[x_spec(i) for _ in xs for i in range(len(counts))],
                pl.BlockSpec((1, experts, width), lambda p, plan: (plan[p], 0, 0)),
                weight_spec,
                weight_spec,
                *([whole] * 3 if last else []),
            ],
            out_specs=out_specs,
            scratch_shapes=scratch,
        ),
        out_shape=out_shape,
        cost_estimate=pl.CostEstimate(
            flops=4 * experts * slots * blocks * width * units,
            bytes_accessed=4 * experts * blocks * width * units,
            transcendentals=0,
        ),
        compiler_params=pltpu.CompilerParams(vmem_limit_bytes=VMEM_LIMIT),
    )(plan, *[x for section in xs for x in section], router_rows, gate_rows, up_rows, *(sums or ()))


def down_kernel(plan_ref, hidden_ref, down_ref, *out_refs):
    experts, slots, _ = hidden_ref.shape
    width = out_refs[0].shape[2]
    part = slots // len(out_refs)
    for j in range(experts):
        share = jnp.dot(hidden_ref[j], down_ref[j], preferred_element_type=F32).astype(BF16)
        for section, out_ref in enumerate(out_refs):
            out_ref[0, j * part : (j + 1) * part, :] = share[section * part : (section + 1) * part]


def down_part(plan, hidden, down_weight, width, sections):
    blocks = plan.shape[0]
    experts, slots, units = hidden.shape
    rows = experts * slots // sections
    return pl.pallas_call(
        down_kernel,
        grid_spec=pltpu.PrefetchScalarGridSpec(
            num_scalar_prefetch=1,
            grid=(blocks,),
            in_specs=[
                pl.BlockSpec(memory_space=pltpu.VMEM),
                pl.BlockSpec((experts, units, width), lambda p, plan: (0, 0, plan[p])),
            ],
            out_specs=[pl.BlockSpec((1, rows, width), lambda p, plan: (p, 0, 0))] * sections,
        ),
        out_shape=[jax.ShapeDtypeStruct((blocks, rows, width), BF16)] * sections,
        cost_estimate=pl.CostEstimate(
            flops=2 * experts * slots * blocks * width * units,
            bytes_accessed=2 * experts * blocks * width * units,
            transcendentals=0,
        ),
        compiler_params=pltpu.CompilerParams(vmem_limit_bytes=VMEM_LIMIT),
    )(plan, hidden, down_weight)


def added(left, right):
    return (left.astype(F32) + right.astype(F32)).astype(BF16)


def swapped(array, axis, even, odd):
    count = lax.axis_size(axis)
    pairs = [(i, i ^ (odd if i % 2 else even)) for i in range(count)]
    return lax.ppermute(array, axis, pairs)


class PairedPlane:
    def __init__(self):
        me = lax.axis_index("exp").astype(jnp.int32)
        other = me ^ 1
        near = jnp.where(me % 2 == 0, 2, 4)
        far = 6 - near
        self.early = jnp.stack([me, me ^ near, other, other ^ far])
        self.late = jnp.stack([me ^ far, me ^ 6, other ^ near, other ^ 6])
        self.mine = jnp.stack([me, me ^ near, me ^ far, me ^ 6])
        self.theirs = jnp.stack([other, other ^ far, other ^ near, other ^ 6])

    def once(self, part):
        return swapped(part, "exp", 2, 4)

    def first(self, part):
        return jnp.stack([part, self.once(part)])

    def second(self, two):
        return swapped(two, "exp", 4, 2)

    def across(self, two):
        return swapped(two, "exp", 1, 1)

def on_device(
    attn_query,
    attn_key,
    attn_value,
    log_decay,
    residual,
    norm_gain,
    expert_ids,
    router_weight,
    gate_weight,
    up_weight,
    down_weight,
):
    heads_here, length = log_decay.shape
    groups = lax.axis_size("seq")
    shares = lax.axis_size("exp")
    width = attn_query.shape[1]
    experts_here = router_weight.shape[1]
    base = (lax.axis_index("seq") * experts_here).astype(jnp.int32).reshape(1)
    router_rows = router_weight.reshape(shares, width, experts_here).transpose(0, 2, 1)
    gate_rows = gate_weight.swapaxes(1, 2)
    up_rows = up_weight.swapaxes(1, 2)

    message, cumulative = section_state(attn_key, attn_value, log_decay)
    intra = intra_section(attn_query, attn_key, attn_value, log_decay, cumulative)
    incoming = incoming_state(message, heads_here)
    stream = make_stream(
        attn_query, intra, cumulative, incoming, residual, norm_gain, expert_ids.T
    )

    half = groups // 2
    chunks = [(0, half)] + [(half + i, i) for i in range(1, half)]
    capacity = 4 * length // (experts_here * groups)
    choices = expert_ids.shape[1]

    def moved(part, offset):
        return swapped(part, "seq", offset, offset)

    def select(part):
        return select_slots(base, part, capacity, choices, experts_here)

    weights = (router_rows, gate_rows, up_rows)
    if shares == 8:
        pieces = paired_chunks(chunks, stream, moved, select, weights, down_weight)
    else:
        order = jnp.arange(shares, dtype=jnp.int32)
        middle = shares // 2
        pieces = {}
        for chunk in chunks:
            chosen = [select(moved(stream, offset) if offset else stream) for offset in chunk]
            gathered = [lax.all_gather(slots, "exp", axis=0) for slots, _ in chosen]
            sums = gate_part(order[:middle], [[x[:middle]] for x in gathered], *weights)
            hidden = gate_part(order[middle:], [[x[middle:]] for x in gathered], *weights, sums)
            partial = down_part(order, hidden, down_weight, width, len(chunk))
            for offset, share, (_, place) in zip(chunk, partial, chosen):
                share = lax.psum_scatter(share, "exp", scatter_dimension=0)
                pieces[offset] = combine_slots(place, [share])
    total = stream[:length].astype(F32)
    for offset, piece in pieces.items():
        if offset:
            piece = moved(piece, offset)
        total = total + piece.astype(F32)
    return total.astype(BF16)


def paired_chunks(chunks, stream, moved, select, weights, down_weight):
    plane = PairedPlane()
    width = stream.shape[1]
    tie = lax.optimization_barrier
    two, far_two, near, near_far, chosen = {}, {}, {}, {}, {}

    def gather(offset, part):
        chosen[offset] = select(part)
        two[offset] = plane.first(chosen[offset][0])
        near[offset] = plane.across(two[offset])
        far_two[offset] = plane.second(two[offset])
        near_far[offset] = plane.across(far_two[offset])

    gather(0, stream)
    later, _ = tie((stream, two[0]))
    arrived = moved(later, chunks[0][1])
    part, _ = tie((arrived, far_two[0]))
    gather(chunks[0][1], part)
    later, _ = tie((stream, arrived))
    parts = {offset: moved(later, offset) for chunk in chunks[1:] for offset in reversed(chunk)}

    pieces = {}
    sent, got_two, one = [], [], []
    for i, chunk in enumerate(chunks):
        after = chunks[i + 1][::-1] if i + 1 < len(chunks) else ()
        early = [[two[offset], near[offset]] for offset in chunk]
        late = [[far_two[offset], near_far[offset]] for offset in chunk]
        if after:
            gather(after[0], parts[after[0]])
            early, _ = tie((early, chosen[after[0]]))
        if sent:
            early, _ = tie((early, sent))
        sums = gate_part(plane.early, early, *weights)
        late, sums = tie((late, sums))
        if after:
            part, _ = tie((parts[after[1]], sums))
            gather(after[1], part)
            late, _ = tie((late, [two[after[0]], chosen[after[1]]]))
        hidden = gate_part(plane.late, late, *weights, sums)
        if after:
            hidden, _ = tie((hidden, [far_two[after[0]], two[after[1]]]))
        if one:
            hidden, _ = tie((hidden, one))
        theirs = down_part(plane.theirs, hidden, down_weight, width, len(chunk))
        hidden, theirs = tie((hidden, theirs))
        mine = down_part(plane.mine, hidden, down_weight, width, len(chunk))
        sent, got_two, one = [], [], []
        for k, offset in enumerate(chunk):
            near_share = plane.across(theirs[k])
            two_share = added(mine[k][2:], near_share[2:])
            sent.append(two_share)
            if got_two and not after:
                two_share, _ = tie((two_share, got_two))
            got_two.append(plane.second(two_share))
            one_share = added(added(mine[k][1], near_share[1]), got_two[k][1])
            one.append(one_share)
            got_one = plane.once(one_share)
            pieces[offset] = combine_slots(
                chosen[offset][1], [mine[k][0], near_share[0], got_two[k][0], got_one]
            )
    return pieces


def solution(mesh):
    in_specs = (
        P("seq", "exp"),
        P("seq", "exp"),
        P("seq", "exp"),
        P("exp", "seq"),
        P("seq", "exp"),
        P("exp"),
        P("seq", None),
        P(None, "seq"),
        P("seq", None, "exp"),
        P("seq", None, "exp"),
        P("seq", "exp", None),
    )
    out_specs = P("seq", "exp")
    return jax.shard_map(
        on_device, mesh=mesh, in_specs=in_specs, out_specs=out_specs, check_vma=False
    )
```

```python
import functools

import jax
import jax.numpy as jnp
from jax import lax
from jax.experimental import pallas as pl
from jax.experimental.pallas import tpu as pltpu
from jax.sharding import PartitionSpec as P

F32 = jnp.float32
BF16 = jnp.bfloat16
HIGHEST = lax.Precision.HIGHEST
VMEM_LIMIT = 40 * 1024 * 1024
ID_ROWS = 16


def lower_ones(length):
    rows = lax.broadcasted_iota(jnp.int32, (length, length), 0)
    columns = lax.broadcasted_iota(jnp.int32, (length, length), 1)
    return rows >= columns


def shifted(array, axis, by):
    count = lax.axis_size(axis)
    pairs = [(i, i + by) for i in range(count) if 0 <= i + by < count]
    return lax.ppermute(array, axis, pairs)


def state_kernel(key_ref, value_ref, decay_ref, message_ref, cumulative_ref):
    heads, length = decay_ref.shape
    size = key_ref.shape[1] // heads
    ones = lower_ones(length).astype(F32)
    cumulative = lax.dot_general(
        ones, decay_ref[...], (((1,), (1,)), ((), ())), precision=HIGHEST, preferred_element_type=F32
    )
    cumulative_ref[...] = cumulative
    last = cumulative[length - 1 : length, :]
    key_fade = jnp.exp(last - cumulative)
    message_ref[heads * size :, :] = jnp.zeros((message_ref.shape[0] - heads * size, size), BF16)
    half = (message_ref.shape[0] - heads * size) // 2
    rows = []
    for h in range(heads):
        columns = slice(h * size, (h + 1) * size)
        scaled = (key_fade[:, h : h + 1] * key_ref[:, columns].astype(F32)).astype(BF16)
        state = lax.dot_general(
            scaled, value_ref[:, columns], (((0,), (0,)), ((), ())), preferred_element_type=F32
        )
        message_ref[columns, :] = state.astype(BF16)
        rows.append(jnp.broadcast_to(jnp.exp(last[:, h : h + 1]), (1, size)))
    rows.append(jnp.zeros((half - heads, size), F32))
    fade = jnp.concatenate(rows, axis=0)
    leading = fade.astype(BF16)
    trailing = (fade - leading.astype(F32)).astype(BF16)
    message_ref[heads * size :, :] = jnp.concatenate([leading, trailing], axis=0)


def section_state(attn_key, attn_value, log_decay):
    heads, length = log_decay.shape
    width = attn_key.shape[1]
    half = -(-heads // 8) * 8
    return pl.pallas_call(
        state_kernel,
        out_shape=(
            jax.ShapeDtypeStruct((width + 2 * half, width // heads), BF16),
            jax.ShapeDtypeStruct((length, heads), F32),
        ),
        cost_estimate=pl.CostEstimate(
            flops=2 * length * width * (width // heads), bytes_accessed=4 * length * width, transcendentals=0
        ),
        compiler_params=pltpu.CompilerParams(vmem_limit_bytes=VMEM_LIMIT),
    )(attn_key, attn_value, log_decay)


def intra_kernel(query_ref, key_ref, value_ref, decay_ref, cumulative_ref, out_ref):
    heads, length = decay_ref.shape
    size = key_ref.shape[1] // heads
    causal = lower_ones(length)
    along = lax.dot_general(
        decay_ref[...],
        causal.astype(F32),
        (((1,), (1,)), ((), ())),
        precision=HIGHEST,
        preferred_element_type=F32,
    )
    for h in range(heads):
        columns = slice(h * size, (h + 1) * size)
        gap = jnp.where(causal, cumulative_ref[:, h : h + 1] - along[h : h + 1, :], 0.0)
        mask = jnp.where(causal, jnp.exp(gap), 0.0)
        scores = lax.dot_general(
            query_ref[:, columns], key_ref[:, columns], (((1,), (1,)), ((), ())), preferred_element_type=F32
        )
        weights = (scores * mask).astype(BF16)
        out_ref[:, columns] = jnp.dot(weights, value_ref[:, columns], preferred_element_type=F32)


def intra_section(attn_query, attn_key, attn_value, log_decay, cumulative):
    length, width = attn_query.shape
    return pl.pallas_call(
        intra_kernel,
        out_shape=jax.ShapeDtypeStruct((length, width), F32),
        cost_estimate=pl.CostEstimate(
            flops=4 * length * length * width, bytes_accessed=10 * length * width, transcendentals=0
        ),
        compiler_params=pltpu.CompilerParams(vmem_limit_bytes=VMEM_LIMIT),
    )(attn_query, attn_key, attn_value, log_decay, cumulative)


def stream_kernel(
    query_ref, intra_ref, cumulative_ref, incoming_ref, residual_ref, gain_ref, ids_ref, out_ref
):
    heads, size = incoming_ref.shape[0], incoming_ref.shape[1]
    length, width = residual_ref.shape
    choices = ids_ref.shape[0]
    below = jnp.concatenate(
        [
            ids_ref[...].astype(F32),
            jnp.zeros((ID_ROWS - choices, length), F32),
        ],
        axis=0,
    )
    out_ref[length:, :] = jnp.concatenate(
        [below, jnp.zeros((ID_ROWS, width - length), F32)], axis=1
    ).astype(BF16)
    faded = jnp.exp(cumulative_ref[...])
    for h in range(heads):
        columns = slice(h * size, (h + 1) * size)
        state = incoming_ref[h]
        leading = state.astype(BF16)
        trailing = (state - leading.astype(F32)).astype(BF16)
        query = query_ref[:, columns]
        inter = jnp.dot(query, leading, preferred_element_type=F32) + jnp.dot(
            query, trailing, preferred_element_type=F32
        )
        attn_out = intra_ref[:, columns] + faded[:, h : h + 1] * inter
        mean_square = jnp.mean(attn_out * attn_out, axis=1, keepdims=True)
        normed = attn_out * lax.rsqrt(mean_square + 1e-06)
        out_ref[:length, columns] = (
            residual_ref[:, columns].astype(F32) + gain_ref[:, columns].astype(F32) * normed
        ).astype(BF16)


def make_stream(attn_query, intra, cumulative, incoming, residual, norm_gain, ids):
    length, width = attn_query.shape
    return pl.pallas_call(
        stream_kernel,
        out_shape=jax.ShapeDtypeStruct((length + ID_ROWS, width), BF16),
        compiler_params=pltpu.CompilerParams(vmem_limit_bytes=VMEM_LIMIT),
    )(attn_query, intra, cumulative, incoming, residual, norm_gain.reshape(1, width), ids)


def read_message(message, heads):
    size = message.shape[1]
    half = (message.shape[0] - heads * size) // 2
    state = message[: heads * size].astype(F32).reshape(heads, size, size)
    tail = message[heads * size :].astype(F32)
    fade = tail[:heads] + tail[half : half + heads]
    return fade[:, None, :], state


def write_message(fade, state, rows):
    heads, size = state.shape[0], state.shape[1]
    half = (rows - heads * size) // 2
    leading = fade[:, 0, :].astype(BF16)
    trailing = (fade[:, 0, :] - leading.astype(F32)).astype(BF16)
    spare = jnp.zeros((half - heads, size), BF16)
    return jnp.concatenate(
        [state.astype(BF16).reshape(heads * size, size), leading, spare, trailing, spare], axis=0
    )


def incoming_state(message, heads):
    count = lax.axis_size("seq")
    window_fade, window = read_message(message, heads)
    incoming_fade, incoming = None, None
    distance = 1
    while distance < count:
        got_fade, got = read_message(shifted(message, "seq", distance), heads)
        if incoming is None:
            incoming_fade, incoming = got_fade, got
        else:
            incoming, incoming_fade = incoming + incoming_fade * got, incoming_fade * got_fade
        window, window_fade = window + window_fade * got, window_fade * got_fade
        distance *= 2
        if distance < count:
            message = write_message(window_fade, window, message.shape[0])
    return incoming


def select_kernel(capacity, choices, experts, base_ref, part_ref, out_ref, place_ref):
    length = part_ref.shape[0] - ID_ROWS
    before = lower_ones(length).astype(BF16)
    slot = lax.broadcasted_iota(jnp.int32, (capacity, length), 0).astype(F32)
    ids = part_ref[length:, :length].astype(F32)
    rows = []
    for j in range(experts):
        expert = (base_ref[0] + j).astype(F32)
        chosen = ids[0:1, :] == expert
        for choice in range(1, choices):
            chosen = chosen | (ids[choice : choice + 1, :] == expert)
        flag = jnp.where(chosen, 1.0, 0.0)
        rank = lax.dot_general(
            jnp.broadcast_to(flag, (16, length)).astype(BF16),
            before,
            (((1,), (1,)), ((), ())),
            preferred_element_type=F32,
        )[0:1, :]
        rank = jnp.where(chosen, rank - 1.0, -1.0)
        rows.append(jnp.where(slot == rank, 1.0, 0.0).astype(BF16))
    place = jnp.concatenate(rows, axis=0)
    place_ref[...] = place
    out_ref[...] = lax.dot_general(
        part_ref[:length, :], place, (((0,), (1,)), ((), ())), preferred_element_type=F32
    ).astype(BF16)


def select_slots(base, part, capacity, choices, experts):
    rows, width = part.shape
    length = rows - ID_ROWS
    slots = experts * capacity
    whole = pl.BlockSpec(memory_space=pltpu.VMEM)
    return pl.pallas_call(
        functools.partial(select_kernel, capacity, choices, experts),
        in_specs=[pl.BlockSpec(memory_space=pltpu.SMEM), whole],
        out_shape=(
            jax.ShapeDtypeStruct((width, slots), BF16),
            jax.ShapeDtypeStruct((slots, length), BF16),
        ),
        cost_estimate=pl.CostEstimate(
            flops=2 * slots * length * width, bytes_accessed=4 * slots * width, transcendentals=0
        ),
        compiler_params=pltpu.CompilerParams(vmem_limit_bytes=VMEM_LIMIT),
    )(base, part)


def combine_kernel(place_ref, *refs):
    shares, out_ref = refs[:-1], refs[-1]
    total = shares[0][...].astype(F32)
    for share in shares[1:]:
        total = total + share[...].astype(F32)
    out_ref[...] = lax.dot_general(
        place_ref[...], total.astype(BF16), (((0,), (0,)), ((), ())), preferred_element_type=F32
    ).astype(BF16)


def combine_slots(place, shares):
    slots, length = place.shape
    width = shares[0].shape[1]
    return pl.pallas_call(
        combine_kernel,
        out_shape=jax.ShapeDtypeStruct((length, width), BF16),
        cost_estimate=pl.CostEstimate(
            flops=2 * slots * length * width, bytes_accessed=8 * slots * width, transcendentals=0
        ),
        compiler_params=pltpu.CompilerParams(vmem_limit_bytes=VMEM_LIMIT),
    )(place, *shares)


def gate_kernel(counts, sections, last, plan_ref, *refs):
    step = pl.program_id(0)
    blocks = sum(counts)
    used = len(counts) * sections
    x_refs, refs = refs[:used], refs[used:]
    router_ref, gate_ref, up_ref = refs[:3]
    refs = refs[3:]
    if last:
        gate_in, up_in, score_in, hidden_ref, gate_acc, up_acc, score_acc = refs
    else:
        gate_acc, up_acc, score_acc = refs
    experts = gate_ref.shape[0]
    width = x_refs[0].shape[1]
    slots = gate_acc.shape[2]
    part = slots // sections

    @pl.when(step == 0)
    def _():
        if last:
            gate_acc[...] = gate_in[...]
            up_acc[...] = up_in[...]
            score_acc[...] = score_in[...]
        else:
            gate_acc[...] = jnp.zeros_like(gate_acc)
            up_acc[...] = jnp.zeros_like(up_acc)
            score_acc[...] = jnp.zeros_like(score_acc)

    xs = []
    for section in range(sections):
        mine = x_refs[section * len(counts) : (section + 1) * len(counts)]
        x = mine[-1][0]
        for i in range(len(counts) - 2, -1, -1):
            x = jnp.where(step < sum(counts[: i + 1]), mine[i][0], x)
        xs.append(x)
    for j in range(experts):
        x = jnp.concatenate([x[:, j * part : (j + 1) * part] for x in xs], axis=1)
        score_acc[j] += jnp.dot(router_ref[0], x, preferred_element_type=F32)
        gate_acc[j] += jnp.dot(gate_ref[j], x, preferred_element_type=F32)
        up_acc[j] += jnp.dot(up_ref[j], x, preferred_element_type=F32)

    if last:

        @pl.when(step == blocks - 1)
        def _():
            for j in range(experts):
                score = score_acc[j, j : j + 1, :]
                gate = gate_acc[j]
                routed = gate / (1.0 + jnp.exp(-gate)) * up_acc[j]
                routed = routed / (1.0 + jnp.exp(-score))
                hidden_ref[j] = routed.T.astype(BF16)


def gate_part(plan, xs, router_rows, gate_rows, up_rows, sums=None):
    counts = tuple(x.shape[0] for x in xs[0])
    blocks = sum(counts)
    _, width, total = xs[0][0].shape
    experts, units, _ = gate_rows.shape
    slots = total // experts * len(xs)
    whole = pl.BlockSpec(memory_space=pltpu.VMEM)
    last = sums is not None

    def x_spec(i):
        before = sum(counts[:i])
        return pl.BlockSpec(
            (1, width, total), lambda p, plan: (jnp.clip(p - before, 0, counts[i] - 1), 0, 0)
        )

    weight_spec = pl.BlockSpec((experts, units, width), lambda p, plan: (0, 0, plan[p]))
    sum_shapes = [(experts, units, slots), (experts, units, slots), (experts, experts, slots)]
    if last:
        out_shape = jax.ShapeDtypeStruct((experts, slots, units), BF16)
        out_specs = whole
        scratch = [pltpu.VMEM(shape, F32) for shape in sum_shapes]
    else:
        out_shape = tuple(jax.ShapeDtypeStruct(shape, F32) for shape in sum_shapes)
        out_specs = (whole, whole, whole)
        scratch = []
    return pl.pallas_call(
        functools.partial(gate_kernel, counts, len(xs), last),
        grid_spec=pltpu.PrefetchScalarGridSpec(
            num_scalar_prefetch=1,
            grid=(blocks,),
            in_specs=[
                *[x_spec(i) for _ in xs for i in range(len(counts))],
                pl.BlockSpec((1, experts, width), lambda p, plan: (plan[p], 0, 0)),
                weight_spec,
                weight_spec,
                *([whole] * 3 if last else []),
            ],
            out_specs=out_specs,
            scratch_shapes=scratch,
        ),
        out_shape=out_shape,
        cost_estimate=pl.CostEstimate(
            flops=4 * experts * slots * blocks * width * units,
            bytes_accessed=4 * experts * blocks * width * units,
            transcendentals=0,
        ),
        compiler_params=pltpu.CompilerParams(vmem_limit_bytes=VMEM_LIMIT),
    )(plan, *[x for section in xs for x in section], router_rows, gate_rows, up_rows, *(sums or ()))


def down_kernel(plan_ref, hidden_ref, down_ref, *out_refs):
    experts, slots, _ = hidden_ref.shape
    width = out_refs[0].shape[2]
    part = slots // len(out_refs)
    for j in range(experts):
        share = jnp.dot(hidden_ref[j], down_ref[j], preferred_element_type=F32).astype(BF16)
        for section, out_ref in enumerate(out_refs):
            out_ref[0, j * part : (j + 1) * part, :] = share[section * part : (section + 1) * part]


def down_part(plan, hidden, down_weight, width, sections):
    blocks = plan.shape[0]
    experts, slots, units = hidden.shape
    rows = experts * slots // sections
    return pl.pallas_call(
        down_kernel,
        grid_spec=pltpu.PrefetchScalarGridSpec(
            num_scalar_prefetch=1,
            grid=(blocks,),
            in_specs=[
                pl.BlockSpec(memory_space=pltpu.VMEM),
                pl.BlockSpec((experts, units, width), lambda p, plan: (0, 0, plan[p])),
            ],
            out_specs=[pl.BlockSpec((1, rows, width), lambda p, plan: (p, 0, 0))] * sections,
        ),
        out_shape=[jax.ShapeDtypeStruct((blocks, rows, width), BF16)] * sections,
        cost_estimate=pl.CostEstimate(
            flops=2 * experts * slots * blocks * width * units,
            bytes_accessed=2 * experts * blocks * width * units,
            transcendentals=0,
        ),
        compiler_params=pltpu.CompilerParams(vmem_limit_bytes=VMEM_LIMIT),
    )(plan, hidden, down_weight)


def added(left, right):
    return (left.astype(F32) + right.astype(F32)).astype(BF16)


def swapped(array, axis, even, odd):
    count = lax.axis_size(axis)
    pairs = [(i, i ^ (odd if i % 2 else even)) for i in range(count)]
    return lax.ppermute(array, axis, pairs)


class PairedPlane:
    def __init__(self):
        me = lax.axis_index("exp").astype(jnp.int32)
        other = me ^ 1
        near = jnp.where(me % 2 == 0, 2, 4)
        far = 6 - near
        self.early = jnp.stack([me, me ^ near, other, other ^ far])
        self.late = jnp.stack([me ^ far, me ^ 6, other ^ near, other ^ 6])
        self.mine = jnp.stack([me, me ^ near, me ^ far, me ^ 6])
        self.theirs = jnp.stack([other, other ^ far, other ^ near, other ^ 6])

    def once(self, part):
        return swapped(part, "exp", 2, 4)

    def first(self, part):
        return jnp.stack([part, self.once(part)])

    def second(self, two):
        return swapped(two, "exp", 4, 2)

    def across(self, two):
        return swapped(two, "exp", 1, 1)

def on_device(
    attn_query,
    attn_key,
    attn_value,
    log_decay,
    residual,
    norm_gain,
    expert_ids,
    router_weight,
    gate_weight,
    up_weight,
    down_weight,
):
    heads_here, length = log_decay.shape
    groups = lax.axis_size("seq")
    shares = lax.axis_size("exp")
    width = attn_query.shape[1]
    experts_here = router_weight.shape[1]
    base = (lax.axis_index("seq") * experts_here).astype(jnp.int32).reshape(1)
    router_rows = router_weight.reshape(shares, width, experts_here).transpose(0, 2, 1)
    gate_rows = gate_weight.swapaxes(1, 2)
    up_rows = up_weight.swapaxes(1, 2)

    message, cumulative = section_state(attn_key, attn_value, log_decay)
    intra = intra_section(attn_query, attn_key, attn_value, log_decay, cumulative)
    incoming = incoming_state(message, heads_here)
    stream = make_stream(
        attn_query, intra, cumulative, incoming, residual, norm_gain, expert_ids.T
    )

    offsets = [*range(1, groups), 0]
    chunks = [tuple(offsets[i : i + 2]) for i in range(0, groups, 2)]
    capacity = 4 * length // (experts_here * groups)
    choices = expert_ids.shape[1]

    def moved(part, offset):
        return swapped(part, "seq", offset, offset)

    def select(part):
        return select_slots(base, part, capacity, choices, experts_here)

    weights = (router_rows, gate_rows, up_rows)
    if shares == 8:
        pieces = paired_chunks(chunks, stream, moved, select, weights, down_weight)
    else:
        order = jnp.arange(shares, dtype=jnp.int32)
        middle = shares // 2
        pieces = {}
        for chunk in chunks:
            chosen = [select(moved(stream, offset) if offset else stream) for offset in chunk]
            gathered = [lax.all_gather(slots, "exp", axis=0) for slots, _ in chosen]
            sums = gate_part(order[:middle], [[x[:middle]] for x in gathered], *weights)
            hidden = gate_part(order[middle:], [[x[middle:]] for x in gathered], *weights, sums)
            partial = down_part(order, hidden, down_weight, width, len(chunk))
            for offset, share, (_, place) in zip(chunk, partial, chosen):
                share = lax.psum_scatter(share, "exp", scatter_dimension=0)
                pieces[offset] = combine_slots(place, [share])
    total = stream[:length].astype(F32)
    for offset, piece in pieces.items():
        if offset:
            piece = moved(piece, offset)
        total = total + piece.astype(F32)
    return total.astype(BF16)


def paired_chunks(chunks, stream, moved, select, weights, down_weight):
    plane = PairedPlane()
    width = stream.shape[1]
    tie = lax.optimization_barrier
    two, far_two, near, near_far, chosen = {}, {}, {}, {}, {}

    def gather(offset, behind=()):
        two[offset], _ = tie((plane.first(chosen[offset][0]), behind))
        near[offset] = plane.across(two[offset])
        far_two[offset] = plane.second(two[offset])
        near_far[offset] = plane.across(far_two[offset])

    parts = {1: moved(stream, 1)}
    chosen[0] = select(stream)
    gather(0, parts[1])
    later, _ = tie((stream, two[0]))
    for offset in range(2, 2 * len(chunks)):
        parts[offset] = moved(later, offset)
        later, _ = tie((stream, parts[offset]))
    chosen[1] = select(parts[1])
    gather(1, [far_two[0], [parts[offset] for offset in chunks[0][1:]]])
    for offset in chunks[0][1:]:
        part, _ = tie((parts[offset], two[1]))
        chosen[offset] = select(part)
        gather(offset, [parts[following] for following in chunks[1] if following])

    pieces = {}
    sent, got_two, one = [], [], []
    for i, chunk in enumerate(chunks):
        after = [offset for following in chunks[i + 1 : i + 2] for offset in following if offset]
        early = [[two[offset], near[offset]] for offset in chunk]
        late = [[far_two[offset], near_far[offset]] for offset in chunk]
        for offset in after:
            chosen[offset] = select(parts[offset])
        early, _ = tie((early, [sent, [chosen[offset] for offset in after]]))
        sums = gate_part(plane.early, early, *weights)
        for offset in after:
            gather(offset, sums)
        late, sums = tie((late, sums))
        late, _ = tie((late, [two[offset] for offset in after]))
        hidden = gate_part(plane.late, late, *weights, sums)
        hidden, _ = tie((hidden, [one, [far_two[offset] for offset in after]]))
        theirs = down_part(plane.theirs, hidden, down_weight, width, len(chunk))
        hidden, theirs = tie((hidden, theirs))
        mine = down_part(plane.mine, hidden, down_weight, width, len(chunk))
        sent, got_two, one = [], [], []
        for k, offset in enumerate(chunk):
            near_share = plane.across(theirs[k])
            two_share = added(mine[k][2:], near_share[2:])
            sent.append(two_share)
            if got_two and not after:
                two_share, _ = tie((two_share, got_two))
            got_two.append(plane.second(two_share))
            one_share = added(added(mine[k][1], near_share[1]), got_two[k][1])
            one.append(one_share)
            got_one = plane.once(one_share)
            pieces[offset] = combine_slots(
                chosen[offset][1], [mine[k][0], near_share[0], got_two[k][0], got_one]
            )
    return pieces


def solution(mesh):
    in_specs = (
        P("seq", "exp"),
        P("seq", "exp"),
        P("seq", "exp"),
        P("exp", "seq"),
        P("seq", "exp"),
        P("exp"),
        P("seq", None),
        P(None, "seq"),
        P("seq", None, "exp"),
        P("seq", None, "exp"),
        P("seq", "exp", None),
    )
    out_specs = P("seq", "exp")
    return jax.shard_map(
        on_device, mesh=mesh, in_specs=in_specs, out_specs=out_specs, check_vma=False
    )
```

```python
import functools

import jax
import jax.numpy as jnp
from jax import lax
from jax.experimental import pallas as pl
from jax.experimental.pallas import tpu as pltpu
from jax.sharding import PartitionSpec as P

F32 = jnp.float32
BF16 = jnp.bfloat16
HIGHEST = lax.Precision.HIGHEST
VMEM_LIMIT = 40 * 1024 * 1024
ID_ROWS = 16


def lower_ones(length):
    rows = lax.broadcasted_iota(jnp.int32, (length, length), 0)
    columns = lax.broadcasted_iota(jnp.int32, (length, length), 1)
    return rows >= columns


def shifted(array, axis, by):
    count = lax.axis_size(axis)
    pairs = [(i, i + by) for i in range(count) if 0 <= i + by < count]
    return lax.ppermute(array, axis, pairs)


def state_kernel(key_ref, value_ref, decay_ref, message_ref, cumulative_ref):
    heads, length = decay_ref.shape
    size = key_ref.shape[1] // heads
    ones = lower_ones(length).astype(F32)
    cumulative = lax.dot_general(
        ones, decay_ref[...], (((1,), (1,)), ((), ())), precision=HIGHEST, preferred_element_type=F32
    )
    cumulative_ref[...] = cumulative
    last = cumulative[length - 1 : length, :]
    key_fade = jnp.exp(last - cumulative)
    message_ref[heads * size :, :] = jnp.zeros((message_ref.shape[0] - heads * size, size), BF16)
    half = (message_ref.shape[0] - heads * size) // 2
    rows = []
    for h in range(heads):
        columns = slice(h * size, (h + 1) * size)
        scaled = (key_fade[:, h : h + 1] * key_ref[:, columns].astype(F32)).astype(BF16)
        state = lax.dot_general(
            scaled, value_ref[:, columns], (((0,), (0,)), ((), ())), preferred_element_type=F32
        )
        message_ref[columns, :] = state.astype(BF16)
        rows.append(jnp.broadcast_to(jnp.exp(last[:, h : h + 1]), (1, size)))
    rows.append(jnp.zeros((half - heads, size), F32))
    fade = jnp.concatenate(rows, axis=0)
    leading = fade.astype(BF16)
    trailing = (fade - leading.astype(F32)).astype(BF16)
    message_ref[heads * size :, :] = jnp.concatenate([leading, trailing], axis=0)


def section_state(attn_key, attn_value, log_decay):
    heads, length = log_decay.shape
    width = attn_key.shape[1]
    half = -(-heads // 8) * 8
    return pl.pallas_call(
        state_kernel,
        out_shape=(
            jax.ShapeDtypeStruct((width + 2 * half, width // heads), BF16),
            jax.ShapeDtypeStruct((length, heads), F32),
        ),
        cost_estimate=pl.CostEstimate(
            flops=2 * length * width * (width // heads), bytes_accessed=4 * length * width, transcendentals=0
        ),
        compiler_params=pltpu.CompilerParams(vmem_limit_bytes=VMEM_LIMIT),
    )(attn_key, attn_value, log_decay)


def intra_kernel(query_ref, key_ref, value_ref, decay_ref, cumulative_ref, out_ref):
    heads, length = decay_ref.shape
    size = key_ref.shape[1] // heads
    causal = lower_ones(length)
    along = lax.dot_general(
        decay_ref[...],
        causal.astype(F32),
        (((1,), (1,)), ((), ())),
        precision=HIGHEST,
        preferred_element_type=F32,
    )
    for h in range(heads):
        columns = slice(h * size, (h + 1) * size)
        gap = jnp.where(causal, cumulative_ref[:, h : h + 1] - along[h : h + 1, :], 0.0)
        mask = jnp.where(causal, jnp.exp(gap), 0.0)
        scores = lax.dot_general(
            query_ref[:, columns], key_ref[:, columns], (((1,), (1,)), ((), ())), preferred_element_type=F32
        )
        weights = (scores * mask).astype(BF16)
        out_ref[:, columns] = jnp.dot(weights, value_ref[:, columns], preferred_element_type=F32)


def intra_section(attn_query, attn_key, attn_value, log_decay, cumulative):
    length, width = attn_query.shape
    return pl.pallas_call(
        intra_kernel,
        out_shape=jax.ShapeDtypeStruct((length, width), F32),
        cost_estimate=pl.CostEstimate(
            flops=4 * length * length * width, bytes_accessed=10 * length * width, transcendentals=0
        ),
        compiler_params=pltpu.CompilerParams(vmem_limit_bytes=VMEM_LIMIT),
    )(attn_query, attn_key, attn_value, log_decay, cumulative)


def stream_kernel(
    query_ref, intra_ref, cumulative_ref, incoming_ref, residual_ref, gain_ref, ids_ref, out_ref
):
    heads, size = incoming_ref.shape[0], incoming_ref.shape[1]
    length, width = residual_ref.shape
    choices = ids_ref.shape[0]
    below = jnp.concatenate(
        [
            ids_ref[...].astype(F32),
            jnp.zeros((ID_ROWS - choices, length), F32),
        ],
        axis=0,
    )
    out_ref[length:, :] = jnp.concatenate(
        [below, jnp.zeros((ID_ROWS, width - length), F32)], axis=1
    ).astype(BF16)
    faded = jnp.exp(cumulative_ref[...])
    for h in range(heads):
        columns = slice(h * size, (h + 1) * size)
        state = incoming_ref[h]
        leading = state.astype(BF16)
        trailing = (state - leading.astype(F32)).astype(BF16)
        query = query_ref[:, columns]
        inter = jnp.dot(query, leading, preferred_element_type=F32) + jnp.dot(
            query, trailing, preferred_element_type=F32
        )
        attn_out = intra_ref[:, columns] + faded[:, h : h + 1] * inter
        mean_square = jnp.mean(attn_out * attn_out, axis=1, keepdims=True)
        normed = attn_out * lax.rsqrt(mean_square + 1e-06)
        out_ref[:length, columns] = (
            residual_ref[:, columns].astype(F32) + gain_ref[:, columns].astype(F32) * normed
        ).astype(BF16)


def make_stream(attn_query, intra, cumulative, incoming, residual, norm_gain, ids):
    length, width = attn_query.shape
    return pl.pallas_call(
        stream_kernel,
        out_shape=jax.ShapeDtypeStruct((length + ID_ROWS, width), BF16),
        compiler_params=pltpu.CompilerParams(vmem_limit_bytes=VMEM_LIMIT),
    )(attn_query, intra, cumulative, incoming, residual, norm_gain.reshape(1, width), ids)


def read_message(message, heads):
    size = message.shape[1]
    half = (message.shape[0] - heads * size) // 2
    state = message[: heads * size].astype(F32).reshape(heads, size, size)
    tail = message[heads * size :].astype(F32)
    fade = tail[:heads] + tail[half : half + heads]
    return fade[:, None, :], state


def write_message(fade, state, rows):
    heads, size = state.shape[0], state.shape[1]
    half = (rows - heads * size) // 2
    leading = fade[:, 0, :].astype(BF16)
    trailing = (fade[:, 0, :] - leading.astype(F32)).astype(BF16)
    spare = jnp.zeros((half - heads, size), BF16)
    return jnp.concatenate(
        [state.astype(BF16).reshape(heads * size, size), leading, spare, trailing, spare], axis=0
    )


def incoming_state(message, heads):
    count = lax.axis_size("seq")
    window_fade, window = read_message(message, heads)
    incoming_fade, incoming = None, None
    distance = 1
    while distance < count:
        got_fade, got = read_message(shifted(message, "seq", distance), heads)
        if incoming is None:
            incoming_fade, incoming = got_fade, got
        else:
            incoming, incoming_fade = incoming + incoming_fade * got, incoming_fade * got_fade
        window, window_fade = window + window_fade * got, window_fade * got_fade
        distance *= 2
        if distance < count:
            message = write_message(window_fade, window, message.shape[0])
    return incoming


def select_kernel(capacity, choices, experts, base_ref, *refs):
    parts, (out_ref, place_ref) = refs[:-2], refs[-2:]
    length = parts[0].shape[0] - ID_ROWS
    part = parts[-1][...]
    for other in parts[:-1]:
        part = jnp.where(base_ref[1] > 0, other[...], part)
    before = lower_ones(length).astype(BF16)
    slot = lax.broadcasted_iota(jnp.int32, (capacity, length), 0).astype(F32)
    ids = part[length:, :length].astype(F32)
    rows = []
    for j in range(experts):
        expert = (base_ref[0] + j).astype(F32)
        chosen = ids[0:1, :] == expert
        for choice in range(1, choices):
            chosen = chosen | (ids[choice : choice + 1, :] == expert)
        flag = jnp.where(chosen, 1.0, 0.0)
        rank = lax.dot_general(
            jnp.broadcast_to(flag, (16, length)).astype(BF16),
            before,
            (((1,), (1,)), ((), ())),
            preferred_element_type=F32,
        )[0:1, :]
        rank = jnp.where(chosen, rank - 1.0, -1.0)
        rows.append(jnp.where(slot == rank, 1.0, 0.0).astype(BF16))
    place = jnp.concatenate(rows, axis=0)
    place_ref[...] = place
    out_ref[...] = lax.dot_general(
        part[:length, :], place, (((0,), (1,)), ((), ())), preferred_element_type=F32
    ).astype(BF16)


def select_slots(base, parts, capacity, choices, experts):
    rows, width = parts[0].shape
    length = rows - ID_ROWS
    slots = experts * capacity
    whole = pl.BlockSpec(memory_space=pltpu.VMEM)
    return pl.pallas_call(
        functools.partial(select_kernel, capacity, choices, experts),
        in_specs=[pl.BlockSpec(memory_space=pltpu.SMEM), *([whole] * len(parts))],
        out_shape=(
            jax.ShapeDtypeStruct((width, slots), BF16),
            jax.ShapeDtypeStruct((slots, length), BF16),
        ),
        cost_estimate=pl.CostEstimate(
            flops=2 * slots * length * width, bytes_accessed=4 * slots * width, transcendentals=0
        ),
        compiler_params=pltpu.CompilerParams(vmem_limit_bytes=VMEM_LIMIT),
    )(base, *parts)


def combine_kernel(place_ref, *refs):
    shares, out_ref = refs[:-1], refs[-1]
    total = shares[0][...].astype(F32)
    for share in shares[1:]:
        total = total + share[...].astype(F32)
    out_ref[...] = lax.dot_general(
        place_ref[...], total.astype(BF16), (((0,), (0,)), ((), ())), preferred_element_type=F32
    ).astype(BF16)


def combine_slots(place, shares):
    slots, length = place.shape
    width = shares[0].shape[1]
    return pl.pallas_call(
        combine_kernel,
        out_shape=jax.ShapeDtypeStruct((length, width), BF16),
        cost_estimate=pl.CostEstimate(
            flops=2 * slots * length * width, bytes_accessed=8 * slots * width, transcendentals=0
        ),
        compiler_params=pltpu.CompilerParams(vmem_limit_bytes=VMEM_LIMIT),
    )(place, *shares)


def gate_kernel(counts, sections, last, plan_ref, *refs):
    step = pl.program_id(0)
    blocks = sum(counts)
    used = len(counts) * sections
    x_refs, refs = refs[:used], refs[used:]
    router_ref, gate_ref, up_ref = refs[:3]
    refs = refs[3:]
    if last:
        gate_in, up_in, score_in, hidden_ref, gate_acc, up_acc, score_acc = refs
    else:
        gate_acc, up_acc, score_acc = refs
    experts = gate_ref.shape[0]
    width = x_refs[0].shape[1]
    slots = gate_acc.shape[2]
    part = slots // sections

    @pl.when(step == 0)
    def _():
        if last:
            gate_acc[...] = gate_in[...]
            up_acc[...] = up_in[...]
            score_acc[...] = score_in[...]
        else:
            gate_acc[...] = jnp.zeros_like(gate_acc)
            up_acc[...] = jnp.zeros_like(up_acc)
            score_acc[...] = jnp.zeros_like(score_acc)

    xs = []
    for section in range(sections):
        mine = x_refs[section * len(counts) : (section + 1) * len(counts)]
        x = mine[-1][0]
        for i in range(len(counts) - 2, -1, -1):
            x = jnp.where(step < sum(counts[: i + 1]), mine[i][0], x)
        xs.append(x)
    for j in range(experts):
        x = jnp.concatenate([x[:, j * part : (j + 1) * part] for x in xs], axis=1)
        score_acc[j] += jnp.dot(router_ref[0], x, preferred_element_type=F32)
        gate_acc[j] += jnp.dot(gate_ref[j], x, preferred_element_type=F32)
        up_acc[j] += jnp.dot(up_ref[j], x, preferred_element_type=F32)

    if last:

        @pl.when(step == blocks - 1)
        def _():
            for j in range(experts):
                score = score_acc[j, j : j + 1, :]
                gate = gate_acc[j]
                routed = gate / (1.0 + jnp.exp(-gate)) * up_acc[j]
                routed = routed / (1.0 + jnp.exp(-score))
                hidden_ref[j] = routed.T.astype(BF16)


def gate_part(plan, xs, router_rows, gate_rows, up_rows, sums=None):
    counts = tuple(x.shape[0] for x in xs[0])
    blocks = sum(counts)
    _, width, total = xs[0][0].shape
    experts, units, _ = gate_rows.shape
    slots = total // experts * len(xs)
    whole = pl.BlockSpec(memory_space=pltpu.VMEM)
    last = sums is not None

    def x_spec(i):
        before = sum(counts[:i])
        return pl.BlockSpec(
            (1, width, total), lambda p, plan: (jnp.clip(p - before, 0, counts[i] - 1), 0, 0)
        )

    weight_spec = pl.BlockSpec((experts, units, width), lambda p, plan: (0, 0, plan[p]))
    sum_shapes = [(experts, units, slots), (experts, units, slots), (experts, experts, slots)]
    if last:
        out_shape = jax.ShapeDtypeStruct((experts, slots, units), BF16)
        out_specs = whole
        scratch = [pltpu.VMEM(shape, F32) for shape in sum_shapes]
    else:
        out_shape = tuple(jax.ShapeDtypeStruct(shape, F32) for shape in sum_shapes)
        out_specs = (whole, whole, whole)
        scratch = []
    return pl.pallas_call(
        functools.partial(gate_kernel, counts, len(xs), last),
        grid_spec=pltpu.PrefetchScalarGridSpec(
            num_scalar_prefetch=1,
            grid=(blocks,),
            in_specs=[
                *[x_spec(i) for _ in xs for i in range(len(counts))],
                pl.BlockSpec((1, experts, width), lambda p, plan: (plan[p], 0, 0)),
                weight_spec,
                weight_spec,
                *([whole] * 3 if last else []),
            ],
            out_specs=out_specs,
            scratch_shapes=scratch,
        ),
        out_shape=out_shape,
        cost_estimate=pl.CostEstimate(
            flops=4 * experts * slots * blocks * width * units,
            bytes_accessed=4 * experts * blocks * width * units,
            transcendentals=0,
        ),
        compiler_params=pltpu.CompilerParams(vmem_limit_bytes=VMEM_LIMIT),
    )(plan, *[x for section in xs for x in section], router_rows, gate_rows, up_rows, *(sums or ()))


def down_kernel(blocks, sections, plan_ref, hidden_ref, down_ref, *out_refs):
    experts, slots, _ = hidden_ref.shape
    part = slots // sections
    turn = pl.program_id(0) // blocks
    for j in range(experts):
        share = jnp.dot(hidden_ref[j], down_ref[j], preferred_element_type=F32).astype(BF16)
        for i in range(len(out_refs) // sections):

            @pl.when(turn == i)
            def _():
                for section in range(sections):
                    out_ref = out_refs[i * sections + section]
                    out_ref[0, j * part : (j + 1) * part, :] = share[
                        section * part : (section + 1) * part
                    ]


def down_part(plans, hidden, down_weight, width, sections):
    blocks = plans[0].shape[0]
    experts, slots, units = hidden.shape
    rows = experts * slots // sections

    def out_spec(i):
        return pl.BlockSpec(
            (1, rows, width), lambda p, plan: (jnp.clip(p - i * blocks, 0, blocks - 1), 0, 0)
        )

    out = pl.pallas_call(
        functools.partial(down_kernel, blocks, sections),
        grid_spec=pltpu.PrefetchScalarGridSpec(
            num_scalar_prefetch=1,
            grid=(len(plans) * blocks,),
            in_specs=[
                pl.BlockSpec(memory_space=pltpu.VMEM),
                pl.BlockSpec((experts, units, width), lambda p, plan: (0, 0, plan[p])),
            ],
            out_specs=[out_spec(i) for i in range(len(plans)) for _ in range(sections)],
        ),
        out_shape=[jax.ShapeDtypeStruct((blocks, rows, width), BF16)] * (len(plans) * sections),
        cost_estimate=pl.CostEstimate(
            flops=2 * experts * slots * len(plans) * blocks * width * units,
            bytes_accessed=2 * experts * len(plans) * blocks * width * units,
            transcendentals=0,
        ),
        compiler_params=pltpu.CompilerParams(vmem_limit_bytes=VMEM_LIMIT),
    )(jnp.concatenate(plans), hidden, down_weight)
    return [out[i * sections : (i + 1) * sections] for i in range(len(plans))]


def added(left, right):
    return (left.astype(F32) + right.astype(F32)).astype(BF16)


def swapped(array, axis, even, odd):
    count = lax.axis_size(axis)
    pairs = [(i, i ^ (odd if i % 2 else even)) for i in range(count)]
    return lax.ppermute(array, axis, pairs)


class PairedPlane:
    def __init__(self):
        me = lax.axis_index("exp").astype(jnp.int32)
        other = me ^ 1
        near = jnp.where(me % 2 == 0, 2, 4)
        far = 6 - near
        self.early = jnp.stack([me, me ^ near, other, other ^ far])
        self.late = jnp.stack([me ^ far, me ^ 6, other ^ near, other ^ 6])
        self.mine = jnp.stack([me, me ^ near, me ^ far, me ^ 6])
        self.theirs = jnp.stack([other, other ^ far, other ^ near, other ^ 6])

    def once(self, part):
        return swapped(part, "exp", 2, 4)

    def first(self, part):
        return jnp.stack([part, self.once(part)])

    def second(self, two):
        return swapped(two, "exp", 4, 2)

    def across(self, two):
        return swapped(two, "exp", 1, 1)

def on_device(
    attn_query,
    attn_key,
    attn_value,
    log_decay,
    residual,
    norm_gain,
    expert_ids,
    router_weight,
    gate_weight,
    up_weight,
    down_weight,
):
    heads_here, length = log_decay.shape
    groups = lax.axis_size("seq")
    shares = lax.axis_size("exp")
    width = attn_query.shape[1]
    experts_here = router_weight.shape[1]
    section = lax.axis_index("seq")
    inner = (section > 0) & (section < groups - 1)
    base = jnp.stack([section * experts_here, inner]).astype(jnp.int32)
    router_rows = router_weight.reshape(shares, width, experts_here).transpose(0, 2, 1)
    gate_rows = gate_weight.swapaxes(1, 2)
    up_rows = up_weight.swapaxes(1, 2)

    message, cumulative = section_state(attn_key, attn_value, log_decay)
    intra = intra_section(attn_query, attn_key, attn_value, log_decay, cumulative)
    incoming = incoming_state(message, heads_here)
    stream = make_stream(
        attn_query, intra, cumulative, incoming, residual, norm_gain, expert_ids.T
    )

    capacity = 4 * length // (experts_here * groups)
    choices = expert_ids.shape[1]

    def select(*parts):
        return select_slots(base, parts, capacity, choices, experts_here)

    weights = (router_rows, gate_rows, up_rows)
    if shares == 8 and groups == 4:
        pieces = paired_chunks(stream, select, weights, down_weight)
    else:
        order = jnp.arange(shares, dtype=jnp.int32)
        middle = shares // 2
        pieces = []
        for first in range(0, groups, 2):
            chunk = (first, first + 1)
            chosen = [
                select(swapped(stream, "seq", offset, offset) if offset else stream)
                for offset in chunk
            ]
            gathered = [lax.all_gather(slots, "exp", axis=0) for slots, _ in chosen]
            sums = gate_part(order[:middle], [[x[:middle]] for x in gathered], *weights)
            hidden = gate_part(order[middle:], [[x[middle:]] for x in gathered], *weights, sums)
            (partial,) = down_part([order], hidden, down_weight, width, len(chunk))
            for offset, share, (_, place) in zip(chunk, partial, chosen):
                share = lax.psum_scatter(share, "exp", scatter_dimension=0)
                piece = combine_slots(place, [share])
                pieces.append(swapped(piece, "seq", offset, offset) if offset else piece)
    total = stream[:length].astype(F32)
    for piece in pieces:
        total = total + piece.astype(F32)
    return total.astype(BF16)


def paired_chunks(stream, select, weights, down_weight):
    plane = PairedPlane()
    width = stream.shape[1]
    tie = lax.optimization_barrier
    two, far_two, near, near_far, chosen = {}, {}, {}, {}, {}

    def across_middle(part):
        return lax.ppermute(part, "seq", [(1, 2), (2, 1)])

    def outward(part):
        return lax.ppermute(part, "seq", [(1, 0), (2, 3)])

    def gather(name, behind):
        two[name], _ = tie((plane.first(chosen[name][0]), behind))
        near[name] = plane.across(two[name])
        far_two[name] = plane.second(two[name])

    neighbour = swapped(stream, "seq", 1, 1)
    third = across_middle(stream)
    chosen["own"] = select(stream)
    gather("own", [neighbour, third])
    passed_third = outward(third)
    fourth = across_middle(neighbour)
    chosen["neighbour"] = select(neighbour)
    gather("neighbour", [passed_third, fourth, far_two["own"]])
    passed_fourth = outward(fourth)
    chosen["third"] = select(third, passed_third)
    gather("third", passed_fourth)
    chosen["fourth"] = select(fourth, passed_fourth)

    pieces = {}
    sent, one = [], []
    for chunk, after in ((("neighbour", "third"), "fourth"), (("fourth", "own"), None)):
        early = [[two[name], near[name]] for name in chunk]
        if after:
            early, _ = tie((early, chosen[after]))
        early, _ = tie((early, sent))
        sums = gate_part(plane.early, early, *weights)
        if after:
            gather(after, sums)
            far_two[chunk[1]], sums = tie((far_two[chunk[1]], sums))
        late = [[far_two[name], plane.across(far_two[name])] for name in chunk]
        if after:
            late, _ = tie((late, two[after]))
        hidden = gate_part(plane.late, late, *weights, sums)
        if after:
            hidden, _ = tie((hidden, far_two[after]))
            (theirs,) = down_part([plane.theirs], hidden, down_weight, width, len(chunk))
            hidden, theirs = tie((hidden, theirs))
            (mine,) = down_part([plane.mine], hidden, down_weight, width, len(chunk))
        else:
            hidden, _ = tie((hidden, one))
            theirs, mine = down_part([plane.theirs, plane.mine], hidden, down_weight, width, len(chunk))
            theirs, _ = tie((theirs, list(pieces.values())))
        sent, got_two, one = [], [], []
        for k, name in enumerate(chunk):
            near_share = plane.across(theirs[k])
            two_share = added(mine[k][2:], near_share[2:])
            sent.append(two_share)
            if got_two and not after:
                two_share, _ = tie((two_share, got_two))
            got_two.append(plane.second(two_share))
            one_share = added(added(mine[k][1], near_share[1]), got_two[k][1])
            one.append(one_share)
            got_one = plane.once(one_share)
            pieces[name] = combine_slots(
                chosen[name][1], [mine[k][0], near_share[0], got_two[k][0], got_one]
            )
    return [
        pieces["own"],
        swapped(pieces["neighbour"], "seq", 1, 1),
        lax.ppermute(pieces["third"], "seq", [(1, 2), (2, 1)]),
        lax.ppermute(pieces["third"], "seq", [(0, 2), (3, 1)]),
        lax.ppermute(pieces["fourth"], "seq", [(1, 3), (2, 0)]),
        lax.ppermute(pieces["fourth"], "seq", [(0, 3), (3, 0)]),
    ]


def solution(mesh):
    in_specs = (
        P("seq", "exp"),
        P("seq", "exp"),
        P("seq", "exp"),
        P("exp", "seq"),
        P("seq", "exp"),
        P("exp"),
        P("seq", None),
        P(None, "seq"),
        P("seq", None, "exp"),
        P("seq", None, "exp"),
        P("seq", "exp", None),
    )
    out_specs = P("seq", "exp")
    return jax.shard_map(
        on_device, mesh=mesh, in_specs=in_specs, out_specs=out_specs, check_vma=False
    )
```

```python
import functools

import jax
import jax.numpy as jnp
from jax import lax
from jax.experimental import pallas as pl
from jax.experimental.pallas import tpu as pltpu
from jax.sharding import PartitionSpec as P

F32 = jnp.float32
BF16 = jnp.bfloat16
HIGHEST = lax.Precision.HIGHEST
VMEM_LIMIT = 22 * 1024 * 1024
ID_ROWS = 16


def in_hbm(array):
    return pltpu.with_memory_space_constraint(array, pltpu.HBM)


def lower_ones(length):
    rows = lax.broadcasted_iota(jnp.int32, (length, length), 0)
    columns = lax.broadcasted_iota(jnp.int32, (length, length), 1)
    return rows >= columns


def shifted(array, axis, by):
    count = lax.axis_size(axis)
    pairs = [(i, i + by) for i in range(count) if 0 <= i + by < count]
    return lax.ppermute(array, axis, pairs)


def state_kernel(key_ref, value_ref, decay_ref, message_ref, cumulative_ref):
    heads, length = decay_ref.shape
    size = key_ref.shape[1] // heads
    ones = lower_ones(length).astype(F32)
    cumulative = lax.dot_general(
        ones, decay_ref[...], (((1,), (1,)), ((), ())), precision=HIGHEST, preferred_element_type=F32
    )
    cumulative_ref[...] = cumulative
    last = cumulative[length - 1 : length, :]
    key_fade = jnp.exp(last - cumulative)
    message_ref[heads * size :, :] = jnp.zeros((message_ref.shape[0] - heads * size, size), BF16)
    half = (message_ref.shape[0] - heads * size) // 2
    rows = []
    for h in range(heads):
        columns = slice(h * size, (h + 1) * size)
        scaled = (key_fade[:, h : h + 1] * key_ref[:, columns].astype(F32)).astype(BF16)
        state = lax.dot_general(
            scaled, value_ref[:, columns], (((0,), (0,)), ((), ())), preferred_element_type=F32
        )
        message_ref[columns, :] = state.astype(BF16)
        rows.append(jnp.broadcast_to(jnp.exp(last[:, h : h + 1]), (1, size)))
    rows.append(jnp.zeros((half - heads, size), F32))
    fade = jnp.concatenate(rows, axis=0)
    leading = fade.astype(BF16)
    trailing = (fade - leading.astype(F32)).astype(BF16)
    message_ref[heads * size :, :] = jnp.concatenate([leading, trailing], axis=0)


def section_state(attn_key, attn_value, log_decay):
    heads, length = log_decay.shape
    width = attn_key.shape[1]
    half = -(-heads // 8) * 8
    return pl.pallas_call(
        state_kernel,
        out_shape=(
            jax.ShapeDtypeStruct((width + 2 * half, width // heads), BF16),
            jax.ShapeDtypeStruct((length, heads), F32),
        ),
        cost_estimate=pl.CostEstimate(
            flops=2 * length * width * (width // heads), bytes_accessed=4 * length * width, transcendentals=0
        ),
        compiler_params=pltpu.CompilerParams(vmem_limit_bytes=VMEM_LIMIT),
    )(in_hbm(attn_key), in_hbm(attn_value), in_hbm(log_decay))


def intra_kernel(query_ref, key_ref, value_ref, decay_ref, cumulative_ref, out_ref):
    heads, length = decay_ref.shape
    size = key_ref.shape[1] // heads
    causal = lower_ones(length)
    along = lax.dot_general(
        decay_ref[...],
        causal.astype(F32),
        (((1,), (1,)), ((), ())),
        precision=HIGHEST,
        preferred_element_type=F32,
    )
    for h in range(heads):
        columns = slice(h * size, (h + 1) * size)
        gap = jnp.where(causal, cumulative_ref[:, h : h + 1] - along[h : h + 1, :], 0.0)
        mask = jnp.where(causal, jnp.exp(gap), 0.0)
        scores = lax.dot_general(
            query_ref[:, columns], key_ref[:, columns], (((1,), (1,)), ((), ())), preferred_element_type=F32
        )
        weights = (scores * mask).astype(BF16)
        out_ref[:, columns] = jnp.dot(weights, value_ref[:, columns], preferred_element_type=F32)


def intra_section(attn_query, attn_key, attn_value, log_decay, cumulative):
    length, width = attn_query.shape
    return pl.pallas_call(
        intra_kernel,
        out_shape=jax.ShapeDtypeStruct((length, width), F32),
        cost_estimate=pl.CostEstimate(
            flops=4 * length * length * width, bytes_accessed=10 * length * width, transcendentals=0
        ),
        compiler_params=pltpu.CompilerParams(vmem_limit_bytes=VMEM_LIMIT),
    )(attn_query, attn_key, attn_value, log_decay, cumulative)


def stream_kernel(
    query_ref, intra_ref, cumulative_ref, incoming_ref, residual_ref, gain_ref, ids_ref, out_ref
):
    heads, size = incoming_ref.shape[0], incoming_ref.shape[1]
    length, width = residual_ref.shape
    choices = ids_ref.shape[0]
    below = jnp.concatenate(
        [
            ids_ref[...].astype(F32),
            jnp.zeros((ID_ROWS - choices, length), F32),
        ],
        axis=0,
    )
    out_ref[length:, :] = jnp.concatenate(
        [below, jnp.zeros((ID_ROWS, width - length), F32)], axis=1
    ).astype(BF16)
    faded = jnp.exp(cumulative_ref[...])
    for h in range(heads):
        columns = slice(h * size, (h + 1) * size)
        state = incoming_ref[h]
        leading = state.astype(BF16)
        trailing = (state - leading.astype(F32)).astype(BF16)
        query = query_ref[:, columns]
        inter = jnp.dot(query, leading, preferred_element_type=F32) + jnp.dot(
            query, trailing, preferred_element_type=F32
        )
        attn_out = intra_ref[:, columns] + faded[:, h : h + 1] * inter
        mean_square = jnp.mean(attn_out * attn_out, axis=1, keepdims=True)
        normed = attn_out * lax.rsqrt(mean_square + 1e-06)
        out_ref[:length, columns] = (
            residual_ref[:, columns].astype(F32) + gain_ref[:, columns].astype(F32) * normed
        ).astype(BF16)


def make_stream(attn_query, intra, cumulative, incoming, residual, norm_gain, ids):
    length, width = attn_query.shape
    return pl.pallas_call(
        stream_kernel,
        out_shape=jax.ShapeDtypeStruct((length + ID_ROWS, width), BF16),
        compiler_params=pltpu.CompilerParams(vmem_limit_bytes=VMEM_LIMIT),
    )(attn_query, intra, cumulative, incoming, residual, norm_gain.reshape(1, width), ids)


def read_message(message, heads):
    size = message.shape[1]
    half = (message.shape[0] - heads * size) // 2
    state = message[: heads * size].astype(F32).reshape(heads, size, size)
    tail = message[heads * size :].astype(F32)
    fade = tail[:heads] + tail[half : half + heads]
    return fade[:, None, :], state


def write_message(fade, state, rows):
    heads, size = state.shape[0], state.shape[1]
    half = (rows - heads * size) // 2
    leading = fade[:, 0, :].astype(BF16)
    trailing = (fade[:, 0, :] - leading.astype(F32)).astype(BF16)
    spare = jnp.zeros((half - heads, size), BF16)
    return jnp.concatenate(
        [state.astype(BF16).reshape(heads * size, size), leading, spare, trailing, spare], axis=0
    )


def incoming_state(message, heads):
    count = lax.axis_size("seq")
    window_fade, window = read_message(message, heads)
    incoming_fade, incoming = None, None
    distance = 1
    while distance < count:
        got_fade, got = read_message(shifted(message, "seq", distance), heads)
        if incoming is None:
            incoming_fade, incoming = got_fade, got
        else:
            incoming, incoming_fade = incoming + incoming_fade * got, incoming_fade * got_fade
        window, window_fade = window + window_fade * got, window_fade * got_fade
        distance *= 2
        if distance < count:
            message = write_message(window_fade, window, message.shape[0])
    return incoming


def select_kernel(capacity, choices, experts, base_ref, *refs):
    parts, (out_ref, place_ref) = refs[:-2], refs[-2:]
    length = parts[0].shape[0] - ID_ROWS
    part = parts[-1][...]
    for other in parts[:-1]:
        part = jnp.where(base_ref[1] > 0, other[...], part)
    before = lower_ones(length).astype(BF16)
    slot = lax.broadcasted_iota(jnp.int32, (capacity, length), 0).astype(F32)
    ids = part[length:, :length].astype(F32)
    rows = []
    for j in range(experts):
        expert = (base_ref[0] + j).astype(F32)
        chosen = ids[0:1, :] == expert
        for choice in range(1, choices):
            chosen = chosen | (ids[choice : choice + 1, :] == expert)
        flag = jnp.where(chosen, 1.0, 0.0)
        rank = lax.dot_general(
            jnp.broadcast_to(flag, (16, length)).astype(BF16),
            before,
            (((1,), (1,)), ((), ())),
            preferred_element_type=F32,
        )[0:1, :]
        rank = jnp.where(chosen, rank - 1.0, -1.0)
        rows.append(jnp.where(slot == rank, 1.0, 0.0).astype(BF16))
    place = jnp.concatenate(rows, axis=0)
    place_ref[...] = place
    out_ref[...] = lax.dot_general(
        part[:length, :], place, (((0,), (1,)), ((), ())), preferred_element_type=F32
    ).astype(BF16)


def select_slots(base, parts, capacity, choices, experts):
    rows, width = parts[0].shape
    length = rows - ID_ROWS
    slots = experts * capacity
    whole = pl.BlockSpec(memory_space=pltpu.VMEM)
    return pl.pallas_call(
        functools.partial(select_kernel, capacity, choices, experts),
        in_specs=[pl.BlockSpec(memory_space=pltpu.SMEM), *([whole] * len(parts))],
        out_shape=(
            jax.ShapeDtypeStruct((width, slots), BF16),
            jax.ShapeDtypeStruct((slots, length), BF16),
        ),
        cost_estimate=pl.CostEstimate(
            flops=2 * slots * length * width, bytes_accessed=4 * slots * width, transcendentals=0
        ),
        compiler_params=pltpu.CompilerParams(vmem_limit_bytes=VMEM_LIMIT),
    )(base, *parts)


def combine_kernel(place_ref, *refs):
    shares, out_ref = refs[:-1], refs[-1]
    total = shares[0][...].astype(F32)
    for share in shares[1:]:
        total = total + share[...].astype(F32)
    out_ref[...] = lax.dot_general(
        place_ref[...], total.astype(BF16), (((0,), (0,)), ((), ())), preferred_element_type=F32
    ).astype(BF16)


def combine_slots(place, shares):
    slots, length = place.shape
    width = shares[0].shape[1]
    return pl.pallas_call(
        combine_kernel,
        out_shape=jax.ShapeDtypeStruct((length, width), BF16),
        cost_estimate=pl.CostEstimate(
            flops=2 * slots * length * width, bytes_accessed=8 * slots * width, transcendentals=0
        ),
        compiler_params=pltpu.CompilerParams(vmem_limit_bytes=VMEM_LIMIT),
    )(place, *shares)


def gate_kernel(counts, sections, last, plan_ref, *refs):
    step = pl.program_id(0)
    blocks = sum(counts)
    used = len(counts) * sections
    x_refs, refs = refs[:used], refs[used:]
    router_ref, gate_ref, up_ref = refs[:3]
    refs = refs[3:]
    if last:
        gate_in, up_in, score_in, hidden_ref, gate_acc, up_acc, score_acc = refs
    else:
        gate_acc, up_acc, score_acc = refs
    experts = gate_ref.shape[0]
    width = x_refs[0].shape[1]
    slots = gate_acc.shape[2]
    part = slots // sections

    @pl.when(step == 0)
    def _():
        if last:
            gate_acc[...] = gate_in[...]
            up_acc[...] = up_in[...]
            score_acc[...] = score_in[...]
        else:
            gate_acc[...] = jnp.zeros_like(gate_acc)
            up_acc[...] = jnp.zeros_like(up_acc)
            score_acc[...] = jnp.zeros_like(score_acc)

    xs = []
    for section in range(sections):
        mine = x_refs[section * len(counts) : (section + 1) * len(counts)]
        x = mine[-1][0]
        for i in range(len(counts) - 2, -1, -1):
            x = jnp.where(step < sum(counts[: i + 1]), mine[i][0], x)
        xs.append(x)
    for j in range(experts):
        x = jnp.concatenate([x[:, j * part : (j + 1) * part] for x in xs], axis=1)
        score_acc[j] += jnp.dot(router_ref[0], x, preferred_element_type=F32)
        gate_acc[j] += jnp.dot(gate_ref[j], x, preferred_element_type=F32)
        up_acc[j] += jnp.dot(up_ref[j], x, preferred_element_type=F32)

    if last:

        @pl.when(step == blocks - 1)
        def _():
            for j in range(experts):
                score = score_acc[j, j : j + 1, :]
                gate = gate_acc[j]
                routed = gate / (1.0 + jnp.exp(-gate)) * up_acc[j]
                routed = routed / (1.0 + jnp.exp(-score))
                hidden_ref[j] = routed.T.astype(BF16)


def gate_part(plan, xs, router_rows, gate_rows, up_rows, sums=None):
    counts = tuple(x.shape[0] for x in xs[0])
    blocks = sum(counts)
    _, width, total = xs[0][0].shape
    experts, units, _ = gate_rows.shape
    slots = total // experts * len(xs)
    whole = pl.BlockSpec(memory_space=pltpu.VMEM)
    last = sums is not None

    def x_spec(i):
        before = sum(counts[:i])
        return pl.BlockSpec(
            (1, width, total), lambda p, plan: (jnp.clip(p - before, 0, counts[i] - 1), 0, 0)
        )

    weight_spec = pl.BlockSpec((experts, units, width), lambda p, plan: (0, 0, plan[p]))
    sum_shapes = [(experts, units, slots), (experts, units, slots), (experts, experts, slots)]
    if last:
        out_shape = jax.ShapeDtypeStruct((experts, slots, units), BF16)
        out_specs = whole
        scratch = [pltpu.VMEM(shape, F32) for shape in sum_shapes]
    else:
        out_shape = tuple(jax.ShapeDtypeStruct(shape, F32) for shape in sum_shapes)
        out_specs = (whole, whole, whole)
        scratch = []
    return pl.pallas_call(
        functools.partial(gate_kernel, counts, len(xs), last),
        grid_spec=pltpu.PrefetchScalarGridSpec(
            num_scalar_prefetch=1,
            grid=(blocks,),
            in_specs=[
                *[x_spec(i) for _ in xs for i in range(len(counts))],
                pl.BlockSpec((1, experts, width), lambda p, plan: (plan[p], 0, 0)),
                weight_spec,
                weight_spec,
                *([whole] * 3 if last else []),
            ],
            out_specs=out_specs,
            scratch_shapes=scratch,
        ),
        out_shape=out_shape,
        cost_estimate=pl.CostEstimate(
            flops=4 * experts * slots * blocks * width * units,
            bytes_accessed=4 * experts * blocks * width * units,
            transcendentals=0,
        ),
        compiler_params=pltpu.CompilerParams(vmem_limit_bytes=VMEM_LIMIT),
    )(
        plan,
        *[x for section in xs for x in section],
        router_rows,
        in_hbm(gate_rows),
        in_hbm(up_rows),
        *(sums or ()),
    )


def down_kernel(blocks, sections, plan_ref, hidden_ref, down_ref, *out_refs):
    experts, slots, _ = hidden_ref.shape
    part = slots // sections
    turn = pl.program_id(0) // blocks
    for j in range(experts):
        share = jnp.dot(hidden_ref[j], down_ref[j], preferred_element_type=F32).astype(BF16)
        for i in range(len(out_refs) // sections):

            @pl.when(turn == i)
            def _():
                for section in range(sections):
                    out_ref = out_refs[i * sections + section]
                    out_ref[0, j * part : (j + 1) * part, :] = share[
                        section * part : (section + 1) * part
                    ]


def down_part(plans, hidden, down_weight, width, sections):
    blocks = plans[0].shape[0]
    experts, slots, units = hidden.shape
    rows = experts * slots // sections

    def out_spec(i):
        return pl.BlockSpec(
            (1, rows, width), lambda p, plan: (jnp.clip(p - i * blocks, 0, blocks - 1), 0, 0)
        )

    out = pl.pallas_call(
        functools.partial(down_kernel, blocks, sections),
        grid_spec=pltpu.PrefetchScalarGridSpec(
            num_scalar_prefetch=1,
            grid=(len(plans) * blocks,),
            in_specs=[
                pl.BlockSpec(memory_space=pltpu.VMEM),
                pl.BlockSpec((experts, units, width), lambda p, plan: (0, 0, plan[p])),
            ],
            out_specs=[out_spec(i) for i in range(len(plans)) for _ in range(sections)],
        ),
        out_shape=[jax.ShapeDtypeStruct((blocks, rows, width), BF16)] * (len(plans) * sections),
        cost_estimate=pl.CostEstimate(
            flops=2 * experts * slots * len(plans) * blocks * width * units,
            bytes_accessed=2 * experts * len(plans) * blocks * width * units,
            transcendentals=0,
        ),
        compiler_params=pltpu.CompilerParams(vmem_limit_bytes=VMEM_LIMIT),
    )(jnp.concatenate(plans), hidden, in_hbm(down_weight))
    return [out[i * sections : (i + 1) * sections] for i in range(len(plans))]


def added(left, right):
    return (left.astype(F32) + right.astype(F32)).astype(BF16)


def swapped(array, axis, even, odd):
    count = lax.axis_size(axis)
    pairs = [(i, i ^ (odd if i % 2 else even)) for i in range(count)]
    return lax.ppermute(array, axis, pairs)


class PairedPlane:
    def __init__(self):
        me = lax.axis_index("exp").astype(jnp.int32)
        other = me ^ 1
        near = jnp.where(me % 2 == 0, 2, 4)
        far = 6 - near
        self.early = jnp.stack([me, me ^ near, other, other ^ far])
        self.late = jnp.stack([me ^ far, me ^ 6, other ^ near, other ^ 6])
        self.mine = jnp.stack([me, me ^ near, me ^ far, me ^ 6])
        self.theirs = jnp.stack([other, other ^ far, other ^ near, other ^ 6])

    def once(self, part):
        return swapped(part, "exp", 2, 4)

    def first(self, part):
        return jnp.stack([part, self.once(part)])

    def second(self, two):
        return swapped(two, "exp", 4, 2)

    def across(self, two):
        return swapped(two, "exp", 1, 1)

def on_device(
    attn_query,
    attn_key,
    attn_value,
    log_decay,
    residual,
    norm_gain,
    expert_ids,
    router_weight,
    gate_weight,
    up_weight,
    down_weight,
):
    heads_here, length = log_decay.shape
    groups = lax.axis_size("seq")
    shares = lax.axis_size("exp")
    width = attn_query.shape[1]
    experts_here = router_weight.shape[1]
    section = lax.axis_index("seq")
    inner = (section > 0) & (section < groups - 1)
    base = jnp.stack([section * experts_here, inner]).astype(jnp.int32)
    router_rows = router_weight.reshape(shares, width, experts_here).transpose(0, 2, 1)
    gate_rows = gate_weight.swapaxes(1, 2)
    up_rows = up_weight.swapaxes(1, 2)

    message, cumulative = section_state(attn_key, attn_value, log_decay)
    intra = intra_section(attn_query, attn_key, attn_value, log_decay, cumulative)
    incoming = incoming_state(message, heads_here)
    stream = make_stream(
        attn_query, intra, cumulative, incoming, residual, norm_gain, expert_ids.T
    )

    capacity = 4 * length // (experts_here * groups)
    choices = expert_ids.shape[1]

    def select(*parts):
        return select_slots(base, parts, capacity, choices, experts_here)

    weights = (router_rows, gate_rows, up_rows)
    if shares == 8 and groups == 4:
        pieces = paired_chunks(stream, select, weights, down_weight)
    else:
        order = jnp.arange(shares, dtype=jnp.int32)
        middle = shares // 2
        pieces = []
        for first in range(0, groups, 2):
            chunk = (first, first + 1)
            chosen = [
                select(swapped(stream, "seq", offset, offset) if offset else stream)
                for offset in chunk
            ]
            gathered = [lax.all_gather(slots, "exp", axis=0) for slots, _ in chosen]
            sums = gate_part(order[:middle], [[x[:middle]] for x in gathered], *weights)
            hidden = gate_part(order[middle:], [[x[middle:]] for x in gathered], *weights, sums)
            (partial,) = down_part([order], hidden, down_weight, width, len(chunk))
            for offset, share, (_, place) in zip(chunk, partial, chosen):
                share = lax.psum_scatter(share, "exp", scatter_dimension=0)
                piece = combine_slots(place, [share])
                pieces.append(swapped(piece, "seq", offset, offset) if offset else piece)
    total = stream[:length].astype(F32)
    for piece in pieces:
        total = total + piece.astype(F32)
    return total.astype(BF16)


def paired_chunks(stream, select, weights, down_weight):
    plane = PairedPlane()
    width = stream.shape[1]
    tie = lax.optimization_barrier
    two, far_two, near, near_far, chosen = {}, {}, {}, {}, {}

    def across_middle(part):
        return lax.ppermute(part, "seq", [(1, 2), (2, 1)])

    def outward(part):
        return lax.ppermute(part, "seq", [(1, 0), (2, 3)])

    def gather(name, behind):
        two[name], _ = tie((plane.first(chosen[name][0]), behind))
        near[name] = plane.across(two[name])
        far_two[name] = plane.second(two[name])

    neighbour = swapped(stream, "seq", 1, 1)
    third = across_middle(stream)
    chosen["own"] = select(stream)
    gather("own", [neighbour, third])
    passed_third = outward(third)
    fourth = across_middle(neighbour)
    chosen["neighbour"] = select(neighbour)
    gather("neighbour", [passed_third, fourth, far_two["own"]])
    passed_fourth = outward(fourth)
    chosen["third"] = select(third, passed_third)
    gather("third", passed_fourth)
    chosen["fourth"] = select(fourth, passed_fourth)

    pieces = {}
    sent, one = [], []
    for chunk, after in ((("neighbour", "third"), "fourth"), (("fourth", "own"), None)):
        early = [[two[name], near[name]] for name in chunk]
        if after:
            early, _ = tie((early, chosen[after]))
        early, _ = tie((early, sent))
        sums = gate_part(plane.early, early, *weights)
        if after:
            gather(after, sums)
            for name in chunk:
                far_two[name], _ = tie((far_two[name], sums))
        late = [[far_two[name], plane.across(far_two[name])] for name in chunk]
        if after:
            late, _ = tie((late, two[after]))
        hidden = gate_part(plane.late, late, *weights, sums)
        if after:
            hidden, _ = tie((hidden, far_two[after]))
            (theirs,) = down_part([plane.theirs], hidden, down_weight, width, len(chunk))
            hidden, theirs = tie((hidden, theirs))
            (mine,) = down_part([plane.mine], hidden, down_weight, width, len(chunk))
        else:
            hidden, _ = tie((hidden, one))
            theirs, mine = down_part([plane.theirs, plane.mine], hidden, down_weight, width, len(chunk))
            theirs, _ = tie((theirs, list(pieces.values())))
        sent, got_two, one = [], [], []
        for k, name in enumerate(chunk):
            near_share = plane.across(theirs[k])
            two_share = added(mine[k][2:], near_share[2:])
            sent.append(two_share)
            if got_two and not after:
                two_share, _ = tie((two_share, got_two))
            got_two.append(plane.second(two_share))
            if not after and k == 0:
                home = [
                    swapped(pieces["neighbour"], "seq", 1, 1),
                    lax.ppermute(pieces["third"], "seq", [(1, 2), (2, 1)]),
                    lax.ppermute(pieces["third"], "seq", [(0, 2), (3, 1)]),
                ]
                got_two[0], _ = tie((got_two[0], home))
            one_share = added(added(mine[k][1], near_share[1]), got_two[k][1])
            one.append(one_share)
            got_one = plane.once(one_share)
            pieces[name] = combine_slots(
                chosen[name][1], [mine[k][0], near_share[0], got_two[k][0], got_one]
            )
    return [
        pieces["own"],
        *home,
        lax.ppermute(pieces["fourth"], "seq", [(1, 3), (2, 0)]),
        lax.ppermute(pieces["fourth"], "seq", [(0, 3), (3, 0)]),
    ]


def solution(mesh):
    in_specs = (
        P("seq", "exp"),
        P("seq", "exp"),
        P("seq", "exp"),
        P("exp", "seq"),
        P("seq", "exp"),
        P("exp"),
        P("seq", None),
        P(None, "seq"),
        P("seq", None, "exp"),
        P("seq", None, "exp"),
        P("seq", "exp", None),
    )
    out_specs = P("seq", "exp")
    return jax.shard_map(
        on_device, mesh=mesh, in_specs=in_specs, out_specs=out_specs, check_vma=False
    )
```

```python
import functools

import jax
import jax.numpy as jnp
from jax import lax
from jax.experimental import pallas as pl
from jax.experimental.pallas import tpu as pltpu
from jax.sharding import PartitionSpec as P

F32 = jnp.float32
BF16 = jnp.bfloat16
HIGHEST = lax.Precision.HIGHEST
VMEM_LIMIT = 22 * 1024 * 1024
ID_ROWS = 16


def in_hbm(array):
    return pltpu.with_memory_space_constraint(array, pltpu.HBM)


def lower_ones(length):
    rows = lax.broadcasted_iota(jnp.int32, (length, length), 0)
    columns = lax.broadcasted_iota(jnp.int32, (length, length), 1)
    return rows >= columns


def shifted(array, axis, by):
    count = lax.axis_size(axis)
    pairs = [(i, i + by) for i in range(count) if 0 <= i + by < count]
    return lax.ppermute(array, axis, pairs)


def state_kernel(key_ref, value_ref, decay_ref, message_ref, cumulative_ref):
    heads, length = decay_ref.shape
    size = key_ref.shape[1] // heads
    ones = lower_ones(length).astype(F32)
    cumulative = lax.dot_general(
        ones, decay_ref[...], (((1,), (1,)), ((), ())), precision=HIGHEST, preferred_element_type=F32
    )
    cumulative_ref[...] = cumulative
    last = cumulative[length - 1 : length, :]
    key_fade = jnp.exp(last - cumulative)
    message_ref[heads * size :, :] = jnp.zeros((message_ref.shape[0] - heads * size, size), BF16)
    half = (message_ref.shape[0] - heads * size) // 2
    rows = []
    for h in range(heads):
        columns = slice(h * size, (h + 1) * size)
        scaled = (key_fade[:, h : h + 1] * key_ref[:, columns].astype(F32)).astype(BF16)
        state = lax.dot_general(
            scaled, value_ref[:, columns], (((0,), (0,)), ((), ())), preferred_element_type=F32
        )
        message_ref[columns, :] = state.astype(BF16)
        rows.append(jnp.broadcast_to(jnp.exp(last[:, h : h + 1]), (1, size)))
    rows.append(jnp.zeros((half - heads, size), F32))
    fade = jnp.concatenate(rows, axis=0)
    leading = fade.astype(BF16)
    trailing = (fade - leading.astype(F32)).astype(BF16)
    message_ref[heads * size :, :] = jnp.concatenate([leading, trailing], axis=0)


def section_state(attn_key, attn_value, log_decay):
    heads, length = log_decay.shape
    width = attn_key.shape[1]
    half = -(-heads // 8) * 8
    return pl.pallas_call(
        state_kernel,
        out_shape=(
            jax.ShapeDtypeStruct((width + 2 * half, width // heads), BF16),
            jax.ShapeDtypeStruct((length, heads), F32),
        ),
        cost_estimate=pl.CostEstimate(
            flops=2 * length * width * (width // heads), bytes_accessed=4 * length * width, transcendentals=0
        ),
        compiler_params=pltpu.CompilerParams(vmem_limit_bytes=VMEM_LIMIT),
    )(in_hbm(attn_key), in_hbm(attn_value), in_hbm(log_decay))


def intra_kernel(query_ref, key_ref, value_ref, decay_ref, cumulative_ref, out_ref):
    heads, length = decay_ref.shape
    size = key_ref.shape[1] // heads
    causal = lower_ones(length)
    along = lax.dot_general(
        decay_ref[...],
        causal.astype(F32),
        (((1,), (1,)), ((), ())),
        precision=HIGHEST,
        preferred_element_type=F32,
    )
    for h in range(heads):
        columns = slice(h * size, (h + 1) * size)
        gap = jnp.where(causal, cumulative_ref[:, h : h + 1] - along[h : h + 1, :], 0.0)
        mask = jnp.where(causal, jnp.exp(gap), 0.0)
        scores = lax.dot_general(
            query_ref[:, columns], key_ref[:, columns], (((1,), (1,)), ((), ())), preferred_element_type=F32
        )
        weights = (scores * mask).astype(BF16)
        out_ref[:, columns] = jnp.dot(weights, value_ref[:, columns], preferred_element_type=F32)


def intra_section(attn_query, attn_key, attn_value, log_decay, cumulative):
    length, width = attn_query.shape
    return pl.pallas_call(
        intra_kernel,
        out_shape=jax.ShapeDtypeStruct((length, width), F32),
        cost_estimate=pl.CostEstimate(
            flops=4 * length * length * width, bytes_accessed=10 * length * width, transcendentals=0
        ),
        compiler_params=pltpu.CompilerParams(vmem_limit_bytes=VMEM_LIMIT),
    )(attn_query, attn_key, attn_value, log_decay, cumulative)


def stream_kernel(
    query_ref, intra_ref, cumulative_ref, incoming_ref, residual_ref, gain_ref, ids_ref, out_ref
):
    heads, size = incoming_ref.shape[0], incoming_ref.shape[1]
    length, width = residual_ref.shape
    choices = ids_ref.shape[0]
    below = jnp.concatenate(
        [
            ids_ref[...].astype(F32),
            jnp.zeros((ID_ROWS - choices, length), F32),
        ],
        axis=0,
    )
    out_ref[length:, :] = jnp.concatenate(
        [below, jnp.zeros((ID_ROWS, width - length), F32)], axis=1
    ).astype(BF16)
    faded = jnp.exp(cumulative_ref[...])
    for h in range(heads):
        columns = slice(h * size, (h + 1) * size)
        state = incoming_ref[h]
        leading = state.astype(BF16)
        trailing = (state - leading.astype(F32)).astype(BF16)
        query = query_ref[:, columns]
        inter = jnp.dot(query, leading, preferred_element_type=F32) + jnp.dot(
            query, trailing, preferred_element_type=F32
        )
        attn_out = intra_ref[:, columns] + faded[:, h : h + 1] * inter
        mean_square = jnp.mean(attn_out * attn_out, axis=1, keepdims=True)
        normed = attn_out * lax.rsqrt(mean_square + 1e-06)
        out_ref[:length, columns] = (
            residual_ref[:, columns].astype(F32) + gain_ref[:, columns].astype(F32) * normed
        ).astype(BF16)


def make_stream(attn_query, intra, cumulative, incoming, residual, norm_gain, ids):
    length, width = attn_query.shape
    return pl.pallas_call(
        stream_kernel,
        out_shape=jax.ShapeDtypeStruct((length + ID_ROWS, width), BF16),
        compiler_params=pltpu.CompilerParams(vmem_limit_bytes=VMEM_LIMIT),
    )(attn_query, intra, cumulative, incoming, residual, norm_gain.reshape(1, width), ids)


def read_message(message, heads):
    size = message.shape[1]
    half = (message.shape[0] - heads * size) // 2
    state = message[: heads * size].astype(F32).reshape(heads, size, size)
    tail = message[heads * size :].astype(F32)
    fade = tail[:heads] + tail[half : half + heads]
    return fade[:, None, :], state


def write_message(fade, state, rows):
    heads, size = state.shape[0], state.shape[1]
    half = (rows - heads * size) // 2
    leading = fade[:, 0, :].astype(BF16)
    trailing = (fade[:, 0, :] - leading.astype(F32)).astype(BF16)
    spare = jnp.zeros((half - heads, size), BF16)
    return jnp.concatenate(
        [state.astype(BF16).reshape(heads * size, size), leading, spare, trailing, spare], axis=0
    )


def incoming_state(message, heads):
    count = lax.axis_size("seq")
    window_fade, window = read_message(message, heads)
    incoming_fade, incoming = None, None
    distance = 1
    while distance < count:
        got_fade, got = read_message(shifted(message, "seq", distance), heads)
        if incoming is None:
            incoming_fade, incoming = got_fade, got
        else:
            incoming, incoming_fade = incoming + incoming_fade * got, incoming_fade * got_fade
        window, window_fade = window + window_fade * got, window_fade * got_fade
        distance *= 2
        if distance < count:
            message = write_message(window_fade, window, message.shape[0])
    return incoming


def select_kernel(capacity, choices, experts, base_ref, *refs):
    parts, (out_ref, place_ref) = refs[:-2], refs[-2:]
    length = parts[0].shape[0] - ID_ROWS
    part = parts[-1][...]
    for other in parts[:-1]:
        part = jnp.where(base_ref[1] > 0, other[...], part)
    before = lower_ones(length).astype(BF16)
    slot = lax.broadcasted_iota(jnp.int32, (capacity, length), 0).astype(F32)
    ids = part[length:, :length].astype(F32)
    rows = []
    for j in range(experts):
        expert = (base_ref[0] + j).astype(F32)
        chosen = ids[0:1, :] == expert
        for choice in range(1, choices):
            chosen = chosen | (ids[choice : choice + 1, :] == expert)
        flag = jnp.where(chosen, 1.0, 0.0)
        rank = lax.dot_general(
            jnp.broadcast_to(flag, (16, length)).astype(BF16),
            before,
            (((1,), (1,)), ((), ())),
            preferred_element_type=F32,
        )[0:1, :]
        rank = jnp.where(chosen, rank - 1.0, -1.0)
        rows.append(jnp.where(slot == rank, 1.0, 0.0).astype(BF16))
    place = jnp.concatenate(rows, axis=0)
    place_ref[...] = place
    out_ref[...] = lax.dot_general(
        part[:length, :], place, (((0,), (1,)), ((), ())), preferred_element_type=F32
    ).astype(BF16)


def select_slots(base, parts, capacity, choices, experts):
    rows, width = parts[0].shape
    length = rows - ID_ROWS
    slots = experts * capacity
    whole = pl.BlockSpec(memory_space=pltpu.VMEM)
    return pl.pallas_call(
        functools.partial(select_kernel, capacity, choices, experts),
        in_specs=[pl.BlockSpec(memory_space=pltpu.SMEM), *([whole] * len(parts))],
        out_shape=(
            jax.ShapeDtypeStruct((width, slots), BF16),
            jax.ShapeDtypeStruct((slots, length), BF16),
        ),
        cost_estimate=pl.CostEstimate(
            flops=2 * slots * length * width, bytes_accessed=4 * slots * width, transcendentals=0
        ),
        compiler_params=pltpu.CompilerParams(vmem_limit_bytes=VMEM_LIMIT),
    )(base, *parts)


def combine_kernel(place_ref, *refs):
    shares, out_ref = refs[:-1], refs[-1]
    total = shares[0][0].astype(F32)
    for share in shares[1:]:
        total = total + share[0].astype(F32)
    out_ref[...] = lax.dot_general(
        place_ref[...], total.astype(BF16), (((0,), (0,)), ((), ())), preferred_element_type=F32
    ).astype(BF16)


def combine_slots(place, shares):
    slots, length = place.shape
    width = shares[0].shape[2]
    first = pl.BlockSpec((1, slots, width), lambda _: (0, 0, 0))
    return pl.pallas_call(
        combine_kernel,
        grid=(1,),
        in_specs=[pl.BlockSpec(memory_space=pltpu.VMEM), *([first] * len(shares))],
        out_shape=jax.ShapeDtypeStruct((length, width), BF16),
        cost_estimate=pl.CostEstimate(
            flops=2 * slots * length * width, bytes_accessed=8 * slots * width, transcendentals=0
        ),
        compiler_params=pltpu.CompilerParams(vmem_limit_bytes=VMEM_LIMIT),
    )(place, *shares)


def gate_kernel(counts, sections, last, plan_ref, *refs):
    step = pl.program_id(0)
    blocks = sum(counts)
    used = len(counts) * sections
    x_refs, refs = refs[:used], refs[used:]
    router_ref, gate_ref, up_ref = refs[:3]
    refs = refs[3:]
    if last:
        gate_in, up_in, score_in, hidden_ref, gate_acc, up_acc, score_acc = refs
    else:
        gate_acc, up_acc, score_acc = refs
    experts = gate_ref.shape[0]
    width = x_refs[0].shape[1]
    slots = gate_acc.shape[2]
    part = slots // sections

    @pl.when(step == 0)
    def _():
        if last:
            gate_acc[...] = gate_in[...]
            up_acc[...] = up_in[...]
            score_acc[...] = score_in[...]
        else:
            gate_acc[...] = jnp.zeros_like(gate_acc)
            up_acc[...] = jnp.zeros_like(up_acc)
            score_acc[...] = jnp.zeros_like(score_acc)

    xs = []
    for section in range(sections):
        mine = x_refs[section * len(counts) : (section + 1) * len(counts)]
        x = mine[-1][0]
        for i in range(len(counts) - 2, -1, -1):
            x = jnp.where(step < sum(counts[: i + 1]), mine[i][0], x)
        xs.append(x)
    for j in range(experts):
        x = jnp.concatenate([x[:, j * part : (j + 1) * part] for x in xs], axis=1)
        score_acc[j] += jnp.dot(router_ref[0], x, preferred_element_type=F32)
        gate_acc[j] += jnp.dot(gate_ref[j], x, preferred_element_type=F32)
        up_acc[j] += jnp.dot(up_ref[j], x, preferred_element_type=F32)

    if last:

        @pl.when(step == blocks - 1)
        def _():
            for j in range(experts):
                score = score_acc[j, j : j + 1, :]
                gate = gate_acc[j]
                routed = gate / (1.0 + jnp.exp(-gate)) * up_acc[j]
                routed = routed / (1.0 + jnp.exp(-score))
                hidden_ref[j] = routed.T.astype(BF16)


def gate_part(plan, xs, router_rows, gate_rows, up_rows, sums=None):
    counts = tuple(x.shape[0] for x in xs[0])
    blocks = sum(counts)
    _, width, total = xs[0][0].shape
    experts, units, _ = gate_rows.shape
    slots = total // experts * len(xs)
    whole = pl.BlockSpec(memory_space=pltpu.VMEM)
    last = sums is not None

    def x_spec(i):
        before = sum(counts[:i])
        return pl.BlockSpec(
            (1, width, total), lambda p, plan: (jnp.clip(p - before, 0, counts[i] - 1), 0, 0)
        )

    weight_spec = pl.BlockSpec((experts, units, width), lambda p, plan: (0, 0, plan[p]))
    sum_shapes = [(experts, units, slots), (experts, units, slots), (experts, experts, slots)]
    if last:
        out_shape = jax.ShapeDtypeStruct((experts, slots, units), BF16)
        out_specs = whole
        scratch = [pltpu.VMEM(shape, F32) for shape in sum_shapes]
    else:
        out_shape = tuple(jax.ShapeDtypeStruct(shape, F32) for shape in sum_shapes)
        out_specs = (whole, whole, whole)
        scratch = []
    return pl.pallas_call(
        functools.partial(gate_kernel, counts, len(xs), last),
        grid_spec=pltpu.PrefetchScalarGridSpec(
            num_scalar_prefetch=1,
            grid=(blocks,),
            in_specs=[
                *[x_spec(i) for _ in xs for i in range(len(counts))],
                pl.BlockSpec((1, experts, width), lambda p, plan: (plan[p], 0, 0)),
                weight_spec,
                weight_spec,
                *([whole] * 3 if last else []),
            ],
            out_specs=out_specs,
            scratch_shapes=scratch,
        ),
        out_shape=out_shape,
        cost_estimate=pl.CostEstimate(
            flops=4 * experts * slots * blocks * width * units,
            bytes_accessed=4 * experts * blocks * width * units,
            transcendentals=0,
        ),
        compiler_params=pltpu.CompilerParams(vmem_limit_bytes=VMEM_LIMIT),
    )(
        plan,
        *[x for section in xs for x in section],
        router_rows,
        in_hbm(gate_rows),
        in_hbm(up_rows),
        *(sums or ()),
    )


def down_kernel(blocks, sections, plan_ref, hidden_ref, down_ref, *out_refs):
    experts, slots, _ = hidden_ref.shape
    part = slots // sections
    turn = pl.program_id(0) // blocks
    for j in range(experts):
        share = jnp.dot(hidden_ref[j], down_ref[j], preferred_element_type=F32).astype(BF16)
        for i in range(len(out_refs) // sections):

            @pl.when(turn == i)
            def _():
                for section in range(sections):
                    out_ref = out_refs[i * sections + section]
                    out_ref[0, j * part : (j + 1) * part, :] = share[
                        section * part : (section + 1) * part
                    ]


def down_part(plans, hidden, down_weight, width, sections):
    blocks = plans[0].shape[0]
    experts, slots, units = hidden.shape
    rows = experts * slots // sections

    def out_spec(i):
        return pl.BlockSpec(
            (1, rows, width), lambda p, plan: (jnp.clip(p - i * blocks, 0, blocks - 1), 0, 0)
        )

    out = pl.pallas_call(
        functools.partial(down_kernel, blocks, sections),
        grid_spec=pltpu.PrefetchScalarGridSpec(
            num_scalar_prefetch=1,
            grid=(len(plans) * blocks,),
            in_specs=[
                pl.BlockSpec(memory_space=pltpu.VMEM),
                pl.BlockSpec((experts, units, width), lambda p, plan: (0, 0, plan[p])),
            ],
            out_specs=[out_spec(i) for i in range(len(plans)) for _ in range(sections)],
        ),
        out_shape=[jax.ShapeDtypeStruct((blocks, rows, width), BF16)] * (len(plans) * sections),
        cost_estimate=pl.CostEstimate(
            flops=2 * experts * slots * len(plans) * blocks * width * units,
            bytes_accessed=2 * experts * len(plans) * blocks * width * units,
            transcendentals=0,
        ),
        compiler_params=pltpu.CompilerParams(vmem_limit_bytes=VMEM_LIMIT),
    )(jnp.concatenate(plans), hidden, in_hbm(down_weight))
    return [out[i * sections : (i + 1) * sections] for i in range(len(plans))]


def added(left, right):
    return (left.astype(F32) + right.astype(F32)).astype(BF16)


def swapped(array, axis, even, odd):
    count = lax.axis_size(axis)
    pairs = [(i, i ^ (odd if i % 2 else even)) for i in range(count)]
    return lax.ppermute(array, axis, pairs)


class PairedPlane:
    def __init__(self):
        me = lax.axis_index("exp").astype(jnp.int32)
        other = me ^ 1
        near = jnp.where(me % 2 == 0, 2, 4)
        far = 6 - near
        self.early = jnp.stack([me, me ^ near, other, other ^ far])
        self.late = jnp.stack([me ^ far, me ^ 6, other ^ near, other ^ 6])
        self.mine = jnp.stack([me, me ^ near, me ^ far, me ^ 6])
        self.theirs = jnp.stack([other, other ^ far, other ^ near, other ^ 6])

    def once(self, part):
        return swapped(part, "exp", 2, 4)

    def first(self, part):
        return jnp.stack([part, self.once(part)])

    def second(self, two):
        return swapped(two, "exp", 4, 2)

    def across(self, two):
        return swapped(two, "exp", 1, 1)

def on_device(
    attn_query,
    attn_key,
    attn_value,
    log_decay,
    residual,
    norm_gain,
    expert_ids,
    router_weight,
    gate_weight,
    up_weight,
    down_weight,
):
    heads_here, length = log_decay.shape
    groups = lax.axis_size("seq")
    shares = lax.axis_size("exp")
    width = attn_query.shape[1]
    experts_here = router_weight.shape[1]
    section = lax.axis_index("seq")
    inner = (section > 0) & (section < groups - 1)
    base = jnp.stack([section * experts_here, inner]).astype(jnp.int32)
    router_rows = router_weight.reshape(shares, width, experts_here).transpose(0, 2, 1)
    gate_rows = gate_weight.swapaxes(1, 2)
    up_rows = up_weight.swapaxes(1, 2)

    message, cumulative = section_state(attn_key, attn_value, log_decay)
    intra = intra_section(attn_query, attn_key, attn_value, log_decay, cumulative)
    incoming = incoming_state(message, heads_here)
    stream = make_stream(
        attn_query, intra, cumulative, incoming, residual, norm_gain, expert_ids.T
    )

    capacity = 4 * length // (experts_here * groups)
    choices = expert_ids.shape[1]

    def select(*parts):
        return select_slots(base, parts, capacity, choices, experts_here)

    weights = (router_rows, gate_rows, up_rows)
    if shares == 8 and groups == 4:
        pieces = paired_chunks(stream, select, weights, down_weight)
    else:
        order = jnp.arange(shares, dtype=jnp.int32)
        middle = shares // 2
        pieces = []
        for first in range(0, groups, 2):
            chunk = (first, first + 1)
            chosen = [
                select(swapped(stream, "seq", offset, offset) if offset else stream)
                for offset in chunk
            ]
            gathered = [lax.all_gather(slots, "exp", axis=0) for slots, _ in chosen]
            sums = gate_part(order[:middle], [[x[:middle]] for x in gathered], *weights)
            hidden = gate_part(order[middle:], [[x[middle:]] for x in gathered], *weights, sums)
            (partial,) = down_part([order], hidden, down_weight, width, len(chunk))
            for offset, share, (_, place) in zip(chunk, partial, chosen):
                share = lax.psum_scatter(share, "exp", scatter_dimension=0)
                piece = combine_slots(place, [share[None]])
                pieces.append(swapped(piece, "seq", offset, offset) if offset else piece)
    total = stream[:length].astype(F32)
    for piece in pieces:
        total = total + piece.astype(F32)
    return total.astype(BF16)


def paired_chunks(stream, select, weights, down_weight):
    plane = PairedPlane()
    width = stream.shape[1]
    tie = lax.optimization_barrier
    two, far_two, near, near_far, chosen = {}, {}, {}, {}, {}

    def across_middle(part):
        return lax.ppermute(part, "seq", [(1, 2), (2, 1)])

    def outward(part):
        return lax.ppermute(part, "seq", [(1, 0), (2, 3)])

    def gather(name, behind):
        two[name], _ = tie((plane.first(chosen[name][0]), behind))
        near[name] = plane.across(two[name])
        far_two[name] = plane.second(two[name])

    neighbour = swapped(stream, "seq", 1, 1)
    third = across_middle(stream)
    chosen["own"] = select(stream)
    gather("own", [neighbour, third])
    passed_third = outward(third)
    fourth = across_middle(neighbour)
    chosen["neighbour"] = select(neighbour)
    gather("neighbour", [passed_third, fourth, two["own"]])
    passed_fourth = outward(fourth)
    chosen["third"] = select(third, passed_third)
    gather("third", passed_fourth)
    chosen["fourth"] = select(fourth, passed_fourth)

    pieces = {}
    sent, finish = [], None
    for chunk, after in ((("neighbour", "third"), "fourth"), (("fourth", "own"), None)):
        early = [[two[name], near[name]] for name in chunk]
        if after:
            early, _ = tie((early, chosen[after]))
        early, _ = tie((early, sent))
        sums = gate_part(plane.early, early, *weights)
        if after:
            gather(after, sums)
            for name in chunk:
                far_two[name], _ = tie((far_two[name], sums))
        late = [[far_two[name], plane.across(far_two[name])] for name in chunk]
        if after:
            late, _ = tie((late, two[after]))
        hidden = gate_part(plane.late, late, *weights, sums)
        if after:
            hidden, _ = tie((hidden, far_two[after]))
            (theirs,) = down_part([plane.theirs], hidden, down_weight, width, len(chunk))
            hidden, theirs = tie((hidden, theirs))
            (mine,) = down_part([plane.mine], hidden, down_weight, width, len(chunk))
        else:
            one = finish(hidden)
            hidden, _ = tie((hidden, one))
            theirs, mine = down_part([plane.theirs, plane.mine], hidden, down_weight, width, len(chunk))
            theirs, _ = tie((theirs, list(pieces.values())))
        near_share = [plane.across(part) for part in theirs]
        sent = [added(kept[2:], got[2:]) for kept, got in zip(mine, near_share)]
        got_two = [plane.second(sent[0])]
        part = sent[1] if after else tie((sent[1], got_two))[0]
        got_two.append(plane.second(part))

        def finish(behind, chunk=chunk, mine=mine, near_share=near_share, got_two=got_two):
            got_two = [tie((far, behind))[0] for far in got_two]
            one = [
                added(added(kept[1], got[1]), far[1])
                for kept, got, far in zip(mine, near_share, got_two)
            ]
            for k, name in enumerate(chunk):
                got_one = plane.once(one[k])[None]
                pieces[name] = combine_slots(
                    chosen[name][1], [mine[k], near_share[k], got_two[k], got_one]
                )
            return one

    finish([])
    return [
        pieces["own"],
        swapped(pieces["neighbour"], "seq", 1, 1),
        lax.ppermute(pieces["third"], "seq", [(1, 2), (2, 1)]),
        lax.ppermute(pieces["third"], "seq", [(0, 2), (3, 1)]),
        lax.ppermute(pieces["fourth"], "seq", [(1, 3), (2, 0)]),
        lax.ppermute(pieces["fourth"], "seq", [(0, 3), (3, 0)]),
    ]


def solution(mesh):
    in_specs = (
        P("seq", "exp"),
        P("seq", "exp"),
        P("seq", "exp"),
        P("exp", "seq"),
        P("seq", "exp"),
        P("exp"),
        P("seq", None),
        P(None, "seq"),
        P("seq", None, "exp"),
        P("seq", None, "exp"),
        P("seq", "exp", None),
    )
    out_specs = P("seq", "exp")
    return jax.shard_map(
        on_device, mesh=mesh, in_specs=in_specs, out_specs=out_specs, check_vma=False
    )
```

```python
import functools

import jax
import jax.numpy as jnp
from jax import lax
from jax.experimental import pallas as pl
from jax.experimental.pallas import tpu as pltpu
from jax.sharding import PartitionSpec as P

F32 = jnp.float32
BF16 = jnp.bfloat16
HIGHEST = lax.Precision.HIGHEST
VMEM_LIMIT = 22 * 1024 * 1024
ID_ROWS = 16


def in_hbm(array):
    return pltpu.with_memory_space_constraint(array, pltpu.HBM)


def lower_ones(length):
    rows = lax.broadcasted_iota(jnp.int32, (length, length), 0)
    columns = lax.broadcasted_iota(jnp.int32, (length, length), 1)
    return rows >= columns


def shifted(array, axis, by):
    count = lax.axis_size(axis)
    pairs = [(i, i + by) for i in range(count) if 0 <= i + by < count]
    return lax.ppermute(array, axis, pairs)


def state_kernel(key_ref, value_ref, decay_ref, message_ref, cumulative_ref):
    heads, length = decay_ref.shape
    size = key_ref.shape[1] // heads
    ones = lower_ones(length).astype(F32)
    cumulative = lax.dot_general(
        ones, decay_ref[...], (((1,), (1,)), ((), ())), precision=HIGHEST, preferred_element_type=F32
    )
    cumulative_ref[...] = cumulative
    last = cumulative[length - 1 : length, :]
    key_fade = jnp.exp(last - cumulative)
    message_ref[heads * size :, :] = jnp.zeros((message_ref.shape[0] - heads * size, size), BF16)
    half = (message_ref.shape[0] - heads * size) // 2
    rows = []
    for h in range(heads):
        columns = slice(h * size, (h + 1) * size)
        scaled = (key_fade[:, h : h + 1] * key_ref[:, columns].astype(F32)).astype(BF16)
        state = lax.dot_general(
            scaled, value_ref[:, columns], (((0,), (0,)), ((), ())), preferred_element_type=F32
        )
        message_ref[columns, :] = state.astype(BF16)
        rows.append(jnp.broadcast_to(jnp.exp(last[:, h : h + 1]), (1, size)))
    rows.append(jnp.zeros((half - heads, size), F32))
    fade = jnp.concatenate(rows, axis=0)
    leading = fade.astype(BF16)
    trailing = (fade - leading.astype(F32)).astype(BF16)
    message_ref[heads * size :, :] = jnp.concatenate([leading, trailing], axis=0)


def section_state(attn_key, attn_value, log_decay):
    heads, length = log_decay.shape
    width = attn_key.shape[1]
    half = -(-heads // 8) * 8
    return pl.pallas_call(
        state_kernel,
        out_shape=(
            jax.ShapeDtypeStruct((width + 2 * half, width // heads), BF16),
            jax.ShapeDtypeStruct((length, heads), F32),
        ),
        cost_estimate=pl.CostEstimate(
            flops=2 * length * width * (width // heads), bytes_accessed=4 * length * width, transcendentals=0
        ),
        compiler_params=pltpu.CompilerParams(vmem_limit_bytes=VMEM_LIMIT),
    )(in_hbm(attn_key), in_hbm(attn_value), in_hbm(log_decay))


def intra_kernel(query_ref, key_ref, value_ref, decay_ref, cumulative_ref, out_ref):
    heads, length = decay_ref.shape
    size = key_ref.shape[1] // heads
    causal = lower_ones(length)
    along = lax.dot_general(
        decay_ref[...],
        causal.astype(F32),
        (((1,), (1,)), ((), ())),
        precision=HIGHEST,
        preferred_element_type=F32,
    )
    for h in range(heads):
        columns = slice(h * size, (h + 1) * size)
        gap = jnp.where(causal, cumulative_ref[:, h : h + 1] - along[h : h + 1, :], 0.0)
        mask = jnp.where(causal, jnp.exp(gap), 0.0)
        scores = lax.dot_general(
            query_ref[:, columns], key_ref[:, columns], (((1,), (1,)), ((), ())), preferred_element_type=F32
        )
        weights = (scores * mask).astype(BF16)
        out_ref[:, columns] = jnp.dot(weights, value_ref[:, columns], preferred_element_type=F32)


def intra_section(attn_query, attn_key, attn_value, log_decay, cumulative):
    length, width = attn_query.shape
    return pl.pallas_call(
        intra_kernel,
        out_shape=jax.ShapeDtypeStruct((length, width), F32),
        cost_estimate=pl.CostEstimate(
            flops=4 * length * length * width, bytes_accessed=10 * length * width, transcendentals=0
        ),
        compiler_params=pltpu.CompilerParams(vmem_limit_bytes=VMEM_LIMIT),
    )(attn_query, attn_key, attn_value, log_decay, cumulative)


def stream_kernel(
    query_ref, intra_ref, cumulative_ref, incoming_ref, residual_ref, gain_ref, ids_ref, out_ref
):
    heads, size = incoming_ref.shape[0], incoming_ref.shape[1]
    length, width = residual_ref.shape
    choices = ids_ref.shape[0]
    below = jnp.concatenate(
        [
            ids_ref[...].astype(F32),
            jnp.zeros((ID_ROWS - choices, length), F32),
        ],
        axis=0,
    )
    out_ref[length:, :] = jnp.concatenate(
        [below, jnp.zeros((ID_ROWS, width - length), F32)], axis=1
    ).astype(BF16)
    faded = jnp.exp(cumulative_ref[...])
    for h in range(heads):
        columns = slice(h * size, (h + 1) * size)
        state = incoming_ref[h]
        leading = state.astype(BF16)
        trailing = (state - leading.astype(F32)).astype(BF16)
        query = query_ref[:, columns]
        inter = jnp.dot(query, leading, preferred_element_type=F32) + jnp.dot(
            query, trailing, preferred_element_type=F32
        )
        attn_out = intra_ref[:, columns] + faded[:, h : h + 1] * inter
        mean_square = jnp.mean(attn_out * attn_out, axis=1, keepdims=True)
        normed = attn_out * lax.rsqrt(mean_square + 1e-06)
        out_ref[:length, columns] = (
            residual_ref[:, columns].astype(F32) + gain_ref[:, columns].astype(F32) * normed
        ).astype(BF16)


def make_stream(attn_query, intra, cumulative, incoming, residual, norm_gain, ids):
    length, width = attn_query.shape
    return pl.pallas_call(
        stream_kernel,
        out_shape=jax.ShapeDtypeStruct((length + ID_ROWS, width), BF16),
        compiler_params=pltpu.CompilerParams(vmem_limit_bytes=VMEM_LIMIT),
    )(attn_query, intra, cumulative, incoming, residual, norm_gain.reshape(1, width), ids)


def read_message(message, heads):
    size = message.shape[1]
    half = (message.shape[0] - heads * size) // 2
    state = message[: heads * size].astype(F32).reshape(heads, size, size)
    tail = message[heads * size :].astype(F32)
    fade = tail[:heads] + tail[half : half + heads]
    return fade[:, None, :], state


def write_message(fade, state, rows):
    heads, size = state.shape[0], state.shape[1]
    half = (rows - heads * size) // 2
    leading = fade[:, 0, :].astype(BF16)
    trailing = (fade[:, 0, :] - leading.astype(F32)).astype(BF16)
    spare = jnp.zeros((half - heads, size), BF16)
    return jnp.concatenate(
        [state.astype(BF16).reshape(heads * size, size), leading, spare, trailing, spare], axis=0
    )


def incoming_state(message, heads):
    count = lax.axis_size("seq")
    window_fade, window = read_message(message, heads)
    incoming_fade, incoming = None, None
    distance = 1
    while distance < count:
        got_fade, got = read_message(shifted(message, "seq", distance), heads)
        if incoming is None:
            incoming_fade, incoming = got_fade, got
        else:
            incoming, incoming_fade = incoming + incoming_fade * got, incoming_fade * got_fade
        window, window_fade = window + window_fade * got, window_fade * got_fade
        distance *= 2
        if distance < count:
            message = write_message(window_fade, window, message.shape[0])
    return incoming


def select_kernel(capacity, choices, experts, base_ref, *refs):
    parts, (out_ref, place_ref) = refs[:-2], refs[-2:]
    length = parts[0].shape[0] - ID_ROWS
    part = parts[-1][...]
    for other in parts[:-1]:
        part = jnp.where(base_ref[1] > 0, other[...], part)
    before = lower_ones(length).astype(BF16)
    slot = lax.broadcasted_iota(jnp.int32, (capacity, length), 0).astype(F32)
    ids = part[length:, :length].astype(F32)
    rows = []
    for j in range(experts):
        expert = (base_ref[0] + j).astype(F32)
        chosen = ids[0:1, :] == expert
        for choice in range(1, choices):
            chosen = chosen | (ids[choice : choice + 1, :] == expert)
        flag = jnp.where(chosen, 1.0, 0.0)
        rank = lax.dot_general(
            jnp.broadcast_to(flag, (16, length)).astype(BF16),
            before,
            (((1,), (1,)), ((), ())),
            preferred_element_type=F32,
        )[0:1, :]
        rank = jnp.where(chosen, rank - 1.0, -1.0)
        rows.append(jnp.where(slot == rank, 1.0, 0.0).astype(BF16))
    place = jnp.concatenate(rows, axis=0)
    place_ref[...] = place
    out_ref[...] = lax.dot_general(
        part[:length, :], place, (((0,), (1,)), ((), ())), preferred_element_type=F32
    ).astype(BF16)


def select_slots(base, parts, capacity, choices, experts):
    rows, width = parts[0].shape
    length = rows - ID_ROWS
    slots = experts * capacity
    whole = pl.BlockSpec(memory_space=pltpu.VMEM)
    return pl.pallas_call(
        functools.partial(select_kernel, capacity, choices, experts),
        in_specs=[pl.BlockSpec(memory_space=pltpu.SMEM), *([whole] * len(parts))],
        out_shape=(
            jax.ShapeDtypeStruct((width, slots), BF16),
            jax.ShapeDtypeStruct((slots, length), BF16),
        ),
        cost_estimate=pl.CostEstimate(
            flops=2 * slots * length * width, bytes_accessed=4 * slots * width, transcendentals=0
        ),
        compiler_params=pltpu.CompilerParams(vmem_limit_bytes=VMEM_LIMIT),
    )(base, *parts)


def combine_kernel(place_ref, *refs):
    shares, out_ref = refs[:-1], refs[-1]
    total = shares[0][0].astype(F32)
    for share in shares[1:]:
        total = total + share[0].astype(F32)
    out_ref[...] = lax.dot_general(
        place_ref[...], total.astype(BF16), (((0,), (0,)), ((), ())), preferred_element_type=F32
    ).astype(BF16)


def combine_slots(place, shares):
    slots, length = place.shape
    width = shares[0].shape[2]
    first = pl.BlockSpec((1, slots, width), lambda _: (0, 0, 0))
    return pl.pallas_call(
        combine_kernel,
        grid=(1,),
        in_specs=[pl.BlockSpec(memory_space=pltpu.VMEM), *([first] * len(shares))],
        out_shape=jax.ShapeDtypeStruct((length, width), BF16),
        cost_estimate=pl.CostEstimate(
            flops=2 * slots * length * width, bytes_accessed=8 * slots * width, transcendentals=0
        ),
        compiler_params=pltpu.CompilerParams(vmem_limit_bytes=VMEM_LIMIT),
    )(place, *shares)


def gate_kernel(counts, sections, last, plan_ref, *refs):
    step = pl.program_id(0)
    blocks = sum(counts)
    used = len(counts) * sections
    x_refs, refs = refs[:used], refs[used:]
    router_ref, gate_ref, up_ref = refs[:3]
    refs = refs[3:]
    if last:
        gate_in, up_in, score_in, hidden_ref, gate_acc, up_acc, score_acc = refs
    else:
        gate_acc, up_acc, score_acc = refs
    experts = gate_ref.shape[0]
    width = x_refs[0].shape[1]
    slots = gate_acc.shape[2]
    part = slots // sections

    @pl.when(step == 0)
    def _():
        if last:
            gate_acc[...] = gate_in[...]
            up_acc[...] = up_in[...]
            score_acc[...] = score_in[...]
        else:
            gate_acc[...] = jnp.zeros_like(gate_acc)
            up_acc[...] = jnp.zeros_like(up_acc)
            score_acc[...] = jnp.zeros_like(score_acc)

    xs = []
    for section in range(sections):
        mine = x_refs[section * len(counts) : (section + 1) * len(counts)]
        x = mine[-1][0]
        for i in range(len(counts) - 2, -1, -1):
            x = jnp.where(step < sum(counts[: i + 1]), mine[i][0], x)
        xs.append(x)
    for j in range(experts):
        x = jnp.concatenate([x[:, j * part : (j + 1) * part] for x in xs], axis=1)
        score_acc[j] += jnp.dot(router_ref[0], x, preferred_element_type=F32)
        gate_acc[j] += jnp.dot(gate_ref[j], x, preferred_element_type=F32)
        up_acc[j] += jnp.dot(up_ref[j], x, preferred_element_type=F32)

    if last:

        @pl.when(step == blocks - 1)
        def _():
            for j in range(experts):
                score = score_acc[j, j : j + 1, :]
                gate = gate_acc[j]
                routed = gate / (1.0 + jnp.exp(-gate)) * up_acc[j]
                routed = routed / (1.0 + jnp.exp(-score))
                hidden_ref[j] = routed.T.astype(BF16)


def gate_part(plan, xs, router_rows, gate_rows, up_rows, sums=None):
    counts = tuple(x.shape[0] for x in xs[0])
    blocks = sum(counts)
    _, width, total = xs[0][0].shape
    experts, units, _ = gate_rows.shape
    slots = total // experts * len(xs)
    whole = pl.BlockSpec(memory_space=pltpu.VMEM)
    last = sums is not None

    def x_spec(i):
        before = sum(counts[:i])
        return pl.BlockSpec(
            (1, width, total), lambda p, plan: (jnp.clip(p - before, 0, counts[i] - 1), 0, 0)
        )

    weight_spec = pl.BlockSpec((experts, units, width), lambda p, plan: (0, 0, plan[p]))
    sum_shapes = [(experts, units, slots), (experts, units, slots), (experts, experts, slots)]
    if last:
        out_shape = jax.ShapeDtypeStruct((experts, slots, units), BF16)
        out_specs = whole
        scratch = [pltpu.VMEM(shape, F32) for shape in sum_shapes]
    else:
        out_shape = tuple(jax.ShapeDtypeStruct(shape, F32) for shape in sum_shapes)
        out_specs = (whole, whole, whole)
        scratch = []
    return pl.pallas_call(
        functools.partial(gate_kernel, counts, len(xs), last),
        grid_spec=pltpu.PrefetchScalarGridSpec(
            num_scalar_prefetch=1,
            grid=(blocks,),
            in_specs=[
                *[x_spec(i) for _ in xs for i in range(len(counts))],
                pl.BlockSpec((1, experts, width), lambda p, plan: (plan[p], 0, 0)),
                weight_spec,
                weight_spec,
                *([whole] * 3 if last else []),
            ],
            out_specs=out_specs,
            scratch_shapes=scratch,
        ),
        out_shape=out_shape,
        cost_estimate=pl.CostEstimate(
            flops=4 * experts * slots * blocks * width * units,
            bytes_accessed=4 * experts * blocks * width * units,
            transcendentals=0,
        ),
        compiler_params=pltpu.CompilerParams(vmem_limit_bytes=VMEM_LIMIT),
    )(
        plan,
        *[x for section in xs for x in section],
        router_rows,
        in_hbm(gate_rows),
        in_hbm(up_rows),
        *(sums or ()),
    )


def down_kernel(blocks, low, part, plan_ref, hidden_ref, down_ref, *out_refs):
    turn = pl.program_id(0) // blocks
    for j in range(hidden_ref.shape[0]):
        mine = hidden_ref[j, low : low + part, :]
        share = jnp.dot(mine, down_ref[j], preferred_element_type=F32).astype(BF16)
        for i, out_ref in enumerate(out_refs):

            @pl.when(turn == i)
            def _():
                out_ref[0, j * part : (j + 1) * part, :] = share


def down_part(plans, hidden, down_weight, width, sections, section):
    blocks = plans[0].shape[0]
    experts, slots, units = hidden.shape
    part = slots // sections

    def out_spec(i):
        return pl.BlockSpec(
            (1, experts * part, width),
            lambda p, plan: (jnp.clip(p - i * blocks, 0, blocks - 1), 0, 0),
        )

    return pl.pallas_call(
        functools.partial(down_kernel, blocks, section * part, part),
        grid_spec=pltpu.PrefetchScalarGridSpec(
            num_scalar_prefetch=1,
            grid=(len(plans) * blocks,),
            in_specs=[
                pl.BlockSpec(memory_space=pltpu.VMEM),
                pl.BlockSpec((experts, units, width), lambda p, plan: (0, 0, plan[p])),
            ],
            out_specs=[out_spec(i) for i in range(len(plans))],
        ),
        out_shape=[jax.ShapeDtypeStruct((blocks, experts * part, width), BF16)] * len(plans),
        cost_estimate=pl.CostEstimate(
            flops=2 * experts * part * len(plans) * blocks * width * units,
            bytes_accessed=2 * experts * len(plans) * blocks * width * units,
            transcendentals=0,
        ),
        compiler_params=pltpu.CompilerParams(vmem_limit_bytes=VMEM_LIMIT),
    )(jnp.concatenate(plans), hidden, in_hbm(down_weight))


def added(left, right):
    return (left.astype(F32) + right.astype(F32)).astype(BF16)


def swapped(array, axis, even, odd):
    count = lax.axis_size(axis)
    pairs = [(i, i ^ (odd if i % 2 else even)) for i in range(count)]
    return lax.ppermute(array, axis, pairs)


class PairedPlane:
    def __init__(self):
        me = lax.axis_index("exp").astype(jnp.int32)
        other = me ^ 1
        near = jnp.where(me % 2 == 0, 2, 4)
        far = 6 - near
        self.early = jnp.stack([me, me ^ near, other, other ^ far])
        self.late = jnp.stack([me ^ far, me ^ 6, other ^ near, other ^ 6])
        self.mine = jnp.stack([me, me ^ near, me ^ far, me ^ 6])
        self.theirs = jnp.stack([other, other ^ far, other ^ near, other ^ 6])

    def once(self, part):
        return swapped(part, "exp", 2, 4)

    def first(self, part):
        return jnp.stack([part, self.once(part)])

    def second(self, two):
        return swapped(two, "exp", 4, 2)

    def across(self, two):
        return swapped(two, "exp", 1, 1)

def on_device(
    attn_query,
    attn_key,
    attn_value,
    log_decay,
    residual,
    norm_gain,
    expert_ids,
    router_weight,
    gate_weight,
    up_weight,
    down_weight,
):
    heads_here, length = log_decay.shape
    groups = lax.axis_size("seq")
    shares = lax.axis_size("exp")
    width = attn_query.shape[1]
    experts_here = router_weight.shape[1]
    section = lax.axis_index("seq")
    inner = (section > 0) & (section < groups - 1)
    base = jnp.stack([section * experts_here, inner]).astype(jnp.int32)
    router_rows = router_weight.reshape(shares, width, experts_here).transpose(0, 2, 1)
    gate_rows = gate_weight.swapaxes(1, 2)
    up_rows = up_weight.swapaxes(1, 2)

    message, cumulative = section_state(attn_key, attn_value, log_decay)
    intra = intra_section(attn_query, attn_key, attn_value, log_decay, cumulative)
    incoming = incoming_state(message, heads_here)
    stream = make_stream(
        attn_query, intra, cumulative, incoming, residual, norm_gain, expert_ids.T
    )

    capacity = 4 * length // (experts_here * groups)
    choices = expert_ids.shape[1]

    def select(*parts):
        return select_slots(base, parts, capacity, choices, experts_here)

    weights = (router_rows, gate_rows, up_rows)
    if shares == 8 and groups == 4:
        pieces = paired_chunks(stream, select, weights, down_weight)
    else:
        order = jnp.arange(shares, dtype=jnp.int32)
        middle = shares // 2
        pieces = []
        for first in range(0, groups, 2):
            chunk = (first, first + 1)
            chosen = [
                select(swapped(stream, "seq", offset, offset) if offset else stream)
                for offset in chunk
            ]
            gathered = [lax.all_gather(slots, "exp", axis=0) for slots, _ in chosen]
            sums = gate_part(order[:middle], [[x[:middle]] for x in gathered], *weights)
            hidden = gate_part(order[middle:], [[x[middle:]] for x in gathered], *weights, sums)
            for i, offset in enumerate(chunk):
                place = chosen[i][1]
                (share,) = down_part([order], hidden, down_weight, width, len(chunk), i)
                share = lax.psum_scatter(share, "exp", scatter_dimension=0)
                piece = combine_slots(place, [share[None]])
                pieces.append(swapped(piece, "seq", offset, offset) if offset else piece)
    total = stream[:length].astype(F32)
    for piece in pieces:
        total = total + piece.astype(F32)
    return total.astype(BF16)


def paired_chunks(stream, select, weights, down_weight):
    plane = PairedPlane()
    width = stream.shape[1]
    tie = lax.optimization_barrier
    two, far_two, near, near_far, chosen = {}, {}, {}, {}, {}

    def across_middle(part):
        return lax.ppermute(part, "seq", [(1, 2), (2, 1)])

    def outward(part):
        return lax.ppermute(part, "seq", [(1, 0), (2, 3)])

    def gather(name, behind):
        two[name], _ = tie((plane.first(chosen[name][0]), behind))
        near[name] = plane.across(two[name])
        far_two[name] = plane.second(two[name])

    swap = swapped(stream, "seq", 1, 1)
    crossed = across_middle(stream)
    chosen["own"] = select(stream)
    gather("own", [swap, crossed])
    passed = outward(crossed)
    crossed_swap = across_middle(swap)
    chosen["neighbour"] = select(swap)
    gather("neighbour", [passed, crossed_swap, two["own"]])
    passed_fourth = outward(crossed_swap)
    chosen["third"] = select(crossed, passed)
    gather("third", [passed_fourth, far_two["neighbour"]])
    chosen["fourth"] = select(crossed_swap, passed_fourth)

    def gate(chunk, behind):
        early = [[two[name], near[name]] for name in chunk]
        return gate_part(plane.early, tie((early, behind))[0], *weights)

    def gate_last(chunk, sums, behind):
        late = [[far_two[name], near_far[name]] for name in chunk]
        (late, sums), _ = tie(((late, sums), behind))
        return gate_part(plane.late, late, *weights, sums)

    def down(hidden, section, behind):
        hidden, _ = tie((hidden, behind))
        plans = [plane.theirs, plane.mine]
        return down_part(plans, hidden, down_weight, width, 2, section)

    class Scatter:
        def __init__(self, name, shares):
            self.name = name
            self.theirs, self.mine = shares

        def two_blocks(self, behind):
            self.near = plane.across(self.theirs)
            self.sent = added(self.mine[2:], self.near[2:])
            self.got_two = plane.second(tie((self.sent, behind))[0])

        def one_block(self, behind):
            got_two, _ = tie((self.got_two, behind))
            self.one = added(added(self.mine[1], self.near[1]), got_two[1])
            self.got_one = plane.once(self.one)

        def own_block(self, behind):
            got_one, _ = tie((self.got_one, behind))
            shares = [self.mine, self.near, self.got_two, got_one[None]]
            return combine_slots(chosen[self.name][1], shares)

    chunk = ("third", "neighbour")
    sums = gate(chunk, chosen["fourth"])
    gather("fourth", sums)
    for name in chunk:
        near_far[name] = plane.across(tie((far_two[name], sums))[0])
    hidden = gate_last(chunk, sums, two["fourth"])
    third = Scatter("third", down(hidden, 0, far_two["fourth"]))
    neighbour = Scatter("neighbour", down(hidden, 1, [third.theirs, far_two["own"]]))
    third.two_blocks([])

    chunk = ("fourth", "own")
    sums = gate(chunk, third.sent)
    for name in chunk:
        near_far[name] = plane.across(tie((far_two[name], third.sent))[0])
    third.one_block(sums)
    neighbour.two_blocks(third.one)
    hidden = gate_last(chunk, sums, [third.one, neighbour.sent])
    third_piece = third.own_block(hidden)
    neighbour.one_block(hidden)
    fourth = Scatter("fourth", down(hidden, 0, third_piece))
    third_home = lax.ppermute(third_piece, "seq", [(1, 2), (2, 1)])
    own = Scatter("own", down(hidden, 1, [fourth.theirs, neighbour.one, third_home]))
    third_piece, _ = tie((third_piece, third_home))
    third_far_home = lax.ppermute(third_piece, "seq", [(0, 2), (3, 1)])
    neighbour_piece = neighbour.own_block([])
    own.theirs, _ = tie((own.theirs, [third_far_home, neighbour_piece]))
    fourth.two_blocks([])
    fourth.one_block([])
    own.two_blocks(fourth.got_two)
    own.one_block([])
    fourth_piece = fourth.own_block([])
    return [
        own.own_block([]),
        swapped(neighbour_piece, "seq", 1, 1),
        third_home,
        third_far_home,
        lax.ppermute(fourth_piece, "seq", [(1, 3), (2, 0)]),
        lax.ppermute(fourth_piece, "seq", [(0, 3), (3, 0)]),
    ]


def solution(mesh):
    in_specs = (
        P("seq", "exp"),
        P("seq", "exp"),
        P("seq", "exp"),
        P("exp", "seq"),
        P("seq", "exp"),
        P("exp"),
        P("seq", None),
        P(None, "seq"),
        P("seq", None, "exp"),
        P("seq", None, "exp"),
        P("seq", "exp", None),
    )
    out_specs = P("seq", "exp")
    return jax.shard_map(
        on_device, mesh=mesh, in_specs=in_specs, out_specs=out_specs, check_vma=False
    )
```

```python
import functools

import jax
import jax.numpy as jnp
from jax import lax
from jax.experimental import pallas as pl
from jax.experimental.pallas import tpu as pltpu
from jax.sharding import PartitionSpec as P

F32 = jnp.float32
BF16 = jnp.bfloat16
HIGHEST = lax.Precision.HIGHEST
VMEM_LIMIT = 32 * 1024 * 1024
ID_ROWS = 16


def in_hbm(array):
    return pltpu.with_memory_space_constraint(array, pltpu.HBM)


def lower_ones(length):
    rows = lax.broadcasted_iota(jnp.int32, (length, length), 0)
    columns = lax.broadcasted_iota(jnp.int32, (length, length), 1)
    return rows >= columns


def shifted(array, axis, by):
    count = lax.axis_size(axis)
    pairs = [(i, i + by) for i in range(count) if 0 <= i + by < count]
    return lax.ppermute(array, axis, pairs)


def state_kernel(key_ref, value_ref, decay_ref, message_ref, cumulative_ref):
    heads, length = decay_ref.shape
    size = key_ref.shape[1] // heads
    ones = lower_ones(length).astype(F32)
    cumulative = lax.dot_general(
        ones, decay_ref[...], (((1,), (1,)), ((), ())), precision=HIGHEST, preferred_element_type=F32
    )
    cumulative_ref[...] = cumulative
    last = cumulative[length - 1 : length, :]
    key_fade = jnp.exp(last - cumulative)
    message_ref[heads * size :, :] = jnp.zeros((message_ref.shape[0] - heads * size, size), BF16)
    half = (message_ref.shape[0] - heads * size) // 2
    rows = []
    for h in range(heads):
        columns = slice(h * size, (h + 1) * size)
        scaled = (key_fade[:, h : h + 1] * key_ref[:, columns].astype(F32)).astype(BF16)
        state = lax.dot_general(
            scaled, value_ref[:, columns], (((0,), (0,)), ((), ())), preferred_element_type=F32
        )
        message_ref[columns, :] = state.astype(BF16)
        rows.append(jnp.broadcast_to(jnp.exp(last[:, h : h + 1]), (1, size)))
    rows.append(jnp.zeros((half - heads, size), F32))
    fade = jnp.concatenate(rows, axis=0)
    leading = fade.astype(BF16)
    trailing = (fade - leading.astype(F32)).astype(BF16)
    message_ref[heads * size :, :] = jnp.concatenate([leading, trailing], axis=0)


def section_state(attn_key, attn_value, log_decay):
    heads, length = log_decay.shape
    width = attn_key.shape[1]
    half = -(-heads // 8) * 8
    return pl.pallas_call(
        state_kernel,
        out_shape=(
            jax.ShapeDtypeStruct((width + 2 * half, width // heads), BF16),
            jax.ShapeDtypeStruct((length, heads), F32),
        ),
        cost_estimate=pl.CostEstimate(
            flops=2 * length * width * (width // heads), bytes_accessed=4 * length * width, transcendentals=0
        ),
        compiler_params=pltpu.CompilerParams(vmem_limit_bytes=VMEM_LIMIT),
    )(in_hbm(attn_key), in_hbm(attn_value), in_hbm(log_decay))


def intra_kernel(query_ref, key_ref, value_ref, decay_ref, cumulative_ref, out_ref):
    heads, length = decay_ref.shape
    size = key_ref.shape[1] // heads
    causal = lower_ones(length)
    along = lax.dot_general(
        decay_ref[...],
        causal.astype(F32),
        (((1,), (1,)), ((), ())),
        precision=HIGHEST,
        preferred_element_type=F32,
    )
    for h in range(heads):
        columns = slice(h * size, (h + 1) * size)
        gap = jnp.where(causal, cumulative_ref[:, h : h + 1] - along[h : h + 1, :], 0.0)
        mask = jnp.where(causal, jnp.exp(gap), 0.0)
        scores = lax.dot_general(
            query_ref[:, columns], key_ref[:, columns], (((1,), (1,)), ((), ())), preferred_element_type=F32
        )
        weights = (scores * mask).astype(BF16)
        out_ref[:, columns] = jnp.dot(weights, value_ref[:, columns], preferred_element_type=F32)


def intra_section(attn_query, attn_key, attn_value, log_decay, cumulative):
    length, width = attn_query.shape
    return pl.pallas_call(
        intra_kernel,
        out_shape=jax.ShapeDtypeStruct((length, width), F32),
        cost_estimate=pl.CostEstimate(
            flops=4 * length * length * width, bytes_accessed=10 * length * width, transcendentals=0
        ),
        compiler_params=pltpu.CompilerParams(vmem_limit_bytes=VMEM_LIMIT),
    )(attn_query, attn_key, attn_value, log_decay, cumulative)


def stream_kernel(
    query_ref, intra_ref, cumulative_ref, incoming_ref, residual_ref, gain_ref, ids_ref, out_ref
):
    heads, size = incoming_ref.shape[0], incoming_ref.shape[1]
    length, width = residual_ref.shape
    choices = ids_ref.shape[0]
    below = jnp.concatenate(
        [
            ids_ref[...].astype(F32),
            jnp.zeros((ID_ROWS - choices, length), F32),
        ],
        axis=0,
    )
    out_ref[length:, :] = jnp.concatenate(
        [below, jnp.zeros((ID_ROWS, width - length), F32)], axis=1
    ).astype(BF16)
    faded = jnp.exp(cumulative_ref[...])
    for h in range(heads):
        columns = slice(h * size, (h + 1) * size)
        state = incoming_ref[h]
        leading = state.astype(BF16)
        trailing = (state - leading.astype(F32)).astype(BF16)
        query = query_ref[:, columns]
        inter = jnp.dot(query, leading, preferred_element_type=F32) + jnp.dot(
            query, trailing, preferred_element_type=F32
        )
        attn_out = intra_ref[:, columns] + faded[:, h : h + 1] * inter
        mean_square = jnp.mean(attn_out * attn_out, axis=1, keepdims=True)
        normed = attn_out * lax.rsqrt(mean_square + 1e-06)
        out_ref[:length, columns] = (
            residual_ref[:, columns].astype(F32) + gain_ref[:, columns].astype(F32) * normed
        ).astype(BF16)


def make_stream(attn_query, intra, cumulative, incoming, residual, norm_gain, ids):
    length, width = attn_query.shape
    return pl.pallas_call(
        stream_kernel,
        out_shape=jax.ShapeDtypeStruct((length + ID_ROWS, width), BF16),
        compiler_params=pltpu.CompilerParams(vmem_limit_bytes=VMEM_LIMIT),
    )(attn_query, intra, cumulative, incoming, residual, norm_gain.reshape(1, width), ids)


def read_message(message, heads):
    size = message.shape[1]
    half = (message.shape[0] - heads * size) // 2
    state = message[: heads * size].astype(F32).reshape(heads, size, size)
    tail = message[heads * size :].astype(F32)
    fade = tail[:heads] + tail[half : half + heads]
    return fade[:, None, :], state


def write_message(fade, state, rows):
    heads, size = state.shape[0], state.shape[1]
    half = (rows - heads * size) // 2
    leading = fade[:, 0, :].astype(BF16)
    trailing = (fade[:, 0, :] - leading.astype(F32)).astype(BF16)
    spare = jnp.zeros((half - heads, size), BF16)
    return jnp.concatenate(
        [state.astype(BF16).reshape(heads * size, size), leading, spare, trailing, spare], axis=0
    )


def incoming_state(message, heads):
    count = lax.axis_size("seq")
    window_fade, window = read_message(message, heads)
    incoming_fade, incoming = None, None
    distance = 1
    while distance < count:
        got_fade, got = read_message(shifted(message, "seq", distance), heads)
        if incoming is None:
            incoming_fade, incoming = got_fade, got
        else:
            incoming, incoming_fade = incoming + incoming_fade * got, incoming_fade * got_fade
        window, window_fade = window + window_fade * got, window_fade * got_fade
        distance *= 2
        if distance < count:
            message = write_message(window_fade, window, message.shape[0])
    return incoming


def select_kernel(capacity, choices, experts, base_ref, *refs):
    parts, (out_ref, place_ref) = refs[:-2], refs[-2:]
    length = parts[0].shape[0] - ID_ROWS
    part = parts[-1][...]
    for other in parts[:-1]:
        part = jnp.where(base_ref[1] > 0, other[...], part)
    before = lower_ones(length).astype(BF16)
    slot = lax.broadcasted_iota(jnp.int32, (capacity, length), 0).astype(F32)
    ids = part[length:, :length].astype(F32)
    rows = []
    for j in range(experts):
        expert = (base_ref[0] + j).astype(F32)
        chosen = ids[0:1, :] == expert
        for choice in range(1, choices):
            chosen = chosen | (ids[choice : choice + 1, :] == expert)
        flag = jnp.where(chosen, 1.0, 0.0)
        rank = lax.dot_general(
            jnp.broadcast_to(flag, (16, length)).astype(BF16),
            before,
            (((1,), (1,)), ((), ())),
            preferred_element_type=F32,
        )[0:1, :]
        rank = jnp.where(chosen, rank - 1.0, -1.0)
        rows.append(jnp.where(slot == rank, 1.0, 0.0).astype(BF16))
    place = jnp.concatenate(rows, axis=0)
    place_ref[...] = place
    out_ref[...] = lax.dot_general(
        part[:length, :], place, (((0,), (1,)), ((), ())), preferred_element_type=F32
    ).astype(BF16)


def select_slots(base, parts, capacity, choices, experts):
    rows, width = parts[0].shape
    length = rows - ID_ROWS
    slots = experts * capacity
    whole = pl.BlockSpec(memory_space=pltpu.VMEM)
    return pl.pallas_call(
        functools.partial(select_kernel, capacity, choices, experts),
        in_specs=[pl.BlockSpec(memory_space=pltpu.SMEM), *([whole] * len(parts))],
        out_shape=(
            jax.ShapeDtypeStruct((width, slots), BF16),
            jax.ShapeDtypeStruct((slots, length), BF16),
        ),
        cost_estimate=pl.CostEstimate(
            flops=2 * slots * length * width, bytes_accessed=4 * slots * width, transcendentals=0
        ),
        compiler_params=pltpu.CompilerParams(vmem_limit_bytes=VMEM_LIMIT),
    )(base, *parts)


def combine_kernel(place_ref, *refs):
    shares, out_ref = refs[:-1], refs[-1]
    total = shares[0][0].astype(F32)
    for share in shares[1:]:
        total = total + share[0].astype(F32)
    out_ref[...] = lax.dot_general(
        place_ref[...], total.astype(BF16), (((0,), (0,)), ((), ())), preferred_element_type=F32
    ).astype(BF16)


def combine_slots(place, shares):
    slots, length = place.shape
    width = shares[0].shape[2]
    first = pl.BlockSpec((1, slots, width), lambda _: (0, 0, 0))
    return pl.pallas_call(
        combine_kernel,
        grid=(1,),
        in_specs=[pl.BlockSpec(memory_space=pltpu.VMEM), *([first] * len(shares))],
        out_shape=jax.ShapeDtypeStruct((length, width), BF16),
        cost_estimate=pl.CostEstimate(
            flops=2 * slots * length * width, bytes_accessed=8 * slots * width, transcendentals=0
        ),
        compiler_params=pltpu.CompilerParams(vmem_limit_bytes=VMEM_LIMIT),
    )(place, *shares)


def gate_kernel(counts, sections, last, plan_ref, *refs):
    step = pl.program_id(0)
    blocks = sum(counts)
    used = len(counts) * sections
    x_refs, refs = refs[:used], refs[used:]
    router_ref, gate_ref, up_ref = refs[:3]
    refs = refs[3:]
    if last:
        gate_in, up_in, score_in, hidden_ref, gate_acc, up_acc, score_acc = refs
    else:
        gate_acc, up_acc, score_acc = refs
    experts = gate_ref.shape[0]
    width = x_refs[0].shape[1]
    slots = gate_acc.shape[2]
    part = slots // sections

    @pl.when(step == 0)
    def _():
        if last:
            gate_acc[...] = gate_in[...]
            up_acc[...] = up_in[...]
            score_acc[...] = score_in[...]
        else:
            gate_acc[...] = jnp.zeros_like(gate_acc)
            up_acc[...] = jnp.zeros_like(up_acc)
            score_acc[...] = jnp.zeros_like(score_acc)

    xs = []
    for section in range(sections):
        mine = x_refs[section * len(counts) : (section + 1) * len(counts)]
        x = mine[-1][0]
        for i in range(len(counts) - 2, -1, -1):
            x = jnp.where(step < sum(counts[: i + 1]), mine[i][0], x)
        xs.append(x)
    for j in range(experts):
        x = jnp.concatenate([x[:, j * part : (j + 1) * part] for x in xs], axis=1)
        score_acc[j] += jnp.dot(router_ref[0], x, preferred_element_type=F32)
        gate_acc[j] += jnp.dot(gate_ref[j], x, preferred_element_type=F32)
        up_acc[j] += jnp.dot(up_ref[j], x, preferred_element_type=F32)

    if last:

        @pl.when(step == blocks - 1)
        def _():
            for j in range(experts):
                score = score_acc[j, j : j + 1, :]
                gate = gate_acc[j]
                routed = gate / (1.0 + jnp.exp(-gate)) * up_acc[j]
                routed = routed / (1.0 + jnp.exp(-score))
                hidden_ref[j] = routed.T.astype(BF16)


def gate_part(plan, xs, router_rows, gate_rows, up_rows, sums=None):
    counts = tuple(x.shape[0] for x in xs[0])
    blocks = sum(counts)
    _, width, total = xs[0][0].shape
    experts, units, _ = gate_rows.shape
    slots = total // experts * len(xs)
    whole = pl.BlockSpec(memory_space=pltpu.VMEM)
    last = sums is not None

    def x_spec(i):
        before = sum(counts[:i])
        return pl.BlockSpec(
            (1, width, total), lambda p, plan: (jnp.clip(p - before, 0, counts[i] - 1), 0, 0)
        )

    weight_spec = pl.BlockSpec((experts, units, width), lambda p, plan: (0, 0, plan[p]))
    sum_shapes = [(experts, units, slots), (experts, units, slots), (experts, experts, slots)]
    sum_specs = [pl.BlockSpec(shape, lambda p, plan: (0, 0, 0)) for shape in sum_shapes]
    if last:
        out_shape = jax.ShapeDtypeStruct((experts, slots, units), BF16)
        out_specs = whole
        scratch = [pltpu.VMEM(shape, F32) for shape in sum_shapes]
    else:
        out_shape = tuple(jax.ShapeDtypeStruct(shape, F32) for shape in sum_shapes)
        out_specs = tuple(sum_specs)
        scratch = []
    return pl.pallas_call(
        functools.partial(gate_kernel, counts, len(xs), last),
        grid_spec=pltpu.PrefetchScalarGridSpec(
            num_scalar_prefetch=1,
            grid=(blocks,),
            in_specs=[
                *[x_spec(i) for _ in xs for i in range(len(counts))],
                pl.BlockSpec((1, experts, width), lambda p, plan: (plan[p], 0, 0)),
                weight_spec,
                weight_spec,
                *(sum_specs if last else []),
            ],
            out_specs=out_specs,
            scratch_shapes=scratch,
        ),
        out_shape=out_shape,
        cost_estimate=pl.CostEstimate(
            flops=4 * experts * slots * blocks * width * units,
            bytes_accessed=4 * experts * blocks * width * units,
            transcendentals=0,
        ),
        compiler_params=pltpu.CompilerParams(vmem_limit_bytes=VMEM_LIMIT),
    )(
        plan,
        *[x for section in xs for x in section],
        router_rows,
        in_hbm(gate_rows),
        in_hbm(up_rows),
        *(sums or ()),
    )


def down_kernel(blocks, sections, plan_ref, hidden_ref, down_ref, *out_refs):
    experts, slots, _ = hidden_ref.shape
    part = slots // sections
    turn = pl.program_id(0) // blocks
    for j in range(experts):
        share = jnp.dot(hidden_ref[j], down_ref[j], preferred_element_type=F32).astype(BF16)
        for i in range(len(out_refs) // sections):

            @pl.when(turn == i)
            def _():
                for section in range(sections):
                    out_ref = out_refs[i * sections + section]
                    out_ref[0, j * part : (j + 1) * part, :] = share[
                        section * part : (section + 1) * part
                    ]


def down_part(plans, hidden, down_weight, width, sections):
    blocks = plans[0].shape[0]
    experts, slots, units = hidden.shape
    rows = experts * slots // sections

    def out_spec(i):
        return pl.BlockSpec(
            (1, rows, width), lambda p, plan: (jnp.clip(p - i * blocks, 0, blocks - 1), 0, 0)
        )

    out = pl.pallas_call(
        functools.partial(down_kernel, blocks, sections),
        grid_spec=pltpu.PrefetchScalarGridSpec(
            num_scalar_prefetch=1,
            grid=(len(plans) * blocks,),
            in_specs=[
                pl.BlockSpec(memory_space=pltpu.VMEM),
                pl.BlockSpec((experts, units, width), lambda p, plan: (0, 0, plan[p])),
            ],
            out_specs=[out_spec(i) for i in range(len(plans)) for _ in range(sections)],
        ),
        out_shape=[jax.ShapeDtypeStruct((blocks, rows, width), BF16)] * (len(plans) * sections),
        cost_estimate=pl.CostEstimate(
            flops=2 * experts * slots * len(plans) * blocks * width * units,
            bytes_accessed=2 * experts * len(plans) * blocks * width * units,
            transcendentals=0,
        ),
        compiler_params=pltpu.CompilerParams(vmem_limit_bytes=VMEM_LIMIT),
    )(jnp.concatenate(plans), hidden, in_hbm(down_weight))
    return [out[i * sections : (i + 1) * sections] for i in range(len(plans))]


def added(left, right):
    return (left.astype(F32) + right.astype(F32)).astype(BF16)


def swapped(array, axis, even, odd):
    count = lax.axis_size(axis)
    pairs = [(i, i ^ (odd if i % 2 else even)) for i in range(count)]
    return lax.ppermute(array, axis, pairs)


class PairedPlane:
    def __init__(self):
        me = lax.axis_index("exp").astype(jnp.int32)
        other = me ^ 1
        near = jnp.where(me % 2 == 0, 2, 4)
        far = 6 - near
        self.early = jnp.stack([me, me ^ near, other, other ^ far])
        self.late = jnp.stack([me ^ far, me ^ 6, other ^ near, other ^ 6])
        self.mine = jnp.stack([me, me ^ near, me ^ far, me ^ 6])
        self.theirs = jnp.stack([other, other ^ far, other ^ near, other ^ 6])

    def once(self, part):
        return swapped(part, "exp", 2, 4)

    def first(self, part):
        return jnp.stack([part, self.once(part)])

    def second(self, two):
        return swapped(two, "exp", 4, 2)

    def across(self, two):
        return swapped(two, "exp", 1, 1)

def on_device(
    attn_query,
    attn_key,
    attn_value,
    log_decay,
    residual,
    norm_gain,
    expert_ids,
    router_weight,
    gate_weight,
    up_weight,
    down_weight,
):
    heads_here, length = log_decay.shape
    groups = lax.axis_size("seq")
    shares = lax.axis_size("exp")
    width = attn_query.shape[1]
    experts_here = router_weight.shape[1]
    section = lax.axis_index("seq")
    inner = (section > 0) & (section < groups - 1)
    base = jnp.stack([section * experts_here, inner]).astype(jnp.int32)
    router_rows = router_weight.reshape(shares, width, experts_here).transpose(0, 2, 1)
    gate_rows = gate_weight.swapaxes(1, 2)
    up_rows = up_weight.swapaxes(1, 2)

    message, cumulative = section_state(attn_key, attn_value, log_decay)
    intra = intra_section(attn_query, attn_key, attn_value, log_decay, cumulative)
    incoming = incoming_state(message, heads_here)
    stream = make_stream(
        attn_query, intra, cumulative, incoming, residual, norm_gain, expert_ids.T
    )

    capacity = 4 * length // (experts_here * groups)
    choices = expert_ids.shape[1]

    def select(*parts):
        return select_slots(base, parts, capacity, choices, experts_here)

    weights = (router_rows, gate_rows, up_rows)
    if shares == 8 and groups == 4:
        pieces = paired_chunks(stream, select, weights, down_weight)
    else:
        order = jnp.arange(shares, dtype=jnp.int32)
        middle = shares // 2
        pieces = []
        for first in range(0, groups, 2):
            chunk = (first, first + 1)
            chosen = [
                select(swapped(stream, "seq", offset, offset) if offset else stream)
                for offset in chunk
            ]
            gathered = [lax.all_gather(slots, "exp", axis=0) for slots, _ in chosen]
            sums = gate_part(order[:middle], [[x[:middle]] for x in gathered], *weights)
            hidden = gate_part(order[middle:], [[x[middle:]] for x in gathered], *weights, sums)
            (partial,) = down_part([order], hidden, down_weight, width, len(chunk))
            for offset, share, (_, place) in zip(chunk, partial, chosen):
                share = lax.psum_scatter(share, "exp", scatter_dimension=0)
                piece = combine_slots(place, [share[None]])
                pieces.append(swapped(piece, "seq", offset, offset) if offset else piece)
    total = stream[:length].astype(F32)
    for piece in pieces:
        total = total + piece.astype(F32)
    return total.astype(BF16)


def paired_chunks(stream, select, weights, down_weight):
    plane = PairedPlane()
    width = stream.shape[1]
    tie = lax.optimization_barrier
    two, far_two, near, near_far, chosen = {}, {}, {}, {}, {}

    def across_middle(part):
        return lax.ppermute(part, "seq", [(1, 2), (2, 1)])

    def outward(part):
        return lax.ppermute(part, "seq", [(1, 0), (2, 3)])

    def gather(name, behind):
        two[name], _ = tie((plane.first(chosen[name][0]), behind))
        near[name] = plane.across(two[name])
        far_two[name] = plane.second(two[name])

    swap = swapped(stream, "seq", 1, 1)
    crossed = across_middle(stream)
    chosen["own"] = select(stream)
    gather("own", [])
    passed = outward(crossed)
    crossed_swap = across_middle(swap)
    chosen["neighbour"] = select(swap)
    gather("neighbour", [passed, crossed_swap, far_two["own"]])
    passed_fourth = outward(crossed_swap)
    chosen["third"] = select(crossed, passed)
    gather("third", [passed_fourth, far_two["neighbour"]])
    chosen["fourth"] = select(crossed_swap, passed_fourth)

    def gate(chunk, behind):
        early = [[two[name], near[name]] for name in chunk]
        return gate_part(plane.early, tie((early, behind))[0], *weights)

    def gate_last(chunk, sums, behind):
        late = [[far_two[name], near_far[name]] for name in chunk]
        (late, sums), _ = tie(((late, sums), behind))
        return gate_part(plane.late, late, *weights, sums)

    def down(plans, hidden, behind):
        hidden, _ = tie((hidden, behind))
        return down_part(plans, hidden, down_weight, width, 2)

    class Scatter:
        def __init__(self, name, theirs, mine):
            self.name, self.theirs, self.mine = name, theirs, mine

        def two_blocks(self, behind):
            self.near = plane.across(self.theirs)
            self.sent = added(self.mine[2:], self.near[2:])
            self.got_two = plane.second(tie((self.sent, behind))[0])

        def one_block(self, behind):
            got_two, _ = tie((self.got_two, behind))
            self.one = added(added(self.mine[1], self.near[1]), got_two[1])
            self.got_one = plane.once(self.one)

        def own_block(self, behind):
            got_one, _ = tie((self.got_one, behind))
            shares = [self.mine, self.near, self.got_two, got_one[None]]
            return combine_slots(chosen[self.name][1], shares)

    chunk = ("third", "neighbour")
    sums = gate(chunk, chosen["fourth"])
    gather("fourth", sums)
    for name in chunk:
        near_far[name] = plane.across(tie((far_two[name], sums))[0])
    hidden = gate_last(chunk, sums, two["fourth"])
    (theirs,) = down([plane.theirs], hidden, far_two["fourth"])
    (mine,) = down([plane.mine], hidden, theirs)
    third, neighbour = (Scatter(*shares) for shares in zip(chunk, theirs, mine))
    third.two_blocks([])

    chunk = ("fourth", "own")
    sums = gate(chunk, third.sent)
    for name in chunk:
        near_far[name] = plane.across(tie((far_two[name], third.sent))[0])
    third.one_block(sums)
    neighbour.two_blocks(third.one)
    hidden = gate_last(chunk, sums, [third.one, neighbour.sent])
    third_piece = third.own_block(hidden)
    neighbour.one_block(hidden)
    third_home = lax.ppermute(third_piece, "seq", [(1, 2), (2, 1)])
    theirs, mine = down([plane.theirs, plane.mine], hidden, neighbour.one)
    neighbour_piece = neighbour.own_block([])
    theirs, _ = tie((theirs, [third_home, neighbour_piece]))
    fourth, own = (Scatter(*shares) for shares in zip(chunk, theirs, mine))
    third_far_home = lax.ppermute(tie((third_piece, third_home))[0], "seq", [(0, 2), (3, 1)])
    neighbour_home = swapped(neighbour_piece, "seq", 1, 1)
    fourth.two_blocks([])
    fourth.one_block([third_far_home, neighbour_home])
    own.two_blocks(fourth.got_one)
    fourth_piece = fourth.own_block([])
    own.one_block(fourth_piece)
    return [
        own.own_block([]),
        neighbour_home,
        third_home,
        third_far_home,
        lax.ppermute(fourth_piece, "seq", [(1, 3), (2, 0)]),
        lax.ppermute(fourth_piece, "seq", [(0, 3), (3, 0)]),
    ]


def solution(mesh):
    in_specs = (
        P("seq", "exp"),
        P("seq", "exp"),
        P("seq", "exp"),
        P("exp", "seq"),
        P("seq", "exp"),
        P("exp"),
        P("seq", None),
        P(None, "seq"),
        P("seq", None, "exp"),
        P("seq", None, "exp"),
        P("seq", "exp", None),
    )
    out_specs = P("seq", "exp")
    return jax.shard_map(
        on_device, mesh=mesh, in_specs=in_specs, out_specs=out_specs, check_vma=False
    )
```

```python
import functools

import jax
import jax.numpy as jnp
from jax import lax
from jax.experimental import pallas as pl
from jax.experimental.pallas import tpu as pltpu
from jax.sharding import PartitionSpec as P

F32 = jnp.float32
BF16 = jnp.bfloat16
HIGHEST = lax.Precision.HIGHEST
VMEM_LIMIT = 32 * 1024 * 1024
ID_ROWS = 16


def in_hbm(array):
    return pltpu.with_memory_space_constraint(array, pltpu.HBM)


def lower_ones(length):
    rows = lax.broadcasted_iota(jnp.int32, (length, length), 0)
    columns = lax.broadcasted_iota(jnp.int32, (length, length), 1)
    return rows >= columns


def shifted(array, axis, by):
    count = lax.axis_size(axis)
    pairs = [(i, i + by) for i in range(count) if 0 <= i + by < count]
    return lax.ppermute(array, axis, pairs)


def state_kernel(key_ref, value_ref, decay_ref, message_ref, cumulative_ref):
    heads, length = decay_ref.shape
    size = key_ref.shape[1] // heads
    ones = lower_ones(length).astype(F32)
    cumulative = lax.dot_general(
        ones, decay_ref[...], (((1,), (1,)), ((), ())), precision=HIGHEST, preferred_element_type=F32
    )
    cumulative_ref[...] = cumulative
    last = cumulative[length - 1 : length, :]
    key_fade = jnp.exp(last - cumulative)
    message_ref[heads * size :, :] = jnp.zeros((message_ref.shape[0] - heads * size, size), BF16)
    half = (message_ref.shape[0] - heads * size) // 2
    rows = []
    for h in range(heads):
        columns = slice(h * size, (h + 1) * size)
        scaled = (key_fade[:, h : h + 1] * key_ref[:, columns].astype(F32)).astype(BF16)
        state = lax.dot_general(
            scaled, value_ref[:, columns], (((0,), (0,)), ((), ())), preferred_element_type=F32
        )
        message_ref[columns, :] = state.astype(BF16)
        rows.append(jnp.broadcast_to(jnp.exp(last[:, h : h + 1]), (1, size)))
    rows.append(jnp.zeros((half - heads, size), F32))
    fade = jnp.concatenate(rows, axis=0)
    leading = fade.astype(BF16)
    trailing = (fade - leading.astype(F32)).astype(BF16)
    message_ref[heads * size :, :] = jnp.concatenate([leading, trailing], axis=0)


def section_state(attn_key, attn_value, log_decay):
    heads, length = log_decay.shape
    width = attn_key.shape[1]
    half = -(-heads // 8) * 8
    return pl.pallas_call(
        state_kernel,
        out_shape=(
            jax.ShapeDtypeStruct((width + 2 * half, width // heads), BF16),
            jax.ShapeDtypeStruct((length, heads), F32),
        ),
        cost_estimate=pl.CostEstimate(
            flops=2 * length * width * (width // heads), bytes_accessed=4 * length * width, transcendentals=0
        ),
        compiler_params=pltpu.CompilerParams(vmem_limit_bytes=VMEM_LIMIT),
    )(in_hbm(attn_key), in_hbm(attn_value), in_hbm(log_decay))


def intra_kernel(query_ref, key_ref, value_ref, decay_ref, cumulative_ref, out_ref):
    heads, length = decay_ref.shape
    size = key_ref.shape[1] // heads
    causal = lower_ones(length)
    along = lax.dot_general(
        decay_ref[...],
        causal.astype(F32),
        (((1,), (1,)), ((), ())),
        precision=HIGHEST,
        preferred_element_type=F32,
    )
    for h in range(heads):
        columns = slice(h * size, (h + 1) * size)
        gap = jnp.where(causal, cumulative_ref[:, h : h + 1] - along[h : h + 1, :], 0.0)
        mask = jnp.where(causal, jnp.exp(gap), 0.0)
        scores = lax.dot_general(
            query_ref[:, columns], key_ref[:, columns], (((1,), (1,)), ((), ())), preferred_element_type=F32
        )
        weights = (scores * mask).astype(BF16)
        out_ref[:, columns] = jnp.dot(weights, value_ref[:, columns], preferred_element_type=F32)


def intra_section(attn_query, attn_key, attn_value, log_decay, cumulative):
    length, width = attn_query.shape
    return pl.pallas_call(
        intra_kernel,
        out_shape=jax.ShapeDtypeStruct((length, width), F32),
        cost_estimate=pl.CostEstimate(
            flops=4 * length * length * width, bytes_accessed=10 * length * width, transcendentals=0
        ),
        compiler_params=pltpu.CompilerParams(vmem_limit_bytes=VMEM_LIMIT),
    )(attn_query, attn_key, attn_value, log_decay, cumulative)


def stream_kernel(
    query_ref, intra_ref, cumulative_ref, incoming_ref, residual_ref, gain_ref, ids_ref, out_ref
):
    heads, size = incoming_ref.shape[0], incoming_ref.shape[1]
    length, width = residual_ref.shape
    choices = ids_ref.shape[0]
    below = jnp.concatenate(
        [
            ids_ref[...].astype(F32),
            jnp.zeros((ID_ROWS - choices, length), F32),
        ],
        axis=0,
    )
    out_ref[length:, :] = jnp.concatenate(
        [below, jnp.zeros((ID_ROWS, width - length), F32)], axis=1
    ).astype(BF16)
    faded = jnp.exp(cumulative_ref[...])
    for h in range(heads):
        columns = slice(h * size, (h + 1) * size)
        state = incoming_ref[h]
        leading = state.astype(BF16)
        trailing = (state - leading.astype(F32)).astype(BF16)
        query = query_ref[:, columns]
        inter = jnp.dot(query, leading, preferred_element_type=F32) + jnp.dot(
            query, trailing, preferred_element_type=F32
        )
        attn_out = intra_ref[:, columns] + faded[:, h : h + 1] * inter
        mean_square = jnp.mean(attn_out * attn_out, axis=1, keepdims=True)
        normed = attn_out * lax.rsqrt(mean_square + 1e-06)
        out_ref[:length, columns] = (
            residual_ref[:, columns].astype(F32) + gain_ref[:, columns].astype(F32) * normed
        ).astype(BF16)


def make_stream(attn_query, intra, cumulative, incoming, residual, norm_gain, ids):
    length, width = attn_query.shape
    return pl.pallas_call(
        stream_kernel,
        out_shape=jax.ShapeDtypeStruct((length + ID_ROWS, width), BF16),
        compiler_params=pltpu.CompilerParams(vmem_limit_bytes=VMEM_LIMIT),
    )(attn_query, intra, cumulative, incoming, residual, norm_gain.reshape(1, width), ids)


def read_message(message, heads):
    size = message.shape[1]
    half = (message.shape[0] - heads * size) // 2
    state = message[: heads * size].astype(F32).reshape(heads, size, size)
    tail = message[heads * size :].astype(F32)
    fade = tail[:heads] + tail[half : half + heads]
    return fade[:, None, :], state


def write_message(fade, state, rows):
    heads, size = state.shape[0], state.shape[1]
    half = (rows - heads * size) // 2
    leading = fade[:, 0, :].astype(BF16)
    trailing = (fade[:, 0, :] - leading.astype(F32)).astype(BF16)
    spare = jnp.zeros((half - heads, size), BF16)
    return jnp.concatenate(
        [state.astype(BF16).reshape(heads * size, size), leading, spare, trailing, spare], axis=0
    )


def incoming_state(message, heads):
    count = lax.axis_size("seq")
    window_fade, window = read_message(message, heads)
    incoming_fade, incoming = None, None
    distance = 1
    while distance < count:
        got_fade, got = read_message(shifted(message, "seq", distance), heads)
        if incoming is None:
            incoming_fade, incoming = got_fade, got
        else:
            incoming, incoming_fade = incoming + incoming_fade * got, incoming_fade * got_fade
        window, window_fade = window + window_fade * got, window_fade * got_fade
        distance *= 2
        if distance < count:
            message = write_message(window_fade, window, message.shape[0])
    return incoming


def select_kernel(capacity, choices, experts, base_ref, *refs):
    parts, (out_ref, place_ref) = refs[:-2], refs[-2:]
    length = parts[0].shape[0] - ID_ROWS
    part = parts[-1][...]
    for other in parts[:-1]:
        part = jnp.where(base_ref[1] > 0, other[...], part)
    before = lower_ones(length).astype(BF16)
    slot = lax.broadcasted_iota(jnp.int32, (capacity, length), 0).astype(F32)
    ids = part[length:, :length].astype(F32)
    rows = []
    for j in range(experts):
        expert = (base_ref[0] + j).astype(F32)
        chosen = ids[0:1, :] == expert
        for choice in range(1, choices):
            chosen = chosen | (ids[choice : choice + 1, :] == expert)
        flag = jnp.where(chosen, 1.0, 0.0)
        rank = lax.dot_general(
            jnp.broadcast_to(flag, (16, length)).astype(BF16),
            before,
            (((1,), (1,)), ((), ())),
            preferred_element_type=F32,
        )[0:1, :]
        rank = jnp.where(chosen, rank - 1.0, -1.0)
        rows.append(jnp.where(slot == rank, 1.0, 0.0).astype(BF16))
    place = jnp.concatenate(rows, axis=0)
    place_ref[...] = place
    out_ref[...] = lax.dot_general(
        part[:length, :], place, (((0,), (1,)), ((), ())), preferred_element_type=F32
    ).astype(BF16)


def select_slots(base, parts, capacity, choices, experts):
    rows, width = parts[0].shape
    length = rows - ID_ROWS
    slots = experts * capacity
    whole = pl.BlockSpec(memory_space=pltpu.VMEM)
    return pl.pallas_call(
        functools.partial(select_kernel, capacity, choices, experts),
        in_specs=[pl.BlockSpec(memory_space=pltpu.SMEM), *([whole] * len(parts))],
        out_shape=(
            jax.ShapeDtypeStruct((width, slots), BF16),
            jax.ShapeDtypeStruct((slots, length), BF16),
        ),
        cost_estimate=pl.CostEstimate(
            flops=2 * slots * length * width, bytes_accessed=4 * slots * width, transcendentals=0
        ),
        compiler_params=pltpu.CompilerParams(vmem_limit_bytes=VMEM_LIMIT),
    )(base, *parts)


def combine_kernel(place_ref, *refs):
    shares, out_ref = refs[:-1], refs[-1]
    total = shares[0][0].astype(F32)
    for share in shares[1:]:
        total = total + share[0].astype(F32)
    out_ref[...] = lax.dot_general(
        place_ref[...], total.astype(BF16), (((0,), (0,)), ((), ())), preferred_element_type=F32
    ).astype(BF16)


def combine_slots(place, shares):
    slots, length = place.shape
    width = shares[0].shape[2]
    first = pl.BlockSpec((1, slots, width), lambda _: (0, 0, 0))
    return pl.pallas_call(
        combine_kernel,
        grid=(1,),
        in_specs=[pl.BlockSpec(memory_space=pltpu.VMEM), *([first] * len(shares))],
        out_shape=jax.ShapeDtypeStruct((length, width), BF16),
        cost_estimate=pl.CostEstimate(
            flops=2 * slots * length * width, bytes_accessed=8 * slots * width, transcendentals=0
        ),
        compiler_params=pltpu.CompilerParams(vmem_limit_bytes=VMEM_LIMIT),
    )(place, *shares)


def gate_kernel(counts, sections, last, plan_ref, *refs):
    step = pl.program_id(0)
    blocks = sum(counts)
    used = len(counts) * sections
    x_refs, refs = refs[:used], refs[used:]
    router_ref, gate_ref, up_ref = refs[:3]
    refs = refs[3:]
    if last:
        gate_in, up_in, score_in, hidden_ref, gate_acc, up_acc, score_acc = refs
    else:
        gate_acc, up_acc, score_acc = refs
    experts = gate_ref.shape[0]
    width = x_refs[0].shape[1]
    slots = gate_acc.shape[2]
    part = slots // sections

    @pl.when(step == 0)
    def _():
        if last:
            gate_acc[...] = gate_in[...]
            up_acc[...] = up_in[...]
            score_acc[...] = score_in[...]
        else:
            gate_acc[...] = jnp.zeros_like(gate_acc)
            up_acc[...] = jnp.zeros_like(up_acc)
            score_acc[...] = jnp.zeros_like(score_acc)

    xs = []
    for section in range(sections):
        mine = x_refs[section * len(counts) : (section + 1) * len(counts)]
        x = mine[-1][0]
        for i in range(len(counts) - 2, -1, -1):
            x = jnp.where(step < sum(counts[: i + 1]), mine[i][0], x)
        xs.append(x)
    for j in range(experts):
        x = jnp.concatenate([x[:, j * part : (j + 1) * part] for x in xs], axis=1)
        score_acc[j] += jnp.dot(router_ref[0], x, preferred_element_type=F32)
        gate_acc[j] += jnp.dot(gate_ref[j], x, preferred_element_type=F32)
        up_acc[j] += jnp.dot(up_ref[j], x, preferred_element_type=F32)

    if last:

        @pl.when(step == blocks - 1)
        def _():
            for j in range(experts):
                score = score_acc[j, j : j + 1, :]
                gate = gate_acc[j]
                routed = gate / (1.0 + jnp.exp(-gate)) * up_acc[j]
                routed = routed / (1.0 + jnp.exp(-score))
                hidden_ref[j] = routed.T.astype(BF16)


def gate_part(plan, xs, router_rows, gate_rows, up_rows, sums=None):
    counts = tuple(x.shape[0] for x in xs[0])
    blocks = sum(counts)
    _, width, total = xs[0][0].shape
    experts, units, _ = gate_rows.shape
    slots = total // experts * len(xs)
    whole = pl.BlockSpec(memory_space=pltpu.VMEM)
    last = sums is not None

    def x_spec(i):
        before = sum(counts[:i])
        return pl.BlockSpec(
            (1, width, total), lambda p, plan: (jnp.clip(p - before, 0, counts[i] - 1), 0, 0)
        )

    weight_spec = pl.BlockSpec((experts, units, width), lambda p, plan: (0, 0, plan[p]))
    sum_shapes = [(experts, units, slots), (experts, units, slots), (experts, experts, slots)]
    sum_specs = [pl.BlockSpec(shape, lambda p, plan: (0, 0, 0)) for shape in sum_shapes]
    if last:
        out_shape = jax.ShapeDtypeStruct((experts, slots, units), BF16)
        out_specs = whole
        scratch = [pltpu.VMEM(shape, F32) for shape in sum_shapes]
    else:
        out_shape = tuple(jax.ShapeDtypeStruct(shape, F32) for shape in sum_shapes)
        out_specs = tuple(sum_specs)
        scratch = []
    return pl.pallas_call(
        functools.partial(gate_kernel, counts, len(xs), last),
        grid_spec=pltpu.PrefetchScalarGridSpec(
            num_scalar_prefetch=1,
            grid=(blocks,),
            in_specs=[
                *[x_spec(i) for _ in xs for i in range(len(counts))],
                pl.BlockSpec((1, experts, width), lambda p, plan: (plan[p], 0, 0)),
                weight_spec,
                weight_spec,
                *(sum_specs if last else []),
            ],
            out_specs=out_specs,
            scratch_shapes=scratch,
        ),
        out_shape=out_shape,
        cost_estimate=pl.CostEstimate(
            flops=4 * experts * slots * blocks * width * units,
            bytes_accessed=4 * experts * blocks * width * units,
            transcendentals=0,
        ),
        compiler_params=pltpu.CompilerParams(vmem_limit_bytes=VMEM_LIMIT),
    )(
        plan,
        *[x for section in xs for x in section],
        router_rows,
        in_hbm(gate_rows),
        in_hbm(up_rows),
        *(sums or ()),
    )


def down_kernel(blocks, sections, plan_ref, hidden_ref, down_ref, *out_refs):
    experts, slots, _ = hidden_ref.shape
    part = slots // sections
    turn = pl.program_id(0) // blocks
    for j in range(experts):
        share = jnp.dot(hidden_ref[j], down_ref[j], preferred_element_type=F32).astype(BF16)
        for i in range(len(out_refs) // sections):

            @pl.when(turn == i)
            def _():
                for section in range(sections):
                    out_ref = out_refs[i * sections + section]
                    out_ref[0, j * part : (j + 1) * part, :] = share[
                        section * part : (section + 1) * part
                    ]


def down_part(plans, hidden, down_weight, width, sections):
    blocks = plans[0].shape[0]
    experts, slots, units = hidden.shape
    rows = experts * slots // sections

    def out_spec(i):
        return pl.BlockSpec(
            (1, rows, width), lambda p, plan: (jnp.clip(p - i * blocks, 0, blocks - 1), 0, 0)
        )

    out = pl.pallas_call(
        functools.partial(down_kernel, blocks, sections),
        grid_spec=pltpu.PrefetchScalarGridSpec(
            num_scalar_prefetch=1,
            grid=(len(plans) * blocks,),
            in_specs=[
                pl.BlockSpec(memory_space=pltpu.VMEM),
                pl.BlockSpec((experts, units, width), lambda p, plan: (0, 0, plan[p])),
            ],
            out_specs=[out_spec(i) for i in range(len(plans)) for _ in range(sections)],
        ),
        out_shape=[jax.ShapeDtypeStruct((blocks, rows, width), BF16)] * (len(plans) * sections),
        cost_estimate=pl.CostEstimate(
            flops=2 * experts * slots * len(plans) * blocks * width * units,
            bytes_accessed=2 * experts * len(plans) * blocks * width * units,
            transcendentals=0,
        ),
        compiler_params=pltpu.CompilerParams(vmem_limit_bytes=VMEM_LIMIT),
    )(jnp.concatenate(plans), hidden, in_hbm(down_weight))
    return [out[i * sections : (i + 1) * sections] for i in range(len(plans))]


def added(left, right):
    return (left.astype(F32) + right.astype(F32)).astype(BF16)


def swapped(array, axis, even, odd):
    count = lax.axis_size(axis)
    pairs = [(i, i ^ (odd if i % 2 else even)) for i in range(count)]
    return lax.ppermute(array, axis, pairs)


class PairedPlane:
    def __init__(self):
        me = lax.axis_index("exp").astype(jnp.int32)
        other = me ^ 1
        near = jnp.where(me % 2 == 0, 2, 4)
        far = 6 - near
        self.early = jnp.stack([me, me ^ near, other, other ^ far])
        self.late = jnp.stack([me ^ far, me ^ 6, other ^ near, other ^ 6])
        self.mine = jnp.stack([me, me ^ near, me ^ far, me ^ 6])
        self.theirs = jnp.stack([other, other ^ far, other ^ near, other ^ 6])

    def once(self, part):
        return swapped(part, "exp", 2, 4)

    def first(self, part):
        return jnp.stack([part, self.once(part)])

    def second(self, two):
        return swapped(two, "exp", 4, 2)

    def across(self, two):
        return swapped(two, "exp", 1, 1)

def on_device(
    attn_query,
    attn_key,
    attn_value,
    log_decay,
    residual,
    norm_gain,
    expert_ids,
    router_weight,
    gate_weight,
    up_weight,
    down_weight,
):
    heads_here, length = log_decay.shape
    groups = lax.axis_size("seq")
    shares = lax.axis_size("exp")
    width = attn_query.shape[1]
    experts_here = router_weight.shape[1]
    section = lax.axis_index("seq")
    inner = (section > 0) & (section < groups - 1)
    base = jnp.stack([section * experts_here, inner]).astype(jnp.int32)
    router_rows = router_weight.reshape(shares, width, experts_here).transpose(0, 2, 1)
    gate_rows = gate_weight.swapaxes(1, 2)
    up_rows = up_weight.swapaxes(1, 2)

    message, cumulative = section_state(attn_key, attn_value, log_decay)
    intra = intra_section(attn_query, attn_key, attn_value, log_decay, cumulative)
    incoming = incoming_state(message, heads_here)
    stream = make_stream(
        attn_query, intra, cumulative, incoming, residual, norm_gain, expert_ids.T
    )

    capacity = 4 * length // (experts_here * groups)
    choices = expert_ids.shape[1]

    def select(*parts):
        return select_slots(base, parts, capacity, choices, experts_here)

    weights = (router_rows, gate_rows, up_rows)
    if shares == 8 and groups == 4:
        pieces = paired_chunks(stream, select, weights, down_weight)
    else:
        order = jnp.arange(shares, dtype=jnp.int32)
        middle = shares // 2
        pieces = []
        for first in range(0, groups, 2):
            chunk = (first, first + 1)
            chosen = [
                select(swapped(stream, "seq", offset, offset) if offset else stream)
                for offset in chunk
            ]
            gathered = [lax.all_gather(slots, "exp", axis=0) for slots, _ in chosen]
            sums = gate_part(order[:middle], [[x[:middle]] for x in gathered], *weights)
            hidden = gate_part(order[middle:], [[x[middle:]] for x in gathered], *weights, sums)
            (partial,) = down_part([order], hidden, down_weight, width, len(chunk))
            for offset, share, (_, place) in zip(chunk, partial, chosen):
                share = lax.psum_scatter(share, "exp", scatter_dimension=0)
                piece = combine_slots(place, [share[None]])
                pieces.append(swapped(piece, "seq", offset, offset) if offset else piece)
    total = stream[:length].astype(F32)
    for piece in pieces:
        total = total + piece.astype(F32)
    return total.astype(BF16)


def paired_chunks(stream, select, weights, down_weight):
    plane = PairedPlane()
    width = stream.shape[1]
    tie = lax.optimization_barrier
    two, far_two, near, near_far, chosen = {}, {}, {}, {}, {}

    def across_middle(part):
        return lax.ppermute(part, "seq", [(1, 2), (2, 1)])

    def outward(part):
        return lax.ppermute(part, "seq", [(1, 0), (2, 3)])

    def gather(name, behind):
        two[name], _ = tie((plane.first(chosen[name][0]), behind))
        near[name] = plane.across(two[name])
        far_two[name] = plane.second(two[name])

    swap = swapped(stream, "seq", 1, 1)
    crossed = across_middle(stream)
    chosen["own"] = select(stream)
    gather("own", [])
    passed = outward(crossed)
    crossed_swap = across_middle(swap)
    chosen["neighbour"] = select(swap)
    gather("neighbour", [passed, crossed_swap])
    passed_swap = outward(crossed_swap)
    chosen["third"] = select(crossed, passed)

    def gate(chunk, behind):
        early = [[two[name], near[name]] for name in chunk]
        return gate_part(plane.early, tie((early, behind))[0], *weights)

    def gate_last(chunk, sums, behind):
        late = [[far_two[name], near_far[name]] for name in chunk]
        (late, sums), _ = tie(((late, sums), behind))
        return gate_part(plane.late, late, *weights, sums)

    def down(plans, hidden, behind):
        hidden, _ = tie((hidden, behind))
        return down_part(plans, hidden, down_weight, width, 2)

    class Scatter:
        def __init__(self, name, theirs, mine):
            self.name, self.theirs, self.mine = name, theirs, mine

        def two_blocks(self, behind):
            self.near = plane.across(self.theirs)
            self.sent = added(self.mine[2:], self.near[2:])
            self.got_two = plane.second(tie((self.sent, behind))[0])

        def one_block(self, behind):
            got_two, _ = tie((self.got_two, behind))
            self.one = added(added(self.mine[1], self.near[1]), got_two[1])
            self.got_one = plane.once(self.one)

        def own_block(self, behind):
            got_one, _ = tie((self.got_one, behind))
            shares = [self.mine, self.near, self.got_two, got_one[None]]
            return combine_slots(chosen[self.name][1], shares)

    chunk = ("neighbour", "own")
    gather("third", [])
    sums = gate(chunk, two["third"])
    for name in chunk:
        near_far[name] = plane.across(tie((far_two[name], sums))[0])
    chosen["fourth"] = select(crossed_swap, passed_swap)
    hidden = gate_last(chunk, sums, [far_two["third"], chosen["fourth"]])
    gather("fourth", hidden)
    theirs, mine = down([plane.theirs, plane.mine], hidden, two["fourth"])
    theirs, _ = tie((theirs, far_two["fourth"]))
    neighbour, own = (Scatter(*shares) for shares in zip(chunk, theirs, mine))
    neighbour.two_blocks([])

    chunk = ("third", "fourth")
    sums = gate(chunk, neighbour.sent)
    for name in chunk:
        near_far[name] = plane.across(tie((far_two[name], neighbour.sent))[0])
    neighbour.one_block(sums)
    own.two_blocks(neighbour.one)
    hidden = gate_last(chunk, sums, [neighbour.one, own.sent])
    neighbour_piece = neighbour.own_block(hidden)
    own.one_block(hidden)
    neighbour_home = swapped(neighbour_piece, "seq", 1, 1)
    theirs, mine = down([plane.theirs, plane.mine], hidden, [neighbour_piece, own.one])
    own_piece = own.own_block([])
    theirs, _ = tie((theirs, [neighbour_home, own_piece]))
    third, fourth = (Scatter(*shares) for shares in zip(chunk, theirs, mine))
    third.two_blocks([])
    third.one_block([])
    fourth.two_blocks(third.got_two)
    fourth.one_block([])
    third_piece = third.own_block([])
    fourth_piece = fourth.own_block([])
    return [
        own_piece,
        neighbour_home,
        lax.ppermute(third_piece, "seq", [(1, 2), (2, 1)]),
        lax.ppermute(third_piece, "seq", [(0, 2), (3, 1)]),
        lax.ppermute(fourth_piece, "seq", [(1, 3), (2, 0)]),
        lax.ppermute(fourth_piece, "seq", [(0, 3), (3, 0)]),
    ]


def solution(mesh):
    in_specs = (
        P("seq", "exp"),
        P("seq", "exp"),
        P("seq", "exp"),
        P("exp", "seq"),
        P("seq", "exp"),
        P("exp"),
        P("seq", None),
        P(None, "seq"),
        P("seq", None, "exp"),
        P("seq", None, "exp"),
        P("seq", "exp", None),
    )
    out_specs = P("seq", "exp")
    return jax.shard_map(
        on_device, mesh=mesh, in_specs=in_specs, out_specs=out_specs, check_vma=False
    )
```

```python
import functools

import jax
import jax.numpy as jnp
from jax import lax
from jax.experimental import pallas as pl
from jax.experimental.pallas import tpu as pltpu
from jax.sharding import PartitionSpec as P

F32 = jnp.float32
BF16 = jnp.bfloat16
HIGHEST = lax.Precision.HIGHEST
VMEM_LIMIT = 32 * 1024 * 1024
ID_ROWS = 16


def in_hbm(array):
    return pltpu.with_memory_space_constraint(array, pltpu.HBM)


def lower_ones(length):
    rows = lax.broadcasted_iota(jnp.int32, (length, length), 0)
    columns = lax.broadcasted_iota(jnp.int32, (length, length), 1)
    return rows >= columns


def shifted(array, axis, by):
    count = lax.axis_size(axis)
    pairs = [(i, i + by) for i in range(count) if 0 <= i + by < count]
    return lax.ppermute(array, axis, pairs)


def state_kernel(key_ref, value_ref, decay_ref, message_ref, cumulative_ref):
    heads, length = decay_ref.shape
    size = key_ref.shape[1] // heads
    ones = lower_ones(length).astype(F32)
    cumulative = lax.dot_general(
        ones, decay_ref[...], (((1,), (1,)), ((), ())), precision=HIGHEST, preferred_element_type=F32
    )
    cumulative_ref[...] = cumulative
    last = cumulative[length - 1 : length, :]
    key_fade = jnp.exp(last - cumulative)
    message_ref[heads * size :, :] = jnp.zeros((message_ref.shape[0] - heads * size, size), BF16)
    half = (message_ref.shape[0] - heads * size) // 2
    rows = []
    for h in range(heads):
        columns = slice(h * size, (h + 1) * size)
        scaled = (key_fade[:, h : h + 1] * key_ref[:, columns].astype(F32)).astype(BF16)
        state = lax.dot_general(
            scaled, value_ref[:, columns], (((0,), (0,)), ((), ())), preferred_element_type=F32
        )
        message_ref[columns, :] = state.astype(BF16)
        rows.append(jnp.broadcast_to(jnp.exp(last[:, h : h + 1]), (1, size)))
    rows.append(jnp.zeros((half - heads, size), F32))
    fade = jnp.concatenate(rows, axis=0)
    leading = fade.astype(BF16)
    trailing = (fade - leading.astype(F32)).astype(BF16)
    message_ref[heads * size :, :] = jnp.concatenate([leading, trailing], axis=0)


def section_state(attn_key, attn_value, log_decay):
    heads, length = log_decay.shape
    width = attn_key.shape[1]
    half = -(-heads // 8) * 8
    return pl.pallas_call(
        state_kernel,
        out_shape=(
            jax.ShapeDtypeStruct((width + 2 * half, width // heads), BF16),
            jax.ShapeDtypeStruct((length, heads), F32),
        ),
        cost_estimate=pl.CostEstimate(
            flops=2 * length * width * (width // heads), bytes_accessed=4 * length * width, transcendentals=0
        ),
        compiler_params=pltpu.CompilerParams(vmem_limit_bytes=VMEM_LIMIT),
    )(in_hbm(attn_key), in_hbm(attn_value), in_hbm(log_decay))


def intra_kernel(query_ref, key_ref, value_ref, decay_ref, cumulative_ref, out_ref):
    heads, length = decay_ref.shape
    size = key_ref.shape[1] // heads
    causal = lower_ones(length)
    along = lax.dot_general(
        decay_ref[...],
        causal.astype(F32),
        (((1,), (1,)), ((), ())),
        precision=HIGHEST,
        preferred_element_type=F32,
    )
    for h in range(heads):
        columns = slice(h * size, (h + 1) * size)
        gap = jnp.where(causal, cumulative_ref[:, h : h + 1] - along[h : h + 1, :], 0.0)
        mask = jnp.where(causal, jnp.exp(gap), 0.0)
        scores = lax.dot_general(
            query_ref[:, columns], key_ref[:, columns], (((1,), (1,)), ((), ())), preferred_element_type=F32
        )
        weights = (scores * mask).astype(BF16)
        out_ref[:, columns] = jnp.dot(weights, value_ref[:, columns], preferred_element_type=F32)


def intra_section(attn_query, attn_key, attn_value, log_decay, cumulative):
    length, width = attn_query.shape
    return pl.pallas_call(
        intra_kernel,
        out_shape=jax.ShapeDtypeStruct((length, width), F32),
        cost_estimate=pl.CostEstimate(
            flops=4 * length * length * width, bytes_accessed=10 * length * width, transcendentals=0
        ),
        compiler_params=pltpu.CompilerParams(vmem_limit_bytes=VMEM_LIMIT),
    )(attn_query, attn_key, attn_value, log_decay, cumulative)


def stream_kernel(
    query_ref, intra_ref, cumulative_ref, incoming_ref, residual_ref, gain_ref, ids_ref, out_ref
):
    heads, size = incoming_ref.shape[0], incoming_ref.shape[1]
    length, width = residual_ref.shape
    choices = ids_ref.shape[0]
    below = jnp.concatenate(
        [
            ids_ref[...].astype(F32),
            jnp.zeros((ID_ROWS - choices, length), F32),
        ],
        axis=0,
    )
    out_ref[length:, :] = jnp.concatenate(
        [below, jnp.zeros((ID_ROWS, width - length), F32)], axis=1
    ).astype(BF16)
    faded = jnp.exp(cumulative_ref[...])
    for h in range(heads):
        columns = slice(h * size, (h + 1) * size)
        state = incoming_ref[h]
        leading = state.astype(BF16)
        trailing = (state - leading.astype(F32)).astype(BF16)
        query = query_ref[:, columns]
        inter = jnp.dot(query, leading, preferred_element_type=F32) + jnp.dot(
            query, trailing, preferred_element_type=F32
        )
        attn_out = intra_ref[:, columns] + faded[:, h : h + 1] * inter
        mean_square = jnp.mean(attn_out * attn_out, axis=1, keepdims=True)
        normed = attn_out * lax.rsqrt(mean_square + 1e-06)
        out_ref[:length, columns] = (
            residual_ref[:, columns].astype(F32) + gain_ref[:, columns].astype(F32) * normed
        ).astype(BF16)


def make_stream(attn_query, intra, cumulative, incoming, residual, norm_gain, ids):
    length, width = attn_query.shape
    return pl.pallas_call(
        stream_kernel,
        out_shape=jax.ShapeDtypeStruct((length + ID_ROWS, width), BF16),
        compiler_params=pltpu.CompilerParams(vmem_limit_bytes=VMEM_LIMIT),
    )(attn_query, intra, cumulative, incoming, residual, norm_gain.reshape(1, width), ids)


def read_message(message, heads):
    size = message.shape[1]
    half = (message.shape[0] - heads * size) // 2
    state = message[: heads * size].astype(F32).reshape(heads, size, size)
    tail = message[heads * size :].astype(F32)
    fade = tail[:heads] + tail[half : half + heads]
    return fade[:, None, :], state


def write_message(fade, state, rows):
    heads, size = state.shape[0], state.shape[1]
    half = (rows - heads * size) // 2
    leading = fade[:, 0, :].astype(BF16)
    trailing = (fade[:, 0, :] - leading.astype(F32)).astype(BF16)
    spare = jnp.zeros((half - heads, size), BF16)
    return jnp.concatenate(
        [state.astype(BF16).reshape(heads * size, size), leading, spare, trailing, spare], axis=0
    )


def incoming_state(message, heads):
    count = lax.axis_size("seq")
    window_fade, window = read_message(message, heads)
    incoming_fade, incoming = None, None
    distance = 1
    while distance < count:
        got_fade, got = read_message(shifted(message, "seq", distance), heads)
        if incoming is None:
            incoming_fade, incoming = got_fade, got
        else:
            incoming, incoming_fade = incoming + incoming_fade * got, incoming_fade * got_fade
        window, window_fade = window + window_fade * got, window_fade * got_fade
        distance *= 2
        if distance < count:
            message = write_message(window_fade, window, message.shape[0])
    return incoming


def select_kernel(capacity, choices, experts, base_ref, *refs):
    parts, (out_ref, place_ref) = refs[:-2], refs[-2:]
    length = parts[0].shape[0] - ID_ROWS
    part = parts[-1][...]
    for other in parts[:-1]:
        part = jnp.where(base_ref[1] > 0, other[...], part)
    before = lower_ones(length).astype(BF16)
    slot = lax.broadcasted_iota(jnp.int32, (capacity, length), 0).astype(F32)
    ids = part[length:, :length].astype(F32)
    rows = []
    for j in range(experts):
        expert = (base_ref[0] + j).astype(F32)
        chosen = ids[0:1, :] == expert
        for choice in range(1, choices):
            chosen = chosen | (ids[choice : choice + 1, :] == expert)
        flag = jnp.where(chosen, 1.0, 0.0)
        rank = lax.dot_general(
            jnp.broadcast_to(flag, (16, length)).astype(BF16),
            before,
            (((1,), (1,)), ((), ())),
            preferred_element_type=F32,
        )[0:1, :]
        rank = jnp.where(chosen, rank - 1.0, -1.0)
        rows.append(jnp.where(slot == rank, 1.0, 0.0).astype(BF16))
    place = jnp.concatenate(rows, axis=0)
    place_ref[...] = place
    out_ref[...] = lax.dot_general(
        part[:length, :], place, (((0,), (1,)), ((), ())), preferred_element_type=F32
    ).astype(BF16)


def select_slots(base, parts, capacity, choices, experts):
    rows, width = parts[0].shape
    length = rows - ID_ROWS
    slots = experts * capacity
    whole = pl.BlockSpec(memory_space=pltpu.VMEM)
    return pl.pallas_call(
        functools.partial(select_kernel, capacity, choices, experts),
        in_specs=[pl.BlockSpec(memory_space=pltpu.SMEM), *([whole] * len(parts))],
        out_shape=(
            jax.ShapeDtypeStruct((width, slots), BF16),
            jax.ShapeDtypeStruct((slots, length), BF16),
        ),
        cost_estimate=pl.CostEstimate(
            flops=2 * slots * length * width, bytes_accessed=4 * slots * width, transcendentals=0
        ),
        compiler_params=pltpu.CompilerParams(vmem_limit_bytes=VMEM_LIMIT),
    )(base, *parts)


def combine_kernel(place_ref, *refs):
    shares, out_ref = refs[:-1], refs[-1]
    total = shares[0][0].astype(F32)
    for share in shares[1:]:
        total = total + share[0].astype(F32)
    out_ref[...] = lax.dot_general(
        place_ref[...], total.astype(BF16), (((0,), (0,)), ((), ())), preferred_element_type=F32
    ).astype(BF16)


def combine_slots(place, shares):
    slots, length = place.shape
    width = shares[0].shape[2]
    first = pl.BlockSpec((1, slots, width), lambda _: (0, 0, 0))
    return pl.pallas_call(
        combine_kernel,
        grid=(1,),
        in_specs=[pl.BlockSpec(memory_space=pltpu.VMEM), *([first] * len(shares))],
        out_shape=jax.ShapeDtypeStruct((length, width), BF16),
        cost_estimate=pl.CostEstimate(
            flops=2 * slots * length * width, bytes_accessed=8 * slots * width, transcendentals=0
        ),
        compiler_params=pltpu.CompilerParams(vmem_limit_bytes=VMEM_LIMIT),
    )(place, *shares)


def gate_kernel(counts, sections, last, plan_ref, *refs):
    step = pl.program_id(0)
    blocks = sum(counts)
    used = len(counts) * sections
    x_refs, refs = refs[:used], refs[used:]
    router_ref, gate_ref, up_ref = refs[:3]
    refs = refs[3:]
    if last:
        gate_in, up_in, score_in, hidden_ref, gate_acc, up_acc, score_acc = refs
    else:
        gate_acc, up_acc, score_acc = refs
    experts = gate_ref.shape[0]
    width = x_refs[0].shape[1]
    slots = gate_acc.shape[2]
    part = slots // sections

    @pl.when(step == 0)
    def _():
        if last:
            gate_acc[...] = gate_in[...]
            up_acc[...] = up_in[...]
            score_acc[...] = score_in[...]
        else:
            gate_acc[...] = jnp.zeros_like(gate_acc)
            up_acc[...] = jnp.zeros_like(up_acc)
            score_acc[...] = jnp.zeros_like(score_acc)

    xs = []
    for section in range(sections):
        mine = x_refs[section * len(counts) : (section + 1) * len(counts)]
        x = mine[-1][0]
        for i in range(len(counts) - 2, -1, -1):
            x = jnp.where(step < sum(counts[: i + 1]), mine[i][0], x)
        xs.append(x)
    for j in range(experts):
        x = jnp.concatenate([x[:, j * part : (j + 1) * part] for x in xs], axis=1)
        score_acc[j] += jnp.dot(router_ref[0], x, preferred_element_type=F32)
        gate_acc[j] += jnp.dot(gate_ref[j], x, preferred_element_type=F32)
        up_acc[j] += jnp.dot(up_ref[j], x, preferred_element_type=F32)

    if last:

        @pl.when(step == blocks - 1)
        def _():
            for j in range(experts):
                score = score_acc[j, j : j + 1, :]
                gate = gate_acc[j]
                routed = gate / (1.0 + jnp.exp(-gate)) * up_acc[j]
                routed = routed / (1.0 + jnp.exp(-score))
                hidden_ref[j] = routed.T.astype(BF16)


def gate_part(plan, xs, router_rows, gate_rows, up_rows, sums=None):
    counts = tuple(x.shape[0] for x in xs[0])
    blocks = sum(counts)
    _, width, total = xs[0][0].shape
    experts, units, _ = gate_rows.shape
    slots = total // experts * len(xs)
    whole = pl.BlockSpec(memory_space=pltpu.VMEM)
    last = sums is not None

    def x_spec(i):
        before = sum(counts[:i])
        return pl.BlockSpec(
            (1, width, total), lambda p, plan: (jnp.clip(p - before, 0, counts[i] - 1), 0, 0)
        )

    weight_spec = pl.BlockSpec((experts, units, width), lambda p, plan: (0, 0, plan[p]))
    sum_shapes = [(experts, units, slots), (experts, units, slots), (experts, experts, slots)]
    sum_specs = [pl.BlockSpec(shape, lambda p, plan: (0, 0, 0)) for shape in sum_shapes]
    if last:
        out_shape = jax.ShapeDtypeStruct((experts, slots, units), BF16)
        out_specs = whole
        scratch = [pltpu.VMEM(shape, F32) for shape in sum_shapes]
    else:
        out_shape = tuple(jax.ShapeDtypeStruct(shape, F32) for shape in sum_shapes)
        out_specs = tuple(sum_specs)
        scratch = []
    return pl.pallas_call(
        functools.partial(gate_kernel, counts, len(xs), last),
        grid_spec=pltpu.PrefetchScalarGridSpec(
            num_scalar_prefetch=1,
            grid=(blocks,),
            in_specs=[
                *[x_spec(i) for _ in xs for i in range(len(counts))],
                pl.BlockSpec((1, experts, width), lambda p, plan: (plan[p], 0, 0)),
                weight_spec,
                weight_spec,
                *(sum_specs if last else []),
            ],
            out_specs=out_specs,
            scratch_shapes=scratch,
        ),
        out_shape=out_shape,
        cost_estimate=pl.CostEstimate(
            flops=4 * experts * slots * blocks * width * units,
            bytes_accessed=4 * experts * blocks * width * units,
            transcendentals=0,
        ),
        compiler_params=pltpu.CompilerParams(vmem_limit_bytes=VMEM_LIMIT),
    )(
        plan,
        *[x for section in xs for x in section],
        router_rows,
        in_hbm(gate_rows),
        in_hbm(up_rows),
        *(sums or ()),
    )


def down_kernel(blocks, sections, plan_ref, hidden_ref, down_ref, *out_refs):
    experts, slots, _ = hidden_ref.shape
    part = slots // sections
    turn = pl.program_id(0) // blocks
    for j in range(experts):
        share = jnp.dot(hidden_ref[j], down_ref[j], preferred_element_type=F32).astype(BF16)
        for i in range(len(out_refs) // sections):

            @pl.when(turn == i)
            def _():
                for section in range(sections):
                    out_ref = out_refs[i * sections + section]
                    out_ref[0, j * part : (j + 1) * part, :] = share[
                        section * part : (section + 1) * part
                    ]


def down_part(plans, hidden, down_weight, width, sections):
    blocks = plans[0].shape[0]
    experts, slots, units = hidden.shape
    rows = experts * slots // sections

    def out_spec(i):
        return pl.BlockSpec(
            (1, rows, width), lambda p, plan: (jnp.clip(p - i * blocks, 0, blocks - 1), 0, 0)
        )

    out = pl.pallas_call(
        functools.partial(down_kernel, blocks, sections),
        grid_spec=pltpu.PrefetchScalarGridSpec(
            num_scalar_prefetch=1,
            grid=(len(plans) * blocks,),
            in_specs=[
                pl.BlockSpec(memory_space=pltpu.VMEM),
                pl.BlockSpec((experts, units, width), lambda p, plan: (0, 0, plan[p])),
            ],
            out_specs=[out_spec(i) for i in range(len(plans)) for _ in range(sections)],
        ),
        out_shape=[jax.ShapeDtypeStruct((blocks, rows, width), BF16)] * (len(plans) * sections),
        cost_estimate=pl.CostEstimate(
            flops=2 * experts * slots * len(plans) * blocks * width * units,
            bytes_accessed=2 * experts * len(plans) * blocks * width * units,
            transcendentals=0,
        ),
        compiler_params=pltpu.CompilerParams(vmem_limit_bytes=VMEM_LIMIT),
    )(jnp.concatenate(plans), hidden, in_hbm(down_weight))
    return [out[i * sections : (i + 1) * sections] for i in range(len(plans))]


def added(left, right):
    return (left.astype(F32) + right.astype(F32)).astype(BF16)


def swapped(array, axis, even, odd):
    count = lax.axis_size(axis)
    pairs = [(i, i ^ (odd if i % 2 else even)) for i in range(count)]
    return lax.ppermute(array, axis, pairs)


class PairedPlane:
    def __init__(self):
        me = lax.axis_index("exp").astype(jnp.int32)
        other = me ^ 1
        near = jnp.where(me % 2 == 0, 2, 4)
        far = 6 - near
        self.early = jnp.stack([me, me ^ near, other, other ^ far])
        self.late = jnp.stack([me ^ far, me ^ 6, other ^ near, other ^ 6])
        self.mine = jnp.stack([me, me ^ near, me ^ far, me ^ 6])
        self.theirs = jnp.stack([other, other ^ far, other ^ near, other ^ 6])

    def once(self, part):
        return swapped(part, "exp", 2, 4)

    def first(self, part):
        return jnp.stack([part, self.once(part)])

    def second(self, two):
        return swapped(two, "exp", 4, 2)

    def across(self, two):
        return swapped(two, "exp", 1, 1)

def on_device(
    attn_query,
    attn_key,
    attn_value,
    log_decay,
    residual,
    norm_gain,
    expert_ids,
    router_weight,
    gate_weight,
    up_weight,
    down_weight,
):
    heads_here, length = log_decay.shape
    groups = lax.axis_size("seq")
    shares = lax.axis_size("exp")
    width = attn_query.shape[1]
    experts_here = router_weight.shape[1]
    section = lax.axis_index("seq")
    inner = (section > 0) & (section < groups - 1)
    base = jnp.stack([section * experts_here, inner]).astype(jnp.int32)
    router_rows = router_weight.reshape(shares, width, experts_here).transpose(0, 2, 1)
    gate_rows = gate_weight.swapaxes(1, 2)
    up_rows = up_weight.swapaxes(1, 2)

    message, cumulative = section_state(attn_key, attn_value, log_decay)
    intra = intra_section(attn_query, attn_key, attn_value, log_decay, cumulative)
    incoming = incoming_state(message, heads_here)
    stream = make_stream(
        attn_query, intra, cumulative, incoming, residual, norm_gain, expert_ids.T
    )

    capacity = 4 * length // (experts_here * groups)
    choices = expert_ids.shape[1]

    def select(*parts):
        return select_slots(base, parts, capacity, choices, experts_here)

    weights = (router_rows, gate_rows, up_rows)
    if shares == 8 and groups == 4:
        pieces = paired_chunks(stream, select, weights, down_weight)
    else:
        order = jnp.arange(shares, dtype=jnp.int32)
        middle = shares // 2
        pieces = []
        for first in range(0, groups, 2):
            chunk = (first, first + 1)
            chosen = [
                select(swapped(stream, "seq", offset, offset) if offset else stream)
                for offset in chunk
            ]
            gathered = [lax.all_gather(slots, "exp", axis=0) for slots, _ in chosen]
            sums = gate_part(order[:middle], [[x[:middle]] for x in gathered], *weights)
            hidden = gate_part(order[middle:], [[x[middle:]] for x in gathered], *weights, sums)
            (partial,) = down_part([order], hidden, down_weight, width, len(chunk))
            for offset, share, (_, place) in zip(chunk, partial, chosen):
                share = lax.psum_scatter(share, "exp", scatter_dimension=0)
                piece = combine_slots(place, [share[None]])
                pieces.append(swapped(piece, "seq", offset, offset) if offset else piece)
    total = stream[:length].astype(F32)
    for piece in pieces:
        total = total + piece.astype(F32)
    return total.astype(BF16)


def paired_chunks(stream, select, weights, down_weight):
    plane = PairedPlane()
    width = stream.shape[1]
    tie = lax.optimization_barrier
    two, far_two, near, near_far, chosen = {}, {}, {}, {}, {}

    def across_middle(part):
        return lax.ppermute(part, "seq", [(1, 2), (2, 1)])

    def outward(part):
        return lax.ppermute(part, "seq", [(1, 0), (2, 3)])

    def gather(name, behind):
        two[name], _ = tie((plane.first(chosen[name][0]), behind))
        near[name] = plane.across(two[name])
        far_two[name] = plane.second(two[name])

    swap = swapped(stream, "seq", 1, 1)
    crossed = across_middle(stream)
    chosen["own"] = select(stream)
    gather("own", [])
    passed = outward(crossed)
    crossed_swap = across_middle(swap)
    chosen["neighbour"] = select(swap)
    gather("neighbour", [passed, crossed_swap, far_two["own"]])
    passed_fourth = outward(crossed_swap)
    chosen["third"] = select(crossed, passed)
    gather("third", [passed_fourth, far_two["neighbour"]])
    chosen["fourth"] = select(crossed_swap, passed_fourth)

    def gate(chunk, behind):
        early = [[two[name], near[name]] for name in chunk]
        return gate_part(plane.early, tie((early, behind))[0], *weights)

    def gate_last(chunk, sums, behind):
        late = [[far_two[name], near_far[name]] for name in chunk]
        (late, sums), _ = tie(((late, sums), behind))
        return gate_part(plane.late, late, *weights, sums)

    def down(plans, hidden, behind):
        hidden, _ = tie((hidden, behind))
        return down_part(plans, hidden, down_weight, width, 2)

    class Scatter:
        def __init__(self, name, theirs, mine):
            self.name, self.theirs, self.mine = name, theirs, mine

        def two_blocks(self, behind):
            self.near = plane.across(self.theirs)
            self.sent = added(self.mine[2:], self.near[2:])
            self.got_two = plane.second(tie((self.sent, behind))[0])

        def one_block(self, behind):
            got_two, _ = tie((self.got_two, behind))
            self.one = added(added(self.mine[1], self.near[1]), got_two[1])
            self.got_one = plane.once(self.one)

        def own_block(self, behind):
            got_one, _ = tie((self.got_one, behind))
            shares = [self.mine, self.near, self.got_two, got_one[None]]
            return combine_slots(chosen[self.name][1], shares)

    chunk = ("third", "neighbour")
    sums = gate(chunk, chosen["fourth"])
    gather("fourth", sums)
    for name in chunk:
        near_far[name] = plane.across(tie((far_two[name], sums))[0])
    hidden = gate_last(chunk, sums, two["fourth"])
    (theirs,) = down([plane.theirs], hidden, far_two["fourth"])
    (mine,) = down([plane.mine], hidden, theirs)
    third, neighbour = (Scatter(*shares) for shares in zip(chunk, theirs, mine))
    third.two_blocks([])

    chunk = ("fourth", "own")
    sums = gate(chunk, third.sent)
    for name in chunk:
        near_far[name] = plane.across(tie((far_two[name], third.sent))[0])
    third.one_block(sums)
    neighbour.two_blocks(third.one)
    hidden = gate_last(chunk, sums, [third.one, neighbour.sent])
    third_piece = third.own_block(hidden)
    third_home = lax.ppermute(third_piece, "seq", [(1, 2), (2, 1)])
    theirs, mine = down([plane.theirs, plane.mine], hidden, [third_piece, neighbour.got_two])
    neighbour.one_block(theirs)
    theirs, _ = tie((theirs, third_home))
    fourth, own = (Scatter(*shares) for shares in zip(chunk, theirs, mine))
    fourth.two_blocks([])
    third_far_home = lax.ppermute(tie((third_piece, third_home))[0], "seq", [(0, 2), (3, 1)])
    neighbour_piece = neighbour.own_block([])
    neighbour_home = swapped(neighbour_piece, "seq", 1, 1)
    fourth.one_block([])
    own.two_blocks(fourth.got_two)
    fourth_piece = fourth.own_block([])
    own.one_block(fourth_piece)
    fourth_piece, _ = tie((fourth_piece, [third_far_home, neighbour_home]))
    return [
        own.own_block([]),
        neighbour_home,
        third_home,
        third_far_home,
        lax.ppermute(fourth_piece, "seq", [(1, 3), (2, 0)]),
        lax.ppermute(fourth_piece, "seq", [(0, 3), (3, 0)]),
    ]


def solution(mesh):
    in_specs = (
        P("seq", "exp"),
        P("seq", "exp"),
        P("seq", "exp"),
        P("exp", "seq"),
        P("seq", "exp"),
        P("exp"),
        P("seq", None),
        P(None, "seq"),
        P("seq", None, "exp"),
        P("seq", None, "exp"),
        P("seq", "exp", None),
    )
    out_specs = P("seq", "exp")
    return jax.shard_map(
        on_device, mesh=mesh, in_specs=in_specs, out_specs=out_specs, check_vma=False
    )
```

```python
import functools

import jax
import jax.numpy as jnp
from jax import lax
from jax.experimental import pallas as pl
from jax.experimental.pallas import tpu as pltpu
from jax.sharding import PartitionSpec as P

F32 = jnp.float32
BF16 = jnp.bfloat16
HIGHEST = lax.Precision.HIGHEST
VMEM_LIMIT = 32 * 1024 * 1024
ID_ROWS = 16


def in_hbm(array):
    return pltpu.with_memory_space_constraint(array, pltpu.HBM)


def lower_ones(length):
    rows = lax.broadcasted_iota(jnp.int32, (length, length), 0)
    columns = lax.broadcasted_iota(jnp.int32, (length, length), 1)
    return rows >= columns


def shifted(array, axis, by):
    count = lax.axis_size(axis)
    pairs = [(i, i + by) for i in range(count) if 0 <= i + by < count]
    return lax.ppermute(array, axis, pairs)


def state_kernel(key_ref, value_ref, decay_ref, message_ref, cumulative_ref):
    heads, length = decay_ref.shape
    size = key_ref.shape[1] // heads
    ones = lower_ones(length).astype(F32)
    cumulative = lax.dot_general(
        ones, decay_ref[...], (((1,), (1,)), ((), ())), precision=HIGHEST, preferred_element_type=F32
    )
    cumulative_ref[...] = cumulative
    last = cumulative[length - 1 : length, :]
    key_fade = jnp.exp(last - cumulative)
    message_ref[heads * size :, :] = jnp.zeros((message_ref.shape[0] - heads * size, size), BF16)
    half = (message_ref.shape[0] - heads * size) // 2
    rows = []
    for h in range(heads):
        columns = slice(h * size, (h + 1) * size)
        scaled = (key_fade[:, h : h + 1] * key_ref[:, columns].astype(F32)).astype(BF16)
        state = lax.dot_general(
            scaled, value_ref[:, columns], (((0,), (0,)), ((), ())), preferred_element_type=F32
        )
        message_ref[columns, :] = state.astype(BF16)
        rows.append(jnp.broadcast_to(jnp.exp(last[:, h : h + 1]), (1, size)))
    rows.append(jnp.zeros((half - heads, size), F32))
    fade = jnp.concatenate(rows, axis=0)
    leading = fade.astype(BF16)
    trailing = (fade - leading.astype(F32)).astype(BF16)
    message_ref[heads * size :, :] = jnp.concatenate([leading, trailing], axis=0)


def section_state(attn_key, attn_value, log_decay):
    heads, length = log_decay.shape
    width = attn_key.shape[1]
    half = -(-heads // 8) * 8
    return pl.pallas_call(
        state_kernel,
        out_shape=(
            jax.ShapeDtypeStruct((width + 2 * half, width // heads), BF16),
            jax.ShapeDtypeStruct((length, heads), F32),
        ),
        cost_estimate=pl.CostEstimate(
            flops=2 * length * width * (width // heads), bytes_accessed=4 * length * width, transcendentals=0
        ),
        compiler_params=pltpu.CompilerParams(vmem_limit_bytes=VMEM_LIMIT),
    )(in_hbm(attn_key), in_hbm(attn_value), in_hbm(log_decay))


def intra_kernel(query_ref, key_ref, value_ref, decay_ref, cumulative_ref, out_ref):
    heads, length = decay_ref.shape
    size = key_ref.shape[1] // heads
    causal = lower_ones(length)
    along = lax.dot_general(
        decay_ref[...],
        causal.astype(F32),
        (((1,), (1,)), ((), ())),
        precision=HIGHEST,
        preferred_element_type=F32,
    )
    for h in range(heads):
        columns = slice(h * size, (h + 1) * size)
        gap = jnp.where(causal, cumulative_ref[:, h : h + 1] - along[h : h + 1, :], 0.0)
        mask = jnp.where(causal, jnp.exp(gap), 0.0)
        scores = lax.dot_general(
            query_ref[:, columns], key_ref[:, columns], (((1,), (1,)), ((), ())), preferred_element_type=F32
        )
        weights = (scores * mask).astype(BF16)
        out_ref[:, columns] = jnp.dot(weights, value_ref[:, columns], preferred_element_type=F32)


def intra_section(attn_query, attn_key, attn_value, log_decay, cumulative):
    length, width = attn_query.shape
    return pl.pallas_call(
        intra_kernel,
        out_shape=jax.ShapeDtypeStruct((length, width), F32),
        cost_estimate=pl.CostEstimate(
            flops=4 * length * length * width, bytes_accessed=10 * length * width, transcendentals=0
        ),
        compiler_params=pltpu.CompilerParams(vmem_limit_bytes=VMEM_LIMIT),
    )(attn_query, attn_key, attn_value, log_decay, cumulative)


def stream_kernel(
    query_ref, intra_ref, cumulative_ref, incoming_ref, residual_ref, gain_ref, ids_ref, out_ref
):
    heads, size = incoming_ref.shape[0], incoming_ref.shape[1]
    length, width = residual_ref.shape
    choices = ids_ref.shape[0]
    below = jnp.concatenate(
        [
            ids_ref[...].astype(F32),
            jnp.zeros((ID_ROWS - choices, length), F32),
        ],
        axis=0,
    )
    out_ref[length:, :] = jnp.concatenate(
        [below, jnp.zeros((ID_ROWS, width - length), F32)], axis=1
    ).astype(BF16)
    faded = jnp.exp(cumulative_ref[...])
    for h in range(heads):
        columns = slice(h * size, (h + 1) * size)
        state = incoming_ref[h]
        leading = state.astype(BF16)
        trailing = (state - leading.astype(F32)).astype(BF16)
        query = query_ref[:, columns]
        inter = jnp.dot(query, leading, preferred_element_type=F32) + jnp.dot(
            query, trailing, preferred_element_type=F32
        )
        attn_out = intra_ref[:, columns] + faded[:, h : h + 1] * inter
        mean_square = jnp.mean(attn_out * attn_out, axis=1, keepdims=True)
        normed = attn_out * lax.rsqrt(mean_square + 1e-06)
        out_ref[:length, columns] = (
            residual_ref[:, columns].astype(F32) + gain_ref[:, columns].astype(F32) * normed
        ).astype(BF16)


def make_stream(attn_query, intra, cumulative, incoming, residual, norm_gain, ids):
    length, width = attn_query.shape
    return pl.pallas_call(
        stream_kernel,
        out_shape=jax.ShapeDtypeStruct((length + ID_ROWS, width), BF16),
        compiler_params=pltpu.CompilerParams(vmem_limit_bytes=VMEM_LIMIT),
    )(attn_query, intra, cumulative, incoming, residual, norm_gain.reshape(1, width), ids)


def read_message(message, heads):
    size = message.shape[1]
    half = (message.shape[0] - heads * size) // 2
    state = message[: heads * size].astype(F32).reshape(heads, size, size)
    tail = message[heads * size :].astype(F32)
    fade = tail[:heads] + tail[half : half + heads]
    return fade[:, None, :], state


def write_message(fade, state, rows):
    heads, size = state.shape[0], state.shape[1]
    half = (rows - heads * size) // 2
    leading = fade[:, 0, :].astype(BF16)
    trailing = (fade[:, 0, :] - leading.astype(F32)).astype(BF16)
    spare = jnp.zeros((half - heads, size), BF16)
    return jnp.concatenate(
        [state.astype(BF16).reshape(heads * size, size), leading, spare, trailing, spare], axis=0
    )


def incoming_state(message, heads):
    count = lax.axis_size("seq")
    window_fade, window = read_message(message, heads)
    incoming_fade, incoming = None, None
    distance = 1
    while distance < count:
        got_fade, got = read_message(shifted(message, "seq", distance), heads)
        if incoming is None:
            incoming_fade, incoming = got_fade, got
        else:
            incoming, incoming_fade = incoming + incoming_fade * got, incoming_fade * got_fade
        window, window_fade = window + window_fade * got, window_fade * got_fade
        distance *= 2
        if distance < count:
            message = write_message(window_fade, window, message.shape[0])
    return incoming


def select_kernel(capacity, choices, experts, base_ref, *refs):
    parts, (out_ref, place_ref) = refs[:-2], refs[-2:]
    length = parts[0].shape[0] - ID_ROWS
    part = parts[-1][...]
    for other in parts[:-1]:
        part = jnp.where(base_ref[1] > 0, other[...], part)
    before = lower_ones(length).astype(BF16)
    slot = lax.broadcasted_iota(jnp.int32, (capacity, length), 0).astype(F32)
    ids = part[length:, :length].astype(F32)
    rows = []
    for j in range(experts):
        expert = (base_ref[0] + j).astype(F32)
        chosen = ids[0:1, :] == expert
        for choice in range(1, choices):
            chosen = chosen | (ids[choice : choice + 1, :] == expert)
        flag = jnp.where(chosen, 1.0, 0.0)
        rank = lax.dot_general(
            jnp.broadcast_to(flag, (16, length)).astype(BF16),
            before,
            (((1,), (1,)), ((), ())),
            preferred_element_type=F32,
        )[0:1, :]
        rank = jnp.where(chosen, rank - 1.0, -1.0)
        rows.append(jnp.where(slot == rank, 1.0, 0.0).astype(BF16))
    place = jnp.concatenate(rows, axis=0)
    place_ref[...] = place
    out_ref[...] = lax.dot_general(
        part[:length, :], place, (((0,), (1,)), ((), ())), preferred_element_type=F32
    ).astype(BF16)


def select_slots(base, parts, capacity, choices, experts):
    rows, width = parts[0].shape
    length = rows - ID_ROWS
    slots = experts * capacity
    whole = pl.BlockSpec(memory_space=pltpu.VMEM)
    return pl.pallas_call(
        functools.partial(select_kernel, capacity, choices, experts),
        in_specs=[pl.BlockSpec(memory_space=pltpu.SMEM), *([whole] * len(parts))],
        out_shape=(
            jax.ShapeDtypeStruct((width, slots), BF16),
            jax.ShapeDtypeStruct((slots, length), BF16),
        ),
        cost_estimate=pl.CostEstimate(
            flops=2 * slots * length * width, bytes_accessed=4 * slots * width, transcendentals=0
        ),
        compiler_params=pltpu.CompilerParams(vmem_limit_bytes=VMEM_LIMIT),
    )(base, *parts)


def combine_kernel(place_ref, *refs):
    shares, out_ref = refs[:-1], refs[-1]
    total = shares[0][0].astype(F32)
    for share in shares[1:]:
        total = total + share[0].astype(F32)
    out_ref[...] = lax.dot_general(
        place_ref[...], total.astype(BF16), (((0,), (0,)), ((), ())), preferred_element_type=F32
    ).astype(BF16)


def combine_slots(place, shares):
    slots, length = place.shape
    width = shares[0].shape[2]
    first = pl.BlockSpec((1, slots, width), lambda _: (0, 0, 0))
    return pl.pallas_call(
        combine_kernel,
        grid=(1,),
        in_specs=[pl.BlockSpec(memory_space=pltpu.VMEM), *([first] * len(shares))],
        out_shape=jax.ShapeDtypeStruct((length, width), BF16),
        cost_estimate=pl.CostEstimate(
            flops=2 * slots * length * width, bytes_accessed=8 * slots * width, transcendentals=0
        ),
        compiler_params=pltpu.CompilerParams(vmem_limit_bytes=VMEM_LIMIT),
    )(place, *shares)


def gate_kernel(counts, sections, last, plan_ref, *refs):
    step = pl.program_id(0)
    blocks = sum(counts)
    used = len(counts) * sections
    x_refs, refs = refs[:used], refs[used:]
    router_ref, gate_ref, up_ref = refs[:3]
    refs = refs[3:]
    if last:
        gate_in, up_in, score_in, hidden_ref, gate_acc, up_acc, score_acc = refs
    else:
        gate_acc, up_acc, score_acc = refs
    experts = gate_ref.shape[0]
    width = x_refs[0].shape[1]
    slots = gate_acc.shape[2]
    part = slots // sections

    @pl.when(step == 0)
    def _():
        if last:
            gate_acc[...] = gate_in[...]
            up_acc[...] = up_in[...]
            score_acc[...] = score_in[...]
        else:
            gate_acc[...] = jnp.zeros_like(gate_acc)
            up_acc[...] = jnp.zeros_like(up_acc)
            score_acc[...] = jnp.zeros_like(score_acc)

    xs = []
    for section in range(sections):
        mine = x_refs[section * len(counts) : (section + 1) * len(counts)]
        x = mine[-1][0]
        for i in range(len(counts) - 2, -1, -1):
            x = jnp.where(step < sum(counts[: i + 1]), mine[i][0], x)
        xs.append(x)
    for j in range(experts):
        x = jnp.concatenate([x[:, j * part : (j + 1) * part] for x in xs], axis=1)
        score_acc[j] += jnp.dot(router_ref[0], x, preferred_element_type=F32)
        gate_acc[j] += jnp.dot(gate_ref[j], x, preferred_element_type=F32)
        up_acc[j] += jnp.dot(up_ref[j], x, preferred_element_type=F32)

    if last:

        @pl.when(step == blocks - 1)
        def _():
            for j in range(experts):
                score = score_acc[j, j : j + 1, :]
                gate = gate_acc[j]
                routed = gate / (1.0 + jnp.exp(-gate)) * up_acc[j]
                routed = routed / (1.0 + jnp.exp(-score))
                hidden_ref[j] = routed.T.astype(BF16)


def gate_part(plan, xs, router_rows, gate_rows, up_rows, sums=None):
    counts = tuple(x.shape[0] for x in xs[0])
    blocks = sum(counts)
    _, width, total = xs[0][0].shape
    experts, units, _ = gate_rows.shape
    slots = total // experts * len(xs)
    whole = pl.BlockSpec(memory_space=pltpu.VMEM)
    last = sums is not None

    def x_spec(i):
        before = sum(counts[:i])
        return pl.BlockSpec(
            (1, width, total), lambda p, plan: (jnp.clip(p - before, 0, counts[i] - 1), 0, 0)
        )

    weight_spec = pl.BlockSpec((experts, units, width), lambda p, plan: (0, 0, plan[p]))
    sum_shapes = [(experts, units, slots), (experts, units, slots), (experts, experts, slots)]
    sum_specs = [pl.BlockSpec(shape, lambda p, plan: (0, 0, 0)) for shape in sum_shapes]
    if last:
        out_shape = jax.ShapeDtypeStruct((experts, slots, units), BF16)
        out_specs = whole
        scratch = [pltpu.VMEM(shape, F32) for shape in sum_shapes]
    else:
        out_shape = tuple(jax.ShapeDtypeStruct(shape, F32) for shape in sum_shapes)
        out_specs = tuple(sum_specs)
        scratch = []
    return pl.pallas_call(
        functools.partial(gate_kernel, counts, len(xs), last),
        grid_spec=pltpu.PrefetchScalarGridSpec(
            num_scalar_prefetch=1,
            grid=(blocks,),
            in_specs=[
                *[x_spec(i) for _ in xs for i in range(len(counts))],
                pl.BlockSpec((1, experts, width), lambda p, plan: (plan[p], 0, 0)),
                weight_spec,
                weight_spec,
                *(sum_specs if last else []),
            ],
            out_specs=out_specs,
            scratch_shapes=scratch,
        ),
        out_shape=out_shape,
        cost_estimate=pl.CostEstimate(
            flops=4 * experts * slots * blocks * width * units,
            bytes_accessed=4 * experts * blocks * width * units,
            transcendentals=0,
        ),
        compiler_params=pltpu.CompilerParams(vmem_limit_bytes=VMEM_LIMIT),
    )(
        plan,
        *[x for section in xs for x in section],
        router_rows,
        in_hbm(gate_rows),
        in_hbm(up_rows),
        *(sums or ()),
    )


def down_kernel(blocks, sections, plan_ref, hidden_ref, down_ref, *out_refs):
    experts, slots, _ = hidden_ref.shape
    part = slots // sections
    turn = pl.program_id(0) // blocks
    for j in range(experts):
        share = jnp.dot(hidden_ref[j], down_ref[j], preferred_element_type=F32).astype(BF16)
        for i in range(len(out_refs) // sections):

            @pl.when(turn == i)
            def _():
                for section in range(sections):
                    out_ref = out_refs[i * sections + section]
                    out_ref[0, j * part : (j + 1) * part, :] = share[
                        section * part : (section + 1) * part
                    ]


def down_part(plans, hidden, down_weight, width, sections):
    blocks = plans[0].shape[0]
    experts, slots, units = hidden.shape
    rows = experts * slots // sections

    def out_spec(i):
        return pl.BlockSpec(
            (1, rows, width), lambda p, plan: (jnp.clip(p - i * blocks, 0, blocks - 1), 0, 0)
        )

    out = pl.pallas_call(
        functools.partial(down_kernel, blocks, sections),
        grid_spec=pltpu.PrefetchScalarGridSpec(
            num_scalar_prefetch=1,
            grid=(len(plans) * blocks,),
            in_specs=[
                pl.BlockSpec(memory_space=pltpu.VMEM),
                pl.BlockSpec((experts, units, width), lambda p, plan: (0, 0, plan[p])),
            ],
            out_specs=[out_spec(i) for i in range(len(plans)) for _ in range(sections)],
        ),
        out_shape=[jax.ShapeDtypeStruct((blocks, rows, width), BF16)] * (len(plans) * sections),
        cost_estimate=pl.CostEstimate(
            flops=2 * experts * slots * len(plans) * blocks * width * units,
            bytes_accessed=2 * experts * len(plans) * blocks * width * units,
            transcendentals=0,
        ),
        compiler_params=pltpu.CompilerParams(vmem_limit_bytes=VMEM_LIMIT),
    )(jnp.concatenate(plans), hidden, in_hbm(down_weight))
    return [out[i * sections : (i + 1) * sections] for i in range(len(plans))]


def added(left, right):
    return (left.astype(F32) + right.astype(F32)).astype(BF16)


def swapped(array, axis, even, odd):
    count = lax.axis_size(axis)
    pairs = [(i, i ^ (odd if i % 2 else even)) for i in range(count)]
    return lax.ppermute(array, axis, pairs)


class PairedPlane:
    def __init__(self):
        me = lax.axis_index("exp").astype(jnp.int32)
        other = me ^ 1
        near = jnp.where(me % 2 == 0, 2, 4)
        far = 6 - near
        self.early = jnp.stack([me, me ^ near, other, other ^ far])
        self.late = jnp.stack([me ^ far, me ^ 6, other ^ near, other ^ 6])
        self.mine = jnp.stack([me, me ^ near, me ^ far, me ^ 6])
        self.theirs = jnp.stack([other, other ^ far, other ^ near, other ^ 6])

    def once(self, part):
        return swapped(part, "exp", 2, 4)

    def first(self, part):
        return jnp.stack([part, self.once(part)])

    def second(self, two):
        return swapped(two, "exp", 4, 2)

    def across(self, two):
        return swapped(two, "exp", 1, 1)

def on_device(
    attn_query,
    attn_key,
    attn_value,
    log_decay,
    residual,
    norm_gain,
    expert_ids,
    router_weight,
    gate_weight,
    up_weight,
    down_weight,
):
    heads_here, length = log_decay.shape
    groups = lax.axis_size("seq")
    shares = lax.axis_size("exp")
    width = attn_query.shape[1]
    experts_here = router_weight.shape[1]
    section = lax.axis_index("seq")
    inner = (section > 0) & (section < groups - 1)
    base = jnp.stack([section * experts_here, inner]).astype(jnp.int32)
    router_rows = router_weight.reshape(shares, width, experts_here).transpose(0, 2, 1)
    gate_rows = gate_weight.swapaxes(1, 2)
    up_rows = up_weight.swapaxes(1, 2)

    message, cumulative = section_state(attn_key, attn_value, log_decay)
    intra = intra_section(attn_query, attn_key, attn_value, log_decay, cumulative)
    incoming = incoming_state(message, heads_here)
    stream = make_stream(
        attn_query, intra, cumulative, incoming, residual, norm_gain, expert_ids.T
    )

    capacity = 4 * length // (experts_here * groups)
    choices = expert_ids.shape[1]

    def select(*parts):
        return select_slots(base, parts, capacity, choices, experts_here)

    weights = (router_rows, gate_rows, up_rows)
    if shares == 8 and groups == 4:
        pieces = paired_chunks(stream, select, weights, down_weight)
    else:
        order = jnp.arange(shares, dtype=jnp.int32)
        middle = shares // 2
        pieces = []
        for first in range(0, groups, 2):
            chunk = (first, first + 1)
            chosen = [
                select(swapped(stream, "seq", offset, offset) if offset else stream)
                for offset in chunk
            ]
            gathered = [lax.all_gather(slots, "exp", axis=0) for slots, _ in chosen]
            sums = gate_part(order[:middle], [[x[:middle]] for x in gathered], *weights)
            hidden = gate_part(order[middle:], [[x[middle:]] for x in gathered], *weights, sums)
            (partial,) = down_part([order], hidden, down_weight, width, len(chunk))
            for offset, share, (_, place) in zip(chunk, partial, chosen):
                share = lax.psum_scatter(share, "exp", scatter_dimension=0)
                piece = combine_slots(place, [share[None]])
                pieces.append(swapped(piece, "seq", offset, offset) if offset else piece)
    total = stream[:length].astype(F32)
    for piece in pieces:
        total = total + piece.astype(F32)
    return total.astype(BF16)


def paired_chunks(stream, select, weights, down_weight):
    plane = PairedPlane()
    width = stream.shape[1]
    tie = lax.optimization_barrier
    two, far_two, near, near_far, chosen = {}, {}, {}, {}, {}

    def across_middle(part):
        return lax.ppermute(part, "seq", [(1, 2), (2, 1)])

    def outward(part):
        return lax.ppermute(part, "seq", [(1, 0), (2, 3)])

    def gather(name, behind):
        two[name], _ = tie((plane.first(chosen[name][0]), behind))
        near[name] = plane.across(two[name])
        far_two[name] = plane.second(two[name])

    swap = swapped(stream, "seq", 1, 1)
    crossed = across_middle(stream)
    chosen["own"] = select(stream)
    gather("own", [])
    passed = outward(crossed)
    crossed_swap = across_middle(swap)
    chosen["neighbour"] = select(swap)
    gather("neighbour", [passed, crossed_swap, far_two["own"]])
    passed_fourth = outward(crossed_swap)
    chosen["third"] = select(crossed, passed)
    gather("third", [passed_fourth, far_two["neighbour"]])
    chosen["fourth"] = select(crossed_swap, passed_fourth)

    def gate(chunk, behind):
        early = [[two[name], near[name]] for name in chunk]
        return gate_part(plane.early, tie((early, behind))[0], *weights)

    def gate_last(chunk, sums, behind):
        late = [[far_two[name], near_far[name]] for name in chunk]
        (late, sums), _ = tie(((late, sums), behind))
        return gate_part(plane.late, late, *weights, sums)

    def down(plans, hidden, behind):
        hidden, _ = tie((hidden, behind))
        return down_part(plans, hidden, down_weight, width, 2)

    class Scatter:
        def __init__(self, name, theirs, mine):
            self.name, self.theirs, self.mine = name, theirs, mine

        def two_blocks(self, behind):
            self.near = plane.across(self.theirs)
            self.sent = added(self.mine[2:], self.near[2:])
            self.got_two = plane.second(tie((self.sent, behind))[0])

        def one_block(self, behind):
            got_two, _ = tie((self.got_two, behind))
            self.one = added(added(self.mine[1], self.near[1]), got_two[1])
            self.got_one = plane.once(self.one)

        def own_block(self, behind):
            got_one, _ = tie((self.got_one, behind))
            shares = [self.mine, self.near, self.got_two, got_one[None]]
            return combine_slots(chosen[self.name][1], shares)

    chunk = ("third", "neighbour")
    sums = gate(chunk, chosen["fourth"])
    gather("fourth", sums)
    for name in chunk:
        near_far[name] = plane.across(tie((far_two[name], sums))[0])
    hidden = gate_last(chunk, sums, two["fourth"])
    (theirs,) = down([plane.theirs], hidden, far_two["fourth"])
    (mine,) = down([plane.mine], hidden, theirs)
    third, neighbour = (Scatter(*shares) for shares in zip(chunk, theirs, mine))
    third.two_blocks([])

    chunk = ("fourth", "own")
    sums = gate(chunk, third.sent)
    for name in chunk:
        near_far[name] = plane.across(tie((far_two[name], third.sent))[0])
    third.one_block(sums)
    neighbour.two_blocks(third.one)
    hidden = gate_last(chunk, sums, [third.one, neighbour.sent])
    third_piece = third.own_block(hidden)
    third_home = lax.ppermute(third_piece, "seq", [(1, 2), (2, 1)])
    theirs, mine = down([plane.theirs, plane.mine], hidden, [third_piece, neighbour.got_two])
    neighbour.one_block(theirs)
    theirs, _ = tie((theirs, third_home))
    fourth, own = (Scatter(*shares) for shares in zip(chunk, theirs, mine))
    fourth.two_blocks([])
    third_far_home = lax.ppermute(tie((third_piece, third_home))[0], "seq", [(0, 2), (3, 1)])
    neighbour_piece = neighbour.own_block([])
    neighbour_home = swapped(neighbour_piece, "seq", 1, 1)
    fourth.one_block([third_far_home, neighbour.got_one])
    own.two_blocks(fourth.got_two)
    fourth_piece = fourth.own_block([])
    own.one_block(fourth_piece)
    fourth_piece, _ = tie((fourth_piece, [third_far_home, neighbour_home]))
    return [
        own.own_block([]),
        neighbour_home,
        third_home,
        third_far_home,
        lax.ppermute(fourth_piece, "seq", [(1, 3), (2, 0)]),
        lax.ppermute(fourth_piece, "seq", [(0, 3), (3, 0)]),
    ]


def solution(mesh):
    in_specs = (
        P("seq", "exp"),
        P("seq", "exp"),
        P("seq", "exp"),
        P("exp", "seq"),
        P("seq", "exp"),
        P("exp"),
        P("seq", None),
        P(None, "seq"),
        P("seq", None, "exp"),
        P("seq", None, "exp"),
        P("seq", "exp", None),
    )
    out_specs = P("seq", "exp")
    return jax.shard_map(
        on_device, mesh=mesh, in_specs=in_specs, out_specs=out_specs, check_vma=False
    )
```

```python
import functools

import jax
import jax.numpy as jnp
from jax import lax
from jax.experimental import pallas as pl
from jax.experimental.pallas import tpu as pltpu
from jax.sharding import PartitionSpec as P

F32 = jnp.float32
BF16 = jnp.bfloat16
HIGHEST = lax.Precision.HIGHEST
VMEM_LIMIT = 32 * 1024 * 1024
ID_ROWS = 16


def in_hbm(array):
    return pltpu.with_memory_space_constraint(array, pltpu.HBM)


def lower_ones(length):
    rows = lax.broadcasted_iota(jnp.int32, (length, length), 0)
    columns = lax.broadcasted_iota(jnp.int32, (length, length), 1)
    return rows >= columns


def shifted(array, axis, by):
    count = lax.axis_size(axis)
    pairs = [(i, i + by) for i in range(count) if 0 <= i + by < count]
    return lax.ppermute(array, axis, pairs)


def state_kernel(key_ref, value_ref, decay_ref, message_ref, cumulative_ref):
    heads, length = decay_ref.shape
    size = key_ref.shape[1] // heads
    ones = lower_ones(length).astype(F32)
    cumulative = lax.dot_general(
        ones, decay_ref[...], (((1,), (1,)), ((), ())), precision=HIGHEST, preferred_element_type=F32
    )
    cumulative_ref[...] = cumulative
    last = cumulative[length - 1 : length, :]
    key_fade = jnp.exp(last - cumulative)
    message_ref[heads * size :, :] = jnp.zeros((message_ref.shape[0] - heads * size, size), BF16)
    half = (message_ref.shape[0] - heads * size) // 2
    rows = []
    for h in range(heads):
        columns = slice(h * size, (h + 1) * size)
        scaled = (key_fade[:, h : h + 1] * key_ref[:, columns].astype(F32)).astype(BF16)
        state = lax.dot_general(
            scaled, value_ref[:, columns], (((0,), (0,)), ((), ())), preferred_element_type=F32
        )
        message_ref[columns, :] = state.astype(BF16)
        rows.append(jnp.broadcast_to(jnp.exp(last[:, h : h + 1]), (1, size)))
    rows.append(jnp.zeros((half - heads, size), F32))
    fade = jnp.concatenate(rows, axis=0)
    leading = fade.astype(BF16)
    trailing = (fade - leading.astype(F32)).astype(BF16)
    message_ref[heads * size :, :] = jnp.concatenate([leading, trailing], axis=0)


def section_state(attn_key, attn_value, log_decay):
    heads, length = log_decay.shape
    width = attn_key.shape[1]
    half = -(-heads // 8) * 8
    return pl.pallas_call(
        state_kernel,
        out_shape=(
            jax.ShapeDtypeStruct((width + 2 * half, width // heads), BF16),
            jax.ShapeDtypeStruct((length, heads), F32),
        ),
        cost_estimate=pl.CostEstimate(
            flops=2 * length * width * (width // heads), bytes_accessed=4 * length * width, transcendentals=0
        ),
        compiler_params=pltpu.CompilerParams(vmem_limit_bytes=VMEM_LIMIT),
    )(in_hbm(attn_key), in_hbm(attn_value), in_hbm(log_decay))


def intra_kernel(query_ref, key_ref, value_ref, decay_ref, cumulative_ref, out_ref):
    heads, length = decay_ref.shape
    size = key_ref.shape[1] // heads
    causal = lower_ones(length)
    along = lax.dot_general(
        decay_ref[...],
        causal.astype(F32),
        (((1,), (1,)), ((), ())),
        precision=HIGHEST,
        preferred_element_type=F32,
    )
    for h in range(heads):
        columns = slice(h * size, (h + 1) * size)
        gap = jnp.where(causal, cumulative_ref[:, h : h + 1] - along[h : h + 1, :], 0.0)
        mask = jnp.where(causal, jnp.exp(gap), 0.0)
        scores = lax.dot_general(
            query_ref[:, columns], key_ref[:, columns], (((1,), (1,)), ((), ())), preferred_element_type=F32
        )
        weights = (scores * mask).astype(BF16)
        out_ref[:, columns] = jnp.dot(weights, value_ref[:, columns], preferred_element_type=F32)


def intra_section(attn_query, attn_key, attn_value, log_decay, cumulative):
    length, width = attn_query.shape
    return pl.pallas_call(
        intra_kernel,
        out_shape=jax.ShapeDtypeStruct((length, width), F32),
        cost_estimate=pl.CostEstimate(
            flops=4 * length * length * width, bytes_accessed=10 * length * width, transcendentals=0
        ),
        compiler_params=pltpu.CompilerParams(vmem_limit_bytes=VMEM_LIMIT),
    )(attn_query, attn_key, attn_value, log_decay, cumulative)


def stream_kernel(
    query_ref, intra_ref, cumulative_ref, incoming_ref, residual_ref, gain_ref, ids_ref, out_ref
):
    heads, size = incoming_ref.shape[0], incoming_ref.shape[1]
    length, width = residual_ref.shape
    choices = ids_ref.shape[0]
    below = jnp.concatenate(
        [
            ids_ref[...].astype(F32),
            jnp.zeros((ID_ROWS - choices, length), F32),
        ],
        axis=0,
    )
    out_ref[length:, :] = jnp.concatenate(
        [below, jnp.zeros((ID_ROWS, width - length), F32)], axis=1
    ).astype(BF16)
    faded = jnp.exp(cumulative_ref[...])
    for h in range(heads):
        columns = slice(h * size, (h + 1) * size)
        state = incoming_ref[h]
        leading = state.astype(BF16)
        trailing = (state - leading.astype(F32)).astype(BF16)
        query = query_ref[:, columns]
        inter = jnp.dot(query, leading, preferred_element_type=F32) + jnp.dot(
            query, trailing, preferred_element_type=F32
        )
        attn_out = intra_ref[:, columns] + faded[:, h : h + 1] * inter
        mean_square = jnp.mean(attn_out * attn_out, axis=1, keepdims=True)
        normed = attn_out * lax.rsqrt(mean_square + 1e-06)
        out_ref[:length, columns] = (
            residual_ref[:, columns].astype(F32) + gain_ref[:, columns].astype(F32) * normed
        ).astype(BF16)


def make_stream(attn_query, intra, cumulative, incoming, residual, norm_gain, ids):
    length, width = attn_query.shape
    return pl.pallas_call(
        stream_kernel,
        out_shape=jax.ShapeDtypeStruct((length + ID_ROWS, width), BF16),
        compiler_params=pltpu.CompilerParams(vmem_limit_bytes=VMEM_LIMIT),
    )(attn_query, intra, cumulative, incoming, residual, norm_gain.reshape(1, width), ids)


def read_message(message, heads):
    size = message.shape[1]
    half = (message.shape[0] - heads * size) // 2
    state = message[: heads * size].astype(F32).reshape(heads, size, size)
    tail = message[heads * size :].astype(F32)
    fade = tail[:heads] + tail[half : half + heads]
    return fade[:, None, :], state


def write_message(fade, state, rows):
    heads, size = state.shape[0], state.shape[1]
    half = (rows - heads * size) // 2
    leading = fade[:, 0, :].astype(BF16)
    trailing = (fade[:, 0, :] - leading.astype(F32)).astype(BF16)
    spare = jnp.zeros((half - heads, size), BF16)
    return jnp.concatenate(
        [state.astype(BF16).reshape(heads * size, size), leading, spare, trailing, spare], axis=0
    )


def incoming_state(message, heads):
    count = lax.axis_size("seq")
    window_fade, window = read_message(message, heads)
    incoming_fade, incoming = None, None
    distance = 1
    while distance < count:
        got_fade, got = read_message(shifted(message, "seq", distance), heads)
        if incoming is None:
            incoming_fade, incoming = got_fade, got
        else:
            incoming, incoming_fade = incoming + incoming_fade * got, incoming_fade * got_fade
        window, window_fade = window + window_fade * got, window_fade * got_fade
        distance *= 2
        if distance < count:
            message = write_message(window_fade, window, message.shape[0])
    return incoming


def select_kernel(capacity, choices, experts, base_ref, *refs):
    parts, (out_ref, place_ref) = refs[:-2], refs[-2:]
    length = parts[0].shape[0] - ID_ROWS
    part = parts[-1][...]
    for other in parts[:-1]:
        part = jnp.where(base_ref[1] > 0, other[...], part)
    before = lower_ones(length).astype(BF16)
    slot = lax.broadcasted_iota(jnp.int32, (capacity, length), 0).astype(F32)
    ids = part[length:, :length].astype(F32)
    rows = []
    for j in range(experts):
        expert = (base_ref[0] + j).astype(F32)
        chosen = ids[0:1, :] == expert
        for choice in range(1, choices):
            chosen = chosen | (ids[choice : choice + 1, :] == expert)
        flag = jnp.where(chosen, 1.0, 0.0)
        rank = lax.dot_general(
            jnp.broadcast_to(flag, (16, length)).astype(BF16),
            before,
            (((1,), (1,)), ((), ())),
            preferred_element_type=F32,
        )[0:1, :]
        rank = jnp.where(chosen, rank - 1.0, -1.0)
        rows.append(jnp.where(slot == rank, 1.0, 0.0).astype(BF16))
    place = jnp.concatenate(rows, axis=0)
    place_ref[...] = place
    out_ref[...] = lax.dot_general(
        part[:length, :], place, (((0,), (1,)), ((), ())), preferred_element_type=F32
    ).astype(BF16)


def select_slots(base, parts, capacity, choices, experts):
    rows, width = parts[0].shape
    length = rows - ID_ROWS
    slots = experts * capacity
    whole = pl.BlockSpec(memory_space=pltpu.VMEM)
    return pl.pallas_call(
        functools.partial(select_kernel, capacity, choices, experts),
        in_specs=[pl.BlockSpec(memory_space=pltpu.SMEM), *([whole] * len(parts))],
        out_shape=(
            jax.ShapeDtypeStruct((width, slots), BF16),
            jax.ShapeDtypeStruct((slots, length), BF16),
        ),
        cost_estimate=pl.CostEstimate(
            flops=2 * slots * length * width, bytes_accessed=4 * slots * width, transcendentals=0
        ),
        compiler_params=pltpu.CompilerParams(vmem_limit_bytes=VMEM_LIMIT),
    )(base, *parts)


def combine_kernel(place_ref, *refs):
    shares, out_ref = refs[:-1], refs[-1]
    total = shares[0][0].astype(F32)
    for share in shares[1:]:
        total = total + share[0].astype(F32)
    out_ref[...] = lax.dot_general(
        place_ref[...], total.astype(BF16), (((0,), (0,)), ((), ())), preferred_element_type=F32
    ).astype(BF16)


def combine_slots(place, shares):
    slots, length = place.shape
    width = shares[0].shape[2]
    first = pl.BlockSpec((1, slots, width), lambda _: (0, 0, 0))
    return pl.pallas_call(
        combine_kernel,
        grid=(1,),
        in_specs=[pl.BlockSpec(memory_space=pltpu.VMEM), *([first] * len(shares))],
        out_shape=jax.ShapeDtypeStruct((length, width), BF16),
        cost_estimate=pl.CostEstimate(
            flops=2 * slots * length * width, bytes_accessed=8 * slots * width, transcendentals=0
        ),
        compiler_params=pltpu.CompilerParams(vmem_limit_bytes=VMEM_LIMIT),
    )(place, *shares)


def gate_kernel(counts, sections, last, plan_ref, *refs):
    step = pl.program_id(0)
    blocks = sum(counts)
    used = len(counts) * sections
    x_refs, refs = refs[:used], refs[used:]
    router_ref, gate_ref, up_ref = refs[:3]
    refs = refs[3:]
    if last:
        gate_in, up_in, score_in, hidden_ref, gate_acc, up_acc, score_acc = refs
    else:
        gate_acc, up_acc, score_acc = refs
    experts = gate_ref.shape[0]
    width = x_refs[0].shape[1]
    slots = gate_acc.shape[2]
    part = slots // sections

    @pl.when(step == 0)
    def _():
        if last:
            gate_acc[...] = gate_in[...]
            up_acc[...] = up_in[...]
            score_acc[...] = score_in[...]
        else:
            gate_acc[...] = jnp.zeros_like(gate_acc)
            up_acc[...] = jnp.zeros_like(up_acc)
            score_acc[...] = jnp.zeros_like(score_acc)

    xs = []
    for section in range(sections):
        mine = x_refs[section * len(counts) : (section + 1) * len(counts)]
        x = mine[-1][0]
        for i in range(len(counts) - 2, -1, -1):
            x = jnp.where(step < sum(counts[: i + 1]), mine[i][0], x)
        xs.append(x)
    for j in range(experts):
        x = jnp.concatenate([x[:, j * part : (j + 1) * part] for x in xs], axis=1)
        score_acc[j] += jnp.dot(router_ref[0], x, preferred_element_type=F32)
        gate_acc[j] += jnp.dot(gate_ref[j], x, preferred_element_type=F32)
        up_acc[j] += jnp.dot(up_ref[j], x, preferred_element_type=F32)

    if last:

        @pl.when(step == blocks - 1)
        def _():
            for j in range(experts):
                score = score_acc[j, j : j + 1, :]
                gate = gate_acc[j]
                routed = gate / (1.0 + jnp.exp(-gate)) * up_acc[j]
                routed = routed / (1.0 + jnp.exp(-score))
                hidden_ref[j] = routed.T.astype(BF16)


def gate_part(plan, xs, router_rows, gate_rows, up_rows, sums=None):
    counts = tuple(x.shape[0] for x in xs[0])
    blocks = sum(counts)
    _, width, total = xs[0][0].shape
    experts, units, _ = gate_rows.shape
    slots = total // experts * len(xs)
    whole = pl.BlockSpec(memory_space=pltpu.VMEM)
    last = sums is not None

    def x_spec(i):
        before = sum(counts[:i])
        return pl.BlockSpec(
            (1, width, total), lambda p, plan: (jnp.clip(p - before, 0, counts[i] - 1), 0, 0)
        )

    weight_spec = pl.BlockSpec((experts, units, width), lambda p, plan: (0, 0, plan[p]))
    sum_shapes = [(experts, units, slots), (experts, units, slots), (experts, experts, slots)]
    sum_specs = [pl.BlockSpec(shape, lambda p, plan: (0, 0, 0)) for shape in sum_shapes]
    if last:
        out_shape = jax.ShapeDtypeStruct((experts, slots, units), BF16)
        out_specs = whole
        scratch = [pltpu.VMEM(shape, F32) for shape in sum_shapes]
    else:
        out_shape = tuple(jax.ShapeDtypeStruct(shape, F32) for shape in sum_shapes)
        out_specs = tuple(sum_specs)
        scratch = []
    return pl.pallas_call(
        functools.partial(gate_kernel, counts, len(xs), last),
        grid_spec=pltpu.PrefetchScalarGridSpec(
            num_scalar_prefetch=1,
            grid=(blocks,),
            in_specs=[
                *[x_spec(i) for _ in xs for i in range(len(counts))],
                pl.BlockSpec((1, experts, width), lambda p, plan: (plan[p], 0, 0)),
                weight_spec,
                weight_spec,
                *(sum_specs if last else []),
            ],
            out_specs=out_specs,
            scratch_shapes=scratch,
        ),
        out_shape=out_shape,
        cost_estimate=pl.CostEstimate(
            flops=4 * experts * slots * blocks * width * units,
            bytes_accessed=4 * experts * blocks * width * units,
            transcendentals=0,
        ),
        compiler_params=pltpu.CompilerParams(vmem_limit_bytes=VMEM_LIMIT),
    )(
        plan,
        *[x for section in xs for x in section],
        router_rows,
        in_hbm(gate_rows),
        in_hbm(up_rows),
        *(sums or ()),
    )


def down_kernel(blocks, sections, plan_ref, hidden_ref, down_ref, *out_refs):
    experts, slots, _ = hidden_ref.shape
    part = slots // sections
    turn = pl.program_id(0) // blocks
    for j in range(experts):
        share = jnp.dot(hidden_ref[j], down_ref[j], preferred_element_type=F32).astype(BF16)
        for i in range(len(out_refs) // sections):

            @pl.when(turn == i)
            def _():
                for section in range(sections):
                    out_ref = out_refs[i * sections + section]
                    out_ref[0, j * part : (j + 1) * part, :] = share[
                        section * part : (section + 1) * part
                    ]


def down_part(plans, hidden, down_weight, width, sections):
    blocks = plans[0].shape[0]
    experts, slots, units = hidden.shape
    rows = experts * slots // sections

    def out_spec(i):
        return pl.BlockSpec(
            (1, rows, width), lambda p, plan: (jnp.clip(p - i * blocks, 0, blocks - 1), 0, 0)
        )

    out = pl.pallas_call(
        functools.partial(down_kernel, blocks, sections),
        grid_spec=pltpu.PrefetchScalarGridSpec(
            num_scalar_prefetch=1,
            grid=(len(plans) * blocks,),
            in_specs=[
                pl.BlockSpec(memory_space=pltpu.VMEM),
                pl.BlockSpec((experts, units, width), lambda p, plan: (0, 0, plan[p])),
            ],
            out_specs=[out_spec(i) for i in range(len(plans)) for _ in range(sections)],
        ),
        out_shape=[jax.ShapeDtypeStruct((blocks, rows, width), BF16)] * (len(plans) * sections),
        cost_estimate=pl.CostEstimate(
            flops=2 * experts * slots * len(plans) * blocks * width * units,
            bytes_accessed=2 * experts * len(plans) * blocks * width * units,
            transcendentals=0,
        ),
        compiler_params=pltpu.CompilerParams(vmem_limit_bytes=VMEM_LIMIT),
    )(jnp.concatenate(plans), hidden, in_hbm(down_weight))
    return [out[i * sections : (i + 1) * sections] for i in range(len(plans))]


def added(left, right):
    return (left.astype(F32) + right.astype(F32)).astype(BF16)


def swapped(array, axis, even, odd):
    count = lax.axis_size(axis)
    pairs = [(i, i ^ (odd if i % 2 else even)) for i in range(count)]
    return lax.ppermute(array, axis, pairs)


class PairedPlane:
    def __init__(self):
        me = lax.axis_index("exp").astype(jnp.int32)
        other = me ^ 1
        near = jnp.where(me % 2 == 0, 2, 4)
        far = 6 - near
        self.early = jnp.stack([me, me ^ near, other, other ^ far])
        self.late = jnp.stack([me ^ far, me ^ 6, other ^ near, other ^ 6])
        self.mine = jnp.stack([me, me ^ near, me ^ far, me ^ 6])
        self.theirs = jnp.stack([other, other ^ far, other ^ near, other ^ 6])

    def once(self, part):
        return swapped(part, "exp", 2, 4)

    def first(self, part):
        return jnp.stack([part, self.once(part)])

    def second(self, two):
        return swapped(two, "exp", 4, 2)

    def across(self, two):
        return swapped(two, "exp", 1, 1)

def on_device(
    attn_query,
    attn_key,
    attn_value,
    log_decay,
    residual,
    norm_gain,
    expert_ids,
    router_weight,
    gate_weight,
    up_weight,
    down_weight,
):
    heads_here, length = log_decay.shape
    groups = lax.axis_size("seq")
    shares = lax.axis_size("exp")
    width = attn_query.shape[1]
    experts_here = router_weight.shape[1]
    section = lax.axis_index("seq")
    inner = (section > 0) & (section < groups - 1)
    base = jnp.stack([section * experts_here, inner]).astype(jnp.int32)
    router_rows = router_weight.reshape(shares, width, experts_here).transpose(0, 2, 1)
    gate_rows = gate_weight.swapaxes(1, 2)
    up_rows = up_weight.swapaxes(1, 2)

    message, cumulative = section_state(attn_key, attn_value, log_decay)
    intra = intra_section(attn_query, attn_key, attn_value, log_decay, cumulative)
    incoming = incoming_state(message, heads_here)
    stream = make_stream(
        attn_query, intra, cumulative, incoming, residual, norm_gain, expert_ids.T
    )

    capacity = 4 * length // (experts_here * groups)
    choices = expert_ids.shape[1]

    def select(*parts):
        return select_slots(base, parts, capacity, choices, experts_here)

    weights = (router_rows, gate_rows, up_rows)
    if shares == 8 and groups == 4:
        pieces = paired_chunks(stream, select, weights, down_weight)
    else:
        order = jnp.arange(shares, dtype=jnp.int32)
        middle = shares // 2
        pieces = []
        for first in range(0, groups, 2):
            chunk = (first, first + 1)
            chosen = [
                select(swapped(stream, "seq", offset, offset) if offset else stream)
                for offset in chunk
            ]
            gathered = [lax.all_gather(slots, "exp", axis=0) for slots, _ in chosen]
            sums = gate_part(order[:middle], [[x[:middle]] for x in gathered], *weights)
            hidden = gate_part(order[middle:], [[x[middle:]] for x in gathered], *weights, sums)
            (partial,) = down_part([order], hidden, down_weight, width, len(chunk))
            for offset, share, (_, place) in zip(chunk, partial, chosen):
                share = lax.psum_scatter(share, "exp", scatter_dimension=0)
                piece = combine_slots(place, [share[None]])
                pieces.append(swapped(piece, "seq", offset, offset) if offset else piece)
    total = stream[:length].astype(F32)
    for piece in pieces:
        total = total + piece.astype(F32)
    return total.astype(BF16)


def paired_chunks(stream, select, weights, down_weight):
    plane = PairedPlane()
    width = stream.shape[1]
    tie = lax.optimization_barrier
    two, far_two, near, near_far, chosen = {}, {}, {}, {}, {}

    def across_middle(part):
        return lax.ppermute(part, "seq", [(1, 2), (2, 1)])

    def outward(part):
        return lax.ppermute(part, "seq", [(1, 0), (2, 3)])

    def gather(name, behind):
        pair = plane.first(chosen[name][0])
        near[name] = plane.across(pair)
        two[name], _ = tie((pair, behind))
        far_two[name] = plane.second(two[name])

    swap = swapped(stream, "seq", 1, 1)
    crossed = across_middle(stream)
    chosen["own"] = select(stream)
    gather("own", [])
    passed = outward(crossed)
    crossed_swap = across_middle(swap)
    chosen["neighbour"] = select(swap)
    gather("neighbour", [passed, crossed_swap, far_two["own"]])
    passed_fourth = outward(crossed_swap)
    chosen["third"] = select(crossed, passed)
    gather("third", [passed_fourth, far_two["neighbour"]])
    chosen["fourth"] = select(crossed_swap, passed_fourth)

    def gate(chunk, behind):
        early = [[two[name], near[name]] for name in chunk]
        return gate_part(plane.early, tie((early, behind))[0], *weights)

    def gate_last(chunk, sums, behind):
        late = [[far_two[name], near_far[name]] for name in chunk]
        (late, sums), _ = tie(((late, sums), behind))
        return gate_part(plane.late, late, *weights, sums)

    def down(plans, hidden, behind):
        hidden, _ = tie((hidden, behind))
        return down_part(plans, hidden, down_weight, width, 2)

    class Scatter:
        def __init__(self, name, theirs, mine):
            self.name, self.theirs, self.mine = name, theirs, mine

        def two_blocks(self, behind):
            self.near = plane.across(self.theirs)
            self.sent = added(self.mine[2:], self.near[2:])
            self.got_two = plane.second(tie((self.sent, behind))[0])

        def one_block(self, behind):
            got_two, _ = tie((self.got_two, behind))
            self.one = added(added(self.mine[1], self.near[1]), got_two[1])
            self.got_one = plane.once(self.one)

        def own_block(self, behind):
            got_one, _ = tie((self.got_one, behind))
            shares = [self.mine, self.near, self.got_two, got_one[None]]
            return combine_slots(chosen[self.name][1], shares)

    chunk = ("third", "neighbour")
    sums = gate(chunk, chosen["fourth"])
    gather("fourth", sums)
    for name in chunk:
        near_far[name] = plane.across(tie((far_two[name], sums))[0])
    hidden = gate_last(chunk, sums, two["fourth"])
    (theirs,) = down([plane.theirs], hidden, far_two["fourth"])
    (mine,) = down([plane.mine], hidden, theirs)
    third, neighbour = (Scatter(*shares) for shares in zip(chunk, theirs, mine))
    third.two_blocks([])

    chunk = ("fourth", "own")
    sums = gate(chunk, third.sent)
    for name in chunk:
        near_far[name] = plane.across(tie((far_two[name], third.sent))[0])
    third.one_block(sums)
    neighbour.two_blocks(third.one)
    hidden = gate_last(chunk, sums, [third.one, neighbour.sent])
    third_piece = third.own_block(hidden)
    third_home = lax.ppermute(third_piece, "seq", [(1, 2), (2, 1)])
    theirs, mine = down([plane.theirs, plane.mine], hidden, [third_piece, neighbour.got_two])
    neighbour.one_block(theirs)
    theirs, _ = tie((theirs, third_home))
    fourth, own = (Scatter(*shares) for shares in zip(chunk, theirs, mine))
    fourth.two_blocks([])
    third_piece, _ = tie((third_piece, [third_home, neighbour.one]))
    third_far_home = lax.ppermute(third_piece, "seq", [(0, 2), (3, 1)])
    neighbour_piece = neighbour.own_block([])
    neighbour_home = swapped(neighbour_piece, "seq", 1, 1)
    fourth.one_block([third_far_home, neighbour.got_one])
    own.two_blocks(fourth.got_two)
    fourth_piece = fourth.own_block([])
    own.one_block(fourth_piece)
    fourth_piece, _ = tie((fourth_piece, [third_far_home, neighbour_home]))
    return [
        own.own_block([]),
        neighbour_home,
        third_home,
        third_far_home,
        lax.ppermute(fourth_piece, "seq", [(1, 3), (2, 0)]),
        lax.ppermute(fourth_piece, "seq", [(0, 3), (3, 0)]),
    ]


def solution(mesh):
    in_specs = (
        P("seq", "exp"),
        P("seq", "exp"),
        P("seq", "exp"),
        P("exp", "seq"),
        P("seq", "exp"),
        P("exp"),
        P("seq", None),
        P(None, "seq"),
        P("seq", None, "exp"),
        P("seq", None, "exp"),
        P("seq", "exp", None),
    )
    out_specs = P("seq", "exp")
    return jax.shard_map(
        on_device, mesh=mesh, in_specs=in_specs, out_specs=out_specs, check_vma=False
    )
```

```python
import functools

import jax
import jax.numpy as jnp
from jax import lax
from jax.experimental import pallas as pl
from jax.experimental.pallas import tpu as pltpu
from jax.sharding import PartitionSpec as P

F32 = jnp.float32
BF16 = jnp.bfloat16
HIGHEST = lax.Precision.HIGHEST
VMEM_LIMIT = 32 * 1024 * 1024
ID_ROWS = 16


def in_hbm(array):
    return pltpu.with_memory_space_constraint(array, pltpu.HBM)


def lower_ones(length):
    rows = lax.broadcasted_iota(jnp.int32, (length, length), 0)
    columns = lax.broadcasted_iota(jnp.int32, (length, length), 1)
    return rows >= columns


def shifted(array, axis, by):
    count = lax.axis_size(axis)
    pairs = [(i, i + by) for i in range(count) if 0 <= i + by < count]
    return lax.ppermute(array, axis, pairs)


def state_kernel(key_ref, value_ref, decay_ref, message_ref, cumulative_ref):
    heads, length = decay_ref.shape
    size = key_ref.shape[1] // heads
    ones = lower_ones(length).astype(F32)
    cumulative = lax.dot_general(
        ones, decay_ref[...], (((1,), (1,)), ((), ())), precision=HIGHEST, preferred_element_type=F32
    )
    cumulative_ref[...] = cumulative
    last = cumulative[length - 1 : length, :]
    key_fade = jnp.exp(last - cumulative)
    message_ref[heads * size :, :] = jnp.zeros((message_ref.shape[0] - heads * size, size), BF16)
    half = (message_ref.shape[0] - heads * size) // 2
    rows = []
    for h in range(heads):
        columns = slice(h * size, (h + 1) * size)
        scaled = (key_fade[:, h : h + 1] * key_ref[:, columns].astype(F32)).astype(BF16)
        state = lax.dot_general(
            scaled, value_ref[:, columns], (((0,), (0,)), ((), ())), preferred_element_type=F32
        )
        message_ref[columns, :] = state.astype(BF16)
        rows.append(jnp.broadcast_to(jnp.exp(last[:, h : h + 1]), (1, size)))
    rows.append(jnp.zeros((half - heads, size), F32))
    fade = jnp.concatenate(rows, axis=0)
    leading = fade.astype(BF16)
    trailing = (fade - leading.astype(F32)).astype(BF16)
    message_ref[heads * size :, :] = jnp.concatenate([leading, trailing], axis=0)


def section_state(attn_key, attn_value, log_decay):
    heads, length = log_decay.shape
    width = attn_key.shape[1]
    half = -(-heads // 8) * 8
    return pl.pallas_call(
        state_kernel,
        out_shape=(
            jax.ShapeDtypeStruct((width + 2 * half, width // heads), BF16),
            jax.ShapeDtypeStruct((length, heads), F32),
        ),
        cost_estimate=pl.CostEstimate(
            flops=2 * length * width * (width // heads), bytes_accessed=4 * length * width, transcendentals=0
        ),
        compiler_params=pltpu.CompilerParams(vmem_limit_bytes=VMEM_LIMIT),
    )(in_hbm(attn_key), in_hbm(attn_value), in_hbm(log_decay))


def intra_kernel(query_ref, key_ref, value_ref, decay_ref, cumulative_ref, out_ref):
    heads, length = decay_ref.shape
    size = key_ref.shape[1] // heads
    causal = lower_ones(length)
    along = lax.dot_general(
        decay_ref[...],
        causal.astype(F32),
        (((1,), (1,)), ((), ())),
        precision=HIGHEST,
        preferred_element_type=F32,
    )
    for h in range(heads):
        columns = slice(h * size, (h + 1) * size)
        gap = jnp.where(causal, cumulative_ref[:, h : h + 1] - along[h : h + 1, :], 0.0)
        mask = jnp.where(causal, jnp.exp(gap), 0.0)
        scores = lax.dot_general(
            query_ref[:, columns], key_ref[:, columns], (((1,), (1,)), ((), ())), preferred_element_type=F32
        )
        weights = (scores * mask).astype(BF16)
        out_ref[:, columns] = jnp.dot(weights, value_ref[:, columns], preferred_element_type=F32)


def intra_section(attn_query, attn_key, attn_value, log_decay, cumulative):
    length, width = attn_query.shape
    return pl.pallas_call(
        intra_kernel,
        out_shape=jax.ShapeDtypeStruct((length, width), F32),
        cost_estimate=pl.CostEstimate(
            flops=4 * length * length * width, bytes_accessed=10 * length * width, transcendentals=0
        ),
        compiler_params=pltpu.CompilerParams(vmem_limit_bytes=VMEM_LIMIT),
    )(attn_query, attn_key, attn_value, log_decay, cumulative)


def stream_kernel(
    query_ref, intra_ref, cumulative_ref, incoming_ref, residual_ref, gain_ref, ids_ref, out_ref
):
    heads, size = incoming_ref.shape[0], incoming_ref.shape[1]
    length, width = residual_ref.shape
    choices = ids_ref.shape[0]
    below = jnp.concatenate(
        [
            ids_ref[...].astype(F32),
            jnp.zeros((ID_ROWS - choices, length), F32),
        ],
        axis=0,
    )
    out_ref[length:, :] = jnp.concatenate(
        [below, jnp.zeros((ID_ROWS, width - length), F32)], axis=1
    ).astype(BF16)
    faded = jnp.exp(cumulative_ref[...])
    for h in range(heads):
        columns = slice(h * size, (h + 1) * size)
        state = incoming_ref[h]
        leading = state.astype(BF16)
        trailing = (state - leading.astype(F32)).astype(BF16)
        query = query_ref[:, columns]
        inter = jnp.dot(query, leading, preferred_element_type=F32) + jnp.dot(
            query, trailing, preferred_element_type=F32
        )
        attn_out = intra_ref[:, columns] + faded[:, h : h + 1] * inter
        mean_square = jnp.mean(attn_out * attn_out, axis=1, keepdims=True)
        normed = attn_out * lax.rsqrt(mean_square + 1e-06)
        out_ref[:length, columns] = (
            residual_ref[:, columns].astype(F32) + gain_ref[:, columns].astype(F32) * normed
        ).astype(BF16)


def make_stream(attn_query, intra, cumulative, incoming, residual, norm_gain, ids):
    length, width = attn_query.shape
    return pl.pallas_call(
        stream_kernel,
        out_shape=jax.ShapeDtypeStruct((length + ID_ROWS, width), BF16),
        compiler_params=pltpu.CompilerParams(vmem_limit_bytes=VMEM_LIMIT),
    )(attn_query, intra, cumulative, incoming, residual, norm_gain.reshape(1, width), ids)


def read_message(message, heads):
    size = message.shape[1]
    half = (message.shape[0] - heads * size) // 2
    state = message[: heads * size].astype(F32).reshape(heads, size, size)
    tail = message[heads * size :].astype(F32)
    fade = tail[:heads] + tail[half : half + heads]
    return fade[:, None, :], state


def write_message(fade, state, rows):
    heads, size = state.shape[0], state.shape[1]
    half = (rows - heads * size) // 2
    leading = fade[:, 0, :].astype(BF16)
    trailing = (fade[:, 0, :] - leading.astype(F32)).astype(BF16)
    spare = jnp.zeros((half - heads, size), BF16)
    return jnp.concatenate(
        [state.astype(BF16).reshape(heads * size, size), leading, spare, trailing, spare], axis=0
    )


def incoming_state(message, heads):
    count = lax.axis_size("seq")
    window_fade, window = read_message(message, heads)
    incoming_fade, incoming = None, None
    distance = 1
    while distance < count:
        got_fade, got = read_message(shifted(message, "seq", distance), heads)
        if incoming is None:
            incoming_fade, incoming = got_fade, got
        else:
            incoming, incoming_fade = incoming + incoming_fade * got, incoming_fade * got_fade
        window, window_fade = window + window_fade * got, window_fade * got_fade
        distance *= 2
        if distance < count:
            message = write_message(window_fade, window, message.shape[0])
    return incoming


def select_kernel(capacity, choices, experts, base_ref, *refs):
    parts, (out_ref, place_ref) = refs[:-2], refs[-2:]
    length = parts[0].shape[0] - ID_ROWS
    part = parts[-1][...]
    for other in parts[:-1]:
        part = jnp.where(base_ref[1] > 0, other[...], part)
    before = lower_ones(length).astype(BF16)
    slot = lax.broadcasted_iota(jnp.int32, (capacity, length), 0).astype(F32)
    ids = part[length:, :length].astype(F32)
    rows = []
    for j in range(experts):
        expert = (base_ref[0] + j).astype(F32)
        chosen = ids[0:1, :] == expert
        for choice in range(1, choices):
            chosen = chosen | (ids[choice : choice + 1, :] == expert)
        flag = jnp.where(chosen, 1.0, 0.0)
        rank = lax.dot_general(
            jnp.broadcast_to(flag, (16, length)).astype(BF16),
            before,
            (((1,), (1,)), ((), ())),
            preferred_element_type=F32,
        )[0:1, :]
        rank = jnp.where(chosen, rank - 1.0, -1.0)
        rows.append(jnp.where(slot == rank, 1.0, 0.0).astype(BF16))
    place = jnp.concatenate(rows, axis=0)
    place_ref[...] = place
    out_ref[...] = lax.dot_general(
        part[:length, :], place, (((0,), (1,)), ((), ())), preferred_element_type=F32
    ).astype(BF16)


def select_slots(base, parts, capacity, choices, experts):
    rows, width = parts[0].shape
    length = rows - ID_ROWS
    slots = experts * capacity
    whole = pl.BlockSpec((rows, width), lambda _: (0, 0))
    return pl.pallas_call(
        functools.partial(select_kernel, capacity, choices, experts),
        grid=(1,),
        in_specs=[pl.BlockSpec(memory_space=pltpu.SMEM), *([whole] * len(parts))],
        out_shape=(
            jax.ShapeDtypeStruct((width, slots), BF16),
            jax.ShapeDtypeStruct((slots, length), BF16),
        ),
        cost_estimate=pl.CostEstimate(
            flops=2 * slots * length * width, bytes_accessed=4 * slots * width, transcendentals=0
        ),
        compiler_params=pltpu.CompilerParams(vmem_limit_bytes=VMEM_LIMIT),
    )(base, *parts)


def combine_kernel(place_ref, *refs):
    shares, out_ref = refs[:-1], refs[-1]
    total = shares[0][0].astype(F32)
    for share in shares[1:]:
        total = total + share[0].astype(F32)
    out_ref[...] = lax.dot_general(
        place_ref[...], total.astype(BF16), (((0,), (0,)), ((), ())), preferred_element_type=F32
    ).astype(BF16)


def combine_slots(place, shares):
    slots, length = place.shape
    width = shares[0].shape[2]
    first = pl.BlockSpec((1, slots, width), lambda _: (0, 0, 0))
    return pl.pallas_call(
        combine_kernel,
        grid=(1,),
        in_specs=[pl.BlockSpec(memory_space=pltpu.VMEM), *([first] * len(shares))],
        out_shape=jax.ShapeDtypeStruct((length, width), BF16),
        cost_estimate=pl.CostEstimate(
            flops=2 * slots * length * width, bytes_accessed=8 * slots * width, transcendentals=0
        ),
        compiler_params=pltpu.CompilerParams(vmem_limit_bytes=VMEM_LIMIT),
    )(place, *shares)


def gate_kernel(counts, sections, last, plan_ref, *refs):
    step = pl.program_id(0)
    blocks = sum(counts)
    used = len(counts) * sections
    x_refs, refs = refs[:used], refs[used:]
    router_ref, gate_ref, up_ref = refs[:3]
    refs = refs[3:]
    if last:
        gate_in, up_in, score_in, hidden_ref, gate_acc, up_acc, score_acc = refs
    else:
        gate_acc, up_acc, score_acc = refs
    experts = gate_ref.shape[0]
    width = x_refs[0].shape[1]
    slots = gate_acc.shape[2]
    part = slots // sections

    @pl.when(step == 0)
    def _():
        if last:
            gate_acc[...] = gate_in[...]
            up_acc[...] = up_in[...]
            score_acc[...] = score_in[...]
        else:
            gate_acc[...] = jnp.zeros_like(gate_acc)
            up_acc[...] = jnp.zeros_like(up_acc)
            score_acc[...] = jnp.zeros_like(score_acc)

    xs = []
    for section in range(sections):
        mine = x_refs[section * len(counts) : (section + 1) * len(counts)]
        x = mine[-1][0]
        for i in range(len(counts) - 2, -1, -1):
            x = jnp.where(step < sum(counts[: i + 1]), mine[i][0], x)
        xs.append(x)
    for j in range(experts):
        x = jnp.concatenate([x[:, j * part : (j + 1) * part] for x in xs], axis=1)
        score_acc[j] += jnp.dot(router_ref[0], x, preferred_element_type=F32)
        gate_acc[j] += jnp.dot(gate_ref[j], x, preferred_element_type=F32)
        up_acc[j] += jnp.dot(up_ref[j], x, preferred_element_type=F32)

    if last:

        @pl.when(step == blocks - 1)
        def _():
            for j in range(experts):
                score = score_acc[j, j : j + 1, :]
                gate = gate_acc[j]
                routed = gate / (1.0 + jnp.exp(-gate)) * up_acc[j]
                routed = routed / (1.0 + jnp.exp(-score))
                hidden_ref[j] = routed.T.astype(BF16)


def gate_part(plan, xs, router_rows, gate_rows, up_rows, sums=None):
    counts = tuple(x.shape[0] for x in xs[0])
    blocks = sum(counts)
    _, width, total = xs[0][0].shape
    experts, units, _ = gate_rows.shape
    slots = total // experts * len(xs)
    whole = pl.BlockSpec(memory_space=pltpu.VMEM)
    last = sums is not None

    def x_spec(i):
        before = sum(counts[:i])
        return pl.BlockSpec(
            (1, width, total), lambda p, plan: (jnp.clip(p - before, 0, counts[i] - 1), 0, 0)
        )

    weight_spec = pl.BlockSpec((experts, units, width), lambda p, plan: (0, 0, plan[p]))
    sum_shapes = [(experts, units, slots), (experts, units, slots), (experts, experts, slots)]
    sum_specs = [pl.BlockSpec(shape, lambda p, plan: (0, 0, 0)) for shape in sum_shapes]
    if last:
        out_shape = jax.ShapeDtypeStruct((experts, slots, units), BF16)
        out_specs = whole
        scratch = [pltpu.VMEM(shape, F32) for shape in sum_shapes]
    else:
        out_shape = tuple(jax.ShapeDtypeStruct(shape, F32) for shape in sum_shapes)
        out_specs = tuple(sum_specs)
        scratch = []
    return pl.pallas_call(
        functools.partial(gate_kernel, counts, len(xs), last),
        grid_spec=pltpu.PrefetchScalarGridSpec(
            num_scalar_prefetch=1,
            grid=(blocks,),
            in_specs=[
                *[x_spec(i) for _ in xs for i in range(len(counts))],
                pl.BlockSpec((1, experts, width), lambda p, plan: (plan[p], 0, 0)),
                weight_spec,
                weight_spec,
                *(sum_specs if last else []),
            ],
            out_specs=out_specs,
            scratch_shapes=scratch,
        ),
        out_shape=out_shape,
        cost_estimate=pl.CostEstimate(
            flops=4 * experts * slots * blocks * width * units,
            bytes_accessed=4 * experts * blocks * width * units,
            transcendentals=0,
        ),
        compiler_params=pltpu.CompilerParams(vmem_limit_bytes=VMEM_LIMIT),
    )(
        plan,
        *[x for section in xs for x in section],
        router_rows,
        in_hbm(gate_rows),
        in_hbm(up_rows),
        *(sums or ()),
    )


def down_kernel(blocks, sections, plan_ref, hidden_ref, down_ref, *out_refs):
    experts, slots, _ = hidden_ref.shape
    part = slots // sections
    turn = pl.program_id(0) // blocks
    for j in range(experts):
        share = jnp.dot(hidden_ref[j], down_ref[j], preferred_element_type=F32).astype(BF16)
        for i in range(len(out_refs) // sections):

            @pl.when(turn == i)
            def _():
                for section in range(sections):
                    out_ref = out_refs[i * sections + section]
                    out_ref[0, j * part : (j + 1) * part, :] = share[
                        section * part : (section + 1) * part
                    ]


def down_part(plans, hidden, down_weight, width, sections):
    blocks = plans[0].shape[0]
    experts, slots, units = hidden.shape
    rows = experts * slots // sections

    def out_spec(i):
        return pl.BlockSpec(
            (1, rows, width), lambda p, plan: (jnp.clip(p - i * blocks, 0, blocks - 1), 0, 0)
        )

    out = pl.pallas_call(
        functools.partial(down_kernel, blocks, sections),
        grid_spec=pltpu.PrefetchScalarGridSpec(
            num_scalar_prefetch=1,
            grid=(len(plans) * blocks,),
            in_specs=[
                pl.BlockSpec(hidden.shape, lambda p, plan: (0, 0, 0)),
                pl.BlockSpec((experts, units, width), lambda p, plan: (0, 0, plan[p])),
            ],
            out_specs=[out_spec(i) for i in range(len(plans)) for _ in range(sections)],
        ),
        out_shape=[jax.ShapeDtypeStruct((blocks, rows, width), BF16)] * (len(plans) * sections),
        cost_estimate=pl.CostEstimate(
            flops=2 * experts * slots * len(plans) * blocks * width * units,
            bytes_accessed=2 * experts * len(plans) * blocks * width * units,
            transcendentals=0,
        ),
        compiler_params=pltpu.CompilerParams(vmem_limit_bytes=VMEM_LIMIT),
    )(jnp.concatenate(plans), hidden, in_hbm(down_weight))
    return [out[i * sections : (i + 1) * sections] for i in range(len(plans))]


def added(left, right):
    return (left.astype(F32) + right.astype(F32)).astype(BF16)


def swapped(array, axis, even, odd):
    count = lax.axis_size(axis)
    pairs = [(i, i ^ (odd if i % 2 else even)) for i in range(count)]
    return lax.ppermute(array, axis, pairs)


class PairedPlane:
    def __init__(self):
        me = lax.axis_index("exp").astype(jnp.int32)
        other = me ^ 1
        near = jnp.where(me % 2 == 0, 2, 4)
        far = 6 - near
        self.early = jnp.stack([me, me ^ near, other, other ^ far])
        self.late = jnp.stack([me ^ far, me ^ 6, other ^ near, other ^ 6])
        self.mine = jnp.stack([me, me ^ near, me ^ far, me ^ 6])
        self.theirs = jnp.stack([other, other ^ far, other ^ near, other ^ 6])

    def once(self, part):
        return swapped(part, "exp", 2, 4)

    def first(self, part):
        return jnp.stack([part, self.once(part)])

    def second(self, two):
        return swapped(two, "exp", 4, 2)

    def across(self, two):
        return swapped(two, "exp", 1, 1)

def on_device(
    attn_query,
    attn_key,
    attn_value,
    log_decay,
    residual,
    norm_gain,
    expert_ids,
    router_weight,
    gate_weight,
    up_weight,
    down_weight,
):
    heads_here, length = log_decay.shape
    groups = lax.axis_size("seq")
    shares = lax.axis_size("exp")
    width = attn_query.shape[1]
    experts_here = router_weight.shape[1]
    section = lax.axis_index("seq")
    inner = (section > 0) & (section < groups - 1)
    base = jnp.stack([section * experts_here, inner]).astype(jnp.int32)
    router_rows = router_weight.reshape(shares, width, experts_here).transpose(0, 2, 1)
    gate_rows = gate_weight.swapaxes(1, 2)
    up_rows = up_weight.swapaxes(1, 2)

    message, cumulative = section_state(attn_key, attn_value, log_decay)
    intra = intra_section(attn_query, attn_key, attn_value, log_decay, cumulative)
    incoming = incoming_state(message, heads_here)
    stream = make_stream(
        attn_query, intra, cumulative, incoming, residual, norm_gain, expert_ids.T
    )

    capacity = 4 * length // (experts_here * groups)
    choices = expert_ids.shape[1]

    def select(*parts):
        return select_slots(base, parts, capacity, choices, experts_here)

    weights = (router_rows, gate_rows, up_rows)
    if shares == 8 and groups == 4:
        pieces = paired_chunks(stream, select, weights, down_weight)
    else:
        order = jnp.arange(shares, dtype=jnp.int32)
        middle = shares // 2
        pieces = []
        for first in range(0, groups, 2):
            chunk = (first, first + 1)
            chosen = [
                select(swapped(stream, "seq", offset, offset) if offset else stream)
                for offset in chunk
            ]
            gathered = [lax.all_gather(slots, "exp", axis=0) for slots, _ in chosen]
            sums = gate_part(order[:middle], [[x[:middle]] for x in gathered], *weights)
            hidden = gate_part(order[middle:], [[x[middle:]] for x in gathered], *weights, sums)
            (partial,) = down_part([order], hidden, down_weight, width, len(chunk))
            for offset, share, (_, place) in zip(chunk, partial, chosen):
                share = lax.psum_scatter(share, "exp", scatter_dimension=0)
                piece = combine_slots(place, [share[None]])
                pieces.append(swapped(piece, "seq", offset, offset) if offset else piece)
    total = stream[:length].astype(F32)
    for piece in pieces:
        total = total + piece.astype(F32)
    return total.astype(BF16)


def paired_chunks(stream, select, weights, down_weight):
    plane = PairedPlane()
    width = stream.shape[1]
    tie = lax.optimization_barrier
    two, far_two, near, near_far, chosen = {}, {}, {}, {}, {}

    def across_middle(part):
        return lax.ppermute(part, "seq", [(1, 2), (2, 1)])

    def outward(part):
        return lax.ppermute(part, "seq", [(1, 0), (2, 3)])

    def gather(name, behind):
        two[name], _ = tie((plane.first(chosen[name][0]), behind))
        near[name] = plane.across(two[name])
        far_two[name] = plane.second(two[name])

    swap = swapped(stream, "seq", 1, 1)
    crossed = across_middle(stream)
    chosen["own"] = select(stream)
    gather("own", [])
    passed = outward(crossed)
    crossed_swap = across_middle(swap)
    chosen["neighbour"] = select(swap)
    gather("neighbour", [passed, crossed_swap, far_two["own"]])
    passed_fourth = outward(crossed_swap)
    chosen["third"] = select(crossed, passed)
    gather("third", [passed_fourth, far_two["neighbour"]])
    chosen["fourth"] = select(crossed_swap, passed_fourth)

    def gate(chunk, behind):
        early = [[two[name], near[name]] for name in chunk]
        return gate_part(plane.early, tie((early, behind))[0], *weights)

    def gate_last(chunk, sums, behind):
        late = [[far_two[name], near_far[name]] for name in chunk]
        (late, sums), _ = tie(((late, sums), behind))
        return gate_part(plane.late, late, *weights, sums)

    def down(plans, hidden, behind):
        hidden, _ = tie((hidden, behind))
        return down_part(plans, hidden, down_weight, width, 2)

    class Scatter:
        def __init__(self, name, theirs, mine):
            self.name, self.theirs, self.mine = name, theirs, mine

        def two_blocks(self, behind):
            self.near = plane.across(self.theirs)
            self.sent = added(self.mine[2:], self.near[2:])
            self.got_two = plane.second(tie((self.sent, behind))[0])

        def one_block(self, behind):
            got_two, _ = tie((self.got_two, behind))
            self.one = added(added(self.mine[1], self.near[1]), got_two[1])
            self.got_one = plane.once(self.one)

        def own_block(self, behind):
            got_one, _ = tie((self.got_one, behind))
            shares = [self.mine, self.near, self.got_two, got_one[None]]
            return combine_slots(chosen[self.name][1], shares)

    chunk = ("third", "neighbour")
    sums = gate(chunk, chosen["fourth"])
    gather("fourth", sums)
    for name in chunk:
        near_far[name] = plane.across(tie((far_two[name], sums))[0])
    hidden = gate_last(chunk, sums, two["fourth"])
    (theirs,) = down([plane.theirs], hidden, far_two["fourth"])
    (mine,) = down([plane.mine], hidden, theirs)
    third, neighbour = (Scatter(*shares) for shares in zip(chunk, theirs, mine))
    third.two_blocks([])

    chunk = ("fourth", "own")
    sums = gate(chunk, third.sent)
    for name in chunk:
        near_far[name] = plane.across(tie((far_two[name], third.sent))[0])
    third.one_block(sums)
    neighbour.two_blocks(third.one)
    hidden = gate_last(chunk, sums, [third.one, neighbour.sent])
    third_piece = third.own_block(hidden)
    third_home = lax.ppermute(third_piece, "seq", [(1, 2), (2, 1)])
    theirs, mine = down([plane.theirs, plane.mine], hidden, [third_piece, neighbour.got_two])
    neighbour.one_block(theirs)
    theirs, _ = tie((theirs, third_home))
    fourth, own = (Scatter(*shares) for shares in zip(chunk, theirs, mine))
    fourth.two_blocks([])
    third_far_home = lax.ppermute(tie((third_piece, third_home))[0], "seq", [(0, 2), (3, 1)])
    neighbour_piece = neighbour.own_block([])
    neighbour_home = swapped(neighbour_piece, "seq", 1, 1)
    fourth.one_block([third_far_home, neighbour.got_one])
    own.two_blocks(fourth.got_two)
    fourth_piece = fourth.own_block([])
    own.one_block(fourth_piece)
    fourth_piece, _ = tie((fourth_piece, [third_far_home, neighbour_home]))
    return [
        own.own_block([]),
        neighbour_home,
        third_home,
        third_far_home,
        lax.ppermute(fourth_piece, "seq", [(1, 3), (2, 0)]),
        lax.ppermute(fourth_piece, "seq", [(0, 3), (3, 0)]),
    ]


def solution(mesh):
    in_specs = (
        P("seq", "exp"),
        P("seq", "exp"),
        P("seq", "exp"),
        P("exp", "seq"),
        P("seq", "exp"),
        P("exp"),
        P("seq", None),
        P(None, "seq"),
        P("seq", None, "exp"),
        P("seq", None, "exp"),
        P("seq", "exp", None),
    )
    out_specs = P("seq", "exp")
    return jax.shard_map(
        on_device, mesh=mesh, in_specs=in_specs, out_specs=out_specs, check_vma=False
    )
```

```python
import functools

import jax
import jax.numpy as jnp
from jax import lax
from jax.experimental import pallas as pl
from jax.experimental.pallas import tpu as pltpu
from jax.sharding import PartitionSpec as P

F32 = jnp.float32
BF16 = jnp.bfloat16
HIGHEST = lax.Precision.HIGHEST
VMEM_LIMIT = 32 * 1024 * 1024
ID_ROWS = 16


def in_hbm(array):
    return pltpu.with_memory_space_constraint(array, pltpu.HBM)


def lower_ones(length):
    rows = lax.broadcasted_iota(jnp.int32, (length, length), 0)
    columns = lax.broadcasted_iota(jnp.int32, (length, length), 1)
    return rows >= columns


def shifted(array, axis, by):
    count = lax.axis_size(axis)
    pairs = [(i, i + by) for i in range(count) if 0 <= i + by < count]
    return lax.ppermute(array, axis, pairs)


def state_kernel(key_ref, value_ref, decay_ref, message_ref, cumulative_ref):
    heads, length = decay_ref.shape
    size = key_ref.shape[1] // heads
    ones = lower_ones(length).astype(F32)
    cumulative = lax.dot_general(
        ones, decay_ref[...], (((1,), (1,)), ((), ())), precision=HIGHEST, preferred_element_type=F32
    )
    cumulative_ref[...] = cumulative
    last = cumulative[length - 1 : length, :]
    key_fade = jnp.exp(last - cumulative)
    message_ref[heads * size :, :] = jnp.zeros((message_ref.shape[0] - heads * size, size), BF16)
    half = (message_ref.shape[0] - heads * size) // 2
    rows = []
    for h in range(heads):
        columns = slice(h * size, (h + 1) * size)
        scaled = (key_fade[:, h : h + 1] * key_ref[:, columns].astype(F32)).astype(BF16)
        state = lax.dot_general(
            scaled, value_ref[:, columns], (((0,), (0,)), ((), ())), preferred_element_type=F32
        )
        message_ref[columns, :] = state.astype(BF16)
        rows.append(jnp.broadcast_to(jnp.exp(last[:, h : h + 1]), (1, size)))
    rows.append(jnp.zeros((half - heads, size), F32))
    fade = jnp.concatenate(rows, axis=0)
    leading = fade.astype(BF16)
    trailing = (fade - leading.astype(F32)).astype(BF16)
    message_ref[heads * size :, :] = jnp.concatenate([leading, trailing], axis=0)


def section_state(attn_key, attn_value, log_decay):
    heads, length = log_decay.shape
    width = attn_key.shape[1]
    half = -(-heads // 8) * 8
    return pl.pallas_call(
        state_kernel,
        out_shape=(
            jax.ShapeDtypeStruct((width + 2 * half, width // heads), BF16),
            jax.ShapeDtypeStruct((length, heads), F32),
        ),
        cost_estimate=pl.CostEstimate(
            flops=2 * length * width * (width // heads), bytes_accessed=4 * length * width, transcendentals=0
        ),
        compiler_params=pltpu.CompilerParams(vmem_limit_bytes=VMEM_LIMIT),
    )(in_hbm(attn_key), in_hbm(attn_value), in_hbm(log_decay))


def intra_kernel(query_ref, key_ref, value_ref, decay_ref, cumulative_ref, out_ref):
    heads, length = decay_ref.shape
    size = key_ref.shape[1] // heads
    causal = lower_ones(length)
    along = lax.dot_general(
        decay_ref[...],
        causal.astype(F32),
        (((1,), (1,)), ((), ())),
        precision=HIGHEST,
        preferred_element_type=F32,
    )
    for h in range(heads):
        columns = slice(h * size, (h + 1) * size)
        gap = jnp.where(causal, cumulative_ref[:, h : h + 1] - along[h : h + 1, :], 0.0)
        mask = jnp.where(causal, jnp.exp(gap), 0.0)
        scores = lax.dot_general(
            query_ref[:, columns], key_ref[:, columns], (((1,), (1,)), ((), ())), preferred_element_type=F32
        )
        weights = (scores * mask).astype(BF16)
        out_ref[:, columns] = jnp.dot(weights, value_ref[:, columns], preferred_element_type=F32)


def intra_section(attn_query, attn_key, attn_value, log_decay, cumulative):
    length, width = attn_query.shape
    return pl.pallas_call(
        intra_kernel,
        out_shape=jax.ShapeDtypeStruct((length, width), F32),
        cost_estimate=pl.CostEstimate(
            flops=4 * length * length * width, bytes_accessed=10 * length * width, transcendentals=0
        ),
        compiler_params=pltpu.CompilerParams(vmem_limit_bytes=VMEM_LIMIT),
    )(attn_query, attn_key, attn_value, log_decay, cumulative)


def stream_kernel(
    query_ref, intra_ref, cumulative_ref, incoming_ref, residual_ref, gain_ref, ids_ref, out_ref
):
    heads, size = incoming_ref.shape[0], incoming_ref.shape[1]
    length, width = residual_ref.shape
    choices = ids_ref.shape[0]
    below = jnp.concatenate(
        [
            ids_ref[...].astype(F32),
            jnp.zeros((ID_ROWS - choices, length), F32),
        ],
        axis=0,
    )
    out_ref[length:, :] = jnp.concatenate(
        [below, jnp.zeros((ID_ROWS, width - length), F32)], axis=1
    ).astype(BF16)
    faded = jnp.exp(cumulative_ref[...])
    for h in range(heads):
        columns = slice(h * size, (h + 1) * size)
        state = incoming_ref[h]
        leading = state.astype(BF16)
        trailing = (state - leading.astype(F32)).astype(BF16)
        query = query_ref[:, columns]
        inter = jnp.dot(query, leading, preferred_element_type=F32) + jnp.dot(
            query, trailing, preferred_element_type=F32
        )
        attn_out = intra_ref[:, columns] + faded[:, h : h + 1] * inter
        mean_square = jnp.mean(attn_out * attn_out, axis=1, keepdims=True)
        normed = attn_out * lax.rsqrt(mean_square + 1e-06)
        out_ref[:length, columns] = (
            residual_ref[:, columns].astype(F32) + gain_ref[:, columns].astype(F32) * normed
        ).astype(BF16)


def make_stream(attn_query, intra, cumulative, incoming, residual, norm_gain, ids):
    length, width = attn_query.shape
    return pl.pallas_call(
        stream_kernel,
        out_shape=jax.ShapeDtypeStruct((length + ID_ROWS, width), BF16),
        compiler_params=pltpu.CompilerParams(vmem_limit_bytes=VMEM_LIMIT),
    )(attn_query, intra, cumulative, incoming, residual, norm_gain.reshape(1, width), ids)


def read_message(message, heads):
    size = message.shape[1]
    half = (message.shape[0] - heads * size) // 2
    state = message[: heads * size].astype(F32).reshape(heads, size, size)
    tail = message[heads * size :].astype(F32)
    fade = tail[:heads] + tail[half : half + heads]
    return fade[:, None, :], state


def write_message(fade, state, rows):
    heads, size = state.shape[0], state.shape[1]
    half = (rows - heads * size) // 2
    leading = fade[:, 0, :].astype(BF16)
    trailing = (fade[:, 0, :] - leading.astype(F32)).astype(BF16)
    spare = jnp.zeros((half - heads, size), BF16)
    return jnp.concatenate(
        [state.astype(BF16).reshape(heads * size, size), leading, spare, trailing, spare], axis=0
    )


def incoming_state(message, heads):
    count = lax.axis_size("seq")
    window_fade, window = read_message(message, heads)
    incoming_fade, incoming = None, None
    distance = 1
    while distance < count:
        got_fade, got = read_message(shifted(message, "seq", distance), heads)
        if incoming is None:
            incoming_fade, incoming = got_fade, got
        else:
            incoming, incoming_fade = incoming + incoming_fade * got, incoming_fade * got_fade
        window, window_fade = window + window_fade * got, window_fade * got_fade
        distance *= 2
        if distance < count:
            message = write_message(window_fade, window, message.shape[0])
    return incoming


def select_kernel(capacity, choices, experts, base_ref, *refs):
    parts, (out_ref, place_ref) = refs[:-2], refs[-2:]
    length = parts[0].shape[0] - ID_ROWS
    part = parts[-1][...]
    for other in parts[:-1]:
        part = jnp.where(base_ref[1] > 0, other[...], part)
    before = lower_ones(length).astype(BF16)
    slot = lax.broadcasted_iota(jnp.int32, (capacity, length), 0).astype(F32)
    ids = part[length:, :length].astype(F32)
    rows = []
    for j in range(experts):
        expert = (base_ref[0] + j).astype(F32)
        chosen = ids[0:1, :] == expert
        for choice in range(1, choices):
            chosen = chosen | (ids[choice : choice + 1, :] == expert)
        flag = jnp.where(chosen, 1.0, 0.0)
        rank = lax.dot_general(
            jnp.broadcast_to(flag, (16, length)).astype(BF16),
            before,
            (((1,), (1,)), ((), ())),
            preferred_element_type=F32,
        )[0:1, :]
        rank = jnp.where(chosen, rank - 1.0, -1.0)
        rows.append(jnp.where(slot == rank, 1.0, 0.0).astype(BF16))
    place = jnp.concatenate(rows, axis=0)
    place_ref[...] = place
    out_ref[...] = lax.dot_general(
        part[:length, :], place, (((0,), (1,)), ((), ())), preferred_element_type=F32
    ).astype(BF16)


def select_slots(base, parts, capacity, choices, experts):
    rows, width = parts[0].shape
    length = rows - ID_ROWS
    slots = experts * capacity
    whole = pl.BlockSpec(memory_space=pltpu.VMEM)
    return pl.pallas_call(
        functools.partial(select_kernel, capacity, choices, experts),
        in_specs=[pl.BlockSpec(memory_space=pltpu.SMEM), *([whole] * len(parts))],
        out_shape=(
            jax.ShapeDtypeStruct((width, slots), BF16),
            jax.ShapeDtypeStruct((slots, length), BF16),
        ),
        cost_estimate=pl.CostEstimate(
            flops=2 * slots * length * width, bytes_accessed=4 * slots * width, transcendentals=0
        ),
        compiler_params=pltpu.CompilerParams(vmem_limit_bytes=VMEM_LIMIT),
    )(base, *parts)


def combine_kernel(place_ref, *refs):
    shares, out_ref = refs[:-1], refs[-1]
    total = shares[0][0].astype(F32)
    for share in shares[1:]:
        total = total + share[0].astype(F32)
    out_ref[...] = lax.dot_general(
        place_ref[...], total.astype(BF16), (((0,), (0,)), ((), ())), preferred_element_type=F32
    ).astype(BF16)


def combine_slots(place, shares):
    slots, length = place.shape
    width = shares[0].shape[2]
    first = pl.BlockSpec((1, slots, width), lambda _: (0, 0, 0))
    return pl.pallas_call(
        combine_kernel,
        grid=(1,),
        in_specs=[pl.BlockSpec(memory_space=pltpu.VMEM), *([first] * len(shares))],
        out_shape=jax.ShapeDtypeStruct((length, width), BF16),
        cost_estimate=pl.CostEstimate(
            flops=2 * slots * length * width, bytes_accessed=8 * slots * width, transcendentals=0
        ),
        compiler_params=pltpu.CompilerParams(vmem_limit_bytes=VMEM_LIMIT),
    )(place, *shares)


def gate_kernel(counts, sections, last, plan_ref, *refs):
    step = pl.program_id(0)
    blocks = sum(counts)
    used = len(counts) * sections
    x_refs, refs = refs[:used], refs[used:]
    router_ref, gate_ref, up_ref = refs[:3]
    refs = refs[3:]
    if last:
        gate_in, up_in, score_in, hidden_ref, gate_acc, up_acc, score_acc = refs
    else:
        gate_acc, up_acc, score_acc = refs
    experts = gate_ref.shape[0]
    width = x_refs[0].shape[1]
    slots = gate_acc.shape[2]
    part = slots // sections

    @pl.when(step == 0)
    def _():
        if last:
            gate_acc[...] = gate_in[...]
            up_acc[...] = up_in[...]
            score_acc[...] = score_in[...]
        else:
            gate_acc[...] = jnp.zeros_like(gate_acc)
            up_acc[...] = jnp.zeros_like(up_acc)
            score_acc[...] = jnp.zeros_like(score_acc)

    xs = []
    for section in range(sections):
        mine = x_refs[section * len(counts) : (section + 1) * len(counts)]
        x = mine[-1][0]
        for i in range(len(counts) - 2, -1, -1):
            x = jnp.where(step < sum(counts[: i + 1]), mine[i][0], x)
        xs.append(x)
    for j in range(experts):
        x = jnp.concatenate([x[:, j * part : (j + 1) * part] for x in xs], axis=1)
        score_acc[j] += jnp.dot(router_ref[0], x, preferred_element_type=F32)
        gate_acc[j] += jnp.dot(gate_ref[j], x, preferred_element_type=F32)
        up_acc[j] += jnp.dot(up_ref[j], x, preferred_element_type=F32)

    if last:

        @pl.when(step == blocks - 1)
        def _():
            for j in range(experts):
                score = score_acc[j, j : j + 1, :]
                gate = gate_acc[j]
                routed = gate / (1.0 + jnp.exp(-gate)) * up_acc[j]
                routed = routed / (1.0 + jnp.exp(-score))
                hidden_ref[j] = routed.T.astype(BF16)


def gate_part(plan, xs, router_rows, gate_rows, up_rows, sums=None):
    counts = tuple(x.shape[0] for x in xs[0])
    blocks = sum(counts)
    _, width, total = xs[0][0].shape
    experts, units, _ = gate_rows.shape
    slots = total // experts * len(xs)
    whole = pl.BlockSpec(memory_space=pltpu.VMEM)
    last = sums is not None

    def x_spec(i):
        before = sum(counts[:i])
        return pl.BlockSpec(
            (1, width, total), lambda p, plan: (jnp.clip(p - before, 0, counts[i] - 1), 0, 0)
        )

    weight_spec = pl.BlockSpec((experts, units, width), lambda p, plan: (0, 0, plan[p]))
    sum_shapes = [(experts, units, slots), (experts, units, slots), (experts, experts, slots)]
    sum_specs = [pl.BlockSpec(shape, lambda p, plan: (0, 0, 0)) for shape in sum_shapes]
    if last:
        out_shape = jax.ShapeDtypeStruct((experts, slots, units), BF16)
        out_specs = whole
        scratch = [pltpu.VMEM(shape, F32) for shape in sum_shapes]
    else:
        out_shape = tuple(jax.ShapeDtypeStruct(shape, F32) for shape in sum_shapes)
        out_specs = tuple(sum_specs)
        scratch = []
    return pl.pallas_call(
        functools.partial(gate_kernel, counts, len(xs), last),
        grid_spec=pltpu.PrefetchScalarGridSpec(
            num_scalar_prefetch=1,
            grid=(blocks,),
            in_specs=[
                *[x_spec(i) for _ in xs for i in range(len(counts))],
                pl.BlockSpec((1, experts, width), lambda p, plan: (plan[p], 0, 0)),
                weight_spec,
                weight_spec,
                *(sum_specs if last else []),
            ],
            out_specs=out_specs,
            scratch_shapes=scratch,
        ),
        out_shape=out_shape,
        cost_estimate=pl.CostEstimate(
            flops=4 * experts * slots * blocks * width * units,
            bytes_accessed=4 * experts * blocks * width * units,
            transcendentals=0,
        ),
        compiler_params=pltpu.CompilerParams(vmem_limit_bytes=VMEM_LIMIT),
    )(
        plan,
        *[x for section in xs for x in section],
        router_rows,
        in_hbm(gate_rows),
        in_hbm(up_rows),
        *(sums or ()),
    )


def down_kernel(blocks, sections, plan_ref, hidden_ref, down_ref, *out_refs):
    experts, slots, _ = hidden_ref.shape
    part = slots // sections
    turn = pl.program_id(0) // blocks
    for j in range(experts):
        share = jnp.dot(hidden_ref[j], down_ref[j], preferred_element_type=F32).astype(BF16)
        for i in range(len(out_refs) // sections):

            @pl.when(turn == i)
            def _():
                for section in range(sections):
                    out_ref = out_refs[i * sections + section]
                    out_ref[0, j * part : (j + 1) * part, :] = share[
                        section * part : (section + 1) * part
                    ]


def down_part(plans, hidden, down_weight, width, sections):
    blocks = plans[0].shape[0]
    experts, slots, units = hidden.shape
    rows = experts * slots // sections

    def out_spec(i):
        return pl.BlockSpec(
            (1, rows, width), lambda p, plan: (jnp.clip(p - i * blocks, 0, blocks - 1), 0, 0)
        )

    out = pl.pallas_call(
        functools.partial(down_kernel, blocks, sections),
        grid_spec=pltpu.PrefetchScalarGridSpec(
            num_scalar_prefetch=1,
            grid=(len(plans) * blocks,),
            in_specs=[
                pl.BlockSpec(memory_space=pltpu.VMEM),
                pl.BlockSpec((experts, units, width), lambda p, plan: (0, 0, plan[p])),
            ],
            out_specs=[out_spec(i) for i in range(len(plans)) for _ in range(sections)],
        ),
        out_shape=[jax.ShapeDtypeStruct((blocks, rows, width), BF16)] * (len(plans) * sections),
        cost_estimate=pl.CostEstimate(
            flops=2 * experts * slots * len(plans) * blocks * width * units,
            bytes_accessed=2 * experts * len(plans) * blocks * width * units,
            transcendentals=0,
        ),
        compiler_params=pltpu.CompilerParams(vmem_limit_bytes=VMEM_LIMIT),
    )(jnp.concatenate(plans), hidden, in_hbm(down_weight))
    return [out[i * sections : (i + 1) * sections] for i in range(len(plans))]


def added(left, right):
    return (left.astype(F32) + right.astype(F32)).astype(BF16)


def swapped(array, axis, even, odd):
    count = lax.axis_size(axis)
    pairs = [(i, i ^ (odd if i % 2 else even)) for i in range(count)]
    return lax.ppermute(array, axis, pairs)


class PairedPlane:
    def __init__(self):
        me = lax.axis_index("exp").astype(jnp.int32)
        other = me ^ 1
        near = jnp.where(me % 2 == 0, 2, 4)
        far = 6 - near
        self.early = jnp.stack([me, me ^ near, other, other ^ far])
        self.late = jnp.stack([me ^ far, me ^ 6, other ^ near, other ^ 6])
        self.mine = jnp.stack([me, me ^ near, me ^ far, me ^ 6])
        self.theirs = jnp.stack([other, other ^ far, other ^ near, other ^ 6])

    def once(self, part):
        return swapped(part, "exp", 2, 4)

    def first(self, part):
        return jnp.stack([part, self.once(part)])

    def second(self, two):
        return swapped(two, "exp", 4, 2)

    def across(self, two):
        return swapped(two, "exp", 1, 1)

def on_device(
    attn_query,
    attn_key,
    attn_value,
    log_decay,
    residual,
    norm_gain,
    expert_ids,
    router_weight,
    gate_weight,
    up_weight,
    down_weight,
):
    heads_here, length = log_decay.shape
    groups = lax.axis_size("seq")
    shares = lax.axis_size("exp")
    width = attn_query.shape[1]
    experts_here = router_weight.shape[1]
    section = lax.axis_index("seq")
    inner = (section > 0) & (section < groups - 1)
    base = jnp.stack([section * experts_here, inner]).astype(jnp.int32)
    router_rows = router_weight.reshape(shares, width, experts_here).transpose(0, 2, 1)
    gate_rows = gate_weight.swapaxes(1, 2)
    up_rows = up_weight.swapaxes(1, 2)

    message, cumulative = section_state(attn_key, attn_value, log_decay)
    intra = intra_section(attn_query, attn_key, attn_value, log_decay, cumulative)
    incoming = incoming_state(message, heads_here)
    stream = make_stream(
        attn_query, intra, cumulative, incoming, residual, norm_gain, expert_ids.T
    )

    capacity = 4 * length // (experts_here * groups)
    choices = expert_ids.shape[1]

    def select(*parts):
        return select_slots(base, parts, capacity, choices, experts_here)

    weights = (router_rows, gate_rows, up_rows)
    if shares == 8 and groups == 4:
        pieces = paired_chunks(stream, select, weights, down_weight)
    else:
        order = jnp.arange(shares, dtype=jnp.int32)
        middle = shares // 2
        pieces = []
        for first in range(0, groups, 2):
            chunk = (first, first + 1)
            chosen = [
                select(swapped(stream, "seq", offset, offset) if offset else stream)
                for offset in chunk
            ]
            gathered = [lax.all_gather(slots, "exp", axis=0) for slots, _ in chosen]
            sums = gate_part(order[:middle], [[x[:middle]] for x in gathered], *weights)
            hidden = gate_part(order[middle:], [[x[middle:]] for x in gathered], *weights, sums)
            (partial,) = down_part([order], hidden, down_weight, width, len(chunk))
            for offset, share, (_, place) in zip(chunk, partial, chosen):
                share = lax.psum_scatter(share, "exp", scatter_dimension=0)
                piece = combine_slots(place, [share[None]])
                pieces.append(swapped(piece, "seq", offset, offset) if offset else piece)
    total = stream[:length].astype(F32)
    for piece in pieces:
        total = total + piece.astype(F32)
    return total.astype(BF16)


def paired_chunks(stream, select, weights, down_weight):
    plane = PairedPlane()
    width = stream.shape[1]
    tie = lax.optimization_barrier
    two, far_two, near, near_far, chosen = {}, {}, {}, {}, {}

    def across_middle(part):
        return lax.ppermute(part, "seq", [(1, 2), (2, 1)])

    def outward(part):
        return lax.ppermute(part, "seq", [(1, 0), (2, 3)])

    def gather(name, behind):
        two[name], _ = tie((plane.first(chosen[name][0]), behind))
        near[name] = plane.across(two[name])
        far_two[name] = plane.second(two[name])

    swap = swapped(stream, "seq", 1, 1)
    crossed = across_middle(stream)
    chosen["own"] = select(stream)
    gather("own", [])
    passed = outward(crossed)
    crossed_swap = across_middle(swap)
    chosen["neighbour"] = select(swap)
    gather("neighbour", [passed, crossed_swap, far_two["own"]])
    passed_fourth = outward(crossed_swap)
    chosen["third"] = select(crossed, passed)
    gather("third", [passed_fourth, far_two["neighbour"]])
    chosen["fourth"] = select(crossed_swap, passed_fourth)

    def gate(chunk, behind):
        early = [[two[name], near[name]] for name in chunk]
        return gate_part(plane.early, tie((early, behind))[0], *weights)

    def gate_last(chunk, sums, behind):
        late = [[far_two[name], near_far[name]] for name in chunk]
        (late, sums), _ = tie(((late, sums), behind))
        return gate_part(plane.late, late, *weights, sums)

    def down(plans, hidden, behind):
        hidden, _ = tie((hidden, behind))
        return down_part(plans, hidden, down_weight, width, 2)

    class Scatter:
        def __init__(self, name, theirs, mine):
            self.name, self.theirs, self.mine = name, theirs, mine

        def two_blocks(self, behind):
            self.near = plane.across(self.theirs)
            self.sent = added(self.mine[2:], self.near[2:])
            self.got_two = plane.second(tie((self.sent, behind))[0])

        def one_block(self, behind):
            got_two, _ = tie((self.got_two, behind))
            self.one = added(added(self.mine[1], self.near[1]), got_two[1])
            self.got_one = plane.once(self.one)

        def own_block(self, behind):
            got_one, _ = tie((self.got_one, behind))
            shares = [self.mine, self.near, self.got_two, got_one[None]]
            return combine_slots(chosen[self.name][1], shares)

    chunk = ("third", "neighbour")
    sums = gate(chunk, chosen["fourth"])
    gather("fourth", sums)
    for name in chunk:
        near_far[name] = plane.across(tie((far_two[name], sums))[0])
    hidden = gate_last(chunk, sums, two["fourth"])
    (theirs,) = down([plane.theirs], hidden, far_two["fourth"])
    (mine,) = down([plane.mine], hidden, theirs)
    third, neighbour = (Scatter(*shares) for shares in zip(chunk, theirs, mine))
    third.two_blocks([])

    chunk = ("fourth", "own")
    sums = gate(chunk, third.sent)
    for name in chunk:
        near_far[name] = plane.across(tie((far_two[name], third.sent))[0])
    third.one_block(sums)
    neighbour.two_blocks(third.one)
    hidden = gate_last(chunk, sums, [third.one, neighbour.sent])
    third_piece = third.own_block(hidden)
    third_home = lax.ppermute(third_piece, "seq", [(1, 2), (2, 1)])
    theirs, mine = down([plane.theirs, plane.mine], hidden, [third_piece, neighbour.got_two])
    neighbour.one_block(theirs)
    theirs, _ = tie((theirs, third_home))
    fourth, own = (Scatter(*shares) for shares in zip(chunk, theirs, mine))
    fourth.two_blocks([])
    third_far_home = lax.ppermute(tie((third_piece, third_home))[0], "seq", [(0, 2), (3, 1)])
    neighbour_piece = neighbour.own_block([])
    neighbour_home = swapped(neighbour_piece, "seq", 1, 1)
    fourth.one_block([third_far_home, neighbour.got_one])
    own.two_blocks([])
    fourth_piece = fourth.own_block([])
    own.one_block(fourth_piece)
    fourth_piece, _ = tie((fourth_piece, [third_far_home, neighbour_home]))
    return [
        own.own_block([]),
        neighbour_home,
        third_home,
        third_far_home,
        lax.ppermute(fourth_piece, "seq", [(1, 3), (2, 0)]),
        lax.ppermute(fourth_piece, "seq", [(0, 3), (3, 0)]),
    ]


def solution(mesh):
    in_specs = (
        P("seq", "exp"),
        P("seq", "exp"),
        P("seq", "exp"),
        P("exp", "seq"),
        P("seq", "exp"),
        P("exp"),
        P("seq", None),
        P(None, "seq"),
        P("seq", None, "exp"),
        P("seq", None, "exp"),
        P("seq", "exp", None),
    )
    out_specs = P("seq", "exp")
    return jax.shard_map(
        on_device, mesh=mesh, in_specs=in_specs, out_specs=out_specs, check_vma=False
    )
```
